32 devices in a mesh: dp: 4 (over y, core), seq: 8 (over z, x).
Axes of the slice: x: 2, y: 2, z: 4, core: 2. Of those that a mesh axis runs over, the one named last changes fastest.
Arguments:
- feats: bfloat16 [8, 1024, 1024], P('dp', 'seq'), may hold values from -6 to 6
- segments: int32 [8, 1024], P('dp'), may hold values from 0 to 4, as said below
- labels: int32 [8, 1024], P('dp', 'seq'), may hold values from 0 to 31
- conv_weight: bfloat16 [8192, 1024], replicated, may hold values from -0.0625 to 0.0625
- w_qkv: bfloat16 [1024, 3072], replicated, may hold values from -0.1875 to 0.1875
- w_out: bfloat16 [1024, 1024], replicated, may hold values from -1 to 1
- w_up: bfloat16 [1024, 4096], replicated, may hold values from -0.1875 to 0.1875
- w_down: bfloat16 [4096, 1024], replicated, may hold values from -0.09375 to 0.09375
- head_w: bfloat16 [1024, 32], replicated, may hold values from -0.375 to 0.375
- head_b: float32 [32], replicated, may hold values from -3 to 3
- gains: float32 [1024, 2], replicated, may hold values from 0.25 to 1.75
- biases: float32 [1024, 7], replicated, may hold values from -2 to 2
- up_bias: float32 [4096], replicated, may hold values from -2 to 2
Outputs:
- layer_out: bfloat16 [8, 1024, 1024], P('dp', 'seq')
- loss: float32 [], replicated
- grad_feats: float32 [8, 1024, 1024], P('dp', 'seq')
- grad_conv_weight: float32 [8192, 1024], P('seq')
- grad_w_qkv: float32 [1024, 3072], P('seq')
- grad_w_out: float32 [1024, 1024], P('seq')
- grad_w_up: float32 [1024, 4096], P('seq')
- grad_w_down: float32 [4096, 1024], P('seq')
- grad_head_w: float32 [1024, 32], P('seq')
- grad_head_b: float32 [32], replicated
- grad_gains: float32 [1024, 2], P('seq')
- grad_biases: float32 [1024, 7], P('seq')
- grad_up_bias: float32 [4096], P('seq')
The draws below stay inside these ranges and needn't reach their ends.
Inputs may be any that keep to these rules, and one draw needn't show every extreme that they name: `segments`: along each row the numbers begin at 0 and rise by 0 or 1 from one frame to the next, up to at most 4; of the 2 rows on each index of dp, one, drawn from the seed, is a single utterance (all 0).
All inputs are finite; a program needn't handle non-finite values.
Results may differ from the reference program's by a relative error of at most 0.015.
Values may be sent and summed in bfloat16 or wider, within the bound.
No kernel may reach another device: no remote copies, remote signals or barrier semaphores. Data moves between devices by JAX's collectives and lax.ppermute only.
A program may use at most 576 MiB of HBM per device.

```python
import jax
import jax.numpy as jnp
from jax import lax

D = 1024
HEADS = 16
FF = 4096
GROUPS = 16
KERNEL = 128
VOCAB = 32
TOK_ROW = 128
ROWS = 2
BATCH = 8
LENGTH = 1024
N_SEQ = 8


def draw_segments(key, part):
    key = jax.random.fold_in(key, 11)
    start_key, pick_key = jax.random.split(key)
    starts = jax.random.randint(start_key, (BATCH, LENGTH), 0, TOK_ROW) == 0
    starts = jnp.logical_and(starts, jnp.arange(LENGTH)[None, :] > 0)
    numbers = jnp.minimum(jnp.cumsum(starts.astype(jnp.int32), axis=1), N_SEQ // 2)
    chosen = jax.random.randint(pick_key, (BATCH // ROWS, 1), 0, ROWS)
    row_place = (jnp.arange(BATCH) % ROWS).reshape(BATCH // ROWS, ROWS)
    single = (row_place == chosen).reshape(BATCH, 1)
    return jnp.where(single, 0, numbers).astype(jnp.int32)


def set_ends(drawn, stream_key, smallest, top_value):
    extent = drawn.shape
    spot = [jax.random.randint(jax.random.fold_in(stream_key, axis), (), 0, extent[axis]) for axis in range(len(extent))]
    drawn = drawn.at[tuple(spot)].set(smallest)
    longest = extent.index(max(extent))
    spot[longest] = (spot[longest] + 1) % extent[longest]
    return drawn.at[tuple(spot)].set(top_value)


def steps_of(rng, shape, pieces, smallest, top_value):
    def one(dim, shards_of):
        draws = jax.random.uniform(jax.random.fold_in(jax.random.fold_in(rng, 6), dim), (shards_of,), jnp.float32, smallest / len(pieces), top_value / len(pieces))
        return jnp.repeat(jnp.exp(draws), shape[dim] // shards_of).reshape((-1,) + (1,) * (len(shape) - dim - 1))

    gain = one(*pieces[0])
    for cut in pieces[1:]:
        gain = gain * one(*cut)
    return gain


def normal_values(key, shape, width, bound, shards=(), kind=jnp.bfloat16):
    values = jax.random.normal(key, shape, jnp.float32) * width
    if len(shards) > 0:
        values = steps_of(key, shape, shards, -0.22, 0.18) * values
    return jnp.clip(values, min=-bound, max=bound).astype(kind)


def setup_inputs(seed: int = 0) -> dict:
    streams_of = jax.random.split(jax.random.key(seed), 14)
    return {
        "feats": normal_values(streams_of[0], (BATCH, LENGTH, D), 1.0, 6.0, ((0, 4), (1, 8))),
        "segments": draw_segments(jax.random.fold_in(streams_of[13], 71), 0),
        "labels": set_ends(jax.random.randint(streams_of[2], (BATCH, LENGTH), 0, VOCAB), jax.random.fold_in(streams_of[2], 1), 0, VOCAB - 1).astype(jnp.int32),
        "conv_weight": normal_values(streams_of[3], (KERNEL * D // GROUPS, D), (KERNEL * D // GROUPS) ** -0.5, 0.0625),
        "w_qkv": normal_values(streams_of[4], (D, 3 * D), D ** -0.5, 0.1875),
        "w_out": normal_values(streams_of[5], (D, D), (D // 32) ** -0.5, 1.0),
        "w_up": normal_values(streams_of[6], (D, FF), D ** -0.5, 0.1875),
        "w_down": normal_values(streams_of[7], (FF, D), FF ** -0.5, 0.09375),
        "head_w": normal_values(streams_of[8], (D, VOCAB), (D // 4) ** -0.5, 0.375),
        "head_b": normal_values(streams_of[9], (VOCAB,), 0.5, 3.0, (), jnp.float32),
        "gains": jnp.clip(1.0 + 0.15 * jax.random.normal(streams_of[10], (D, 2), jnp.float32), 0.25, 1.75),
        "biases": normal_values(streams_of[11], (D, 7), 0.3, 2.0, (), jnp.float32),
        "up_bias": normal_values(streams_of[12], (FF,), 0.3, 2.0, (), jnp.float32),
    }


epsilon = 1e-05
masked_score = -1e+30
highest = lax.Precision.HIGHEST

@jax.custom_vjp
def low(v):
    return lax.optimization_barrier(v.astype(jnp.bfloat16)).astype(jnp.float32)

@jax.custom_vjp
def low_back(v):
    return v

def low_keep(v):
    return (low(v), None)

def low_pass(kept, grad):
    return (grad,)

def back_keep(v):
    return (v, None)

def back_low(kept, grad):
    return (low(grad),)
low.defvjp(low_keep, low_pass)
low_back.defvjp(back_keep, back_low)

def layer_norm(values, gain_row, shift_row):
    center = values - lax.optimization_barrier(jnp.mean(values, axis=-1, keepdims=True))
    spread = lax.optimization_barrier(jnp.mean(center * center, axis=-1, keepdims=True))
    return center * lax.rsqrt(spread + epsilon) * gain_row + shift_row

def matmul(left_side, right_side):
    return jnp.dot(left_side, right_side, precision=highest, preferred_element_type=jnp.float32)

def conv_term(feat_row, seg_row, conv_weight):
    frames, features = feat_row.shape
    group_width = features // GROUPS
    tap_count = conv_weight.shape[0] // group_width
    rim_width = tap_count // 2
    padded = jnp.pad(feat_row, ((rim_width, rim_width), (0, 0)))
    seg_padded = jnp.pad(seg_row, (rim_width, rim_width), constant_values=-1)
    grouped = conv_weight.reshape(tap_count, group_width, GROUPS, group_width)

    def one_block(running, tap_block):
        windows = []
        for tap_inner in range(8):
            offset = tap_block * 8 + tap_inner
            window = lax.dynamic_slice_in_dim(padded, offset, frames, 0)
            near_ids = lax.dynamic_slice_in_dim(seg_padded, offset, frames, 0)
            windows.append(jnp.where((near_ids == seg_row)[:, None], window, jnp.zeros_like(window)))
        stacked = jnp.stack(windows, axis=1).reshape(frames, 8, GROUPS, group_width)
        weight_part = lax.dynamic_slice_in_dim(grouped, tap_block * 8, 8, 0)
        return (running + jnp.einsum('tkgi,kigo->tgo', stacked, weight_part, precision=highest), None)
    start_sum = jnp.zeros((frames, GROUPS, group_width), jnp.float32)
    running, unused = lax.scan(jax.checkpoint(one_block), start_sum, jnp.arange(tap_count // 8, dtype=jnp.int32))
    return running.reshape(frames, features)

def attend_rows(queries, keys, values, seg_row):
    frames, head_count, head_width = queries.shape
    score_scale = head_width ** (-0.5)
    block_rows = 512 if frames % 512 == 0 else frames

    def one_block(block_index):
        query_block = lax.dynamic_slice_in_dim(queries, block_index * block_rows, block_rows, 0)
        seg_block = lax.dynamic_slice_in_dim(seg_row, block_index * block_rows, block_rows, 0)
        scores = low_back(score_scale * jnp.einsum('qhe,khe->qhk', query_block, keys, precision=highest))
        allowed = (seg_block[:, None] == seg_row[None, :])[:, None, :]
        scores = jnp.where(allowed, scores, masked_score)
        row_top = lax.optimization_barrier(jnp.max(scores, axis=-1, keepdims=True))
        weights = jnp.where(allowed, jnp.exp(scores - row_top), 0.0)
        probs = weights / lax.optimization_barrier(jnp.sum(weights, axis=-1, keepdims=True))
        return jnp.einsum('qhk,khe->qhe', low(probs), values, precision=highest)
    blocks = lax.map(jax.checkpoint(one_block), jnp.arange(frames // block_rows, dtype=jnp.int32))
    return blocks.reshape(frames, head_count, head_width)

def gelu_exact(values):
    return jax.nn.gelu(values, approximate=False)

def row_forward(weights_all, feat_row, seg_row, label_row):
    conv_weight, w_qkv, w_out, w_up, w_down, head_w, head_b, gains, biases, up_bias = weights_all
    frames, features = feat_row.shape
    head_width = features // HEADS
    conv_sum = low_back(conv_term(feat_row, seg_row, conv_weight) + biases[:, 0])
    position = feat_row + gelu_exact(conv_sum)
    normed = low(layer_norm(position, gains[:, 0], biases[:, 1]))
    qkv_bias = jnp.concatenate([biases[:, 2], jnp.zeros((features,), jnp.float32), biases[:, 3]])
    mixed = low(low_back(matmul(normed, w_qkv) + qkv_bias))
    queries = mixed[:, :features].reshape(frames, HEADS, head_width)
    keys = mixed[:, features:2 * features].reshape(frames, HEADS, head_width)
    values = mixed[:, 2 * features:].reshape(frames, HEADS, head_width)
    attended = attend_rows(queries, keys, values, seg_row).reshape(frames, features)
    attended = low(low_back(attended))
    resid = position + low_back(matmul(attended, w_out) + biases[:, 4])
    normed_second = low(layer_norm(resid, gains[:, 1], biases[:, 5]))
    up_sum = low_back(matmul(normed_second, w_up) + up_bias)
    active = low(gelu_exact(up_sum))
    output = resid + low_back(matmul(active, w_down) + biases[:, 6])
    logits = low_back(matmul(low(output), head_w) + head_b)
    row_top = lax.optimization_barrier(jnp.max(logits, axis=-1, keepdims=True))
    log_sum = row_top[:, 0] + jnp.log(lax.optimization_barrier(jnp.sum(jnp.exp(logits - row_top), axis=-1)))
    onehot = label_row[:, None] == jnp.arange(VOCAB, dtype=jnp.int32)[None, :]
    picked = lax.optimization_barrier(jnp.sum(jnp.where(onehot, logits, 0.0), axis=-1))
    return (jnp.sum(log_sum - picked), output)

def reference(feats, segments, labels, conv_weight, w_qkv, w_out, w_up, w_down, head_w, head_b, gains, biases, up_bias):
    weights_all = tuple((item.astype(jnp.float32) for item in (conv_weight, w_qkv, w_out, w_up, w_down, head_w, head_b, gains, biases, up_bias)))

    def one_row(running, inputs):
        feat_row, seg_row, label_row = inputs

        def forward(weight_set, feat_values):
            return row_forward(weight_set, feat_values, seg_row, label_row)
        (row_loss, output), pull = jax.vjp(forward, weights_all, feat_row.astype(jnp.float32))
        grad_weights, grad_feat = pull((jnp.ones((), jnp.float32), jnp.zeros_like(output)))
        running = jax.tree.map(jnp.add, running, (grad_weights, row_loss))
        return (running, (output.astype(jnp.bfloat16), grad_feat))
    start_sums = (tuple((jnp.zeros_like(item) for item in weights_all)), jnp.zeros((), jnp.float32))
    (grad_weights, loss_sum), (layer_out, grad_feats) = lax.scan(one_row, start_sums, (feats, segments, labels))
    loss = loss_sum / (BATCH * LENGTH)
    return (layer_out, loss, grad_feats, grad_weights[0], grad_weights[1], grad_weights[2], grad_weights[3], grad_weights[4], grad_weights[5], grad_weights[6], grad_weights[7], grad_weights[8], grad_weights[9])
```

```python
from functools import partial
import math

import jax
import jax.numpy as jnp
from jax import lax
from jax.experimental import pallas as pl
from jax.experimental.pallas import tpu as pltpu
from jax.sharding import Mesh, PartitionSpec as P

HEADS = 16
GROUPS = 16
KERNEL = 128
VOCAB = 32
TAP_BLOCKS = 33
VMEM_LIMIT = 56 * 1024 * 1024


epsilon = 1e-05
masked_score = -1e30
tap_group = 8


def extended(cells, sides, width):
    for axis, dim in sides:
        count = lax.axis_size(axis)
        ends = count - 1
        head = lax.slice_in_dim(cells, 0, width, axis=dim)
        tail = lax.slice_in_dim(cells, cells.shape[dim] - width, cells.shape[dim], axis=dim)
        cells = jnp.concatenate(
            [
                lax.ppermute(tail, axis, [(i, (i + 1) % count) for i in range(ends)]),
                cells,
                lax.ppermute(head, axis, [((i + 1) % count, i) for i in range(ends)]),
            ],
            axis=dim,
        )
    return cells


def layer_norm(values, gain_row, shift_row):
    center = values - jnp.mean(values, axis=-1, keepdims=True)
    spread = jnp.mean(center * center, axis=-1, keepdims=True)
    return center * lax.rsqrt(spread + epsilon) * gain_row + shift_row


def gelu_exact(values):
    return jax.nn.gelu(values, approximate=False)


def outer_sum(left_side, right_side):
    return lax.dot_general(
        left_side, right_side, (((0,), (0,)), ((), ())), preferred_element_type=jnp.float32
    )


def back_product(grad_rows, weight):
    return lax.dot_general(
        grad_rows, weight, (((1,), (1,)), ((), ())), preferred_element_type=jnp.float32
    )


def masked_windows(source, seg_padded, seg_local, offsets, frames):
    windows = []
    for offset in offsets:
        window = lax.dynamic_slice_in_dim(source, offset, frames, 1)
        near_ids = lax.dynamic_slice_in_dim(seg_padded, offset, frames, 1)
        keep_mask = (near_ids == seg_local)[:, :, None]
        windows.append(jnp.where(keep_mask, window, jnp.zeros_like(window)))
    return jnp.stack(windows, axis=2)


def conv_forward(feats_rim, seg_padded, seg_local, conv_weight):
    row_count, frames = seg_local.shape
    features = feats_rim.shape[2]
    group_width = features // GROUPS
    tap_count = conv_weight.shape[0] // group_width
    grouped = conv_weight.reshape(tap_count, group_width, GROUPS, group_width)

    def one_block(tap_block, running):
        offsets = [tap_block * tap_group + tap_inner for tap_inner in range(tap_group)]
        stacked = masked_windows(feats_rim, seg_padded, seg_local, offsets, frames)
        stacked = stacked.reshape(row_count, frames, tap_group, GROUPS, group_width)
        weight_part = lax.dynamic_slice_in_dim(grouped, tap_block * tap_group, tap_group, 0)
        return running + jnp.einsum(
            "rtkgi,kigo->rtgo", stacked, weight_part, preferred_element_type=jnp.float32
        )

    start_sum = jnp.zeros((row_count, frames, GROUPS, group_width), jnp.float32)
    running = lax.fori_loop(0, tap_count // tap_group, one_block, start_sum)
    return running.reshape(row_count, frames, features)


def conv_weight_grad(feats_rim, seg_padded, seg_local, grad_conv_low, tap_count):
    row_count, frames = seg_local.shape
    features = feats_rim.shape[2]
    group_width = features // GROUPS
    grad_grouped = grad_conv_low.reshape(row_count, frames, GROUPS, group_width)

    def one_block(tap_block, running):
        offsets = [tap_block * tap_group + tap_inner for tap_inner in range(tap_group)]
        stacked = masked_windows(feats_rim, seg_padded, seg_local, offsets, frames)
        stacked = stacked.reshape(row_count, frames, tap_group, GROUPS, group_width)
        block_grad = jnp.einsum(
            "rtkgi,rtgo->kigo", stacked, grad_grouped, preferred_element_type=jnp.float32
        )
        return lax.dynamic_update_slice_in_dim(running, block_grad, tap_block * tap_group, 0)

    start_sum = jnp.zeros((tap_count, group_width, GROUPS, group_width), jnp.float32)
    running = lax.fori_loop(0, tap_count // tap_group, one_block, start_sum)
    return running.reshape(tap_count * group_width, features)


def conv_input_grad(grad_rim, seg_padded, seg_local, conv_weight):
    row_count, frames = seg_local.shape
    features = grad_rim.shape[2]
    group_width = features // GROUPS
    tap_count = conv_weight.shape[0] // group_width
    grouped = conv_weight.reshape(tap_count, group_width, GROUPS, group_width)

    def one_block(tap_block, running):
        offsets = [
            tap_count - (tap_block * tap_group + tap_inner) for tap_inner in range(tap_group)
        ]
        stacked = masked_windows(grad_rim, seg_padded, seg_local, offsets, frames)
        stacked = stacked.reshape(row_count, frames, tap_group, GROUPS, group_width)
        weight_part = lax.dynamic_slice_in_dim(grouped, tap_block * tap_group, tap_group, 0)
        return running + jnp.einsum(
            "rtkgo,kigo->rtgi", stacked, weight_part, preferred_element_type=jnp.float32
        )

    start_sum = jnp.zeros((row_count, frames, GROUPS, group_width), jnp.float32)
    running = lax.fori_loop(0, tap_count // tap_group, one_block, start_sum)
    return running.reshape(row_count, frames, features)


def span_size(piece_rows, frames):
    return math.gcd(piece_rows, 8 * frames)


def attend_row(row_state, query_row, key_row, value_row, seg_query, seg_key, score_scale):
    running_max, running_sum, weighted = row_state
    scores = score_scale * jnp.einsum(
        "qhe,khe->qhk", query_row, key_row, preferred_element_type=jnp.float32
    )
    allowed = (seg_query[:, None] == seg_key[None, :])[:, None, :]
    scores = jnp.where(allowed, scores, masked_score)
    new_max = jnp.maximum(running_max, jnp.max(scores, axis=-1))
    rescale = jnp.exp(running_max - new_max)
    weights = jnp.where(allowed, jnp.exp(scores - new_max[:, :, None]), 0.0)
    running_sum = running_sum * rescale + jnp.sum(weights, axis=-1)
    weighted = weighted * rescale[:, :, None] + jnp.einsum(
        "qhk,khe->qhe", weights.astype(jnp.bfloat16), value_row, preferred_element_type=jnp.float32
    )
    return (new_max, running_sum, weighted)


def query_grad_row(
    grad_query,
    query_row,
    key_row,
    value_row,
    seg_query,
    seg_key,
    lse_row,
    dots_row,
    grad_row,
    score_scale,
):
    scores = score_scale * jnp.einsum(
        "qhe,khe->qhk", query_row, key_row, preferred_element_type=jnp.float32
    )
    allowed = (seg_query[:, None] == seg_key[None, :])[:, None, :]
    probs = jnp.where(allowed, jnp.exp(scores - lse_row[:, :, None]), 0.0)
    grad_probs = jnp.einsum("qhe,khe->qhk", grad_row, value_row, preferred_element_type=jnp.float32)
    grad_scores = (probs * (grad_probs - dots_row[:, :, None])).astype(jnp.bfloat16)
    return grad_query + score_scale * jnp.einsum(
        "qhk,khe->qhe", grad_scores, key_row, preferred_element_type=jnp.float32
    )


def key_grad_row(
    grads_pair,
    key_row,
    value_row,
    query_row,
    grad_row,
    lse_row,
    dots_row,
    seg_query,
    seg_key,
    score_scale,
):
    scores = score_scale * jnp.einsum(
        "qhe,khe->qhk", query_row, key_row, preferred_element_type=jnp.float32
    )
    allowed = (seg_query[:, None] == seg_key[None, :])[:, None, :]
    probs = jnp.where(allowed, jnp.exp(scores - lse_row[:, :, None]), 0.0)
    grad_value = jnp.einsum(
        "qhk,qhe->khe", probs.astype(jnp.bfloat16), grad_row, preferred_element_type=jnp.float32
    )
    grad_probs = jnp.einsum("qhe,khe->qhk", grad_row, value_row, preferred_element_type=jnp.float32)
    grad_scores = (probs * (grad_probs - dots_row[:, :, None])).astype(jnp.bfloat16)
    grad_key = score_scale * jnp.einsum(
        "qhk,qhe->khe", grad_scores, query_row, preferred_element_type=jnp.float32
    )
    return (grad_key, grad_value)


def body(
    feats,
    segments,
    labels,
    conv_weight,
    w_qkv,
    w_out,
    w_up,
    w_down,
    head_w,
    head_b,
    gains,
    biases,
    up_bias,
):
    row_count, frames, features = feats.shape
    head_count = HEADS
    head_width = features // head_count
    score_scale = head_width ** (-0.5)
    tokens = row_count * frames
    tap_count = KERNEL
    rim_width = tap_count // 2
    own_first = lax.axis_index("seq") * frames
    seg_local = lax.dynamic_slice_in_dim(segments, own_first, frames, 1)
    seg_wide = jnp.pad(segments, ((0, 0), (rim_width, rim_width)), constant_values=-1)
    seg_padded = lax.dynamic_slice_in_dim(seg_wide, own_first, frames + 2 * rim_width, 1)
    feats_rim = extended(feats, (("seq", 1),), rim_width)
    conv_sum = conv_forward(feats_rim, seg_padded, seg_local, conv_weight) + biases[:, 0]
    activated, conv_pull = jax.vjp(gelu_exact, conv_sum)
    position = feats.astype(jnp.float32) + activated
    normed, first_pull = jax.vjp(layer_norm, position, gains[:, 0], biases[:, 1])
    normed_low = normed.astype(jnp.bfloat16).reshape(tokens, features)
    qkv_bias = jnp.concatenate([biases[:, 2], jnp.zeros((features,), jnp.float32), biases[:, 3]])
    mixed = (jnp.dot(normed_low, w_qkv, preferred_element_type=jnp.float32) + qkv_bias).astype(
        jnp.bfloat16
    )
    queries = mixed[:, :features].reshape(row_count, frames, head_count, head_width)
    keys = mixed[:, features : 2 * features].reshape(row_count, frames, features)
    values = mixed[:, 2 * features :].reshape(row_count, frames, features)
    start_state = (
        jnp.full((row_count, frames, head_count), masked_score, jnp.float32),
        jnp.zeros((row_count, frames, head_count), jnp.float32),
        jnp.zeros((row_count, frames, head_count, head_width), jnp.float32),
    )
    key_shard = lax.all_gather(keys, "seq", axis=1, tiled=True)
    value_shard = lax.all_gather(values, "seq", axis=1, tiled=True)
    piece_rows = key_shard.shape[1]
    span = span_size(piece_rows, frames)

    def forward_one_span(span_index, state):
        offset = span_index * span
        key_part = lax.dynamic_slice_in_dim(key_shard, offset, span, 1)
        value_part = lax.dynamic_slice_in_dim(value_shard, offset, span, 1)
        seg_keys = lax.dynamic_slice_in_dim(segments, offset, span, 1)
        results = []
        for row_index in range(row_count):
            action = partial(
                attend_row,
                query_row=queries[row_index],
                key_row=key_part[row_index].reshape(span, head_count, head_width),
                value_row=value_part[row_index].reshape(span, head_count, head_width),
                seg_query=seg_local[row_index],
                seg_key=seg_keys[row_index],
                score_scale=score_scale,
            )
            row_state = (state[0][row_index], state[1][row_index], state[2][row_index])
            results.append(action(row_state))
        return (
            jnp.stack([item[0] for item in results]),
            jnp.stack([item[1] for item in results]),
            jnp.stack([item[2] for item in results]),
        )

    running_max, running_sum, weighted = lax.fori_loop(
        0, piece_rows // span, forward_one_span, start_state
    )
    attended = weighted / running_sum[:, :, :, None]
    log_total = running_max + jnp.log(running_sum)
    attended_low = attended.reshape(tokens, features).astype(jnp.bfloat16)
    resid = (
        position.reshape(tokens, features)
        + jnp.dot(attended_low, w_out, preferred_element_type=jnp.float32)
        + biases[:, 4]
    )
    normed_second, second_pull = jax.vjp(layer_norm, resid, gains[:, 1], biases[:, 5])
    second_low = normed_second.astype(jnp.bfloat16)
    up_sum = jnp.dot(second_low, w_up, preferred_element_type=jnp.float32) + up_bias
    up_active, up_pull = jax.vjp(gelu_exact, up_sum)
    active_low = up_active.astype(jnp.bfloat16)
    output = resid + jnp.dot(active_low, w_down, preferred_element_type=jnp.float32) + biases[:, 6]
    output_low = output.astype(jnp.bfloat16)
    logits = jnp.dot(output_low, head_w, preferred_element_type=jnp.float32) + head_b
    row_top = jnp.max(logits, axis=-1, keepdims=True)
    shifted = jnp.exp(logits - row_top)
    exp_sums = jnp.sum(shifted, axis=-1, keepdims=True)
    onehot = labels.reshape(tokens)[:, None] == jnp.arange(VOCAB, dtype=jnp.int32)[None, :]
    picked = jnp.sum(jnp.where(onehot, logits, 0.0), axis=-1)
    local_loss = jnp.sum(row_top[:, 0] + jnp.log(exp_sums[:, 0]) - picked)
    grad_logits = (shifted / exp_sums - onehot.astype(jnp.float32)).astype(jnp.bfloat16)
    grad_head_w = outer_sum(output_low, grad_logits)
    grad_head_b = jnp.sum(grad_logits.astype(jnp.float32), axis=0)
    grad_output = back_product(grad_logits, head_w)
    grad_output_low = grad_output.astype(jnp.bfloat16)
    grad_w_down = outer_sum(active_low, grad_output_low)
    grad_down_bias = jnp.sum(grad_output_low.astype(jnp.float32), axis=0)
    grad_active = back_product(grad_output_low, w_down)
    grad_up_low = up_pull(grad_active)[0].astype(jnp.bfloat16)
    grad_w_up = outer_sum(second_low, grad_up_low)
    grad_up_bias = jnp.sum(grad_up_low.astype(jnp.float32), axis=0)
    grad_second = back_product(grad_up_low, w_up)
    grad_resid_part, grad_gain_second, grad_shift_second = second_pull(grad_second)
    grad_resid = grad_output + grad_resid_part
    grad_branch_low = grad_resid.astype(jnp.bfloat16)
    grad_w_out = outer_sum(attended_low, grad_branch_low)
    grad_out_bias = jnp.sum(grad_branch_low.astype(jnp.float32), axis=0)
    grad_attended = back_product(grad_branch_low, w_out).astype(jnp.bfloat16)
    grad_heads = grad_attended.reshape(row_count, frames, head_count, head_width)
    head_dots = jnp.sum(grad_heads.astype(jnp.float32) * attended, axis=-1)
    zero_grads = jnp.zeros((row_count, frames, head_count, head_width), jnp.float32)
    all_keys, all_values = (
        lax.all_gather(keys, "seq", axis=1, tiled=True),
        lax.all_gather(values, "seq", axis=1, tiled=True),
    )
    length = all_keys.shape[1]
    key_span = 8 * frames

    def query_block(block_index, grad_query):
        first_row = block_index * key_span
        key_block = lax.dynamic_slice_in_dim(all_keys, first_row, key_span, 1)
        value_block = lax.dynamic_slice_in_dim(all_values, first_row, key_span, 1)
        seg_keys = lax.dynamic_slice_in_dim(segments, first_row, key_span, 1)
        results = []
        for row_index in range(row_count):
            action = partial(
                query_grad_row,
                query_row=queries[row_index],
                key_row=key_block[row_index].reshape(key_span, head_count, head_width),
                value_row=value_block[row_index].reshape(key_span, head_count, head_width),
                seg_query=seg_local[row_index],
                seg_key=seg_keys[row_index],
                lse_row=log_total[row_index],
                dots_row=head_dots[row_index],
                grad_row=grad_heads[row_index],
                score_scale=score_scale,
            )
            results.append(action(grad_query[row_index]))
        return jnp.stack(results)

    grad_queries = lax.fori_loop(0, length // key_span, query_block, zero_grads)

    def key_term(piece_rows):
        span = math.gcd(piece_rows, key_span)

        def key_one_span(span_index, gathered_terms):
            offset = span_index * span
            key_block = lax.dynamic_slice_in_dim(all_keys, offset, span, 1)
            value_block = lax.dynamic_slice_in_dim(all_values, offset, span, 1)
            seg_keys = lax.dynamic_slice_in_dim(segments, offset, span, 1)
            empty_row = jnp.zeros((span, head_count, head_width), jnp.float32)
            results = []
            for row_index in range(row_count):
                action = partial(
                    key_grad_row,
                    key_row=key_block[row_index].reshape(span, head_count, head_width),
                    value_row=value_block[row_index].reshape(span, head_count, head_width),
                    query_row=queries[row_index],
                    grad_row=grad_heads[row_index],
                    lse_row=log_total[row_index],
                    dots_row=head_dots[row_index],
                    seg_query=seg_local[row_index],
                    seg_key=seg_keys[row_index],
                    score_scale=score_scale,
                )
                results.append(action((empty_row, empty_row)))
            key_part = jnp.stack([item[0] for item in results], axis=1).reshape(
                span, row_count, features
            )
            value_part = jnp.stack([item[1] for item in results], axis=1).reshape(
                span, row_count, features
            )
            both_parts = jnp.concatenate([key_part, value_part], axis=2)
            return lax.dynamic_update_slice_in_dim(gathered_terms, both_parts, offset, 0)

        empty_terms = jnp.zeros((piece_rows, row_count, 2 * features), jnp.float32)
        return lax.fori_loop(0, piece_rows // span, key_one_span, empty_terms)

    both_grads = lax.psum_scatter(
        key_term(frames * lax.axis_size("seq")), "seq", scatter_dimension=0, tiled=True
    )
    grad_keys = jnp.transpose(both_grads[:, :, :features], (1, 0, 2)).reshape(
        row_count, frames, head_count, head_width
    )
    grad_values = jnp.transpose(both_grads[:, :, features:], (1, 0, 2)).reshape(
        row_count, frames, head_count, head_width
    )
    grad_mixed = jnp.concatenate(
        [
            grad_queries.reshape(tokens, features),
            grad_keys.reshape(tokens, features),
            grad_values.reshape(tokens, features),
        ],
        axis=1,
    ).astype(jnp.bfloat16)
    grad_w_qkv = outer_sum(normed_low, grad_mixed)
    mixed_sums = jnp.sum(grad_mixed.astype(jnp.float32), axis=0)
    grad_normed = back_product(grad_mixed, w_qkv).reshape(row_count, frames, features)
    grad_position_part, grad_gain_first, grad_shift_first = first_pull(grad_normed)
    grad_position = grad_resid.reshape(row_count, frames, features) + grad_position_part
    grad_conv_low = conv_pull(grad_position)[0].astype(jnp.bfloat16)
    grad_conv_bias = jnp.sum(grad_conv_low.astype(jnp.float32), axis=(0, 1))
    grad_conv_weight = conv_weight_grad(feats_rim, seg_padded, seg_local, grad_conv_low, tap_count)
    grad_rim = extended(grad_conv_low, (("seq", 1),), rim_width)
    grad_feats = grad_position + conv_input_grad(grad_rim, seg_padded, seg_local, conv_weight)
    grad_gains = jnp.stack([grad_gain_first, grad_gain_second], axis=1)
    grad_biases = jnp.stack(
        [
            grad_conv_bias,
            grad_shift_first,
            mixed_sums[:features],
            mixed_sums[2 * features :],
            grad_out_bias,
            grad_shift_second,
            grad_down_bias,
        ],
        axis=1,
    )
    shared = (
        lax.psum_scatter(grad_conv_weight, "seq", scatter_dimension=0, tiled=True),
        lax.psum_scatter(grad_w_qkv, "seq", scatter_dimension=0, tiled=True),
        lax.psum_scatter(grad_w_out, "seq", scatter_dimension=0, tiled=True),
        lax.psum_scatter(grad_w_up, "seq", scatter_dimension=0, tiled=True),
        lax.psum_scatter(grad_w_down, "seq", scatter_dimension=0, tiled=True),
        lax.psum_scatter(grad_head_w, "seq", scatter_dimension=0, tiled=True),
        lax.psum_scatter(grad_gains, "seq", scatter_dimension=0, tiled=True),
        lax.psum_scatter(grad_biases, "seq", scatter_dimension=0, tiled=True),
        lax.psum_scatter(grad_up_bias, "seq", scatter_dimension=0, tiled=True),
    )
    summed = (
        lax.psum(shared[0].astype(jnp.bfloat16), "dp").astype(jnp.float32),
        lax.psum(shared[1].astype(jnp.bfloat16), "dp").astype(jnp.float32),
        lax.psum(shared[2].astype(jnp.bfloat16), "dp").astype(jnp.float32),
        lax.psum(shared[3].astype(jnp.bfloat16), "dp").astype(jnp.float32),
        lax.psum(shared[4].astype(jnp.bfloat16), "dp").astype(jnp.float32),
        lax.psum(shared[5].astype(jnp.bfloat16), "dp").astype(jnp.float32),
        lax.psum(shared[6].astype(jnp.bfloat16), "dp").astype(jnp.float32),
        lax.psum(shared[7].astype(jnp.bfloat16), "dp").astype(jnp.float32),
        lax.psum(shared[8].astype(jnp.bfloat16), "dp").astype(jnp.float32),
    )
    loss_total, head_bias_total = lax.psum((local_loss, grad_head_b), ("dp", "seq"))
    loss = loss_total / (tokens * lax.axis_size("dp") * lax.axis_size("seq"))
    layer_out = output_low.reshape(row_count, frames, features)
    return (
        layer_out,
        loss,
        grad_feats,
        summed[0],
        summed[1],
        summed[2],
        summed[3],
        summed[4],
        summed[5],
        head_bias_total,
        summed[6],
        summed[7],
        summed[8],
    )


def whole_solution(mesh):
    placed = (
        P("dp", "seq", None),
        P("dp", None),
        P("dp", "seq"),
        P(),
        P(),
        P(),
        P(),
        P(),
        P(),
        P(),
        P(),
        P(),
        P(),
    )
    return jax.shard_map(
        body,
        mesh=mesh,
        in_specs=placed,
        out_specs=(
            P("dp", "seq", None),
            P(),
            P("dp", "seq", None),
            P("seq", None),
            P("seq", None),
            P("seq", None),
            P("seq", None),
            P("seq", None),
            P("seq", None),
            P(),
            P("seq", None),
            P("seq", None),
            P("seq"),
        ),
        check_vma=False,
    )


def tile_lists(seg_ext, rise):
    row_count = seg_ext.shape[0]
    frames = seg_ext.shape[1] - KERNEL
    tiles = frames // 64
    center = seg_ext[:, KERNEL // 2 : KERNEL // 2 + frames].reshape(row_count, tiles, 64)
    first = center[:, :, 0].reshape(-1)
    counts = (center[:, :, 63].reshape(-1) - first + 1).astype(jnp.int32)
    ends = jnp.cumsum(counts)
    slots = row_count * (tiles + rise)
    slot = jnp.arange(slots, dtype=jnp.int32)
    tile = jnp.sum((slot[:, None] >= ends[None, :]).astype(jnp.int32), axis=1)
    used = tile < row_count * tiles
    tile = jnp.minimum(tile, row_count * tiles - 1)
    onehot = tile[:, None] == jnp.arange(row_count * tiles, dtype=jnp.int32)[None, :]
    begin = jnp.sum(jnp.where(onehot, (ends - counts)[None, :], 0), axis=1)
    number = jnp.sum(jnp.where(onehot, first[None, :], 0), axis=1) + slot - begin
    number = jnp.where(used, number, -2)
    in_block = tile + (tile // tiles) * (KERNEL // 64)
    return in_block.astype(jnp.int32), tile.astype(jnp.int32), number.astype(jnp.int32)


def lane_low(rows):
    return lax.broadcasted_iota(jnp.int32, (rows, 128), 1) < 64


def half_roll(block):
    return pltpu.roll(block, 64, 1)


def quad_rows(src, rows, side):
    low = lane_low(rows)
    parts = [src[pl.ds(j, rows, stride=4), :] for j in range(4)]
    halves = []
    for a, b in ((0, 1), (2, 3)):
        if side == 0:
            halves.append(jnp.where(low, parts[a], half_roll(parts[b])))
        else:
            halves.append(jnp.where(low, half_roll(parts[a]), parts[b]))
    return halves


def conv_setup(meta, slots, seg_ref, flat, shifts, masks):
    rows4 = seg_ref.shape[0]
    blocks = rows4 // 16
    flat[0:rows4, :] = seg_ref[...]
    flat[rows4:, :] = jnp.zeros((16, 256), jnp.float32)
    for p in range(16):
        shifts[p] = flat[pl.ds(p, rows4), :].astype(jnp.bfloat16).reshape(blocks, 16, 256)

    @pl.loop(0, slots)
    def _(v):
        at = meta[1 + v]
        number = meta[1 + 2 * slots + v].astype(jnp.float32)
        row = pl.multiple_of(v * 16, 16)
        for b in range(TAP_BLOCKS):
            ids = shifts[b % 16, at + b // 16].astype(jnp.float32)
            masks[pl.ds(row, 16), b * 256 : (b + 1) * 256] = jnp.where(ids == number, 1.0, 0.0).astype(jnp.bfloat16)


def conv_patches(meta, slots, wide, side, flat, shifts, masks, patches):
    rows4 = shifts.shape[1] * 16
    halves = quad_rows(wide, rows4, side)
    flat[0:rows4, 0:128] = halves[0]
    flat[0:rows4, 128:256] = halves[1]
    for p in range(16):
        shifts[p] = flat[pl.ds(p, rows4), :].astype(jnp.bfloat16).reshape(rows4 // 16, 16, 256)

    @pl.loop(0, slots)
    def _(v):
        at = meta[1 + v]
        row = pl.multiple_of(v * 16, 16)
        for b in range(TAP_BLOCKS):
            span = slice(b * 256, (b + 1) * 256)
            patches[pl.ds(row, 16), span] = shifts[b % 16, at + b // 16] * masks[pl.ds(row, 16), span]


def conv_taps(w_ref, taps):
    low = lane_low(64)
    zero = jnp.zeros((64, 128), jnp.bfloat16)
    count = w_ref.shape[0] // 64
    for side in range(2):
        taps[side, 0:128, :] = jnp.zeros((128, 128), jnp.bfloat16)
        taps[side, 128 + w_ref.shape[0] + 64 :, :] = jnp.zeros(
            (taps.shape[1] - 192 - w_ref.shape[0], 128), jnp.bfloat16
        )
    first = w_ref[0:64, :]
    taps[0, 128:192, :] = jnp.where(low, first, zero)
    taps[1, 128:192, :] = jnp.where(low, half_roll(first), zero)
    last = w_ref[(count - 1) * 64 :, :]
    taps[0, 128 + count * 64 : 192 + count * 64, :] = jnp.where(low, zero, half_roll(last))
    taps[1, 128 + count * 64 : 192 + count * 64, :] = jnp.where(low, zero, last)

    @pl.loop(1, count, unroll=4)
    def _(k):
        here = w_ref[pl.ds(pl.multiple_of(k * 64, 64), 64), :]
        before = w_ref[pl.ds(pl.multiple_of((k - 1) * 64, 64), 64), :]
        to = pl.ds(pl.multiple_of(128 + k * 64, 64), 64)
        taps[0, to, :] = jnp.where(low, here, half_roll(before))
        taps[1, to, :] = jnp.where(low, half_roll(here), before)


def conv_kernel(slots, backward, meta, x_ref, seg_ref, w_ref, o_ref, wide, flat, shifts, masks, patches, taps, sums, outs):
    @pl.when(pl.program_id(0) == 0)
    def _():
        conv_setup(meta, slots, seg_ref, flat, shifts, masks)

    wide[...] = x_ref[...].astype(jnp.float32)
    conv_taps(w_ref, taps)
    out_rows = o_ref.shape[0] // 4
    for side in range(2):
        conv_patches(meta, slots, wide, side, flat, shifts, masks, patches)
        total = jnp.zeros((slots * 16, 256), jnp.float32)
        for b in range(TAP_BLOCKS):
            weight = jnp.concatenate(
                [taps[side, 128 + b * 256 : 384 + b * 256, :], taps[side, b * 256 : 256 + b * 256, :]], axis=1
            )
            if backward:
                c = TAP_BLOCKS - 1 - b
                total = total + lax.dot_general(
                    patches[:, c * 256 : (c + 1) * 256], weight, (((1,), (1,)), ((), ())),
                    preferred_element_type=jnp.float32,
                )
            else:
                total = total + jnp.dot(
                    patches[:, b * 256 : (b + 1) * 256], weight, preferred_element_type=jnp.float32
                )
        sums[...] = total

        @pl.loop(0, slots)
        def _(v):
            to = pl.ds(pl.multiple_of(meta[1 + slots + v] * 16, 16), 16)
            row = pl.ds(pl.multiple_of(v * 16, 16), 16)
            keep = masks[row, 16 * 256 : 17 * 256].astype(jnp.float32) > 0.5
            outs[side, to, :] = jnp.where(keep, sums[row, :], outs[side, to, :])

    low = lane_low(out_rows)
    for half in range(2):
        zero_side = outs[0, :, half * 128 : (half + 1) * 128]
        one_side = outs[1, :, half * 128 : (half + 1) * 128]
        o_ref[pl.ds(2 * half, out_rows, stride=4), :] = jnp.where(low, zero_side, half_roll(one_side))
        o_ref[pl.ds(2 * half + 1, out_rows, stride=4), :] = jnp.where(low, half_roll(zero_side), one_side)


def seg_quads(seg_ext):
    quads = seg_ext.astype(jnp.float32).reshape(-1, 4)
    return jnp.repeat(quads, 64, axis=1)


def grouped_conv(x_ext, seg_ext, weight, first_pair, rise, backward):
    row_count, length, width = x_ext.shape
    frames = length - KERNEL
    pairs = width // 128
    in_block, tile, number = tile_lists(seg_ext, rise)
    slots = in_block.shape[0]
    meta = jnp.concatenate([jnp.reshape(first_pair, (1,)).astype(jnp.int32), in_block, tile, number])
    rows4 = row_count * length // 4
    out4 = row_count * frames // 4
    depth = TAP_BLOCKS * 256
    return pl.pallas_call(
        partial(conv_kernel, slots, backward),
        grid_spec=pltpu.PrefetchScalarGridSpec(
            num_scalar_prefetch=1,
            grid=(pairs,),
            in_specs=[
                pl.BlockSpec((row_count * length, 128), lambda p, meta: (0, p)),
                pl.BlockSpec((rows4, 256), lambda p, meta: (0, 0)),
                pl.BlockSpec((weight.shape[0], 128), lambda p, meta: (0, meta[0] + p)),
            ],
            out_specs=pl.BlockSpec((row_count * frames, 128), lambda p, meta: (0, p)),
            scratch_shapes=[
                pltpu.VMEM((row_count * length, 128), jnp.float32),
                pltpu.VMEM((rows4 + 16, 256), jnp.float32),
                pltpu.VMEM((16, rows4 // 16, 16, 256), jnp.bfloat16),
                pltpu.VMEM((slots * 16, depth), jnp.bfloat16),
                pltpu.VMEM((slots * 16, depth), jnp.bfloat16),
                pltpu.VMEM((2, 128 + depth, 128), jnp.bfloat16),
                pltpu.VMEM((slots * 16, 256), jnp.float32),
                pltpu.VMEM((2, out4, 256), jnp.float32),
            ],
        ),
        out_shape=jax.ShapeDtypeStruct((row_count * frames, width), jnp.float32),
        compiler_params=pltpu.CompilerParams(vmem_limit_bytes=VMEM_LIMIT, dimension_semantics=("arbitrary",)),
        cost_estimate=pl.CostEstimate(
            flops=2 * pairs * 2 * slots * 16 * 256 * depth, bytes_accessed=pairs * weight.shape[0] * 256, transcendentals=0
        ),
        name="conv_back" if backward else "conv_forth",
    )(meta, x_ext.reshape(row_count * length, width), seg_quads(seg_ext), weight)


def conv_weight_kernel(slots, meta, x_ref, seg_ref, g_ref, o_ref, wide, wide_g, flat, shifts, masks, patches, quads, picks, sums):
    @pl.when(pl.program_id(0) == 0)
    def _():
        conv_setup(meta, slots, seg_ref, flat, shifts, masks)

    wide[...] = x_ref[...].astype(jnp.float32)
    wide_g[...] = g_ref[...].astype(jnp.float32)
    out_rows = g_ref.shape[0] // 4
    low = lane_low(64)
    for side in range(2):
        conv_patches(meta, slots, wide, side, flat, shifts, masks, patches)
        halves = quad_rows(wide_g, out_rows, side)
        quads[:, 0:128] = halves[0].astype(jnp.bfloat16)
        quads[:, 128:256] = halves[1].astype(jnp.bfloat16)

        @pl.loop(0, slots)
        def _(v):
            at = pl.ds(pl.multiple_of(meta[1 + slots + v] * 16, 16), 16)
            row = pl.ds(pl.multiple_of(v * 16, 16), 16)
            picks[row, :] = quads[at, :] * masks[row, 16 * 256 : 17 * 256]

        for b in range(TAP_BLOCKS):
            sums[:, b * 256 : (b + 1) * 256] = lax.dot_general(
                picks[...], patches[:, b * 256 : (b + 1) * 256], (((0,), (0,)), ((), ())),
                preferred_element_type=jnp.float32,
            )

        def piece(j, q):
            return sums[j * 64 : (j + 1) * 64, q * 128 : (q + 1) * 128]

        def odd(q):
            return half_roll(piece(1, q) + piece(3, q + 1))

        left = odd(0)
        for q in range(2 * (TAP_BLOCKS - 1)):
            right = odd(q + 1)
            part = piece(0, q) + piece(2, q + 1) + jnp.where(low, left, right)
            o_ref[side * 64 : (side + 1) * 64, q * 128 : (q + 1) * 128] = part.astype(o_ref.dtype)
            left = right


def grouped_conv_weight(x_ext, seg_ext, grad, rise):
    row_count, length, width = x_ext.shape
    frames = length - KERNEL
    pairs = width // 128
    in_block, tile, number = tile_lists(seg_ext, rise)
    slots = in_block.shape[0]
    meta = jnp.concatenate([jnp.zeros((1,), jnp.int32), in_block, tile, number])
    rows4 = row_count * length // 4
    out4 = row_count * frames // 4
    depth = TAP_BLOCKS * 256
    return pl.pallas_call(
        partial(conv_weight_kernel, slots),
        grid_spec=pltpu.PrefetchScalarGridSpec(
            num_scalar_prefetch=1,
            grid=(pairs,),
            in_specs=[
                pl.BlockSpec((row_count * length, 128), lambda p, meta: (0, p)),
                pl.BlockSpec((rows4, 256), lambda p, meta: (0, 0)),
                pl.BlockSpec((row_count * frames, 128), lambda p, meta: (0, p)),
            ],
            out_specs=pl.BlockSpec((128, KERNEL * 64), lambda p, meta: (p, 0)),
            scratch_shapes=[
                pltpu.VMEM((row_count * length, 128), jnp.float32),
                pltpu.VMEM((row_count * frames, 128), jnp.float32),
                pltpu.VMEM((rows4 + 16, 256), jnp.float32),
                pltpu.VMEM((16, rows4 // 16, 16, 256), jnp.bfloat16),
                pltpu.VMEM((slots * 16, depth), jnp.bfloat16),
                pltpu.VMEM((slots * 16, depth), jnp.bfloat16),
                pltpu.VMEM((out4, 256), jnp.bfloat16),
                pltpu.VMEM((slots * 16, 256), jnp.bfloat16),
                pltpu.VMEM((256, depth), jnp.float32),
            ],
        ),
        out_shape=jax.ShapeDtypeStruct((width, KERNEL * 64), jnp.bfloat16),
        compiler_params=pltpu.CompilerParams(vmem_limit_bytes=VMEM_LIMIT, dimension_semantics=("arbitrary",)),
        cost_estimate=pl.CostEstimate(
            flops=2 * pairs * 2 * slots * 16 * 256 * depth, bytes_accessed=width * KERNEL * 128, transcendentals=0
        ),
        name="conv_weight_grad",
    )(meta, x_ext.reshape(row_count * length, width), seg_quads(seg_ext), grad)


def lanes_dot(a, b):
    return lax.dot_general(a, b, (((1,), (1,)), ((), ())), preferred_element_type=jnp.float32)


def rows_dot(a, b):
    return lax.dot_general(a, b, (((0,), (0,)), ((), ())), preferred_element_type=jnp.float32)


def attend_kernel(seg_q_ref, seg_k_ref, q_ref, k_ref, v_ref, out_ref, lse_ref):
    queries = q_ref[...] * jnp.bfloat16(0.125)
    key_count, query_count = k_ref.shape[0], q_ref.shape[0]
    low = lax.broadcasted_iota(jnp.int32, (key_count, 128), 1) < 64
    keys, values = k_ref[...], v_ref[...]
    allowed = seg_k_ref[...] == seg_q_ref[...]
    pieces = []
    for side in range(2):
        mine = low if side == 0 else jnp.logical_not(low)
        scores = lanes_dot(jnp.where(mine, keys, jnp.zeros_like(keys)), queries)
        scores = jnp.where(allowed, scores, masked_score)
        top = jnp.max(scores, axis=0, keepdims=True)
        weights = jnp.exp(scores - top)
        total = jnp.sum(weights, axis=0, keepdims=True)
        mixed = rows_dot(values, weights.astype(jnp.bfloat16))
        pieces.append(mixed[side * 64 : (side + 1) * 64, :] / total)
        lse_ref[0, side : side + 1, :] = top + jnp.log(total)
    out_ref[...] = jnp.concatenate(pieces, axis=0).T


def attend_heads(queries, keys, values, seg_q, seg_k):
    frames, width = queries.shape
    length = keys.shape[0]
    pairs = width // 128
    return pl.pallas_call(
        attend_kernel,
        grid=(pairs,),
        in_specs=[
            pl.BlockSpec((1, frames), lambda p: (0, 0)),
            pl.BlockSpec((length, 1), lambda p: (0, 0)),
            pl.BlockSpec((frames, 128), lambda p: (0, p)),
            pl.BlockSpec((length, 128), lambda p: (0, p)),
            pl.BlockSpec((length, 128), lambda p: (0, p)),
        ],
        out_specs=[
            pl.BlockSpec((frames, 128), lambda p: (0, p)),
            pl.BlockSpec((1, 8, frames), lambda p: (p, 0, 0)),
        ],
        out_shape=[
            jax.ShapeDtypeStruct((frames, width), jnp.float32),
            jax.ShapeDtypeStruct((pairs, 8, frames), jnp.float32),
        ],
        compiler_params=pltpu.CompilerParams(vmem_limit_bytes=VMEM_LIMIT),
        cost_estimate=pl.CostEstimate(
            flops=8 * pairs * frames * length * 128, bytes_accessed=8 * frames * width, transcendentals=2 * pairs * frames * length
        ),
        name="attend",
    )(seg_q.reshape(1, -1), seg_k.reshape(-1, 1), queries, keys, values)


def attend_back_kernel(seg_q_ref, seg_k_ref, q_ref, k_ref, v_ref, g_ref, a_ref, lse_ref, dq_ref, dk_ref, dv_ref):
    queries = q_ref[...] * jnp.bfloat16(0.125)
    key_count = k_ref.shape[0]
    low = lax.broadcasted_iota(jnp.int32, (key_count, 128), 1) < 64
    keys, values, grads = k_ref[...], v_ref[...], g_ref[...]
    allowed = seg_k_ref[...] == seg_q_ref[...]
    products = (grads.astype(jnp.float32) * a_ref[...]).T
    dq, dk, dv = [], [], []
    for side in range(2):
        mine = low if side == 0 else jnp.logical_not(low)
        zero = jnp.zeros_like(keys)
        scores = lanes_dot(jnp.where(mine, keys, zero), queries)
        probs = jnp.where(allowed, jnp.exp(scores - lse_ref[0, side : side + 1, :]), 0.0)
        dots = jnp.sum(products[side * 64 : (side + 1) * 64, :], axis=0, keepdims=True)
        dv.append(jnp.dot(probs.astype(jnp.bfloat16), grads, preferred_element_type=jnp.float32))
        grad_probs = lanes_dot(jnp.where(mine, values, zero), grads)
        grad_scores = (probs * (grad_probs - dots)).astype(jnp.bfloat16)
        dk.append(jnp.dot(grad_scores, queries, preferred_element_type=jnp.float32))
        dq.append(rows_dot(keys, grad_scores)[side * 64 : (side + 1) * 64, :])
    dq_ref[...] = 0.125 * jnp.concatenate(dq, axis=0).T
    dk_ref[...] = jnp.where(low, dk[0], dk[1]).astype(dk_ref.dtype)
    dv_ref[...] = jnp.where(low, dv[0], dv[1]).astype(dv_ref.dtype)


def attend_heads_back(queries, keys, values, grads, attended, lse, seg_q, seg_k, kind):
    frames, width = queries.shape
    length = keys.shape[0]
    pairs = width // 128
    return pl.pallas_call(
        attend_back_kernel,
        grid=(pairs,),
        in_specs=[
            pl.BlockSpec((1, frames), lambda p: (0, 0)),
            pl.BlockSpec((length, 1), lambda p: (0, 0)),
            pl.BlockSpec((frames, 128), lambda p: (0, p)),
            pl.BlockSpec((length, 128), lambda p: (0, p)),
            pl.BlockSpec((length, 128), lambda p: (0, p)),
            pl.BlockSpec((frames, 128), lambda p: (0, p)),
            pl.BlockSpec((frames, 128), lambda p: (0, p)),
            pl.BlockSpec((1, 8, frames), lambda p: (p, 0, 0)),
        ],
        out_specs=[
            pl.BlockSpec((frames, 128), lambda p: (0, p)),
            pl.BlockSpec((length, 128), lambda p: (0, p)),
            pl.BlockSpec((length, 128), lambda p: (0, p)),
        ],
        out_shape=[
            jax.ShapeDtypeStruct((frames, width), jnp.float32),
            jax.ShapeDtypeStruct((length, width), kind),
            jax.ShapeDtypeStruct((length, width), kind),
        ],
        compiler_params=pltpu.CompilerParams(vmem_limit_bytes=VMEM_LIMIT),
        cost_estimate=pl.CostEstimate(
            flops=20 * pairs * frames * length * 128, bytes_accessed=16 * frames * width, transcendentals=2 * pairs * frames * length
        ),
        name="attend_back",
    )(seg_q.reshape(1, -1), seg_k.reshape(-1, 1), queries, keys, values, grads, attended, lse)


AXES = ("y", "c", "z", "x")


def device_pairs(place):
    pairs = []
    for y in range(2):
        for c in range(2):
            for z in range(4):
                for x in range(2):
                    ty, tc, tz, tx = place(y, c, z, x)
                    pairs.append((((y * 2 + c) * 4 + z) * 2 + x, ((ty * 2 + tc) * 4 + tz) * 2 + tx))
    return pairs


def move(values, place):
    return lax.ppermute(values, AXES, device_pairs(place))


def swap_core(values):
    return lax.ppermute(values, "c", [(0, 1), (1, 0)])


def swap_x(values):
    return lax.ppermute(values, "x", [(0, 1), (1, 0)])


def swap_y(values):
    return lax.ppermute(values, "y", [(0, 1), (1, 0)])


def take(values, index, size, axis):
    return lax.dynamic_slice_in_dim(values, index * size, size, axis)


def ordered(index, mine, other, axis):
    first = jnp.where(index == 0, mine, other)
    second = jnp.where(index == 0, other, mine)
    return jnp.concatenate([first, second], axis=axis)


def to_rows(blocks, x, z):
    got = []
    for turn in range(2):
        mine = lax.dynamic_index_in_dim(blocks, x ^ turn, 0, keepdims=False)
        got.append(move(mine, lambda y, c, z, x: (y, z & 1, 2 * c + (x ^ turn), z >> 1)))
    return ordered(z & 1, got[0], got[1], 0)


def from_rows(frames, x, z):
    half = frames.shape[0] // 2
    got = []
    for turn in range(2):
        mine = take(frames, (z & 1) ^ turn, half, 0)
        got.append(move(mine, lambda y, c, z, x: (y, z >> 1, 2 * x + c, (z & 1) ^ turn)))
    return ordered(x, got[0][None], got[1][None], 0)


def split_body(
    feats, segments, labels, conv_weight, w_qkv, w_out, w_up, w_down, head_w, head_b, gains, biases, up_bias
):
    y, c, z, x = (lax.axis_index(name) for name in AXES)
    features = feats.shape[2]
    half = features // 2
    frames = 2 * feats.shape[1]
    chip_frames = 2 * frames
    tokens = frames
    rim = KERNEL // 2
    rise = lax.axis_size("z") * lax.axis_size("x") // 2

    feats_own = to_rows(feats, x, z)
    labels_own = to_rows(labels, x, z)
    seg_rows = ordered(c, segments, swap_core(segments), 0)
    seg_row = lax.dynamic_index_in_dim(seg_rows, z, 0, keepdims=False)
    seg_chip = take(seg_row, x, chip_frames, 0)
    seg_far = take(seg_row, 1 - x, chip_frames, 0)
    seg_wide = jnp.pad(seg_row, (rim, rim), constant_values=-1)
    seg_ext = lax.dynamic_slice_in_dim(seg_wide, x * chip_frames, chip_frames + 2 * rim, 0)[None]

    def to_chip(values):
        return ordered(c, take(values, c, half, 1), swap_core(take(values, 1 - c, half, 1)), 0)

    def to_tokens(values):
        return ordered(c, take(values, c, frames, 0), swap_core(take(values, 1 - c, frames, 0)), 1)

    def with_rim(values):
        edge = swap_x(jnp.where(x == 0, values[chip_frames - rim :], values[:rim]))
        empty = jnp.zeros_like(edge)
        before = jnp.where(x == 0, empty, edge)
        after = jnp.where(x == 0, edge, empty)
        return jnp.concatenate([before, values, after], axis=0)[None]

    def both_cores(values):
        return jnp.concatenate([values, swap_core(values)], axis=0)

    def half_of_both(values):
        width = values.shape[1] // 2
        return jnp.concatenate([take(values, c, width, 1), swap_core(take(values, 1 - c, width, 1))], axis=0)

    def to_groups(values):
        width = half // 2
        wide = ordered(x, take(values, x, width, 1), swap_x(take(values, 1 - x, width, 1)), 0)
        return ordered(y, take(wide, y, 128, 1)[None], swap_y(take(wide, 1 - y, 128, 1))[None], 0)

    feats_chip = to_chip(feats_own)
    feats_group = to_groups(feats_chip)
    conv_sum = grouped_conv(with_rim(feats_chip), seg_ext, conv_weight, 4 * c, rise, False)
    conv_sum = conv_sum + take(biases[:, 0], c, half, 0)
    activated, conv_pull = jax.vjp(gelu_exact, conv_sum)
    position = to_tokens(feats_chip.astype(jnp.float32) + activated)
    normed, first_pull = jax.vjp(layer_norm, position, gains[:, 0], biases[:, 1])
    normed_low = normed.astype(jnp.bfloat16)
    qkv_bias = jnp.concatenate([biases[:, 2], jnp.zeros((features,), jnp.float32), biases[:, 3]])
    mixed = (jnp.dot(normed_low, w_qkv, preferred_element_type=jnp.float32) + qkv_bias).astype(jnp.bfloat16)
    split = mixed.reshape(tokens, 3, 2, half)
    mine = lax.dynamic_index_in_dim(split, c, 2, keepdims=False).reshape(tokens, 3 * half)
    theirs = lax.dynamic_index_in_dim(split, 1 - c, 2, keepdims=False).reshape(tokens, 3 * half)
    mixed_chip = ordered(c, mine, swap_core(theirs), 0)
    queries = mixed_chip[:, :half]
    near = mixed_chip[:, half:]
    far = swap_x(near)
    both = jnp.concatenate([near, far], axis=0)
    seg_both = jnp.concatenate([seg_chip, seg_far])
    attended, lse = attend_heads(queries, both[:, :half], both[:, half:], seg_chip, seg_both)
    attended_low = to_tokens(attended.astype(jnp.bfloat16))
    resid = position + jnp.dot(attended_low, w_out, preferred_element_type=jnp.float32) + biases[:, 4]
    normed_second, second_pull = jax.vjp(layer_norm, resid, gains[:, 1], biases[:, 5])
    second_low = normed_second.astype(jnp.bfloat16)
    up_sum = jnp.dot(second_low, w_up, preferred_element_type=jnp.float32) + up_bias
    up_active, up_pull = jax.vjp(gelu_exact, up_sum)
    active_low = up_active.astype(jnp.bfloat16)
    output = resid + jnp.dot(active_low, w_down, preferred_element_type=jnp.float32) + biases[:, 6]
    output_low = output.astype(jnp.bfloat16)
    layer_out = from_rows(output_low, x, z)
    logits = jnp.dot(output_low, head_w, preferred_element_type=jnp.float32) + head_b
    row_top = jnp.max(logits, axis=-1, keepdims=True)
    shifted = jnp.exp(logits - row_top)
    exp_sums = jnp.sum(shifted, axis=-1, keepdims=True)
    onehot = labels_own[:, None] == jnp.arange(VOCAB, dtype=jnp.int32)[None, :]
    picked = jnp.sum(jnp.where(onehot, logits, 0.0), axis=-1)
    local_loss = jnp.sum(row_top[:, 0] + jnp.log(exp_sums[:, 0]) - picked)
    grad_logits = (shifted / exp_sums - onehot.astype(jnp.float32)).astype(jnp.bfloat16)

    grad_head_w = outer_sum(grad_logits, output_low)
    grad_head_b = jnp.sum(grad_logits.astype(jnp.float32), axis=0)
    grad_output = back_product(grad_logits, head_w)
    grad_output_low = grad_output.astype(jnp.bfloat16)
    grad_down_bias = jnp.sum(grad_output_low.astype(jnp.float32), axis=0)
    grad_active = back_product(grad_output_low, w_down)
    grad_up_low = up_pull(grad_active)[0].astype(jnp.bfloat16)
    grad_up_bias = jnp.sum(grad_up_low.astype(jnp.float32), axis=0)
    grad_second = back_product(grad_up_low, w_up)
    grad_resid_part, grad_gain_second, grad_shift_second = second_pull(grad_second)
    grad_resid = grad_output + grad_resid_part
    grad_branch_low = grad_resid.astype(jnp.bfloat16)
    grad_out_bias = jnp.sum(grad_branch_low.astype(jnp.float32), axis=0)
    grad_attended = back_product(grad_branch_low, w_out).astype(jnp.bfloat16)
    grad_heads = to_chip(grad_attended)
    dq_far, dk_far, dv_far = attend_heads_back(
        queries, far[:, :half], far[:, half:], grad_heads, attended, lse, seg_chip, seg_far, jnp.bfloat16
    )
    got = swap_x(jnp.concatenate([dk_far, dv_far], axis=1)).astype(jnp.float32)
    dq, dk, dv = attend_heads_back(
        queries, near[:, :half], near[:, half:], grad_heads, attended, lse, seg_chip, seg_chip, jnp.float32
    )
    grad_chip = jnp.concatenate([dq + dq_far, dk + got[:, :half], dv + got[:, half:]], axis=1).astype(jnp.bfloat16)
    mine = take(grad_chip, c, frames, 0).reshape(tokens, 3, 1, half)
    theirs = swap_core(take(grad_chip, 1 - c, frames, 0)).reshape(tokens, 3, 1, half)
    grad_mixed = ordered(c, mine, theirs, 2).reshape(tokens, 3 * features)
    mixed_sums = jnp.sum(grad_mixed.astype(jnp.float32), axis=0)
    grad_normed = back_product(grad_mixed, w_qkv)
    grad_position_part, grad_gain_first, grad_shift_first = first_pull(grad_normed)
    grad_position = to_chip(grad_resid + grad_position_part)
    grad_conv_low = conv_pull(grad_position)[0].astype(jnp.bfloat16)
    grad_conv_bias = jnp.sum(grad_conv_low.astype(jnp.float32), axis=0)
    grad_group = to_groups(grad_conv_low)
    conv_input = grouped_conv(with_rim(grad_conv_low), seg_ext, conv_weight, 4 * c, rise, True)
    grad_feats = from_rows(to_tokens((grad_position + conv_input).astype(jnp.bfloat16)), x, z)

    def reduced(half_grad):
        rows, width = half_grad.shape
        quarter = width // 2
        kept = take(half_grad, y, quarter, 1) + swap_y(take(half_grad, 1 - y, quarter, 1)).astype(jnp.float32)
        kept = kept.reshape(4, 2, rows // 8, quarter)
        away = lax.dynamic_index_in_dim(kept, 1 - x, 1, keepdims=False).astype(jnp.bfloat16)
        stay = lax.dynamic_index_in_dim(kept, x, 1, keepdims=False)
        stay = (stay + swap_x(away).astype(jnp.float32)).astype(jnp.bfloat16)
        shard = lax.psum_scatter(stay, "z", scatter_dimension=0, tiled=True)[0]
        return shard

    def spread(shard):
        wide = ordered(y, shard, swap_y(shard), 1)
        return wide, swap_core(wide)

    def weight_grad(left, right):
        half_grad = outer_sum(left, right)
        rows, width = half_grad.shape
        low = half_grad.astype(jnp.bfloat16)
        mine, theirs = spread(reduced(low))
        return mine, theirs

    active_both, second_both, attended_both, normed_both = (
        both_cores(item) for item in (active_low, second_low, attended_low, normed_low)
    )
    mine, theirs = weight_grad(active_both, half_of_both(grad_output_low))
    grad_w_down = ordered(c, mine, theirs, 1).astype(jnp.float32)
    mine, theirs = weight_grad(second_both, half_of_both(grad_up_low))
    grad_w_up = ordered(c, mine, theirs, 1).astype(jnp.float32)
    mine, theirs = weight_grad(attended_both, half_of_both(grad_branch_low))
    grad_w_out = ordered(c, mine, theirs, 1).astype(jnp.float32)
    grad_own_first = jnp.concatenate([take(grad_chip, c, frames, 0), take(grad_chip, 1 - c, frames, 0)], axis=0)
    mine, theirs = weight_grad(normed_both, grad_own_first)
    mine, theirs = (item.reshape(-1, 3, 1, half) for item in (mine, theirs))
    grad_w_qkv = ordered(c, mine, theirs, 2).reshape(-1, 3 * features).astype(jnp.float32)

    seg_y = ordered(y, seg_row[None], swap_y(seg_row)[None], 0)
    pad = ((0, 0), (rim, rim))
    conv_grad = grouped_conv_weight(
        jnp.pad(feats_group, pad + ((0, 0),)),
        jnp.pad(seg_y, pad, constant_values=-1),
        grad_group.reshape(-1, 128),
        rise,
    )
    conv_grad = lax.psum_scatter(conv_grad.reshape(128, 4, -1), "z", scatter_dimension=1, tiled=True)[:, 0]
    width = conv_grad.shape[1] // 2
    conv_grad = ordered(x, take(conv_grad, x, width, 1)[None], swap_x(take(conv_grad, 1 - x, width, 1))[None], 0)
    conv_grad = ordered(y, conv_grad[:, None], swap_y(conv_grad)[:, None], 1)
    conv_grad = ordered(c, conv_grad[None], swap_core(conv_grad)[None], 0)
    grad_conv_weight = conv_grad.reshape(features, width).T.astype(jnp.float32)

    zero_half = jnp.zeros((half,), jnp.float32)
    conv_bias = jnp.concatenate([jnp.where(c == 0, grad_conv_bias, zero_half), jnp.where(c == 1, grad_conv_bias, zero_half)])
    last_row = jnp.concatenate([grad_head_b, local_loss[None], jnp.zeros((features - VOCAB - 1,), jnp.float32)])
    early = jnp.concatenate(
        [
            grad_head_w,
            jnp.stack([grad_gain_second, grad_out_bias, grad_shift_second, grad_down_bias]),
            grad_up_bias.reshape(4, features),
            last_row[None],
        ],
        axis=0,
    )
    late = jnp.stack(
        [grad_gain_first, conv_bias, grad_shift_first, mixed_sums[:features], mixed_sums[2 * features :]]
    )
    early = lax.psum(early, AXES)
    late = lax.psum(late, AXES)
    loss = early[VOCAB + 8, VOCAB] / (tokens * 32)
    head_bias_total = early[VOCAB + 8, :VOCAB]
    block = 2 * z + x
    early_part = take(early, block, features // 8, 1)
    late_part = take(late, block, features // 8, 1)
    gain_part = jnp.stack([late_part[0], early_part[VOCAB]], axis=1)
    bias_part = jnp.stack(
        [
            late_part[1],
            late_part[2],
            late_part[3],
            late_part[4],
            early_part[VOCAB + 1],
            early_part[VOCAB + 2],
            early_part[VOCAB + 3],
        ],
        axis=1,
    )
    up_total = early[VOCAB + 4 : VOCAB + 8].reshape(-1)
    up_part = take(up_total, block, up_total.shape[0] // 8, 0)
    return (
        layer_out,
        loss,
        grad_feats.astype(jnp.float32),
        grad_conv_weight,
        grad_w_qkv,
        grad_w_out,
        grad_w_up,
        grad_w_down,
        early_part[:VOCAB].T,
        head_bias_total,
        gain_part,
        bias_part,
        up_part,
    )


def split_solution(mesh):
    fine = Mesh(mesh.devices.reshape(2, 2, 4, 2), AXES)
    rows, parts = ("y", "c"), ("z", "x")
    return jax.shard_map(
        split_body,
        mesh=fine,
        in_specs=(P(rows, parts, None), P(rows, None), P(rows, parts)) + (P(),) * 10,
        out_specs=(
            P(rows, parts, None),
            P(),
            P(rows, parts, None),
            P(parts, None),
            P(parts, None),
            P(parts, None),
            P(parts, None),
            P(parts, None),
            P(parts, None),
            P(),
            P(parts, None),
            P(parts, None),
            P(parts),
        ),
        check_vma=False,
    )


def solution(mesh):
    if mesh.shape["dp"] == 4 and mesh.shape["seq"] == 8:
        return split_solution(mesh)
    return whole_solution(mesh)
```

```python
from functools import partial
import math

import jax
import jax.numpy as jnp
from jax import lax
from jax.experimental import pallas as pl
from jax.experimental.pallas import tpu as pltpu
from jax.sharding import Mesh, PartitionSpec as P

HEADS = 16
GROUPS = 16
KERNEL = 128
VOCAB = 32
TAP_BLOCKS = 33
VMEM_LIMIT = 56 * 1024 * 1024
DW_UNROLL = 11
COST_SHARE = 0.001


epsilon = 1e-05
masked_score = -1e30
tap_group = 8


def extended(cells, sides, width):
    for axis, dim in sides:
        count = lax.axis_size(axis)
        ends = count - 1
        head = lax.slice_in_dim(cells, 0, width, axis=dim)
        tail = lax.slice_in_dim(cells, cells.shape[dim] - width, cells.shape[dim], axis=dim)
        cells = jnp.concatenate(
            [
                lax.ppermute(tail, axis, [(i, (i + 1) % count) for i in range(ends)]),
                cells,
                lax.ppermute(head, axis, [((i + 1) % count, i) for i in range(ends)]),
            ],
            axis=dim,
        )
    return cells


def layer_norm(values, gain_row, shift_row):
    center = values - jnp.mean(values, axis=-1, keepdims=True)
    spread = jnp.mean(center * center, axis=-1, keepdims=True)
    return center * lax.rsqrt(spread + epsilon) * gain_row + shift_row


def gelu_exact(values):
    return jax.nn.gelu(values, approximate=False)


def outer_sum(left_side, right_side):
    return lax.dot_general(
        left_side, right_side, (((0,), (0,)), ((), ())), preferred_element_type=jnp.float32
    )


def back_product(grad_rows, weight):
    return lax.dot_general(
        grad_rows, weight, (((1,), (1,)), ((), ())), preferred_element_type=jnp.float32
    )


def masked_windows(source, seg_padded, seg_local, offsets, frames):
    windows = []
    for offset in offsets:
        window = lax.dynamic_slice_in_dim(source, offset, frames, 1)
        near_ids = lax.dynamic_slice_in_dim(seg_padded, offset, frames, 1)
        keep_mask = (near_ids == seg_local)[:, :, None]
        windows.append(jnp.where(keep_mask, window, jnp.zeros_like(window)))
    return jnp.stack(windows, axis=2)


def conv_forward(feats_rim, seg_padded, seg_local, conv_weight):
    row_count, frames = seg_local.shape
    features = feats_rim.shape[2]
    group_width = features // GROUPS
    tap_count = conv_weight.shape[0] // group_width
    grouped = conv_weight.reshape(tap_count, group_width, GROUPS, group_width)

    def one_block(tap_block, running):
        offsets = [tap_block * tap_group + tap_inner for tap_inner in range(tap_group)]
        stacked = masked_windows(feats_rim, seg_padded, seg_local, offsets, frames)
        stacked = stacked.reshape(row_count, frames, tap_group, GROUPS, group_width)
        weight_part = lax.dynamic_slice_in_dim(grouped, tap_block * tap_group, tap_group, 0)
        return running + jnp.einsum(
            "rtkgi,kigo->rtgo", stacked, weight_part, preferred_element_type=jnp.float32
        )

    start_sum = jnp.zeros((row_count, frames, GROUPS, group_width), jnp.float32)
    running = lax.fori_loop(0, tap_count // tap_group, one_block, start_sum)
    return running.reshape(row_count, frames, features)


def conv_weight_grad(feats_rim, seg_padded, seg_local, grad_conv_low, tap_count):
    row_count, frames = seg_local.shape
    features = feats_rim.shape[2]
    group_width = features // GROUPS
    grad_grouped = grad_conv_low.reshape(row_count, frames, GROUPS, group_width)

    def one_block(tap_block, running):
        offsets = [tap_block * tap_group + tap_inner for tap_inner in range(tap_group)]
        stacked = masked_windows(feats_rim, seg_padded, seg_local, offsets, frames)
        stacked = stacked.reshape(row_count, frames, tap_group, GROUPS, group_width)
        block_grad = jnp.einsum(
            "rtkgi,rtgo->kigo", stacked, grad_grouped, preferred_element_type=jnp.float32
        )
        return lax.dynamic_update_slice_in_dim(running, block_grad, tap_block * tap_group, 0)

    start_sum = jnp.zeros((tap_count, group_width, GROUPS, group_width), jnp.float32)
    running = lax.fori_loop(0, tap_count // tap_group, one_block, start_sum)
    return running.reshape(tap_count * group_width, features)


def conv_input_grad(grad_rim, seg_padded, seg_local, conv_weight):
    row_count, frames = seg_local.shape
    features = grad_rim.shape[2]
    group_width = features // GROUPS
    tap_count = conv_weight.shape[0] // group_width
    grouped = conv_weight.reshape(tap_count, group_width, GROUPS, group_width)

    def one_block(tap_block, running):
        offsets = [
            tap_count - (tap_block * tap_group + tap_inner) for tap_inner in range(tap_group)
        ]
        stacked = masked_windows(grad_rim, seg_padded, seg_local, offsets, frames)
        stacked = stacked.reshape(row_count, frames, tap_group, GROUPS, group_width)
        weight_part = lax.dynamic_slice_in_dim(grouped, tap_block * tap_group, tap_group, 0)
        return running + jnp.einsum(
            "rtkgo,kigo->rtgi", stacked, weight_part, preferred_element_type=jnp.float32
        )

    start_sum = jnp.zeros((row_count, frames, GROUPS, group_width), jnp.float32)
    running = lax.fori_loop(0, tap_count // tap_group, one_block, start_sum)
    return running.reshape(row_count, frames, features)


def span_size(piece_rows, frames):
    return math.gcd(piece_rows, 8 * frames)


def attend_row(row_state, query_row, key_row, value_row, seg_query, seg_key, score_scale):
    running_max, running_sum, weighted = row_state
    scores = score_scale * jnp.einsum(
        "qhe,khe->qhk", query_row, key_row, preferred_element_type=jnp.float32
    )
    allowed = (seg_query[:, None] == seg_key[None, :])[:, None, :]
    scores = jnp.where(allowed, scores, masked_score)
    new_max = jnp.maximum(running_max, jnp.max(scores, axis=-1))
    rescale = jnp.exp(running_max - new_max)
    weights = jnp.where(allowed, jnp.exp(scores - new_max[:, :, None]), 0.0)
    running_sum = running_sum * rescale + jnp.sum(weights, axis=-1)
    weighted = weighted * rescale[:, :, None] + jnp.einsum(
        "qhk,khe->qhe", weights.astype(jnp.bfloat16), value_row, preferred_element_type=jnp.float32
    )
    return (new_max, running_sum, weighted)


def query_grad_row(
    grad_query,
    query_row,
    key_row,
    value_row,
    seg_query,
    seg_key,
    lse_row,
    dots_row,
    grad_row,
    score_scale,
):
    scores = score_scale * jnp.einsum(
        "qhe,khe->qhk", query_row, key_row, preferred_element_type=jnp.float32
    )
    allowed = (seg_query[:, None] == seg_key[None, :])[:, None, :]
    probs = jnp.where(allowed, jnp.exp(scores - lse_row[:, :, None]), 0.0)
    grad_probs = jnp.einsum("qhe,khe->qhk", grad_row, value_row, preferred_element_type=jnp.float32)
    grad_scores = (probs * (grad_probs - dots_row[:, :, None])).astype(jnp.bfloat16)
    return grad_query + score_scale * jnp.einsum(
        "qhk,khe->qhe", grad_scores, key_row, preferred_element_type=jnp.float32
    )


def key_grad_row(
    grads_pair,
    key_row,
    value_row,
    query_row,
    grad_row,
    lse_row,
    dots_row,
    seg_query,
    seg_key,
    score_scale,
):
    scores = score_scale * jnp.einsum(
        "qhe,khe->qhk", query_row, key_row, preferred_element_type=jnp.float32
    )
    allowed = (seg_query[:, None] == seg_key[None, :])[:, None, :]
    probs = jnp.where(allowed, jnp.exp(scores - lse_row[:, :, None]), 0.0)
    grad_value = jnp.einsum(
        "qhk,qhe->khe", probs.astype(jnp.bfloat16), grad_row, preferred_element_type=jnp.float32
    )
    grad_probs = jnp.einsum("qhe,khe->qhk", grad_row, value_row, preferred_element_type=jnp.float32)
    grad_scores = (probs * (grad_probs - dots_row[:, :, None])).astype(jnp.bfloat16)
    grad_key = score_scale * jnp.einsum(
        "qhk,qhe->khe", grad_scores, query_row, preferred_element_type=jnp.float32
    )
    return (grad_key, grad_value)


def body(
    feats,
    segments,
    labels,
    conv_weight,
    w_qkv,
    w_out,
    w_up,
    w_down,
    head_w,
    head_b,
    gains,
    biases,
    up_bias,
):
    row_count, frames, features = feats.shape
    head_count = HEADS
    head_width = features // head_count
    score_scale = head_width ** (-0.5)
    tokens = row_count * frames
    tap_count = KERNEL
    rim_width = tap_count // 2
    own_first = lax.axis_index("seq") * frames
    seg_local = lax.dynamic_slice_in_dim(segments, own_first, frames, 1)
    seg_wide = jnp.pad(segments, ((0, 0), (rim_width, rim_width)), constant_values=-1)
    seg_padded = lax.dynamic_slice_in_dim(seg_wide, own_first, frames + 2 * rim_width, 1)
    feats_rim = extended(feats, (("seq", 1),), rim_width)
    conv_sum = conv_forward(feats_rim, seg_padded, seg_local, conv_weight) + biases[:, 0]
    activated, conv_pull = jax.vjp(gelu_exact, conv_sum)
    position = feats.astype(jnp.float32) + activated
    normed, first_pull = jax.vjp(layer_norm, position, gains[:, 0], biases[:, 1])
    normed_low = normed.astype(jnp.bfloat16).reshape(tokens, features)
    qkv_bias = jnp.concatenate([biases[:, 2], jnp.zeros((features,), jnp.float32), biases[:, 3]])
    mixed = (jnp.dot(normed_low, w_qkv, preferred_element_type=jnp.float32) + qkv_bias).astype(
        jnp.bfloat16
    )
    queries = mixed[:, :features].reshape(row_count, frames, head_count, head_width)
    keys = mixed[:, features : 2 * features].reshape(row_count, frames, features)
    values = mixed[:, 2 * features :].reshape(row_count, frames, features)
    start_state = (
        jnp.full((row_count, frames, head_count), masked_score, jnp.float32),
        jnp.zeros((row_count, frames, head_count), jnp.float32),
        jnp.zeros((row_count, frames, head_count, head_width), jnp.float32),
    )
    key_shard = lax.all_gather(keys, "seq", axis=1, tiled=True)
    value_shard = lax.all_gather(values, "seq", axis=1, tiled=True)
    piece_rows = key_shard.shape[1]
    span = span_size(piece_rows, frames)

    def forward_one_span(span_index, state):
        offset = span_index * span
        key_part = lax.dynamic_slice_in_dim(key_shard, offset, span, 1)
        value_part = lax.dynamic_slice_in_dim(value_shard, offset, span, 1)
        seg_keys = lax.dynamic_slice_in_dim(segments, offset, span, 1)
        results = []
        for row_index in range(row_count):
            action = partial(
                attend_row,
                query_row=queries[row_index],
                key_row=key_part[row_index].reshape(span, head_count, head_width),
                value_row=value_part[row_index].reshape(span, head_count, head_width),
                seg_query=seg_local[row_index],
                seg_key=seg_keys[row_index],
                score_scale=score_scale,
            )
            row_state = (state[0][row_index], state[1][row_index], state[2][row_index])
            results.append(action(row_state))
        return (
            jnp.stack([item[0] for item in results]),
            jnp.stack([item[1] for item in results]),
            jnp.stack([item[2] for item in results]),
        )

    running_max, running_sum, weighted = lax.fori_loop(
        0, piece_rows // span, forward_one_span, start_state
    )
    attended = weighted / running_sum[:, :, :, None]
    log_total = running_max + jnp.log(running_sum)
    attended_low = attended.reshape(tokens, features).astype(jnp.bfloat16)
    resid = (
        position.reshape(tokens, features)
        + jnp.dot(attended_low, w_out, preferred_element_type=jnp.float32)
        + biases[:, 4]
    )
    normed_second, second_pull = jax.vjp(layer_norm, resid, gains[:, 1], biases[:, 5])
    second_low = normed_second.astype(jnp.bfloat16)
    up_sum = jnp.dot(second_low, w_up, preferred_element_type=jnp.float32) + up_bias
    up_active, up_pull = jax.vjp(gelu_exact, up_sum)
    active_low = up_active.astype(jnp.bfloat16)
    output = resid + jnp.dot(active_low, w_down, preferred_element_type=jnp.float32) + biases[:, 6]
    output_low = output.astype(jnp.bfloat16)
    logits = jnp.dot(output_low, head_w, preferred_element_type=jnp.float32) + head_b
    row_top = jnp.max(logits, axis=-1, keepdims=True)
    shifted = jnp.exp(logits - row_top)
    exp_sums = jnp.sum(shifted, axis=-1, keepdims=True)
    onehot = labels.reshape(tokens)[:, None] == jnp.arange(VOCAB, dtype=jnp.int32)[None, :]
    picked = jnp.sum(jnp.where(onehot, logits, 0.0), axis=-1)
    local_loss = jnp.sum(row_top[:, 0] + jnp.log(exp_sums[:, 0]) - picked)
    grad_logits = (shifted / exp_sums - onehot.astype(jnp.float32)).astype(jnp.bfloat16)
    grad_head_w = outer_sum(output_low, grad_logits)
    grad_head_b = jnp.sum(grad_logits.astype(jnp.float32), axis=0)
    grad_output = back_product(grad_logits, head_w)
    grad_output_low = grad_output.astype(jnp.bfloat16)
    grad_w_down = outer_sum(active_low, grad_output_low)
    grad_down_bias = jnp.sum(grad_output_low.astype(jnp.float32), axis=0)
    grad_active = back_product(grad_output_low, w_down)
    grad_up_low = up_pull(grad_active)[0].astype(jnp.bfloat16)
    grad_w_up = outer_sum(second_low, grad_up_low)
    grad_up_bias = jnp.sum(grad_up_low.astype(jnp.float32), axis=0)
    grad_second = back_product(grad_up_low, w_up)
    grad_resid_part, grad_gain_second, grad_shift_second = second_pull(grad_second)
    grad_resid = grad_output + grad_resid_part
    grad_branch_low = grad_resid.astype(jnp.bfloat16)
    grad_w_out = outer_sum(attended_low, grad_branch_low)
    grad_out_bias = jnp.sum(grad_branch_low.astype(jnp.float32), axis=0)
    grad_attended = back_product(grad_branch_low, w_out).astype(jnp.bfloat16)
    grad_heads = grad_attended.reshape(row_count, frames, head_count, head_width)
    head_dots = jnp.sum(grad_heads.astype(jnp.float32) * attended, axis=-1)
    zero_grads = jnp.zeros((row_count, frames, head_count, head_width), jnp.float32)
    all_keys, all_values = (
        lax.all_gather(keys, "seq", axis=1, tiled=True),
        lax.all_gather(values, "seq", axis=1, tiled=True),
    )
    length = all_keys.shape[1]
    key_span = 8 * frames

    def query_block(block_index, grad_query):
        first_row = block_index * key_span
        key_block = lax.dynamic_slice_in_dim(all_keys, first_row, key_span, 1)
        value_block = lax.dynamic_slice_in_dim(all_values, first_row, key_span, 1)
        seg_keys = lax.dynamic_slice_in_dim(segments, first_row, key_span, 1)
        results = []
        for row_index in range(row_count):
            action = partial(
                query_grad_row,
                query_row=queries[row_index],
                key_row=key_block[row_index].reshape(key_span, head_count, head_width),
                value_row=value_block[row_index].reshape(key_span, head_count, head_width),
                seg_query=seg_local[row_index],
                seg_key=seg_keys[row_index],
                lse_row=log_total[row_index],
                dots_row=head_dots[row_index],
                grad_row=grad_heads[row_index],
                score_scale=score_scale,
            )
            results.append(action(grad_query[row_index]))
        return jnp.stack(results)

    grad_queries = lax.fori_loop(0, length // key_span, query_block, zero_grads)

    def key_term(piece_rows):
        span = math.gcd(piece_rows, key_span)

        def key_one_span(span_index, gathered_terms):
            offset = span_index * span
            key_block = lax.dynamic_slice_in_dim(all_keys, offset, span, 1)
            value_block = lax.dynamic_slice_in_dim(all_values, offset, span, 1)
            seg_keys = lax.dynamic_slice_in_dim(segments, offset, span, 1)
            empty_row = jnp.zeros((span, head_count, head_width), jnp.float32)
            results = []
            for row_index in range(row_count):
                action = partial(
                    key_grad_row,
                    key_row=key_block[row_index].reshape(span, head_count, head_width),
                    value_row=value_block[row_index].reshape(span, head_count, head_width),
                    query_row=queries[row_index],
                    grad_row=grad_heads[row_index],
                    lse_row=log_total[row_index],
                    dots_row=head_dots[row_index],
                    seg_query=seg_local[row_index],
                    seg_key=seg_keys[row_index],
                    score_scale=score_scale,
                )
                results.append(action((empty_row, empty_row)))
            key_part = jnp.stack([item[0] for item in results], axis=1).reshape(
                span, row_count, features
            )
            value_part = jnp.stack([item[1] for item in results], axis=1).reshape(
                span, row_count, features
            )
            both_parts = jnp.concatenate([key_part, value_part], axis=2)
            return lax.dynamic_update_slice_in_dim(gathered_terms, both_parts, offset, 0)

        empty_terms = jnp.zeros((piece_rows, row_count, 2 * features), jnp.float32)
        return lax.fori_loop(0, piece_rows // span, key_one_span, empty_terms)

    both_grads = lax.psum_scatter(
        key_term(frames * lax.axis_size("seq")), "seq", scatter_dimension=0, tiled=True
    )
    grad_keys = jnp.transpose(both_grads[:, :, :features], (1, 0, 2)).reshape(
        row_count, frames, head_count, head_width
    )
    grad_values = jnp.transpose(both_grads[:, :, features:], (1, 0, 2)).reshape(
        row_count, frames, head_count, head_width
    )
    grad_mixed = jnp.concatenate(
        [
            grad_queries.reshape(tokens, features),
            grad_keys.reshape(tokens, features),
            grad_values.reshape(tokens, features),
        ],
        axis=1,
    ).astype(jnp.bfloat16)
    grad_w_qkv = outer_sum(normed_low, grad_mixed)
    mixed_sums = jnp.sum(grad_mixed.astype(jnp.float32), axis=0)
    grad_normed = back_product(grad_mixed, w_qkv).reshape(row_count, frames, features)
    grad_position_part, grad_gain_first, grad_shift_first = first_pull(grad_normed)
    grad_position = grad_resid.reshape(row_count, frames, features) + grad_position_part
    grad_conv_low = conv_pull(grad_position)[0].astype(jnp.bfloat16)
    grad_conv_bias = jnp.sum(grad_conv_low.astype(jnp.float32), axis=(0, 1))
    grad_conv_weight = conv_weight_grad(feats_rim, seg_padded, seg_local, grad_conv_low, tap_count)
    grad_rim = extended(grad_conv_low, (("seq", 1),), rim_width)
    grad_feats = grad_position + conv_input_grad(grad_rim, seg_padded, seg_local, conv_weight)
    grad_gains = jnp.stack([grad_gain_first, grad_gain_second], axis=1)
    grad_biases = jnp.stack(
        [
            grad_conv_bias,
            grad_shift_first,
            mixed_sums[:features],
            mixed_sums[2 * features :],
            grad_out_bias,
            grad_shift_second,
            grad_down_bias,
        ],
        axis=1,
    )
    shared = (
        lax.psum_scatter(grad_conv_weight, "seq", scatter_dimension=0, tiled=True),
        lax.psum_scatter(grad_w_qkv, "seq", scatter_dimension=0, tiled=True),
        lax.psum_scatter(grad_w_out, "seq", scatter_dimension=0, tiled=True),
        lax.psum_scatter(grad_w_up, "seq", scatter_dimension=0, tiled=True),
        lax.psum_scatter(grad_w_down, "seq", scatter_dimension=0, tiled=True),
        lax.psum_scatter(grad_head_w, "seq", scatter_dimension=0, tiled=True),
        lax.psum_scatter(grad_gains, "seq", scatter_dimension=0, tiled=True),
        lax.psum_scatter(grad_biases, "seq", scatter_dimension=0, tiled=True),
        lax.psum_scatter(grad_up_bias, "seq", scatter_dimension=0, tiled=True),
    )
    summed = (
        lax.psum(shared[0].astype(jnp.bfloat16), "dp").astype(jnp.float32),
        lax.psum(shared[1].astype(jnp.bfloat16), "dp").astype(jnp.float32),
        lax.psum(shared[2].astype(jnp.bfloat16), "dp").astype(jnp.float32),
        lax.psum(shared[3].astype(jnp.bfloat16), "dp").astype(jnp.float32),
        lax.psum(shared[4].astype(jnp.bfloat16), "dp").astype(jnp.float32),
        lax.psum(shared[5].astype(jnp.bfloat16), "dp").astype(jnp.float32),
        lax.psum(shared[6].astype(jnp.bfloat16), "dp").astype(jnp.float32),
        lax.psum(shared[7].astype(jnp.bfloat16), "dp").astype(jnp.float32),
        lax.psum(shared[8].astype(jnp.bfloat16), "dp").astype(jnp.float32),
    )
    loss_total, head_bias_total = lax.psum((local_loss, grad_head_b), ("dp", "seq"))
    loss = loss_total / (tokens * lax.axis_size("dp") * lax.axis_size("seq"))
    layer_out = output_low.reshape(row_count, frames, features)
    return (
        layer_out,
        loss,
        grad_feats,
        summed[0],
        summed[1],
        summed[2],
        summed[3],
        summed[4],
        summed[5],
        head_bias_total,
        summed[6],
        summed[7],
        summed[8],
    )


def whole_solution(mesh):
    placed = (
        P("dp", "seq", None),
        P("dp", None),
        P("dp", "seq"),
        P(),
        P(),
        P(),
        P(),
        P(),
        P(),
        P(),
        P(),
        P(),
        P(),
    )
    return jax.shard_map(
        body,
        mesh=mesh,
        in_specs=placed,
        out_specs=(
            P("dp", "seq", None),
            P(),
            P("dp", "seq", None),
            P("seq", None),
            P("seq", None),
            P("seq", None),
            P("seq", None),
            P("seq", None),
            P("seq", None),
            P(),
            P("seq", None),
            P("seq", None),
            P("seq"),
        ),
        check_vma=False,
    )


def cost(flops, bytes_accessed, transcendentals):
    return pl.CostEstimate(
        flops=int(flops * COST_SHARE), bytes_accessed=int(bytes_accessed * COST_SHARE), transcendentals=int(transcendentals * COST_SHARE)
    )


def lanes_dot(a, b):
    return lax.dot_general(a, b, (((1,), (1,)), ((), ())), preferred_element_type=jnp.float32)


def rows_dot(a, b):
    return lax.dot_general(a, b, (((0,), (0,)), ((), ())), preferred_element_type=jnp.float32)


def attend_parts(side, queries, keys, values, allowed, low):
    mine = low if side == 0 else jnp.logical_not(low)
    scores = lanes_dot(jnp.where(mine, keys, jnp.zeros_like(keys)), queries)
    scores = jnp.where(allowed, scores, masked_score)
    top = jnp.max(scores, axis=0, keepdims=True)
    return scores, top


def attend_kernel(seg_q_ref, seg_k_ref, q_ref, k_ref, v_ref, mixed_ref, state_ref):
    queries = q_ref[...] * jnp.bfloat16(0.125)
    low = lax.broadcasted_iota(jnp.int32, k_ref.shape, 1) < 64
    allowed = seg_k_ref[...] == seg_q_ref[...]
    for side in range(2):
        scores, top = attend_parts(side, queries, k_ref[...], None, allowed, low)
        weights = jnp.exp(scores - top)
        state_ref[0, side : side + 1, :] = top
        state_ref[0, side + 2 : side + 3, :] = jnp.sum(weights, axis=0, keepdims=True)
        mixed = rows_dot(v_ref[...], weights.astype(jnp.bfloat16))
        mixed_ref[side * 64 : (side + 1) * 64, :] = mixed[side * 64 : (side + 1) * 64, :]


def attend_far_kernel(seg_q_ref, seg_k_ref, q_ref, k_ref, v_ref, mixed_ref, state_ref, out_ref, low_ref, away_ref, lse_ref):
    queries = q_ref[...] * jnp.bfloat16(0.125)
    low = lax.broadcasted_iota(jnp.int32, k_ref.shape, 1) < 64
    allowed = seg_k_ref[...] == seg_q_ref[...]
    pieces = []
    for side in range(2):
        scores, top = attend_parts(side, queries, k_ref[...], None, allowed, low)
        near_top = state_ref[0, side : side + 1, :]
        top = jnp.maximum(top, near_top)
        weights = jnp.exp(scores - top)
        rescale = jnp.exp(near_top - top)
        total = state_ref[0, side + 2 : side + 3, :] * rescale + jnp.sum(weights, axis=0, keepdims=True)
        mixed = rows_dot(v_ref[...], weights.astype(jnp.bfloat16))[side * 64 : (side + 1) * 64, :]
        pieces.append((mixed + mixed_ref[side * 64 : (side + 1) * 64, :] * rescale) / total)
        lse_ref[0, side : side + 1, :] = top + jnp.log(total)
    attended = jnp.concatenate(pieces, axis=0).T
    own = low_ref.shape[0]
    out_ref[...] = attended
    low_ref[...] = attended[:own, :].astype(jnp.bfloat16)
    away_ref[...] = attended[own:, :].astype(jnp.bfloat16)


def attend_specs(frames, length, pairs):
    return [
        pl.BlockSpec((1, frames), lambda p: (0, 0)),
        pl.BlockSpec((length, 1), lambda p: (0, 0)),
        pl.BlockSpec((frames, 128), lambda p: (0, p)),
        pl.BlockSpec((length, 128), lambda p: (0, p)),
        pl.BlockSpec((length, 128), lambda p: (0, pairs + p)),
    ]


def attend_cost(frames, length, pairs, products):
    return cost(
        flops=4 * products * pairs * frames * length * 128,
        bytes_accessed=16 * frames * pairs * 128,
        transcendentals=2 * pairs * frames * length,
    )


def attend_near(queries, pair, seg_q, seg_k):
    frames, width = queries.shape
    length = pair.shape[0]
    pairs = width // 128
    return pl.pallas_call(
        attend_kernel,
        grid=(pairs,),
        in_specs=attend_specs(frames, length, pairs),
        out_specs=[
            pl.BlockSpec((128, frames), lambda p: (p, 0)),
            pl.BlockSpec((1, 8, frames), lambda p: (p, 0, 0)),
        ],
        out_shape=[
            jax.ShapeDtypeStruct((width, frames), jnp.float32),
            jax.ShapeDtypeStruct((pairs, 8, frames), jnp.float32),
        ],
        compiler_params=pltpu.CompilerParams(vmem_limit_bytes=VMEM_LIMIT),
        cost_estimate=attend_cost(frames, length, pairs, 2),
        name="attend_near",
    )(seg_q.reshape(1, -1), seg_k.reshape(-1, 1), queries, pair, pair)


def attend_far(queries, pair, seg_q, seg_k, mixed, state):
    frames, width = queries.shape
    length = pair.shape[0]
    pairs = width // 128
    return pl.pallas_call(
        attend_far_kernel,
        grid=(pairs,),
        in_specs=attend_specs(frames, length, pairs)
        + [
            pl.BlockSpec((128, frames), lambda p: (p, 0)),
            pl.BlockSpec((1, 8, frames), lambda p: (p, 0, 0)),
        ],
        out_specs=[
            pl.BlockSpec((frames, 128), lambda p: (0, p)),
            pl.BlockSpec((frames // 2, 128), lambda p: (0, p)),
            pl.BlockSpec((frames // 2, 128), lambda p: (0, p)),
            pl.BlockSpec((1, 8, frames), lambda p: (p, 0, 0)),
        ],
        out_shape=[
            jax.ShapeDtypeStruct((frames, width), jnp.float32),
            jax.ShapeDtypeStruct((frames // 2, width), jnp.bfloat16),
            jax.ShapeDtypeStruct((frames // 2, width), jnp.bfloat16),
            jax.ShapeDtypeStruct((pairs, 8, frames), jnp.float32),
        ],
        compiler_params=pltpu.CompilerParams(vmem_limit_bytes=VMEM_LIMIT),
        cost_estimate=attend_cost(frames, length, pairs, 2),
        name="attend_far",
    )(seg_q.reshape(1, -1), seg_k.reshape(-1, 1), queries, pair, pair, mixed, state)


def attend_back_kernel(seg_q_ref, seg_k_ref, q_ref, k_ref, v_ref, g_ref, a_ref, lse_ref, after_ref, dq_ref, dkv_ref):
    queries = q_ref[...] * jnp.bfloat16(0.125)
    key_count = k_ref.shape[0]
    low = lax.broadcasted_iota(jnp.int32, (key_count, 128), 1) < 64
    keys, values, grads = k_ref[...], v_ref[...], g_ref[...]
    allowed = seg_k_ref[...] == seg_q_ref[...]
    products = (grads.astype(jnp.float32) * a_ref[...]).T
    dq, dk, dv = [], [], []
    for side in range(2):
        mine = low if side == 0 else jnp.logical_not(low)
        zero = jnp.zeros_like(keys)
        scores = lanes_dot(jnp.where(mine, keys, zero), queries)
        probs = jnp.where(allowed, jnp.exp(scores - lse_ref[0, side : side + 1, :]), 0.0)
        dots = jnp.sum(products[side * 64 : (side + 1) * 64, :], axis=0, keepdims=True)
        dv.append(jnp.dot(probs.astype(jnp.bfloat16), grads, preferred_element_type=jnp.float32))
        grad_probs = lanes_dot(jnp.where(mine, values, zero), grads)
        grad_scores = (probs * (grad_probs - dots)).astype(jnp.bfloat16)
        dk.append(jnp.dot(grad_scores, queries, preferred_element_type=jnp.float32))
        dq.append(rows_dot(keys, grad_scores)[side * 64 : (side + 1) * 64, :])
    dq_ref[...] = 0.125 * jnp.concatenate(dq, axis=0).T
    dkv_ref[0] = jnp.where(low, dk[0], dk[1]).astype(dkv_ref.dtype)
    dkv_ref[1] = jnp.where(low, dv[0], dv[1]).astype(dkv_ref.dtype)


def attend_back(queries, pair, grads, attended, lse, seg_q, seg_k, kind, after):
    frames, width = queries.shape
    length = pair.shape[0]
    pairs = width // 128
    return pl.pallas_call(
        attend_back_kernel,
        grid=(pairs,),
        in_specs=attend_specs(frames, length, pairs)
        + [
            pl.BlockSpec((frames, 128), lambda p: (0, p)),
            pl.BlockSpec((frames, 128), lambda p: (0, p)),
            pl.BlockSpec((1, 8, frames), lambda p: (p, 0, 0)),
            pl.BlockSpec(memory_space=pl.ANY),
        ],
        out_specs=[
            pl.BlockSpec((frames, 128), lambda p: (0, p)),
            pl.BlockSpec((2, length, 128), lambda p: (0, 0, p)),
        ],
        out_shape=[
            jax.ShapeDtypeStruct((frames, width), jnp.float32),
            jax.ShapeDtypeStruct((2, length, width), kind),
        ],
        compiler_params=pltpu.CompilerParams(vmem_limit_bytes=VMEM_LIMIT),
        cost_estimate=attend_cost(frames, length, pairs, 5),
        name="attend_back",
    )(seg_q.reshape(1, -1), seg_k.reshape(-1, 1), queries, pair, pair, grads, attended, lse, after)


def phi_parts(values):
    below = 0.5 * (1.0 + lax.erf(values * (0.5**0.5)))
    density = jnp.exp(-0.5 * values * values) * (1.0 / math.sqrt(2.0 * math.pi))
    return below, density


def norm_parts(values):
    center = values - jnp.mean(values, axis=-1, keepdims=True)
    scale = lax.rsqrt(jnp.mean(center * center, axis=-1, keepdims=True) + epsilon)
    return center * scale, scale


def norm_back(grad, hat, scale, gain):
    inner = grad * gain
    mean_inner = jnp.mean(inner, axis=-1, keepdims=True)
    mean_hat = jnp.mean(inner * hat, axis=-1, keepdims=True)
    return (inner - mean_inner - hat * mean_hat) * scale


def column_sum(values):
    return jnp.sum(values, axis=0, keepdims=True)


def by_core(core, mine, other):
    return jnp.where(core == 0, mine, other), jnp.where(core == 0, other, mine)


def mix_kernel(first, meta, *refs):
    if first:
        mine_ref, other_ref, gain_ref, shift_ref, w_ref, bias_ref, theirs_ref, ours_ref, normed_ref, position_ref = refs
    else:
        normed_ref, w_ref, bias_ref, theirs_ref, ours_ref = refs
    step = pl.program_id(0)
    half = w_ref.shape[1]
    if first:

        @pl.when(step == 0)
        def _():
            left, right = by_core(meta[0], mine_ref[...], other_ref[...])
            position_ref[:, :half] = left
            position_ref[:, half:] = right
            hat, _ = norm_parts(position_ref[...])
            normed_ref[...] = (hat * gain_ref[...] + shift_ref[...]).astype(jnp.bfloat16)

    block = jnp.dot(normed_ref[...], w_ref[...], preferred_element_type=jnp.float32) + bias_ref[...]
    block = block.astype(jnp.bfloat16)
    parts = theirs_ref.shape[1] // half

    @pl.when(step < parts)
    def _():
        theirs_ref[:, pl.ds(pl.multiple_of(step * half, half), half)] = block

    @pl.when(step >= parts)
    def _():
        ours_ref[:, pl.ds(pl.multiple_of((step - parts) * half, half), half)] = block


def mix_rows(core, sources, weight, bias, begin, parts):
    first = len(sources) > 1
    tokens = sources[0].shape[0]
    features = weight.shape[0]
    half = features // 2

    def column(i, meta):
        return 2 * (begin + i % parts) + jnp.where(i < parts, 1 - meta[0], meta[0])

    whole = lambda shape: pl.BlockSpec(shape, lambda i, meta: (0, 0))
    out_specs = [whole((tokens, parts * half))] * 2
    out_shape = [jax.ShapeDtypeStruct((tokens, parts * half), jnp.bfloat16)] * 2
    if first:
        out_specs = out_specs + [whole((tokens, features))] * 2
        out_shape = out_shape + [jax.ShapeDtypeStruct((tokens, features), kind) for kind in (jnp.bfloat16, jnp.float32)]
    return pl.pallas_call(
        partial(mix_kernel, first),
        grid_spec=pltpu.PrefetchScalarGridSpec(
            num_scalar_prefetch=1,
            grid=(2 * parts,),
            in_specs=[whole(item.shape) for item in sources]
            + [
                pl.BlockSpec((features, half), lambda i, meta: (0, column(i, meta))),
                pl.BlockSpec((1, half), lambda i, meta: (0, column(i, meta))),
            ],
            out_specs=out_specs,
        ),
        out_shape=out_shape,
        compiler_params=pltpu.CompilerParams(vmem_limit_bytes=VMEM_LIMIT, dimension_semantics=("arbitrary",)),
        cost_estimate=cost(
            flops=4 * parts * tokens * half * features, bytes_accessed=4 * parts * half * features, transcendentals=0
        ),
        name="norm_keys_values" if first else "queries",
    )(core, *sources, weight, bias)


def unmix_kernel(
    meta, mine_ref, other_ref, w_ref, position_ref, resid_ref, gain_ref, *refs
):
    ours_ref, theirs_ref, sums_ref, total = refs[-4:]
    step = pl.program_id(0)
    half = theirs_ref.shape[1]

    @pl.when(step == 0)
    def _():
        total[...] = jnp.zeros_like(total)

    block = jnp.where(step < 3, mine_ref[...], other_ref[...])
    total[...] += lanes_dot(block, w_ref[...])

    @pl.when(step == 5)
    def _():
        grad = total[...]
        hat, scale = norm_parts(position_ref[...])
        sums_ref[0:1, :] = column_sum(grad * hat)
        sums_ref[1:2, :] = column_sum(grad)
        sums_ref[2:8, :] = jnp.zeros((6, 2 * half), jnp.float32)
        result = resid_ref[...] + norm_back(grad, hat, scale, gain_ref[...])
        low_half, high_half = result[:, :half], result[:, half:]
        ours_ref[...] = jnp.where(meta[0] == 0, low_half, high_half)
        theirs_ref[...] = jnp.where(meta[0] == 0, high_half, low_half)


def unmix_rows(core, mine, other, weight, position, grad_resid, gain, after):
    tokens, features = position.shape
    half = features // 2

    def column(i, meta):
        return 2 * (i % 3) + jnp.where(i < 3, meta[0], 1 - meta[0])

    whole = lambda shape: pl.BlockSpec(shape, lambda i, meta: (0, 0))
    return pl.pallas_call(
        unmix_kernel,
        grid_spec=pltpu.PrefetchScalarGridSpec(
            num_scalar_prefetch=1,
            grid=(6,),
            in_specs=[
                pl.BlockSpec((tokens, half), lambda i, meta: (0, i % 3)),
                pl.BlockSpec((tokens, half), lambda i, meta: (0, i % 3)),
                pl.BlockSpec((features, half), lambda i, meta: (0, column(i, meta))),
                whole((tokens, features)),
                whole((tokens, features)),
                whole((1, features)),
            ]
            + [pl.BlockSpec(memory_space=pl.ANY)] * len(after),
            out_specs=[whole((tokens, half)), whole((tokens, half)), whole((8, features))],
            scratch_shapes=[pltpu.VMEM((tokens, features), jnp.float32)],
        ),
        out_shape=[
            jax.ShapeDtypeStruct((tokens, half), jnp.float32),
            jax.ShapeDtypeStruct((tokens, half), jnp.float32),
            jax.ShapeDtypeStruct((8, features), jnp.float32),
        ],
        compiler_params=pltpu.CompilerParams(vmem_limit_bytes=VMEM_LIMIT, dimension_semantics=("arbitrary",)),
        cost_estimate=cost(flops=12 * tokens * half * features, bytes_accessed=14 * half * features, transcendentals=0),
        name="qkv_and_norm_back",
    )(core, mine, other, weight, position, grad_resid, gain, *after)


def pack_places(features, width):
    places, at = {}, 0
    for name, size in (
        ("active", width), ("second", features), ("attended", features), ("up", width // 2),
        ("out", features // 2), ("branch", features // 2),
    ):
        places[name] = at
        at += size
    places["all"] = at
    return places


def middle_kernel(
    meta, mine_ref, other_ref, position_ref, w_out_ref, w_up_ref, w_down_ref, up_bias_ref, head_w_ref, head_b_ref,
    labels_ref, rows_ref, after_a, after_b,
    pack_ref, output_ref, out_low_ours, up_ours, branch_ours, att_ours, att_theirs, resid_grad_ref, sums_ref,
    up_sums_ref, head_ref, last_ref,
    resid, total, slope, grad_out, grad_low,
):
    step = pl.program_id(0)
    chunks = slope.shape[0]
    core = meta[0]
    half = mine_ref.shape[1]
    features = 2 * half
    chunk_width = slope.shape[2]
    places = pack_places(features, chunks * chunk_width)

    def at(name, size):
        return slice(places[name], places[name] + size)

    second_at, attended_at = at("second", features), at("attended", features)

    def store_halves(ours, theirs, values):
        low_half, high_half = values[:, :half], values[:, half:]
        ours[...] = jnp.where(core == 0, low_half, high_half)
        theirs[...] = jnp.where(core == 0, high_half, low_half)

    @pl.when(step == 0)
    def _():
        left, right = by_core(core, mine_ref[...].astype(jnp.float32), other_ref[...].astype(jnp.float32))
        pack_ref[:, places["attended"] : places["attended"] + half] = left.astype(jnp.bfloat16)
        pack_ref[:, places["attended"] + half : places["attended"] + features] = right.astype(jnp.bfloat16)
        resid[...] = (
            position_ref[...]
            + jnp.dot(pack_ref[:, attended_at], w_out_ref[...], preferred_element_type=jnp.float32)
            + rows_ref[2:3, :]
        )
        hat, _ = norm_parts(resid[...])
        pack_ref[:, second_at] = (hat * rows_ref[0:1, :] + rows_ref[1:2, :]).astype(jnp.bfloat16)
        total[...] = jnp.zeros_like(total)

    @pl.when(step < chunks)
    def _():
        raised = jnp.dot(pack_ref[:, second_at], w_up_ref[...], preferred_element_type=jnp.float32) + up_bias_ref[...]
        below, density = phi_parts(raised)
        slope[step] = below + raised * density
        active = (raised * below).astype(jnp.bfloat16)
        pack_ref[:, pl.ds(pl.multiple_of(places["active"] + step * chunk_width, chunk_width), chunk_width)] = active
        total[...] += jnp.dot(active, w_down_ref[...], preferred_element_type=jnp.float32)

    @pl.when(step == chunks - 1)
    def _():
        low = (resid[...] + total[...] + rows_ref[3:4, :]).astype(jnp.bfloat16)
        output_ref[...] = low
        logits = jnp.dot(low, head_w_ref[...], preferred_element_type=jnp.float32) + head_b_ref[...]
        top = jnp.max(logits, axis=-1, keepdims=True)
        shifted = jnp.exp(logits - top)
        sums = jnp.sum(shifted, axis=-1, keepdims=True)
        onehot = labels_ref[...] == lax.broadcasted_iota(jnp.int32, logits.shape, 1)
        picked = jnp.sum(jnp.where(onehot, logits, 0.0), axis=-1, keepdims=True)
        loss = jnp.sum(top + jnp.log(sums) - picked)
        grad_logits = (shifted / sums - onehot.astype(jnp.float32)).astype(jnp.bfloat16)
        head_ref[...] = rows_dot(grad_logits, low)
        last_ref[...] = jnp.zeros_like(last_ref)
        last_ref[0:1, 0:VOCAB] = column_sum(grad_logits.astype(jnp.float32))
        last_ref[1:2, :] = jnp.full((1, 128), loss, jnp.float32)
        grad = lanes_dot(grad_logits, head_w_ref[...])
        grad_out[...] = grad
        grad_low[...] = grad.astype(jnp.bfloat16)
        store_halves(out_low_ours, pack_ref.at[:, at("out", half)], grad_low[...])
        sums_ref[3:4, :] = column_sum(grad_low[...].astype(jnp.float32))
        sums_ref[4:8, :] = jnp.zeros((4, 2 * half), jnp.float32)
        total[...] = jnp.zeros_like(total)

    @pl.when(step >= chunks)
    def _():
        chunk = 2 * chunks - 1 - step
        grad = lanes_dot(grad_low[...], w_down_ref[...]) * slope[chunk]
        low = grad.astype(jnp.bfloat16)
        up_sums_ref[0] = jnp.broadcast_to(column_sum(low.astype(jnp.float32)), up_sums_ref.shape[1:])
        total[...] += lanes_dot(low, w_up_ref[...])
        ours = (chunk >= chunks // 2) == (core == 1)

        @pl.when(ours)
        def _():
            up_ours[...] = low

        @pl.when(jnp.logical_not(ours))
        def _():
            place = places["up"] + (chunk & (chunks // 2 - 1)) * chunk_width
            pack_ref[:, pl.ds(pl.multiple_of(place, chunk_width), chunk_width)] = low

    @pl.when(step == 2 * chunks - 1)
    def _():
        hat, scale = norm_parts(resid[...])
        grad = total[...]
        sums_ref[0:1, :] = column_sum(grad * hat)
        sums_ref[2:3, :] = column_sum(grad)
        result = grad_out[...] + norm_back(grad, hat, scale, rows_ref[0:1, :])
        resid_grad_ref[...] = result
        branch = result.astype(jnp.bfloat16)
        store_halves(branch_ours, pack_ref.at[:, at("branch", half)], branch)
        sums_ref[1:2, :] = column_sum(branch.astype(jnp.float32))
        store_halves(att_ours, att_theirs, lanes_dot(branch, w_out_ref[...]).astype(jnp.bfloat16))


def middle(core, mine, other, position, w_out, w_up, w_down, up_bias, head_w, head_b, labels, rows, after):
    tokens, features = position.shape
    half = features // 2
    width = w_up.shape[1]
    chunks = 8
    chunk = width // chunks
    vocab = head_w.shape[1]
    last = 2 * chunks - 1

    def part(i):
        return jnp.where(i < chunks, i, last - i)

    def own_up(i, meta):
        back = part(jnp.maximum(i, chunks))
        return jnp.where(meta[0] == 0, jnp.minimum(back, chunks // 2 - 1), jnp.maximum(back - chunks // 2, 0))

    whole = lambda shape: pl.BlockSpec(shape, lambda i, meta: tuple(0 for _ in shape))
    low = lambda *shape: jax.ShapeDtypeStruct(shape, jnp.bfloat16)
    full = lambda *shape: jax.ShapeDtypeStruct(shape, jnp.float32)
    return pl.pallas_call(
        middle_kernel,
        grid_spec=pltpu.PrefetchScalarGridSpec(
            num_scalar_prefetch=1,
            grid=(2 * chunks,),
            in_specs=[
                whole((tokens, half)),
                whole((tokens, half)),
                whole((tokens, features)),
                whole((features, features)),
                pl.BlockSpec((features, chunk), lambda i, meta: (0, part(i))),
                pl.BlockSpec((chunk, features), lambda i, meta: (part(i), 0)),
                pl.BlockSpec((1, chunk), lambda i, meta: (0, part(i))),
                whole((features, vocab)),
                whole((1, vocab)),
                whole((tokens, 1)),
                whole((8, features)),
                pl.BlockSpec(memory_space=pl.ANY),
                pl.BlockSpec(memory_space=pl.ANY),
            ],
            out_specs=[
                whole((tokens, pack_places(features, width)["all"])),
                whole((tokens, features)),
                whole((tokens, half)),
                pl.BlockSpec((tokens, chunk), lambda i, meta: (0, own_up(i, meta))),
                whole((tokens, half)),
                whole((tokens, half)),
                whole((tokens, half)),
                whole((tokens, features)),
                whole((8, features)),
                pl.BlockSpec((1, 8, chunk), lambda i, meta: (part(jnp.maximum(i, chunks)), 0, 0)),
                whole((vocab, features)),
                whole((8, 128)),
            ],
            scratch_shapes=[
                pltpu.VMEM((tokens, features), jnp.float32),
                pltpu.VMEM((tokens, features), jnp.float32),
                pltpu.VMEM((chunks, tokens, chunk), jnp.float32),
                pltpu.VMEM((tokens, features), jnp.float32),
                pltpu.VMEM((tokens, features), jnp.bfloat16),
            ],
        ),
        out_shape=[
            low(tokens, pack_places(features, width)["all"]),
            low(tokens, features),
            low(tokens, half),
            low(tokens, width // 2),
            low(tokens, half),
            low(tokens, half),
            low(tokens, half),
            full(tokens, features),
            full(8, features),
            full(chunks, 8, chunk),
            full(vocab, features),
            full(8, 128),
        ],
        compiler_params=pltpu.CompilerParams(vmem_limit_bytes=VMEM_LIMIT, dimension_semantics=("arbitrary",)),
        cost_estimate=cost(
            flops=8 * tokens * features * width, bytes_accessed=8 * features * width, transcendentals=2 * tokens * width
        ),
        name="middle",
    )(core, mine, other, position, w_out, w_up, w_down, up_bias, head_w, head_b, labels, rows, *after)


def conv_grad_kernel(meta, ours_ref, got_ref, slope_ref, *refs):
    position_ref, grad_ref, edge_ref, own_ref, to_x_ref, to_y_ref, to_xy_ref, sums_ref = refs[-8:]
    core, y, x = meta[0], meta[1], meta[2]
    frames = ours_ref.shape[0]
    rim = edge_ref.shape[0]
    ours, got = ours_ref[...], got_ref[...]
    position_ref[0:frames, :] = jnp.where(core == 0, ours, got)
    position_ref[frames:, :] = jnp.where(core == 0, got, ours)
    grad_ref[...] = (position_ref[...] * slope_ref[...]).astype(jnp.bfloat16)
    edge_ref[...] = jnp.where(x == 0, grad_ref[2 * frames - rim :, :], grad_ref[0:rim, :])
    sums_ref[...] = jnp.broadcast_to(column_sum(grad_ref[...].astype(jnp.float32)), sums_ref.shape)
    for ref, yy, xx in ((own_ref, y, x), (to_x_ref, y, 1 - x), (to_y_ref, 1 - y, x), (to_xy_ref, 1 - y, 1 - x)):
        ref[...] = grad_ref[:, pl.ds(pl.multiple_of(256 * xx + 128 * yy, 128), 128)]


def conv_grad_rows(meta, ours, got, slope, after):
    frames, half = ours.shape
    operands = (ours, got, slope)
    shapes = [((2 * frames, half), jnp.float32), ((2 * frames, half), jnp.bfloat16), ((KERNEL // 2, half), jnp.bfloat16)]
    shapes += [((2 * frames, 128), jnp.bfloat16)] * 4 + [((8, half), jnp.float32)]
    return pl.pallas_call(
        conv_grad_kernel,
        grid_spec=pltpu.PrefetchScalarGridSpec(
            num_scalar_prefetch=1,
            grid=(1,),
            in_specs=[pl.BlockSpec(item.shape, lambda i, m: (0, 0)) for item in operands]
            + [pl.BlockSpec(memory_space=pl.ANY)] * len(after),
            out_specs=[pl.BlockSpec(shape, lambda i, m: (0, 0)) for shape, _ in shapes],
        ),
        out_shape=[jax.ShapeDtypeStruct(shape, kind) for shape, kind in shapes],
        compiler_params=pltpu.CompilerParams(vmem_limit_bytes=VMEM_LIMIT, dimension_semantics=("arbitrary",)),
        cost_estimate=cost(flops=0, bytes_accessed=4000000, transcendentals=0),
        name="conv_grad_rows",
    )(meta, *operands, *after)


def weight_kernel(tasks, out_count, carries, meta, *refs):
    refs = list(refs)
    step = pl.program_id(0)
    if carries:
        carried_ref = refs.pop()
        carry_ref = refs.pop(-1 - out_count)

        @pl.when(step == 0)
        def _():
            carried_ref[...] = carry_ref[...]

    inputs = []
    for task in tasks:
        inputs.append([refs.pop(0) for _ in range(5 if task["add"] is not None else 4)])
    outs = refs[-out_count:]
    begin = 0
    for task, ins in zip(tasks, inputs):
        rows, columns = task["rows"], task["columns"]

        def store(where, values, at, task=task):
            index, column = where
            size = values.shape[0]
            span = pl.ds(pl.multiple_of(at * size, size), size)
            outs[index][span, column : column + values.shape[1]] = values.astype(jnp.bfloat16)

        @pl.when(jnp.logical_and(step >= begin, step < begin + task["blocks"]))
        def _(task=task, ins=ins, begin=begin, store=store, rows=rows, columns=columns):
            total = rows_dot(ins[0][...], ins[2][...]) + rows_dot(ins[1][...], ins[3][...])
            if task["add"] is not None:
                total = total + ins[4][...].astype(jnp.float32)
            at = step - begin + task["place"]
            if task["split"] is None:
                store(task["outs"][0], total, at)
                return
            if task["split"] == "columns":
                first, second = total[:, : columns // 2], total[:, columns // 2 :]
            else:
                blocks = total.reshape(-1, 2, task["unit"], columns)
                first, second = (blocks[:, k].reshape(rows // 2, columns) for k in range(2))
            bit = task["bit"](meta)
            store(task["outs"][0], jnp.where(bit == 0, second, first), at)
            store(task["outs"][1], jnp.where(bit == 0, first, second), at)

        begin = begin + task["blocks"]


def weight_task(
    outs, left, right, rows, blocks, row_of, columns, column_of, add=None, add_of=None, split=None, bit=None, unit=0, place=0
):
    return dict(
        outs=outs, left=left, right=right, rows=rows, blocks=blocks, row_of=row_of, columns=columns,
        column_of=column_of, add=add, add_of=add_of, split=split, bit=bit, unit=unit, place=place,
    )


def weight_parts(meta, tasks, shapes, name, after, carry=None):
    in_specs, operands = [], []
    begin, flops, moved = 0, 0, 0
    for task in tasks:
        rows, columns, blocks = task["rows"], task["columns"], task["blocks"]
        tokens = task["left"][0][0].shape[0]

        def local(i, begin=begin, blocks=blocks):
            return jnp.clip(i - begin, 0, blocks - 1)

        for array, base in task["left"]:
            in_specs.append(
                pl.BlockSpec(
                    (tokens, rows), lambda i, m, t=task, local=local, base=base: (0, base // t["rows"] + t["row_of"](local(i), m))
                )
            )
            operands.append(array)
        for array, base in task["right"]:
            in_specs.append(
                pl.BlockSpec((tokens, columns), lambda i, m, t=task, base=base: (0, base // t["columns"] + t["column_of"](m)))
            )
            operands.append(array)
        if task["add"] is not None:
            in_specs.append(pl.BlockSpec((rows, columns), lambda i, m, t=task, local=local: t["add_of"](local(i), m)))
            operands.append(task["add"])
        begin += blocks
        flops += 4 * tokens * rows * blocks * columns
        moved += 2 * rows * blocks * columns + 4 * tokens * (rows * blocks + columns)
    in_specs.append(pl.BlockSpec(memory_space=pl.ANY))
    operands.append(after)
    out_shapes = list(shapes)
    if carry is not None:
        in_specs.append(pl.BlockSpec(carry.shape, lambda i, m: (0, 0)))
        operands.append(carry)
        out_shapes.append(carry.shape)
    return pl.pallas_call(
        partial(weight_kernel, tasks, len(shapes), carry is not None),
        grid_spec=pltpu.PrefetchScalarGridSpec(
            num_scalar_prefetch=1,
            grid=(begin,),
            in_specs=in_specs,
            out_specs=[pl.BlockSpec(shape, lambda i, m: (0, 0)) for shape in out_shapes],
        ),
        out_shape=[jax.ShapeDtypeStruct(shape, jnp.bfloat16) for shape in out_shapes],
        compiler_params=pltpu.CompilerParams(vmem_limit_bytes=VMEM_LIMIT, dimension_semantics=("arbitrary",)),
        cost_estimate=cost(flops=flops, bytes_accessed=moved, transcendentals=0),
        name=name,
    )(meta, *operands)


def flip_kernel(meta, in_ref, out_ref):
    out_ref[...] = in_ref[0].astype(jnp.float32).T


def flip_columns(meta, pieces):
    count, width, rows = pieces.shape

    def column(i, m):
        return 4 * (m[0] ^ (i >> 2)) + 2 * (i & 1) + (m[1] ^ ((i >> 1) & 1))

    return pl.pallas_call(
        flip_kernel,
        grid_spec=pltpu.PrefetchScalarGridSpec(
            num_scalar_prefetch=1,
            grid=(count,),
            in_specs=[pl.BlockSpec((1, width, rows), lambda i, m: (i, 0, 0))],
            out_specs=pl.BlockSpec((rows, width), lambda i, m: (0, column(i, m))),
        ),
        out_shape=jax.ShapeDtypeStruct((rows, count * width), jnp.float32),
        compiler_params=pltpu.CompilerParams(vmem_limit_bytes=VMEM_LIMIT, dimension_semantics=("arbitrary",)),
        cost_estimate=cost(flops=0, bytes_accessed=6 * count * width * rows, transcendentals=0),
        name="flip_columns",
    )(meta, pieces)


def small_kernel(meta, head_ref, mid_ref, first_ref, conv_ref, ours_ref, got_ref, up_ref, last_ref, after_ref, out_ref):
    core = meta[0]
    half = conv_ref.shape[1]
    zero = jnp.zeros((1, half), jnp.float32)

    def wide(left, right):
        return jnp.concatenate([left, right], axis=1)

    def halves(part):
        ours = ours_ref[0:1, part * half : (part + 1) * half]
        got = got_ref[0:1, part * half : (part + 1) * half]
        return wide(jnp.where(core == 0, ours, got), jnp.where(core == 0, got, ours))

    conv = conv_ref[0:1, :]
    rows = jnp.concatenate(
        [
            mid_ref[0:4, :],
            first_ref[0:2, :],
            wide(jnp.where(core == 0, conv, zero), jnp.where(core == 0, zero, conv)),
            halves(0),
            halves(2),
        ],
        axis=0,
    )
    unit = out_ref.shape[2]
    for j in range(8):
        span = slice(j * unit, (j + 1) * unit)
        out_ref[j, 0:VOCAB, :] = head_ref[:, span]
        out_ref[j, VOCAB : VOCAB + 9, :] = rows[:, span]
        for r in range(4):
            out_ref[j, VOCAB + 9 + r : VOCAB + 10 + r, :] = up_ref[j, 0:1, r * unit : (r + 1) * unit]
        out_ref[j, VOCAB + 13 : VOCAB + 15, :] = last_ref[0:2, :]
        out_ref[j, VOCAB + 15 : VOCAB + 16, :] = last_ref[2:3, :]


def small_sums(meta, head, mid, first, conv, ours, got, up, last, after):
    operands = (head, mid, first, conv, ours, got, up, last)
    return pl.pallas_call(
        small_kernel,
        grid_spec=pltpu.PrefetchScalarGridSpec(
            num_scalar_prefetch=1,
            grid=(1,),
            in_specs=[pl.BlockSpec(item.shape, lambda i, m, n=item.ndim: (0,) * n) for item in operands]
            + [pl.BlockSpec(memory_space=pl.ANY)],
            out_specs=pl.BlockSpec((8, 48, 128), lambda i, m: (0, 0, 0)),
        ),
        out_shape=jax.ShapeDtypeStruct((8, 48, 128), jnp.float32),
        compiler_params=pltpu.CompilerParams(vmem_limit_bytes=VMEM_LIMIT, dimension_semantics=("arbitrary",)),
        cost_estimate=cost(flops=0, bytes_accessed=400000, transcendentals=0),
        name="small_sums",
    )(meta, *operands, after)


def tile_lists(seg_ext, rise):
    row_count = seg_ext.shape[0]
    frames = seg_ext.shape[1] - KERNEL
    tiles = frames // 64
    center = seg_ext[:, KERNEL // 2 : KERNEL // 2 + frames].reshape(row_count, tiles, 64)
    first = center[:, :, 0].reshape(-1)
    counts = (center[:, :, 63].reshape(-1) - first + 1).astype(jnp.int32)
    ends = jnp.cumsum(counts)
    slots = row_count * (tiles + rise)
    slot = jnp.arange(slots, dtype=jnp.int32)
    tile = jnp.sum((slot[:, None] >= ends[None, :]).astype(jnp.int32), axis=1)
    used = tile < row_count * tiles
    tile = jnp.minimum(tile, row_count * tiles - 1)
    onehot = tile[:, None] == jnp.arange(row_count * tiles, dtype=jnp.int32)[None, :]
    begin = jnp.sum(jnp.where(onehot, (ends - counts)[None, :], 0), axis=1)
    number = jnp.sum(jnp.where(onehot, first[None, :], 0), axis=1) + slot - begin
    number = jnp.where(used, number, -2)
    in_block = tile + (tile // tiles) * (KERNEL // 64)
    return in_block.astype(jnp.int32), tile.astype(jnp.int32), number.astype(jnp.int32)


def lane_low(rows):
    return lax.broadcasted_iota(jnp.int32, (rows, 128), 1) < 64


def half_roll(block):
    return pltpu.roll(block, 64, 1)


def quad_rows(src, rows, side):
    low = lane_low(rows)
    parts = [src[pl.ds(j, rows, stride=4), :] for j in range(4)]
    halves = []
    for a, b in ((0, 1), (2, 3)):
        if side == 0:
            halves.append(jnp.where(low, parts[a], half_roll(parts[b])))
        else:
            halves.append(jnp.where(low, half_roll(parts[a]), parts[b]))
    return halves


def conv_setup(meta, slots, seg_ref, flat, shifts, masks):
    rows4 = seg_ref.shape[0]
    blocks = rows4 // 16
    one, zero = jnp.ones((16, 256), jnp.bfloat16), jnp.zeros((16, 256), jnp.bfloat16)
    flat[0:rows4, :] = seg_ref[...]
    flat[rows4:, :] = jnp.zeros((16, 256), jnp.float32)
    for p in range(16):
        shifts[p] = flat[pl.ds(p, rows4), :].astype(jnp.bfloat16).reshape(blocks, 16, 256)

    @pl.loop(0, slots)
    def _(v):
        at = meta[1 + v]
        number = jnp.full((16, 256), meta[1 + 2 * slots + v].astype(jnp.float32), jnp.float32).astype(jnp.bfloat16)
        row = pl.multiple_of(v * 16, 16)
        for b in range(TAP_BLOCKS):
            ids = shifts[b % 16, at + b // 16]
            masks[pl.ds(row, 16), b * 256 : (b + 1) * 256] = jnp.where(ids == number, one, zero)


def conv_shifts(wide, side, flat, shifts):
    rows4 = shifts.shape[1] * 16
    halves = quad_rows(wide, rows4, side)
    flat[0:rows4, 0:128] = halves[0]
    flat[0:rows4, 128:256] = halves[1]
    for p in range(16):
        shifts[p] = flat[pl.ds(p, rows4), :].astype(jnp.bfloat16).reshape(rows4 // 16, 16, 256)


def conv_patch(places, b, shifts, masks):
    span = slice(b * 256, (b + 1) * 256)
    pieces = [
        shifts[b % 16, at + b // 16] * masks[v * 16 : (v + 1) * 16, span] for v, at in enumerate(places)
    ]
    return jnp.concatenate(pieces, axis=0)


def conv_taps(w_ref, side, b, taps):
    rows = 256
    low = lane_low(rows)
    depth = w_ref.shape[0]
    zero = jnp.zeros((64, 128), jnp.bfloat16)
    if b == 0:
        here, before = w_ref[0:rows, :], jnp.concatenate([zero, w_ref[0 : rows - 64, :]], axis=0)
    elif b * rows < depth:
        here, before = w_ref[b * rows : (b + 1) * rows, :], w_ref[b * rows - 64 : (b + 1) * rows - 64, :]
    else:
        here, before = jnp.concatenate([zero] * 4, axis=0), jnp.concatenate([w_ref[depth - 64 :, :]] + [zero] * 3, axis=0)
    block = jnp.where(low, here, half_roll(before)) if side == 0 else jnp.where(low, half_roll(here), before)
    taps[128 + b * rows : 128 + (b + 1) * rows, :] = block
    return jnp.concatenate([block, taps[b * rows : (b + 1) * rows, :]], axis=1)


def conv_kernel(slots, backward, meta, x_ref, seg_ref, w_ref, extra_ref, *refs):
    refs = refs[1:] if backward else refs
    o_ref, *refs = refs
    if backward:
        wide, flat, shifts, masks, taps, sums, outs = refs
    else:
        slope_ref, wide, flat, shifts, masks, taps, sums, outs = refs

    @pl.when(pl.program_id(0) == 0)
    def _():
        conv_setup(meta, slots, seg_ref, flat, shifts, masks)

    wide[...] = x_ref[...].astype(jnp.float32)
    taps[0:128, :] = jnp.zeros((128, 128), jnp.bfloat16)
    out_rows = o_ref.shape[0] // 4
    places = [meta[1 + v] for v in range(slots)]
    for side in range(2):
        conv_shifts(wide, side, flat, shifts)
        total = jnp.zeros((256, slots * 16) if backward else (slots * 16, 256), jnp.float32)
        for b in range(TAP_BLOCKS):
            weight = conv_taps(w_ref, side, b, taps)
            if backward:
                total = total + lanes_dot(weight, conv_patch(places, TAP_BLOCKS - 1 - b, shifts, masks))
            else:
                total = total + jnp.dot(
                    conv_patch(places, b, shifts, masks), weight, preferred_element_type=jnp.float32
                )
        sums[...] = total.T if backward else total

        @pl.loop(0, slots)
        def _(v):
            to = pl.ds(pl.multiple_of(meta[1 + slots + v] * 16, 16), 16)
            row = pl.ds(pl.multiple_of(v * 16, 16), 16)
            keep = masks[row, 16 * 256 : 17 * 256].astype(jnp.float32) > 0.5
            outs[side, to, :] = jnp.where(keep, sums[row, :], outs[side, to, :])

    low = lane_low(out_rows)
    for half in range(2):
        zero_side = outs[0, :, half * 128 : (half + 1) * 128]
        one_side = outs[1, :, half * 128 : (half + 1) * 128]
        wide[pl.ds(2 * half, out_rows, stride=4), :] = jnp.where(low, zero_side, half_roll(one_side))
        wide[pl.ds(2 * half + 1, out_rows, stride=4), :] = jnp.where(low, half_roll(zero_side), one_side)
    result = wide[0 : 4 * out_rows, :]
    if backward:
        o_ref[...] = (extra_ref[...] + result).astype(o_ref.dtype)
    else:
        result = result + extra_ref[...]
        below, density = phi_parts(result)
        center = x_ref[KERNEL // 2 : KERNEL // 2 + 4 * out_rows, :].astype(jnp.float32)
        o_ref[...] = center + result * below
        slope_ref[...] = below + result * density


def seg_quads(seg_ext):
    quads = seg_ext.astype(jnp.float32).reshape(-1, 4)
    return jnp.repeat(quads, 64, axis=1)


def grouped_conv(x_ext, seg_ext, weight, extra, first_pair, rise, backward, after=None):
    row_count, length, width = x_ext.shape
    frames = length - KERNEL
    pairs = width // 128
    in_block, tile, number = tile_lists(seg_ext, rise)
    slots = in_block.shape[0]
    meta = jnp.concatenate([jnp.reshape(first_pair, (1,)).astype(jnp.int32), in_block, tile, number])
    rows4 = row_count * length // 4
    out4 = row_count * frames // 4
    depth = TAP_BLOCKS * 256
    return pl.pallas_call(
        partial(conv_kernel, slots, backward),
        grid_spec=pltpu.PrefetchScalarGridSpec(
            num_scalar_prefetch=1,
            grid=(pairs,),
            in_specs=[
                pl.BlockSpec((row_count * length, 128), lambda p, meta: (0, p)),
                pl.BlockSpec((rows4, 256), lambda p, meta: (0, 0)),
                pl.BlockSpec((weight.shape[0], 128), lambda p, meta: (0, meta[0] + p)),
                pl.BlockSpec((extra.shape[0], 128), lambda p, meta: (0, p)),
            ]
            + [pl.BlockSpec(memory_space=pl.ANY)] * (1 if backward else 0),
            out_specs=[pl.BlockSpec((row_count * frames, 128), lambda p, meta: (0, p))] * (1 if backward else 2),
            scratch_shapes=[
                pltpu.VMEM((row_count * length, 128), jnp.float32),
                pltpu.VMEM((rows4 + 16, 256), jnp.float32),
                pltpu.VMEM((16, rows4 // 16, 16, 256), jnp.bfloat16),
                pltpu.VMEM((slots * 16, depth), jnp.bfloat16),
                pltpu.VMEM((128 + depth, 128), jnp.bfloat16),
                pltpu.VMEM((slots * 16, 256), jnp.float32),
                pltpu.VMEM((2, out4, 256), jnp.float32),
            ],
        ),
        out_shape=[jax.ShapeDtypeStruct((row_count * frames, width), jnp.bfloat16 if backward else jnp.float32)]
        * (1 if backward else 2),
        compiler_params=pltpu.CompilerParams(vmem_limit_bytes=VMEM_LIMIT, dimension_semantics=("arbitrary",)),
        cost_estimate=cost(
            flops=2 * pairs * 2 * slots * 16 * 256 * depth, bytes_accessed=pairs * weight.shape[0] * 256, transcendentals=0
        ),
        name="conv_back" if backward else "conv_forth",
    )(meta, x_ext.reshape(row_count * length, width), seg_quads(seg_ext), weight, extra, *([after] if backward else []))


def at_block(b):
    return pl.ds(b * 256, 256) if isinstance(b, int) else pl.ds(pl.multiple_of(b * 256, 256), 256)


def id_block(number):
    return jnp.full((16, 256), number, jnp.float32).astype(jnp.bfloat16)


def conv_ids(seg_ref, flat, ids):
    rows4 = seg_ref.shape[0]
    flat[0:rows4, :] = seg_ref[...]
    flat[rows4:, :] = jnp.zeros((16, 256), jnp.float32)
    for p in range(16):
        ids[p] = flat[pl.ds(p, rows4), :].astype(jnp.bfloat16).reshape(rows4 // 16, 16, 256)


def conv_cut(places, numbers, b, shifts, ids):
    nothing = jnp.zeros((16, 256), jnp.bfloat16)
    pieces = []
    for at, number in zip(places, numbers):
        same = ids[b & 15, at + (b >> 4)] == id_block(number)
        pieces.append(jnp.where(same, shifts[b & 15, at + (b >> 4)], nothing))
    return jnp.concatenate(pieces, axis=0)


def conv_weight_kernel(slots, meta, x_ref, seg_ref, g_ref, after_ref, o_ref, wide, wide_g, flat, shifts, masks, quads, picks, sums):
    @pl.when(pl.program_id(0) == 0)
    def _():
        conv_ids(seg_ref, flat, masks)

    wide[...] = x_ref[...].astype(jnp.float32)
    wide_g[...] = g_ref[...].astype(jnp.float32)
    out_rows = g_ref.shape[0] // 4
    low = lane_low(64)
    places = [meta[1 + v] for v in range(slots)]
    numbers = [meta[1 + 2 * slots + v].astype(jnp.float32) for v in range(slots)]
    nothing = jnp.zeros((16, 256), jnp.bfloat16)
    for side in range(2):
        conv_shifts(wide, side, flat, shifts)
        halves = quad_rows(wide_g, out_rows, side)
        quads[:, 0:128] = halves[0].astype(jnp.bfloat16)
        quads[:, 128:256] = halves[1].astype(jnp.bfloat16)

        for v in range(slots):
            at = pl.ds(pl.multiple_of(meta[1 + slots + v] * 16, 16), 16)
            same = masks[0, places[v] + 1] == id_block(numbers[v])
            picks[v * 16 : (v + 1) * 16, :] = jnp.where(same, quads[at, :], nothing)

        turned = picks[...].T

        @pl.loop(0, TAP_BLOCKS, unroll=DW_UNROLL)
        def _(b):
            sums[:, at_block(b)] = jnp.dot(
                turned, conv_cut(places, numbers, b, shifts, masks), preferred_element_type=jnp.float32
            )

        def piece(j, q):
            return sums[j * 64 : (j + 1) * 64, q * 128 : (q + 1) * 128]

        def odd(q):
            return half_roll(piece(1, q) + piece(3, q + 1))

        left = odd(0)
        for q in range(2 * (TAP_BLOCKS - 1)):
            right = odd(q + 1)
            part = piece(0, q) + piece(2, q + 1) + jnp.where(low, left, right)
            columns = slice(q % 16 * 128, (q % 16 + 1) * 128)
            o_ref[q // 16, side * 64 : (side + 1) * 64, columns] = part.astype(o_ref.dtype)
            left = right


def grouped_conv_weight(x_ext, seg_ext, grad, rise, after):
    row_count, length, width = x_ext.shape
    frames = length - KERNEL
    pairs = width // 128
    in_block, tile, number = tile_lists(seg_ext, rise)
    slots = in_block.shape[0]
    meta = jnp.concatenate([jnp.zeros((1,), jnp.int32), in_block, tile, number])
    rows4 = row_count * length // 4
    out4 = row_count * frames // 4
    depth = TAP_BLOCKS * 256
    return pl.pallas_call(
        partial(conv_weight_kernel, slots),
        grid_spec=pltpu.PrefetchScalarGridSpec(
            num_scalar_prefetch=1,
            grid=(pairs,),
            in_specs=[
                pl.BlockSpec((row_count * length, 128), lambda p, meta: (0, p)),
                pl.BlockSpec((rows4, 256), lambda p, meta: (0, 0)),
                pl.BlockSpec((row_count * frames, 128), lambda p, meta: (0, p)),
                pl.BlockSpec(memory_space=pl.ANY),
            ],
            out_specs=pl.BlockSpec((4, 128, KERNEL * 16), lambda p, meta: (0, p, 0)),
            scratch_shapes=[
                pltpu.VMEM((row_count * length, 128), jnp.float32),
                pltpu.VMEM((row_count * frames, 128), jnp.float32),
                pltpu.VMEM((rows4 + 16, 256), jnp.float32),
                pltpu.VMEM((16, rows4 // 16, 16, 256), jnp.bfloat16),
                pltpu.VMEM((16, rows4 // 16, 16, 256), jnp.bfloat16),
                pltpu.VMEM((out4, 256), jnp.bfloat16),
                pltpu.VMEM((slots * 16, 256), jnp.bfloat16),
                pltpu.VMEM((256, depth), jnp.float32),
            ],
        ),
        out_shape=jax.ShapeDtypeStruct((4, width, KERNEL * 16), jnp.bfloat16),
        compiler_params=pltpu.CompilerParams(vmem_limit_bytes=VMEM_LIMIT, dimension_semantics=("arbitrary",)),
        cost_estimate=cost(
            flops=2 * pairs * 2 * slots * 16 * 256 * depth, bytes_accessed=width * KERNEL * 128, transcendentals=0
        ),
        name="conv_weight_grad",
    )(meta, x_ext.reshape(row_count * length, width), seg_quads(seg_ext), grad, after)


AXES = ("y", "c", "z", "x")


def device_pairs(place):
    pairs = []
    for y in range(2):
        for c in range(2):
            for z in range(4):
                for x in range(2):
                    ty, tc, tz, tx = place(y, c, z, x)
                    pairs.append((((y * 2 + c) * 4 + z) * 2 + x, ((ty * 2 + tc) * 4 + tz) * 2 + tx))
    return pairs


def move(values, place):
    return lax.ppermute(values, AXES, device_pairs(place))


def swap_core(values):
    return lax.ppermute(values, "c", [(0, 1), (1, 0)])


def swap_x(values):
    return lax.ppermute(values, "x", [(0, 1), (1, 0)])


def swap_y(values):
    return lax.ppermute(values, "y", [(0, 1), (1, 0)])


def swap_xy(values):
    return lax.ppermute(values, ("y", "x"), [(0, 3), (3, 0), (1, 2), (2, 1)])


def swap_z1(values):
    return lax.ppermute(values, "z", [(0, 1), (1, 0), (2, 3), (3, 2)])


def swap_z2(values):
    return lax.ppermute(values, "z", [(0, 2), (2, 0), (1, 3), (3, 1)])


def take(values, index, size, axis):
    return lax.dynamic_slice_in_dim(values, index * size, size, axis)


def once(values, *earlier):
    return lax.optimization_barrier((values,) + earlier)[0]


def ordered(index, mine, other, axis):
    first = jnp.where(index == 0, mine, other)
    second = jnp.where(index == 0, other, mine)
    return jnp.concatenate([first, second], axis=axis)


def to_rows(blocks, x, z):
    got = []
    for turn in range(2):
        mine = lax.dynamic_index_in_dim(blocks, x ^ turn, 0, keepdims=False)
        got.append(move(mine, lambda y, c, z, x: (y, z & 1, 2 * c + (x ^ turn), z >> 1)))
    flip = (z & 1) == 0
    return jnp.where(flip, got[0], got[1]), jnp.where(flip, got[1], got[0])


def from_rows(frames, x, z):
    half = frames.shape[0] // 2
    got = []
    for turn in range(2):
        mine = take(frames, (z & 1) ^ turn, half, 0)
        got.append(move(mine, lambda y, c, z, x: (y, z >> 1, 2 * x + c, (z & 1) ^ turn)))
    return ordered(x, got[0][None], got[1][None], 0)


def split_body(
    feats, segments, labels, conv_weight, w_qkv, w_out, w_up, w_down, head_w, head_b, gains, biases, up_bias
):
    y, c, z, x = (lax.axis_index(name) for name in AXES)
    block, features = feats.shape[1:]
    half = features // 2
    frames = 2 * block
    chip_frames = 2 * frames
    tokens = frames
    rim = KERNEL // 2
    rise = lax.axis_size("z") * lax.axis_size("x") // 2
    meta = jnp.stack([c, y, x, z]).astype(jnp.int32)

    label_rows = jnp.pad(labels.astype(jnp.bfloat16)[:, None, :], ((0, 0), (0, 15), (0, features - block)))
    first_block, second_block = to_rows(jnp.concatenate([feats, label_rows], axis=1), x, z)
    feats_own = jnp.concatenate([first_block[:block], second_block[:block]], axis=0)
    labels_own = jnp.concatenate([first_block[block, :block], second_block[block, :block]]).astype(jnp.int32)
    seg_rows = ordered(c, segments, swap_core(segments), 0)
    seg_row = lax.dynamic_index_in_dim(seg_rows, z, 0, keepdims=False)
    seg_halves = seg_row.reshape(2, 2, frames)
    seg_near = lax.dynamic_index_in_dim(seg_halves, x, 0, keepdims=False)
    seg_far = lax.dynamic_index_in_dim(seg_halves, 1 - x, 0, keepdims=False)
    seg_near, seg_far = (jnp.where(c == 0, item, item[::-1]).reshape(-1) for item in (seg_near, seg_far))
    seg_wide = jnp.pad(seg_row, (rim, rim), constant_values=-1)
    seg_ext = lax.dynamic_slice_in_dim(seg_wide, x * chip_frames, chip_frames + 2 * rim, 0)[None]

    def to_chip(values):
        return ordered(c, take(values, c, half, 1), swap_core(take(values, 1 - c, half, 1)), 0)

    def rimmed(values, edge):
        empty = jnp.zeros_like(edge)
        before = jnp.where(x == 0, empty, edge)
        after = jnp.where(x == 0, edge, empty)
        return jnp.concatenate([before, values, after], axis=0)[None]

    def with_rim(values):
        return rimmed(values, swap_x(jnp.where(x == 0, values[chip_frames - rim :], values[:rim])))

    def grouped(own, got_x, got_y, got_xy):
        return ordered(y, ordered(x, own, got_x, 0)[None], ordered(x, got_y, got_xy, 0)[None], 0)

    def to_groups(values):
        def part(yy, xx):
            return lax.dynamic_slice_in_dim(values, 256 * xx + 128 * yy, 128, 1)

        return grouped(
            part(y, x), swap_x(part(y, 1 - x)), swap_y(part(1 - y, x)), swap_xy(part(1 - y, 1 - x))
        )

    shift_bias = biases.T
    qkv_bias = jnp.concatenate([shift_bias[2], jnp.zeros((features,), jnp.float32), shift_bias[3]])[None]
    gain_rows = gains.T
    feats_chip = to_chip(feats_own)
    position_chip, slope = grouped_conv(
        with_rim(feats_chip), seg_ext, conv_weight, take(shift_bias[0:1], c, half, 1), 4 * c, rise, False
    )
    theirs, ours, normed, position = mix_rows(
        meta,
        (
            take(position_chip, c, frames, 0),
            swap_core(take(position_chip, 1 - c, frames, 0)),
            gain_rows[0:1],
            shift_bias[1:2],
        ),
        w_qkv,
        qkv_bias,
        1,
        2,
    )
    near = jnp.concatenate([ours, swap_core(theirs)], axis=0)
    got_normed = swap_core(normed)
    far = swap_x(near)
    theirs, ours = mix_rows(meta, (normed,), w_qkv, qkv_bias, 0, 1)
    queries = jnp.concatenate([ours, swap_core(theirs)], axis=0)
    mixed, state = attend_near(queries, near, seg_near, seg_near)
    attended, attended_ours, attended_away, lse = attend_far(queries, far, seg_near, seg_far, mixed, state)
    feats_group = jnp.pad(to_groups(feats_chip), ((0, 0), (rim, rim), (0, 0)))
    seg_pair = ordered(y, seg_row[None], swap_y(seg_row)[None], 0)
    seg_pair = jnp.pad(seg_pair, ((0, 0), (rim, rim)), constant_values=-1)
    zero_row = jnp.zeros((features,), jnp.float32)
    rows = jnp.stack([gain_rows[1], shift_bias[5], shift_bias[4], shift_bias[6]] + [zero_row] * 4)
    (
        pack, output_low, out_ours, up_ours, branch_ours, att_ours, att_theirs, grad_resid, mid_sums, up_sums,
        grad_head_w, last,
    ) = middle(
        meta,
        attended_ours,
        swap_core(attended_away),
        position,
        w_out,
        w_up,
        w_down,
        up_bias[None],
        head_w,
        head_b[None],
        labels_own[:, None],
        rows,
        (feats_group, seg_pair),
    )

    grad_heads = jnp.concatenate([att_ours, swap_core(att_theirs)], axis=0)
    dq_far, dkv_far = attend_back(queries, far, grad_heads, attended, lse, seg_near, seg_far, jnp.bfloat16, att_ours)
    got_kv = swap_x(dkv_far)

    C, Y, X, Z = 0, 1, 2, 3
    places = pack_places(features, w_up.shape[1])
    got_pack = swap_core(pack)
    up_pair = ((up_ours, 0), (got_pack, places["up"]))
    down_pair = ((out_ours, 0), (got_pack, places["out"]))
    branch_pair = ((branch_ours, 0), (got_pack, places["branch"]))
    second_pair, active_pair, attended_pair = (
        ((pack, places[name]), (got_pack, places[name])) for name in ("second", "active", "attended")
    )
    unit = features // 8
    down_rows = w_down.shape[0] // 4
    up_wide = w_up.shape[1] // 4
    quarter = half // 2
    eighth = 3 * half // 4
    up_low, up_high, down_away, down_home = weight_parts(
        meta,
        [
            weight_task([(0, 0)], second_pair, up_pair, half, 1, lambda i, m: 0, up_wide, lambda m: 1 - m[Y]),
            weight_task(
                [(2, 0)], active_pair, down_pair, down_rows, 1,
                lambda i, m: 2 * (1 - (m[Z] >> 1)) + 1 - (m[Z] & 1), half, lambda m: 0,
            ),
            weight_task([(1, 0)], second_pair, up_pair, half, 1, lambda i, m: 1, up_wide, lambda m: 1 - m[Y]),
            weight_task(
                [(3, 0)], active_pair, down_pair, down_rows, 1,
                lambda i, m: 2 * (m[Z] >> 1) + 1 - (m[Z] & 1), half, lambda m: 0,
            ),
        ],
        [(half, up_wide), (half, up_wide), (down_rows, half), (down_rows, half)],
        "weight_first",
        dkv_far,
    )
    got_up_low, got_down_away = swap_y(up_low), swap_z1(down_away)
    got_up_high, got_down_home = swap_y(up_high), swap_z1(down_home)
    dq, dkv = attend_back(queries, near, grad_heads, attended, lse, seg_near, seg_near, jnp.float32, down_home)

    def mixed_grad(part):
        piece = slice(part * frames, (part + 1) * frames)
        return jnp.concatenate(
            [
                dq[piece] + dq_far[piece],
                dkv[0, piece] + got_kv[0, piece].astype(jnp.float32),
                dkv[1, piece] + got_kv[1, piece].astype(jnp.float32),
            ],
            axis=1,
        ).astype(jnp.bfloat16)

    grad_theirs = mixed_grad(1)
    grad_got = swap_core(grad_theirs)
    grad_ours = mixed_grad(0)
    position_ours, position_theirs, first_sums = unmix_rows(
        meta, grad_ours, grad_got, w_qkv, position, grad_resid, gain_rows[0:1], (got_up_low, got_down_away)
    )
    grad_position, grad_conv, edge, own_part, to_x, to_y, to_xy, conv_bias = conv_grad_rows(
        meta, position_ours, swap_core(position_theirs), slope, (got_up_high, got_down_home)
    )
    grad_rim = rimmed(grad_conv, swap_x(edge))
    grad_group = grouped(own_part, swap_x(to_x), swap_y(to_y), swap_xy(to_xy))

    x_bit, y_bit = (lambda m: m[X]), (lambda m: m[Y])
    up_send, up_kept, down_send, down_kept = weight_parts(
        meta,
        [
            weight_task(
                [(0, 0), (1, 0)], second_pair, up_pair, half, 1, lambda i, m: 0, up_wide, lambda m: m[Y],
                got_up_low, lambda i, m: (0, 0), "rows", x_bit, unit,
            ),
            weight_task(
                [(0, 0), (1, 0)], second_pair, up_pair, half, 1, lambda i, m: 1, up_wide, lambda m: m[Y],
                got_up_high, lambda i, m: (0, 0), "rows", x_bit, unit, 1,
            ),
            weight_task(
                [(2, 0)], active_pair, down_pair, down_rows, 1,
                lambda i, m: 2 * (1 - (m[Z] >> 1)) + (m[Z] & 1), half, lambda m: 0, got_down_away, lambda i, m: (0, 0),
            ),
            weight_task(
                [(3, 0)], active_pair, down_pair, down_rows, 1,
                lambda i, m: 2 * (m[Z] >> 1) + (m[Z] & 1), half, lambda m: 0, got_down_home, lambda i, m: (0, 0),
            ),
        ],
        [(half, up_wide), (half, up_wide), (down_rows, half), (down_rows, half)],
        "weight_second",
        grad_conv,
    )
    up_got, down_got = swap_x(up_send), swap_z2(down_send)
    conv_grad = grouped_conv_weight(feats_group, seg_pair, grad_group.reshape(-1, 128), rise, up_kept)

    normed_pair = ((normed, 0), (got_normed, 0))
    qkv_pair = ((grad_ours, 0), (grad_theirs, 0))
    a_first, b_first, output_late = weight_parts(
        meta,
        [
            weight_task([(0, 0)], normed_pair, qkv_pair, features, 1, lambda i, m: 0, eighth, lambda m: 1 - m[Y]),
            weight_task(
                [(0, eighth)], attended_pair, branch_pair, features, 1, lambda i, m: 0, quarter, lambda m: 1 - m[Y]
            ),
            weight_task([(1, 0)], normed_pair, qkv_pair, unit, 4, lambda i, m: 2 * i + 1 - m[X], 2 * eighth, lambda m: 1),
        ],
        [(features, eighth + quarter), (half, 2 * eighth)],
        "weight_qkv_first",
        conv_grad,
        output_low,
    )
    layer_out = from_rows(output_late, x, z)
    got_a, got_b = swap_y(a_first), swap_x(b_first)

    (conv_input,) = grouped_conv(grad_rim, seg_ext, conv_weight, grad_position, 4 * c, rise, True, a_first)
    away = swap_core(take(conv_input, 1 - c, frames, 0))
    grad_feats = from_rows(ordered(c, take(conv_input, c, frames, 0), away, 1), x, z)
    a_send, b_send, qkv_kept = weight_parts(
        meta,
        [
            weight_task(
                [(0, 0), (2, 0)], normed_pair, qkv_pair, features, 1, lambda i, m: 0, eighth, lambda m: m[Y],
                got_a, lambda i, m: (0, 0), "rows", x_bit, unit,
            ),
            weight_task(
                [(0, eighth), (2, eighth)], attended_pair, branch_pair, features, 1, lambda i, m: 0, 128,
                lambda m: 2 * m[Y], got_a, lambda i, m: (0, eighth // 128), "rows", x_bit, unit,
            ),
            weight_task(
                [(0, eighth + 128), (2, eighth + 128)], attended_pair, branch_pair, features, 1, lambda i, m: 0, 128,
                lambda m: 2 * m[Y] + 1, got_a, lambda i, m: (0, eighth // 128 + 1), "rows", x_bit, unit,
            ),
            weight_task(
                [(1, 0), (2, eighth + quarter)], normed_pair, qkv_pair, unit, 4, lambda i, m: 2 * i + m[X], 2 * eighth,
                lambda m: 1, got_b, lambda i, m: (i, 0), "columns", y_bit,
            ),
        ],
        [(half, eighth + quarter), (half, eighth), (half, 2 * eighth + quarter)],
        "weight_qkv_second",
        conv_input,
    )
    a_got, b_got = swap_x(a_send), swap_y(b_send)

    def fold(kept, got, axis, bit, swap):
        total = kept.astype(jnp.float32) + got.astype(jnp.float32)
        send = lax.dynamic_index_in_dim(total, 1 - bit, axis, keepdims=False).astype(jnp.bfloat16)
        return lax.dynamic_index_in_dim(total, bit, axis, keepdims=False), swap(send)

    def add(kept, got):
        return (kept + got.astype(jnp.float32)).astype(jnp.bfloat16)

    def spread(shard):
        other = swap_y(shard)
        return jnp.where(y == 0, shard, other), jnp.where(y == 0, other, shard)

    kept, got = (item.reshape(2, 2, unit, up_wide) for item in (up_kept, up_got))
    kept, got = fold(kept, got, 1, z & 1, swap_z1)
    kept, got = fold(kept, got, 0, z >> 1, swap_z2)
    mine = jnp.concatenate(spread(add(kept, got)), axis=1)
    grad_w_up = ordered(c, mine, swap_core(mine), 1).astype(jnp.float32)

    kept, got = (item.reshape(2, down_rows // 2, half) for item in (down_kept, down_got))
    kept, got = fold(kept, got, 0, x, swap_x)
    mine = add(kept, got)
    mine = add(mine.astype(jnp.float32), swap_y(mine))
    grad_w_down = ordered(c, mine, swap_core(mine), 1).astype(jnp.float32)

    qkv_got = jnp.concatenate([a_got, b_got], axis=1)
    kept, got = fold(qkv_kept.reshape(2, 2, unit, -1), qkv_got.reshape(2, 2, unit, -1), 1, z & 1, swap_z1)
    kept, got = fold(kept, got, 0, z >> 1, swap_z2)
    low_half, high_half = spread(add(kept, got))
    out_at = eighth + quarter
    mine = jnp.concatenate(
        [
            low_half[:, :eighth], high_half[:, :eighth], low_half[:, out_at:], high_half[:, out_at:],
            low_half[:, eighth:out_at], high_half[:, eighth:out_at],
        ],
        axis=1,
    )
    theirs = swap_core(mine)
    left, right = jnp.where(c == 0, mine, theirs), jnp.where(c == 0, theirs, mine)
    grad_w_qkv = jnp.concatenate(
        [piece[:, part * half : (part + 1) * half] for part in range(3) for piece in (left, right)], axis=1
    ).astype(jnp.float32)
    grad_w_out = jnp.concatenate([left[:, 3 * half :], right[:, 3 * half :]], axis=1).astype(jnp.float32)

    pieces = conv_grad.reshape(2, 2, 128, -1)
    mine = lax.dynamic_index_in_dim(pieces, z & 1, 1, keepdims=False)
    got = swap_z1(lax.dynamic_index_in_dim(pieces, 1 - (z & 1), 1, keepdims=False))
    mine, got = fold(mine, got, 0, z >> 1, swap_z2)
    shard = (mine + got.astype(jnp.float32)).astype(jnp.bfloat16)
    width = shard.shape[1] // 2
    shard = ordered(x, take(shard, x, width, 1)[None], swap_x(take(shard, 1 - x, width, 1))[None], 0)
    shard = jnp.concatenate([shard, swap_y(shard)], axis=0)
    grad_conv_weight = flip_columns(meta, jnp.concatenate([shard, swap_core(shard)], axis=0))

    own_sums, got_sums = (jnp.sum(item.astype(jnp.float32), axis=0, keepdims=True) for item in (grad_ours, grad_got))
    total = small_sums(
        meta, grad_head_w, mid_sums, first_sums, conv_bias, own_sums, got_sums, up_sums, last, b_send
    )
    total = total + swap_core(total)
    total = total + swap_y(total)
    total = total.reshape(2, 2, 2, -1, unit)

    def half_sum(values, axis, bit, swap):
        mine = lax.dynamic_index_in_dim(values, bit, axis, keepdims=False)
        return mine + swap(lax.dynamic_index_in_dim(values, 1 - bit, axis, keepdims=False))

    total = half_sum(total, 2, x, swap_x)
    total = half_sum(total, 1, z & 1, swap_z1)
    total = half_sum(total, 0, z >> 1, swap_z2)
    v = VOCAB
    loss = total[v + 14, 0] / (tokens * 32)
    gain_part = jnp.stack([total[v + 4], total[v]], axis=1)
    bias_part = jnp.stack(
        [total[v + 6], total[v + 5], total[v + 7], total[v + 8], total[v + 1], total[v + 2], total[v + 3]], axis=1
    )
    return (
        layer_out,
        loss,
        grad_feats.astype(jnp.float32),
        grad_conv_weight,
        grad_w_qkv,
        grad_w_out,
        grad_w_up,
        grad_w_down,
        total[:v].T,
        total[v + 13, :v],
        gain_part,
        bias_part,
        total[v + 9 : v + 13].reshape(-1),
    )


def split_solution(mesh):
    fine = Mesh(mesh.devices.reshape(2, 2, 4, 2), AXES)
    rows, parts = ("y", "c"), ("z", "x")
    return jax.shard_map(
        split_body,
        mesh=fine,
        in_specs=(P(rows, parts, None), P(rows, None), P(rows, parts)) + (P(),) * 10,
        out_specs=(
            P(rows, parts, None),
            P(),
            P(rows, parts, None),
            P(parts, None),
            P(parts, None),
            P(parts, None),
            P(parts, None),
            P(parts, None),
            P(parts, None),
            P(),
            P(parts, None),
            P(parts, None),
            P(parts),
        ),
        check_vma=False,
    )


def solution(mesh):
    if mesh.shape["dp"] == 4 and mesh.shape["seq"] == 8:
        return split_solution(mesh)
    return whole_solution(mesh)
```

```python
from functools import partial
import math

import jax
import jax.numpy as jnp
from jax import lax
from jax.experimental import pallas as pl
from jax.experimental.pallas import tpu as pltpu
from jax.sharding import Mesh, PartitionSpec as P

HEADS = 16
GROUPS = 16
KERNEL = 128
VOCAB = 32
TAP_BLOCKS = 33
VMEM_LIMIT = 56 * 1024 * 1024
DW_UNROLL = 11
COST_SHARE = 0.001


epsilon = 1e-05
masked_score = -1e30
tap_group = 8


def extended(cells, sides, width):
    for axis, dim in sides:
        count = lax.axis_size(axis)
        ends = count - 1
        head = lax.slice_in_dim(cells, 0, width, axis=dim)
        tail = lax.slice_in_dim(cells, cells.shape[dim] - width, cells.shape[dim], axis=dim)
        cells = jnp.concatenate(
            [
                lax.ppermute(tail, axis, [(i, (i + 1) % count) for i in range(ends)]),
                cells,
                lax.ppermute(head, axis, [((i + 1) % count, i) for i in range(ends)]),
            ],
            axis=dim,
        )
    return cells


def layer_norm(values, gain_row, shift_row):
    center = values - jnp.mean(values, axis=-1, keepdims=True)
    spread = jnp.mean(center * center, axis=-1, keepdims=True)
    return center * lax.rsqrt(spread + epsilon) * gain_row + shift_row


def gelu_exact(values):
    return jax.nn.gelu(values, approximate=False)


def outer_sum(left_side, right_side):
    return lax.dot_general(
        left_side, right_side, (((0,), (0,)), ((), ())), preferred_element_type=jnp.float32
    )


def back_product(grad_rows, weight):
    return lax.dot_general(
        grad_rows, weight, (((1,), (1,)), ((), ())), preferred_element_type=jnp.float32
    )


def masked_windows(source, seg_padded, seg_local, offsets, frames):
    windows = []
    for offset in offsets:
        window = lax.dynamic_slice_in_dim(source, offset, frames, 1)
        near_ids = lax.dynamic_slice_in_dim(seg_padded, offset, frames, 1)
        keep_mask = (near_ids == seg_local)[:, :, None]
        windows.append(jnp.where(keep_mask, window, jnp.zeros_like(window)))
    return jnp.stack(windows, axis=2)


def conv_forward(feats_rim, seg_padded, seg_local, conv_weight):
    row_count, frames = seg_local.shape
    features = feats_rim.shape[2]
    group_width = features // GROUPS
    tap_count = conv_weight.shape[0] // group_width
    grouped = conv_weight.reshape(tap_count, group_width, GROUPS, group_width)

    def one_block(tap_block, running):
        offsets = [tap_block * tap_group + tap_inner for tap_inner in range(tap_group)]
        stacked = masked_windows(feats_rim, seg_padded, seg_local, offsets, frames)
        stacked = stacked.reshape(row_count, frames, tap_group, GROUPS, group_width)
        weight_part = lax.dynamic_slice_in_dim(grouped, tap_block * tap_group, tap_group, 0)
        return running + jnp.einsum(
            "rtkgi,kigo->rtgo", stacked, weight_part, preferred_element_type=jnp.float32
        )

    start_sum = jnp.zeros((row_count, frames, GROUPS, group_width), jnp.float32)
    running = lax.fori_loop(0, tap_count // tap_group, one_block, start_sum)
    return running.reshape(row_count, frames, features)


def conv_weight_grad(feats_rim, seg_padded, seg_local, grad_conv_low, tap_count):
    row_count, frames = seg_local.shape
    features = feats_rim.shape[2]
    group_width = features // GROUPS
    grad_grouped = grad_conv_low.reshape(row_count, frames, GROUPS, group_width)

    def one_block(tap_block, running):
        offsets = [tap_block * tap_group + tap_inner for tap_inner in range(tap_group)]
        stacked = masked_windows(feats_rim, seg_padded, seg_local, offsets, frames)
        stacked = stacked.reshape(row_count, frames, tap_group, GROUPS, group_width)
        block_grad = jnp.einsum(
            "rtkgi,rtgo->kigo", stacked, grad_grouped, preferred_element_type=jnp.float32
        )
        return lax.dynamic_update_slice_in_dim(running, block_grad, tap_block * tap_group, 0)

    start_sum = jnp.zeros((tap_count, group_width, GROUPS, group_width), jnp.float32)
    running = lax.fori_loop(0, tap_count // tap_group, one_block, start_sum)
    return running.reshape(tap_count * group_width, features)


def conv_input_grad(grad_rim, seg_padded, seg_local, conv_weight):
    row_count, frames = seg_local.shape
    features = grad_rim.shape[2]
    group_width = features // GROUPS
    tap_count = conv_weight.shape[0] // group_width
    grouped = conv_weight.reshape(tap_count, group_width, GROUPS, group_width)

    def one_block(tap_block, running):
        offsets = [
            tap_count - (tap_block * tap_group + tap_inner) for tap_inner in range(tap_group)
        ]
        stacked = masked_windows(grad_rim, seg_padded, seg_local, offsets, frames)
        stacked = stacked.reshape(row_count, frames, tap_group, GROUPS, group_width)
        weight_part = lax.dynamic_slice_in_dim(grouped, tap_block * tap_group, tap_group, 0)
        return running + jnp.einsum(
            "rtkgo,kigo->rtgi", stacked, weight_part, preferred_element_type=jnp.float32
        )

    start_sum = jnp.zeros((row_count, frames, GROUPS, group_width), jnp.float32)
    running = lax.fori_loop(0, tap_count // tap_group, one_block, start_sum)
    return running.reshape(row_count, frames, features)


def span_size(piece_rows, frames):
    return math.gcd(piece_rows, 8 * frames)


def attend_row(row_state, query_row, key_row, value_row, seg_query, seg_key, score_scale):
    running_max, running_sum, weighted = row_state
    scores = score_scale * jnp.einsum(
        "qhe,khe->qhk", query_row, key_row, preferred_element_type=jnp.float32
    )
    allowed = (seg_query[:, None] == seg_key[None, :])[:, None, :]
    scores = jnp.where(allowed, scores, masked_score)
    new_max = jnp.maximum(running_max, jnp.max(scores, axis=-1))
    rescale = jnp.exp(running_max - new_max)
    weights = jnp.where(allowed, jnp.exp(scores - new_max[:, :, None]), 0.0)
    running_sum = running_sum * rescale + jnp.sum(weights, axis=-1)
    weighted = weighted * rescale[:, :, None] + jnp.einsum(
        "qhk,khe->qhe", weights.astype(jnp.bfloat16), value_row, preferred_element_type=jnp.float32
    )
    return (new_max, running_sum, weighted)


def query_grad_row(
    grad_query,
    query_row,
    key_row,
    value_row,
    seg_query,
    seg_key,
    lse_row,
    dots_row,
    grad_row,
    score_scale,
):
    scores = score_scale * jnp.einsum(
        "qhe,khe->qhk", query_row, key_row, preferred_element_type=jnp.float32
    )
    allowed = (seg_query[:, None] == seg_key[None, :])[:, None, :]
    probs = jnp.where(allowed, jnp.exp(scores - lse_row[:, :, None]), 0.0)
    grad_probs = jnp.einsum("qhe,khe->qhk", grad_row, value_row, preferred_element_type=jnp.float32)
    grad_scores = (probs * (grad_probs - dots_row[:, :, None])).astype(jnp.bfloat16)
    return grad_query + score_scale * jnp.einsum(
        "qhk,khe->qhe", grad_scores, key_row, preferred_element_type=jnp.float32
    )


def key_grad_row(
    grads_pair,
    key_row,
    value_row,
    query_row,
    grad_row,
    lse_row,
    dots_row,
    seg_query,
    seg_key,
    score_scale,
):
    scores = score_scale * jnp.einsum(
        "qhe,khe->qhk", query_row, key_row, preferred_element_type=jnp.float32
    )
    allowed = (seg_query[:, None] == seg_key[None, :])[:, None, :]
    probs = jnp.where(allowed, jnp.exp(scores - lse_row[:, :, None]), 0.0)
    grad_value = jnp.einsum(
        "qhk,qhe->khe", probs.astype(jnp.bfloat16), grad_row, preferred_element_type=jnp.float32
    )
    grad_probs = jnp.einsum("qhe,khe->qhk", grad_row, value_row, preferred_element_type=jnp.float32)
    grad_scores = (probs * (grad_probs - dots_row[:, :, None])).astype(jnp.bfloat16)
    grad_key = score_scale * jnp.einsum(
        "qhk,qhe->khe", grad_scores, query_row, preferred_element_type=jnp.float32
    )
    return (grad_key, grad_value)


def body(
    feats,
    segments,
    labels,
    conv_weight,
    w_qkv,
    w_out,
    w_up,
    w_down,
    head_w,
    head_b,
    gains,
    biases,
    up_bias,
):
    row_count, frames, features = feats.shape
    head_count = HEADS
    head_width = features // head_count
    score_scale = head_width ** (-0.5)
    tokens = row_count * frames
    tap_count = KERNEL
    rim_width = tap_count // 2
    own_first = lax.axis_index("seq") * frames
    seg_local = lax.dynamic_slice_in_dim(segments, own_first, frames, 1)
    seg_wide = jnp.pad(segments, ((0, 0), (rim_width, rim_width)), constant_values=-1)
    seg_padded = lax.dynamic_slice_in_dim(seg_wide, own_first, frames + 2 * rim_width, 1)
    feats_rim = extended(feats, (("seq", 1),), rim_width)
    conv_sum = conv_forward(feats_rim, seg_padded, seg_local, conv_weight) + biases[:, 0]
    activated, conv_pull = jax.vjp(gelu_exact, conv_sum)
    position = feats.astype(jnp.float32) + activated
    normed, first_pull = jax.vjp(layer_norm, position, gains[:, 0], biases[:, 1])
    normed_low = normed.astype(jnp.bfloat16).reshape(tokens, features)
    qkv_bias = jnp.concatenate([biases[:, 2], jnp.zeros((features,), jnp.float32), biases[:, 3]])
    mixed = (jnp.dot(normed_low, w_qkv, preferred_element_type=jnp.float32) + qkv_bias).astype(
        jnp.bfloat16
    )
    queries = mixed[:, :features].reshape(row_count, frames, head_count, head_width)
    keys = mixed[:, features : 2 * features].reshape(row_count, frames, features)
    values = mixed[:, 2 * features :].reshape(row_count, frames, features)
    start_state = (
        jnp.full((row_count, frames, head_count), masked_score, jnp.float32),
        jnp.zeros((row_count, frames, head_count), jnp.float32),
        jnp.zeros((row_count, frames, head_count, head_width), jnp.float32),
    )
    key_shard = lax.all_gather(keys, "seq", axis=1, tiled=True)
    value_shard = lax.all_gather(values, "seq", axis=1, tiled=True)
    piece_rows = key_shard.shape[1]
    span = span_size(piece_rows, frames)

    def forward_one_span(span_index, state):
        offset = span_index * span
        key_part = lax.dynamic_slice_in_dim(key_shard, offset, span, 1)
        value_part = lax.dynamic_slice_in_dim(value_shard, offset, span, 1)
        seg_keys = lax.dynamic_slice_in_dim(segments, offset, span, 1)
        results = []
        for row_index in range(row_count):
            action = partial(
                attend_row,
                query_row=queries[row_index],
                key_row=key_part[row_index].reshape(span, head_count, head_width),
                value_row=value_part[row_index].reshape(span, head_count, head_width),
                seg_query=seg_local[row_index],
                seg_key=seg_keys[row_index],
                score_scale=score_scale,
            )
            row_state = (state[0][row_index], state[1][row_index], state[2][row_index])
            results.append(action(row_state))
        return (
            jnp.stack([item[0] for item in results]),
            jnp.stack([item[1] for item in results]),
            jnp.stack([item[2] for item in results]),
        )

    running_max, running_sum, weighted = lax.fori_loop(
        0, piece_rows // span, forward_one_span, start_state
    )
    attended = weighted / running_sum[:, :, :, None]
    log_total = running_max + jnp.log(running_sum)
    attended_low = attended.reshape(tokens, features).astype(jnp.bfloat16)
    resid = (
        position.reshape(tokens, features)
        + jnp.dot(attended_low, w_out, preferred_element_type=jnp.float32)
        + biases[:, 4]
    )
    normed_second, second_pull = jax.vjp(layer_norm, resid, gains[:, 1], biases[:, 5])
    second_low = normed_second.astype(jnp.bfloat16)
    up_sum = jnp.dot(second_low, w_up, preferred_element_type=jnp.float32) + up_bias
    up_active, up_pull = jax.vjp(gelu_exact, up_sum)
    active_low = up_active.astype(jnp.bfloat16)
    output = resid + jnp.dot(active_low, w_down, preferred_element_type=jnp.float32) + biases[:, 6]
    output_low = output.astype(jnp.bfloat16)
    logits = jnp.dot(output_low, head_w, preferred_element_type=jnp.float32) + head_b
    row_top = jnp.max(logits, axis=-1, keepdims=True)
    shifted = jnp.exp(logits - row_top)
    exp_sums = jnp.sum(shifted, axis=-1, keepdims=True)
    onehot = labels.reshape(tokens)[:, None] == jnp.arange(VOCAB, dtype=jnp.int32)[None, :]
    picked = jnp.sum(jnp.where(onehot, logits, 0.0), axis=-1)
    local_loss = jnp.sum(row_top[:, 0] + jnp.log(exp_sums[:, 0]) - picked)
    grad_logits = (shifted / exp_sums - onehot.astype(jnp.float32)).astype(jnp.bfloat16)
    grad_head_w = outer_sum(output_low, grad_logits)
    grad_head_b = jnp.sum(grad_logits.astype(jnp.float32), axis=0)
    grad_output = back_product(grad_logits, head_w)
    grad_output_low = grad_output.astype(jnp.bfloat16)
    grad_w_down = outer_sum(active_low, grad_output_low)
    grad_down_bias = jnp.sum(grad_output_low.astype(jnp.float32), axis=0)
    grad_active = back_product(grad_output_low, w_down)
    grad_up_low = up_pull(grad_active)[0].astype(jnp.bfloat16)
    grad_w_up = outer_sum(second_low, grad_up_low)
    grad_up_bias = jnp.sum(grad_up_low.astype(jnp.float32), axis=0)
    grad_second = back_product(grad_up_low, w_up)
    grad_resid_part, grad_gain_second, grad_shift_second = second_pull(grad_second)
    grad_resid = grad_output + grad_resid_part
    grad_branch_low = grad_resid.astype(jnp.bfloat16)
    grad_w_out = outer_sum(attended_low, grad_branch_low)
    grad_out_bias = jnp.sum(grad_branch_low.astype(jnp.float32), axis=0)
    grad_attended = back_product(grad_branch_low, w_out).astype(jnp.bfloat16)
    grad_heads = grad_attended.reshape(row_count, frames, head_count, head_width)
    head_dots = jnp.sum(grad_heads.astype(jnp.float32) * attended, axis=-1)
    zero_grads = jnp.zeros((row_count, frames, head_count, head_width), jnp.float32)
    all_keys, all_values = (
        lax.all_gather(keys, "seq", axis=1, tiled=True),
        lax.all_gather(values, "seq", axis=1, tiled=True),
    )
    length = all_keys.shape[1]
    key_span = 8 * frames

    def query_block(block_index, grad_query):
        first_row = block_index * key_span
        key_block = lax.dynamic_slice_in_dim(all_keys, first_row, key_span, 1)
        value_block = lax.dynamic_slice_in_dim(all_values, first_row, key_span, 1)
        seg_keys = lax.dynamic_slice_in_dim(segments, first_row, key_span, 1)
        results = []
        for row_index in range(row_count):
            action = partial(
                query_grad_row,
                query_row=queries[row_index],
                key_row=key_block[row_index].reshape(key_span, head_count, head_width),
                value_row=value_block[row_index].reshape(key_span, head_count, head_width),
                seg_query=seg_local[row_index],
                seg_key=seg_keys[row_index],
                lse_row=log_total[row_index],
                dots_row=head_dots[row_index],
                grad_row=grad_heads[row_index],
                score_scale=score_scale,
            )
            results.append(action(grad_query[row_index]))
        return jnp.stack(results)

    grad_queries = lax.fori_loop(0, length // key_span, query_block, zero_grads)

    def key_term(piece_rows):
        span = math.gcd(piece_rows, key_span)

        def key_one_span(span_index, gathered_terms):
            offset = span_index * span
            key_block = lax.dynamic_slice_in_dim(all_keys, offset, span, 1)
            value_block = lax.dynamic_slice_in_dim(all_values, offset, span, 1)
            seg_keys = lax.dynamic_slice_in_dim(segments, offset, span, 1)
            empty_row = jnp.zeros((span, head_count, head_width), jnp.float32)
            results = []
            for row_index in range(row_count):
                action = partial(
                    key_grad_row,
                    key_row=key_block[row_index].reshape(span, head_count, head_width),
                    value_row=value_block[row_index].reshape(span, head_count, head_width),
                    query_row=queries[row_index],
                    grad_row=grad_heads[row_index],
                    lse_row=log_total[row_index],
                    dots_row=head_dots[row_index],
                    seg_query=seg_local[row_index],
                    seg_key=seg_keys[row_index],
                    score_scale=score_scale,
                )
                results.append(action((empty_row, empty_row)))
            key_part = jnp.stack([item[0] for item in results], axis=1).reshape(
                span, row_count, features
            )
            value_part = jnp.stack([item[1] for item in results], axis=1).reshape(
                span, row_count, features
            )
            both_parts = jnp.concatenate([key_part, value_part], axis=2)
            return lax.dynamic_update_slice_in_dim(gathered_terms, both_parts, offset, 0)

        empty_terms = jnp.zeros((piece_rows, row_count, 2 * features), jnp.float32)
        return lax.fori_loop(0, piece_rows // span, key_one_span, empty_terms)

    both_grads = lax.psum_scatter(
        key_term(frames * lax.axis_size("seq")), "seq", scatter_dimension=0, tiled=True
    )
    grad_keys = jnp.transpose(both_grads[:, :, :features], (1, 0, 2)).reshape(
        row_count, frames, head_count, head_width
    )
    grad_values = jnp.transpose(both_grads[:, :, features:], (1, 0, 2)).reshape(
        row_count, frames, head_count, head_width
    )
    grad_mixed = jnp.concatenate(
        [
            grad_queries.reshape(tokens, features),
            grad_keys.reshape(tokens, features),
            grad_values.reshape(tokens, features),
        ],
        axis=1,
    ).astype(jnp.bfloat16)
    grad_w_qkv = outer_sum(normed_low, grad_mixed)
    mixed_sums = jnp.sum(grad_mixed.astype(jnp.float32), axis=0)
    grad_normed = back_product(grad_mixed, w_qkv).reshape(row_count, frames, features)
    grad_position_part, grad_gain_first, grad_shift_first = first_pull(grad_normed)
    grad_position = grad_resid.reshape(row_count, frames, features) + grad_position_part
    grad_conv_low = conv_pull(grad_position)[0].astype(jnp.bfloat16)
    grad_conv_bias = jnp.sum(grad_conv_low.astype(jnp.float32), axis=(0, 1))
    grad_conv_weight = conv_weight_grad(feats_rim, seg_padded, seg_local, grad_conv_low, tap_count)
    grad_rim = extended(grad_conv_low, (("seq", 1),), rim_width)
    grad_feats = grad_position + conv_input_grad(grad_rim, seg_padded, seg_local, conv_weight)
    grad_gains = jnp.stack([grad_gain_first, grad_gain_second], axis=1)
    grad_biases = jnp.stack(
        [
            grad_conv_bias,
            grad_shift_first,
            mixed_sums[:features],
            mixed_sums[2 * features :],
            grad_out_bias,
            grad_shift_second,
            grad_down_bias,
        ],
        axis=1,
    )
    shared = (
        lax.psum_scatter(grad_conv_weight, "seq", scatter_dimension=0, tiled=True),
        lax.psum_scatter(grad_w_qkv, "seq", scatter_dimension=0, tiled=True),
        lax.psum_scatter(grad_w_out, "seq", scatter_dimension=0, tiled=True),
        lax.psum_scatter(grad_w_up, "seq", scatter_dimension=0, tiled=True),
        lax.psum_scatter(grad_w_down, "seq", scatter_dimension=0, tiled=True),
        lax.psum_scatter(grad_head_w, "seq", scatter_dimension=0, tiled=True),
        lax.psum_scatter(grad_gains, "seq", scatter_dimension=0, tiled=True),
        lax.psum_scatter(grad_biases, "seq", scatter_dimension=0, tiled=True),
        lax.psum_scatter(grad_up_bias, "seq", scatter_dimension=0, tiled=True),
    )
    summed = (
        lax.psum(shared[0].astype(jnp.bfloat16), "dp").astype(jnp.float32),
        lax.psum(shared[1].astype(jnp.bfloat16), "dp").astype(jnp.float32),
        lax.psum(shared[2].astype(jnp.bfloat16), "dp").astype(jnp.float32),
        lax.psum(shared[3].astype(jnp.bfloat16), "dp").astype(jnp.float32),
        lax.psum(shared[4].astype(jnp.bfloat16), "dp").astype(jnp.float32),
        lax.psum(shared[5].astype(jnp.bfloat16), "dp").astype(jnp.float32),
        lax.psum(shared[6].astype(jnp.bfloat16), "dp").astype(jnp.float32),
        lax.psum(shared[7].astype(jnp.bfloat16), "dp").astype(jnp.float32),
        lax.psum(shared[8].astype(jnp.bfloat16), "dp").astype(jnp.float32),
    )
    loss_total, head_bias_total = lax.psum((local_loss, grad_head_b), ("dp", "seq"))
    loss = loss_total / (tokens * lax.axis_size("dp") * lax.axis_size("seq"))
    layer_out = output_low.reshape(row_count, frames, features)
    return (
        layer_out,
        loss,
        grad_feats,
        summed[0],
        summed[1],
        summed[2],
        summed[3],
        summed[4],
        summed[5],
        head_bias_total,
        summed[6],
        summed[7],
        summed[8],
    )


def whole_solution(mesh):
    placed = (
        P("dp", "seq", None),
        P("dp", None),
        P("dp", "seq"),
        P(),
        P(),
        P(),
        P(),
        P(),
        P(),
        P(),
        P(),
        P(),
        P(),
    )
    return jax.shard_map(
        body,
        mesh=mesh,
        in_specs=placed,
        out_specs=(
            P("dp", "seq", None),
            P(),
            P("dp", "seq", None),
            P("seq", None),
            P("seq", None),
            P("seq", None),
            P("seq", None),
            P("seq", None),
            P("seq", None),
            P(),
            P("seq", None),
            P("seq", None),
            P("seq"),
        ),
        check_vma=False,
    )


def cost(flops, bytes_accessed, transcendentals):
    return pl.CostEstimate(
        flops=int(flops * COST_SHARE), bytes_accessed=int(bytes_accessed * COST_SHARE), transcendentals=int(transcendentals * COST_SHARE)
    )


def lanes_dot(a, b):
    return lax.dot_general(a, b, (((1,), (1,)), ((), ())), preferred_element_type=jnp.float32)


def rows_dot(a, b):
    return lax.dot_general(a, b, (((0,), (0,)), ((), ())), preferred_element_type=jnp.float32)


def attend_parts(side, queries, keys, values, allowed, low):
    mine = low if side == 0 else jnp.logical_not(low)
    scores = lanes_dot(jnp.where(mine, keys, jnp.zeros_like(keys)), queries)
    scores = jnp.where(allowed, scores, masked_score)
    top = jnp.max(scores, axis=0, keepdims=True)
    return scores, top


def attend_kernel(seg_q_ref, seg_k_ref, q_ref, k_ref, v_ref, mixed_ref, state_ref):
    queries = q_ref[...] * jnp.bfloat16(0.125)
    low = lax.broadcasted_iota(jnp.int32, k_ref.shape, 1) < 64
    allowed = seg_k_ref[...] == seg_q_ref[...]
    for side in range(2):
        scores, top = attend_parts(side, queries, k_ref[...], None, allowed, low)
        weights = jnp.exp(scores - top)
        state_ref[0, side : side + 1, :] = top
        state_ref[0, side + 2 : side + 3, :] = jnp.sum(weights, axis=0, keepdims=True)
        mixed = rows_dot(v_ref[...], weights.astype(jnp.bfloat16))
        mixed_ref[side * 64 : (side + 1) * 64, :] = mixed[side * 64 : (side + 1) * 64, :]


def attend_far_kernel(seg_q_ref, seg_k_ref, q_ref, k_ref, v_ref, mixed_ref, state_ref, out_ref, low_ref, away_ref, lse_ref):
    queries = q_ref[...] * jnp.bfloat16(0.125)
    low = lax.broadcasted_iota(jnp.int32, k_ref.shape, 1) < 64
    allowed = seg_k_ref[...] == seg_q_ref[...]
    pieces = []
    for side in range(2):
        scores, top = attend_parts(side, queries, k_ref[...], None, allowed, low)
        near_top = state_ref[0, side : side + 1, :]
        top = jnp.maximum(top, near_top)
        weights = jnp.exp(scores - top)
        rescale = jnp.exp(near_top - top)
        total = state_ref[0, side + 2 : side + 3, :] * rescale + jnp.sum(weights, axis=0, keepdims=True)
        mixed = rows_dot(v_ref[...], weights.astype(jnp.bfloat16))[side * 64 : (side + 1) * 64, :]
        pieces.append((mixed + mixed_ref[side * 64 : (side + 1) * 64, :] * rescale) / total)
        lse_ref[0, side : side + 1, :] = top + jnp.log(total)
    attended = jnp.concatenate(pieces, axis=0).T
    own = low_ref.shape[0]
    out_ref[...] = attended
    low_ref[...] = attended[:own, :].astype(jnp.bfloat16)
    away_ref[...] = attended[own:, :].astype(jnp.bfloat16)


def attend_specs(frames, length, pairs):
    return [
        pl.BlockSpec((1, frames), lambda p: (0, 0)),
        pl.BlockSpec((length, 1), lambda p: (0, 0)),
        pl.BlockSpec((frames, 128), lambda p: (0, p)),
        pl.BlockSpec((length, 128), lambda p: (0, p)),
        pl.BlockSpec((length, 128), lambda p: (0, pairs + p)),
    ]


def attend_cost(frames, length, pairs, products):
    return cost(
        flops=4 * products * pairs * frames * length * 128,
        bytes_accessed=16 * frames * pairs * 128,
        transcendentals=2 * pairs * frames * length,
    )


def attend_near(queries, pair, seg_q, seg_k):
    frames, width = queries.shape
    length = pair.shape[0]
    pairs = width // 128
    return pl.pallas_call(
        attend_kernel,
        grid=(pairs,),
        in_specs=attend_specs(frames, length, pairs),
        out_specs=[
            pl.BlockSpec((128, frames), lambda p: (p, 0)),
            pl.BlockSpec((1, 8, frames), lambda p: (p, 0, 0)),
        ],
        out_shape=[
            jax.ShapeDtypeStruct((width, frames), jnp.float32),
            jax.ShapeDtypeStruct((pairs, 8, frames), jnp.float32),
        ],
        compiler_params=pltpu.CompilerParams(vmem_limit_bytes=VMEM_LIMIT),
        cost_estimate=attend_cost(frames, length, pairs, 2),
        name="attend_near",
    )(seg_q.reshape(1, -1), seg_k.reshape(-1, 1), queries, pair, pair)


def attend_far(queries, pair, seg_q, seg_k, mixed, state):
    frames, width = queries.shape
    length = pair.shape[0]
    pairs = width // 128
    return pl.pallas_call(
        attend_far_kernel,
        grid=(pairs,),
        in_specs=attend_specs(frames, length, pairs)
        + [
            pl.BlockSpec((128, frames), lambda p: (p, 0)),
            pl.BlockSpec((1, 8, frames), lambda p: (p, 0, 0)),
        ],
        out_specs=[
            pl.BlockSpec((frames, 128), lambda p: (0, p)),
            pl.BlockSpec((frames // 2, 128), lambda p: (0, p)),
            pl.BlockSpec((frames // 2, 128), lambda p: (0, p)),
            pl.BlockSpec((1, 8, frames), lambda p: (p, 0, 0)),
        ],
        out_shape=[
            jax.ShapeDtypeStruct((frames, width), jnp.float32),
            jax.ShapeDtypeStruct((frames // 2, width), jnp.bfloat16),
            jax.ShapeDtypeStruct((frames // 2, width), jnp.bfloat16),
            jax.ShapeDtypeStruct((pairs, 8, frames), jnp.float32),
        ],
        compiler_params=pltpu.CompilerParams(vmem_limit_bytes=VMEM_LIMIT),
        cost_estimate=attend_cost(frames, length, pairs, 2),
        name="attend_far",
    )(seg_q.reshape(1, -1), seg_k.reshape(-1, 1), queries, pair, pair, mixed, state)


def attend_back_kernel(seg_q_ref, seg_k_ref, q_ref, k_ref, v_ref, g_ref, a_ref, lse_ref, after_ref, dq_ref, dkv_ref):
    queries = q_ref[...] * jnp.bfloat16(0.125)
    key_count = k_ref.shape[0]
    low = lax.broadcasted_iota(jnp.int32, (key_count, 128), 1) < 64
    keys, values, grads = k_ref[...], v_ref[...], g_ref[...]
    allowed = seg_k_ref[...] == seg_q_ref[...]
    products = (grads.astype(jnp.float32) * a_ref[...]).T
    dq, dk, dv = [], [], []
    for side in range(2):
        mine = low if side == 0 else jnp.logical_not(low)
        zero = jnp.zeros_like(keys)
        scores = lanes_dot(jnp.where(mine, keys, zero), queries)
        probs = jnp.where(allowed, jnp.exp(scores - lse_ref[0, side : side + 1, :]), 0.0)
        dots = jnp.sum(products[side * 64 : (side + 1) * 64, :], axis=0, keepdims=True)
        dv.append(jnp.dot(probs.astype(jnp.bfloat16), grads, preferred_element_type=jnp.float32))
        grad_probs = lanes_dot(jnp.where(mine, values, zero), grads)
        grad_scores = (probs * (grad_probs - dots)).astype(jnp.bfloat16)
        dk.append(jnp.dot(grad_scores, queries, preferred_element_type=jnp.float32))
        dq.append(rows_dot(keys, grad_scores)[side * 64 : (side + 1) * 64, :])
    dq_ref[...] = 0.125 * jnp.concatenate(dq, axis=0).T
    dkv_ref[0] = jnp.where(low, dk[0], dk[1]).astype(dkv_ref.dtype)
    dkv_ref[1] = jnp.where(low, dv[0], dv[1]).astype(dkv_ref.dtype)


def attend_back(queries, pair, grads, attended, lse, seg_q, seg_k, kind, after):
    frames, width = queries.shape
    length = pair.shape[0]
    pairs = width // 128
    return pl.pallas_call(
        attend_back_kernel,
        grid=(pairs,),
        in_specs=attend_specs(frames, length, pairs)
        + [
            pl.BlockSpec((frames, 128), lambda p: (0, p)),
            pl.BlockSpec((frames, 128), lambda p: (0, p)),
            pl.BlockSpec((1, 8, frames), lambda p: (p, 0, 0)),
            pl.BlockSpec(memory_space=pl.ANY),
        ],
        out_specs=[
            pl.BlockSpec((frames, 128), lambda p: (0, p)),
            pl.BlockSpec((2, length, 128), lambda p: (0, 0, p)),
        ],
        out_shape=[
            jax.ShapeDtypeStruct((frames, width), jnp.float32),
            jax.ShapeDtypeStruct((2, length, width), kind),
        ],
        compiler_params=pltpu.CompilerParams(vmem_limit_bytes=VMEM_LIMIT),
        cost_estimate=attend_cost(frames, length, pairs, 5),
        name="attend_back",
    )(seg_q.reshape(1, -1), seg_k.reshape(-1, 1), queries, pair, pair, grads, attended, lse, after)


def phi_parts(values):
    below = 0.5 * (1.0 + lax.erf(values * (0.5**0.5)))
    density = jnp.exp(-0.5 * values * values) * (1.0 / math.sqrt(2.0 * math.pi))
    return below, density


def norm_parts(values):
    center = values - jnp.mean(values, axis=-1, keepdims=True)
    scale = lax.rsqrt(jnp.mean(center * center, axis=-1, keepdims=True) + epsilon)
    return center * scale, scale


def norm_back(grad, hat, scale, gain):
    inner = grad * gain
    mean_inner = jnp.mean(inner, axis=-1, keepdims=True)
    mean_hat = jnp.mean(inner * hat, axis=-1, keepdims=True)
    return (inner - mean_inner - hat * mean_hat) * scale


def column_sum(values):
    return jnp.sum(values, axis=0, keepdims=True)


def by_core(core, mine, other):
    return jnp.where(core == 0, mine, other), jnp.where(core == 0, other, mine)


def mix_kernel(first, meta, *refs):
    if first:
        mine_ref, other_ref, gain_ref, shift_ref, w_ref, bias_ref = refs[:6]
        theirs_ref, ours_ref, normed_ref, position_ref = refs[-4:]
    else:
        normed_ref, w_ref, bias_ref = refs[:3]
        theirs_ref, ours_ref = refs[-2:]
    step = pl.program_id(0)
    half = w_ref.shape[1]
    if first:

        @pl.when(step == 0)
        def _():
            left, right = by_core(meta[0], mine_ref[...], other_ref[...])
            position_ref[:, :half] = left
            position_ref[:, half:] = right
            hat, _ = norm_parts(position_ref[...])
            normed_ref[...] = (hat * gain_ref[...] + shift_ref[...]).astype(jnp.bfloat16)

    block = jnp.dot(normed_ref[...], w_ref[...], preferred_element_type=jnp.float32) + bias_ref[...]
    block = block.astype(jnp.bfloat16)
    parts = theirs_ref.shape[1] // half

    @pl.when(step < parts)
    def _():
        theirs_ref[:, pl.ds(pl.multiple_of(step * half, half), half)] = block

    @pl.when(step >= parts)
    def _():
        ours_ref[:, pl.ds(pl.multiple_of((step - parts) * half, half), half)] = block


def mix_rows(core, sources, weight, bias, begin, parts, after=()):
    first = len(sources) > 1
    tokens = sources[0].shape[0]
    features = weight.shape[0]
    half = features // 2

    def column(i, meta):
        return 2 * (begin + i % parts) + jnp.where(i < parts, 1 - meta[0], meta[0])

    whole = lambda shape: pl.BlockSpec(shape, lambda i, meta: (0, 0))
    out_specs = [whole((tokens, parts * half))] * 2
    out_shape = [jax.ShapeDtypeStruct((tokens, parts * half), jnp.bfloat16)] * 2
    if first:
        out_specs = out_specs + [whole((tokens, features))] * 2
        out_shape = out_shape + [jax.ShapeDtypeStruct((tokens, features), kind) for kind in (jnp.bfloat16, jnp.float32)]
    return pl.pallas_call(
        partial(mix_kernel, first),
        grid_spec=pltpu.PrefetchScalarGridSpec(
            num_scalar_prefetch=1,
            grid=(2 * parts,),
            in_specs=[whole(item.shape) for item in sources]
            + [
                pl.BlockSpec((features, half), lambda i, meta: (0, column(i, meta))),
                pl.BlockSpec((1, half), lambda i, meta: (0, column(i, meta))),
            ]
            + [pl.BlockSpec(memory_space=pl.ANY)] * len(after),
            out_specs=out_specs,
        ),
        out_shape=out_shape,
        compiler_params=pltpu.CompilerParams(vmem_limit_bytes=VMEM_LIMIT, dimension_semantics=("arbitrary",)),
        cost_estimate=cost(
            flops=4 * parts * tokens * half * features, bytes_accessed=4 * parts * half * features, transcendentals=0
        ),
        name="norm_keys_values" if first else "queries",
    )(core, *sources, weight, bias, *after)


def unmix_kernel(
    meta, mine_ref, other_ref, w_ref, position_ref, resid_ref, gain_ref, *refs
):
    ours_ref, theirs_ref, sums_ref, total = refs[-4:]
    step = pl.program_id(0)
    half = theirs_ref.shape[1]

    @pl.when(step == 0)
    def _():
        total[...] = jnp.zeros_like(total)

    block = jnp.where(step < 3, mine_ref[...], other_ref[...])
    total[...] += lanes_dot(block, w_ref[...])

    @pl.when(step == 5)
    def _():
        grad = total[...]
        hat, scale = norm_parts(position_ref[...])
        sums_ref[0:1, :] = column_sum(grad * hat)
        sums_ref[1:2, :] = column_sum(grad)
        sums_ref[2:8, :] = jnp.zeros((6, 2 * half), jnp.float32)
        result = resid_ref[...] + norm_back(grad, hat, scale, gain_ref[...])
        low_half, high_half = result[:, :half], result[:, half:]
        ours_ref[...] = jnp.where(meta[0] == 0, low_half, high_half)
        theirs_ref[...] = jnp.where(meta[0] == 0, high_half, low_half)


def unmix_rows(core, mine, other, weight, position, grad_resid, gain, after):
    tokens, features = position.shape
    half = features // 2

    def column(i, meta):
        return 2 * (i % 3) + jnp.where(i < 3, meta[0], 1 - meta[0])

    whole = lambda shape: pl.BlockSpec(shape, lambda i, meta: (0, 0))
    return pl.pallas_call(
        unmix_kernel,
        grid_spec=pltpu.PrefetchScalarGridSpec(
            num_scalar_prefetch=1,
            grid=(6,),
            in_specs=[
                pl.BlockSpec((tokens, half), lambda i, meta: (0, i % 3)),
                pl.BlockSpec((tokens, half), lambda i, meta: (0, i % 3)),
                pl.BlockSpec((features, half), lambda i, meta: (0, column(i, meta))),
                whole((tokens, features)),
                whole((tokens, features)),
                whole((1, features)),
            ]
            + [pl.BlockSpec(memory_space=pl.ANY)] * len(after),
            out_specs=[whole((tokens, half)), whole((tokens, half)), whole((8, features))],
            scratch_shapes=[pltpu.VMEM((tokens, features), jnp.float32)],
        ),
        out_shape=[
            jax.ShapeDtypeStruct((tokens, half), jnp.float32),
            jax.ShapeDtypeStruct((tokens, half), jnp.float32),
            jax.ShapeDtypeStruct((8, features), jnp.float32),
        ],
        compiler_params=pltpu.CompilerParams(vmem_limit_bytes=VMEM_LIMIT, dimension_semantics=("arbitrary",)),
        cost_estimate=cost(flops=12 * tokens * half * features, bytes_accessed=14 * half * features, transcendentals=0),
        name="qkv_and_norm_back",
    )(core, mine, other, weight, position, grad_resid, gain, *after)


def pack_places(features, width):
    places, at = {}, 0
    for name, size in (
        ("active", width), ("second", features), ("attended", features), ("up", width // 2),
        ("out", features // 2), ("branch", features // 2),
    ):
        places[name] = at
        at += size
    places["all"] = at
    return places


def middle_kernel(
    meta, mine_ref, other_ref, position_ref, w_out_ref, w_up_ref, w_down_ref, up_bias_ref, head_w_ref, head_b_ref,
    labels_ref, rows_ref,
    pack_ref, output_ref, out_low_ours, up_ours, branch_ours, att_ours, att_theirs, resid_grad_ref, sums_ref,
    up_sums_ref, head_ref, last_ref,
    resid, total, slope, grad_out, grad_low,
):
    step = pl.program_id(0)
    chunks = slope.shape[0]
    core = meta[0]
    half = mine_ref.shape[1]
    features = 2 * half
    chunk_width = slope.shape[2]
    places = pack_places(features, chunks * chunk_width)

    def at(name, size):
        return slice(places[name], places[name] + size)

    second_at, attended_at = at("second", features), at("attended", features)

    def store_halves(ours, theirs, values):
        low_half, high_half = values[:, :half], values[:, half:]
        ours[...] = jnp.where(core == 0, low_half, high_half)
        theirs[...] = jnp.where(core == 0, high_half, low_half)

    @pl.when(step == 0)
    def _():
        left, right = by_core(core, mine_ref[...].astype(jnp.float32), other_ref[...].astype(jnp.float32))
        pack_ref[:, places["attended"] : places["attended"] + half] = left.astype(jnp.bfloat16)
        pack_ref[:, places["attended"] + half : places["attended"] + features] = right.astype(jnp.bfloat16)
        resid[...] = (
            position_ref[...]
            + jnp.dot(pack_ref[:, attended_at], w_out_ref[...], preferred_element_type=jnp.float32)
            + rows_ref[2:3, :]
        )
        hat, _ = norm_parts(resid[...])
        pack_ref[:, second_at] = (hat * rows_ref[0:1, :] + rows_ref[1:2, :]).astype(jnp.bfloat16)
        total[...] = jnp.zeros_like(total)

    @pl.when(step < chunks)
    def _():
        raised = jnp.dot(pack_ref[:, second_at], w_up_ref[...], preferred_element_type=jnp.float32) + up_bias_ref[...]
        below, density = phi_parts(raised)
        slope[step] = below + raised * density
        active = (raised * below).astype(jnp.bfloat16)
        pack_ref[:, pl.ds(pl.multiple_of(places["active"] + step * chunk_width, chunk_width), chunk_width)] = active
        total[...] += jnp.dot(active, w_down_ref[...], preferred_element_type=jnp.float32)

    @pl.when(step == chunks - 1)
    def _():
        low = (resid[...] + total[...] + rows_ref[3:4, :]).astype(jnp.bfloat16)
        output_ref[...] = low
        logits = jnp.dot(low, head_w_ref[...], preferred_element_type=jnp.float32) + head_b_ref[...]
        top = jnp.max(logits, axis=-1, keepdims=True)
        shifted = jnp.exp(logits - top)
        sums = jnp.sum(shifted, axis=-1, keepdims=True)
        onehot = labels_ref[...] == lax.broadcasted_iota(jnp.int32, logits.shape, 1)
        picked = jnp.sum(jnp.where(onehot, logits, 0.0), axis=-1, keepdims=True)
        loss = jnp.sum(top + jnp.log(sums) - picked)
        grad_logits = (shifted / sums - onehot.astype(jnp.float32)).astype(jnp.bfloat16)
        head_ref[...] = rows_dot(grad_logits, low)
        last_ref[...] = jnp.zeros_like(last_ref)
        last_ref[0:1, 0:VOCAB] = column_sum(grad_logits.astype(jnp.float32))
        last_ref[1:2, :] = jnp.full((1, 128), loss, jnp.float32)
        grad = lanes_dot(grad_logits, head_w_ref[...])
        grad_out[...] = grad
        grad_low[...] = grad.astype(jnp.bfloat16)
        store_halves(out_low_ours, pack_ref.at[:, at("out", half)], grad_low[...])
        sums_ref[3:4, :] = column_sum(grad_low[...].astype(jnp.float32))
        sums_ref[4:8, :] = jnp.zeros((4, 2 * half), jnp.float32)
        total[...] = jnp.zeros_like(total)

    @pl.when(step >= chunks)
    def _():
        chunk = 2 * chunks - 1 - step
        grad = lanes_dot(grad_low[...], w_down_ref[...]) * slope[chunk]
        low = grad.astype(jnp.bfloat16)
        up_sums_ref[0] = jnp.broadcast_to(column_sum(low.astype(jnp.float32)), up_sums_ref.shape[1:])
        total[...] += lanes_dot(low, w_up_ref[...])
        ours = (chunk >= chunks // 2) == (core == 1)

        @pl.when(ours)
        def _():
            up_ours[...] = low

        @pl.when(jnp.logical_not(ours))
        def _():
            place = places["up"] + (chunk & (chunks // 2 - 1)) * chunk_width
            pack_ref[:, pl.ds(pl.multiple_of(place, chunk_width), chunk_width)] = low

    @pl.when(step == 2 * chunks - 1)
    def _():
        hat, scale = norm_parts(resid[...])
        grad = total[...]
        sums_ref[0:1, :] = column_sum(grad * hat)
        sums_ref[2:3, :] = column_sum(grad)
        result = grad_out[...] + norm_back(grad, hat, scale, rows_ref[0:1, :])
        resid_grad_ref[...] = result
        branch = result.astype(jnp.bfloat16)
        store_halves(branch_ours, pack_ref.at[:, at("branch", half)], branch)
        sums_ref[1:2, :] = column_sum(branch.astype(jnp.float32))
        store_halves(att_ours, att_theirs, lanes_dot(branch, w_out_ref[...]).astype(jnp.bfloat16))


def middle(core, mine, other, position, w_out, w_up, w_down, up_bias, head_w, head_b, labels, rows):
    tokens, features = position.shape
    half = features // 2
    width = w_up.shape[1]
    chunks = 8
    chunk = width // chunks
    vocab = head_w.shape[1]
    last = 2 * chunks - 1

    def part(i):
        return jnp.where(i < chunks, i, last - i)

    def own_up(i, meta):
        back = part(jnp.maximum(i, chunks))
        return jnp.where(meta[0] == 0, jnp.minimum(back, chunks // 2 - 1), jnp.maximum(back - chunks // 2, 0))

    whole = lambda shape: pl.BlockSpec(shape, lambda i, meta: tuple(0 for _ in shape))
    low = lambda *shape: jax.ShapeDtypeStruct(shape, jnp.bfloat16)
    full = lambda *shape: jax.ShapeDtypeStruct(shape, jnp.float32)
    return pl.pallas_call(
        middle_kernel,
        grid_spec=pltpu.PrefetchScalarGridSpec(
            num_scalar_prefetch=1,
            grid=(2 * chunks,),
            in_specs=[
                whole((tokens, half)),
                whole((tokens, half)),
                whole((tokens, features)),
                whole((features, features)),
                pl.BlockSpec((features, chunk), lambda i, meta: (0, part(i))),
                pl.BlockSpec((chunk, features), lambda i, meta: (part(i), 0)),
                pl.BlockSpec((1, chunk), lambda i, meta: (0, part(i))),
                whole((features, vocab)),
                whole((1, vocab)),
                whole((tokens, 1)),
                whole((8, features)),
            ],
            out_specs=[
                whole((tokens, pack_places(features, width)["all"])),
                whole((tokens, features)),
                whole((tokens, half)),
                pl.BlockSpec((tokens, chunk), lambda i, meta: (0, own_up(i, meta))),
                whole((tokens, half)),
                whole((tokens, half)),
                whole((tokens, half)),
                whole((tokens, features)),
                whole((8, features)),
                pl.BlockSpec((1, 8, chunk), lambda i, meta: (part(jnp.maximum(i, chunks)), 0, 0)),
                whole((vocab, features)),
                whole((8, 128)),
            ],
            scratch_shapes=[
                pltpu.VMEM((tokens, features), jnp.float32),
                pltpu.VMEM((tokens, features), jnp.float32),
                pltpu.VMEM((chunks, tokens, chunk), jnp.float32),
                pltpu.VMEM((tokens, features), jnp.float32),
                pltpu.VMEM((tokens, features), jnp.bfloat16),
            ],
        ),
        out_shape=[
            low(tokens, pack_places(features, width)["all"]),
            low(tokens, features),
            low(tokens, half),
            low(tokens, width // 2),
            low(tokens, half),
            low(tokens, half),
            low(tokens, half),
            full(tokens, features),
            full(8, features),
            full(chunks, 8, chunk),
            full(vocab, features),
            full(8, 128),
        ],
        compiler_params=pltpu.CompilerParams(vmem_limit_bytes=VMEM_LIMIT, dimension_semantics=("arbitrary",)),
        cost_estimate=cost(
            flops=8 * tokens * features * width, bytes_accessed=8 * features * width, transcendentals=2 * tokens * width
        ),
        name="middle",
    )(core, mine, other, position, w_out, w_up, w_down, up_bias, head_w, head_b, labels, rows)


def conv_grad_kernel(meta, ours_ref, got_ref, slope_ref, *refs):
    position_ref, grad_ref, edge_ref, own_ref, to_x_ref, to_y_ref, to_xy_ref, sums_ref = refs[-8:]
    core, y, x = meta[0], meta[1], meta[2]
    frames = ours_ref.shape[0]
    rim = edge_ref.shape[0]
    ours, got = ours_ref[...], got_ref[...]
    position_ref[0:frames, :] = jnp.where(core == 0, ours, got)
    position_ref[frames:, :] = jnp.where(core == 0, got, ours)
    grad_ref[...] = (position_ref[...] * slope_ref[...]).astype(jnp.bfloat16)
    edge_ref[...] = jnp.where(x == 0, grad_ref[2 * frames - rim :, :], grad_ref[0:rim, :])
    sums_ref[...] = jnp.broadcast_to(column_sum(grad_ref[...].astype(jnp.float32)), sums_ref.shape)
    for ref, yy, xx in ((own_ref, y, x), (to_x_ref, y, 1 - x), (to_y_ref, 1 - y, x), (to_xy_ref, 1 - y, 1 - x)):
        ref[...] = grad_ref[:, pl.ds(pl.multiple_of(256 * xx + 128 * yy, 128), 128)]


def conv_grad_rows(meta, ours, got, slope, after):
    frames, half = ours.shape
    operands = (ours, got, slope)
    shapes = [((2 * frames, half), jnp.float32), ((2 * frames, half), jnp.bfloat16), ((KERNEL // 2, half), jnp.bfloat16)]
    shapes += [((2 * frames, 128), jnp.bfloat16)] * 4 + [((8, half), jnp.float32)]
    return pl.pallas_call(
        conv_grad_kernel,
        grid_spec=pltpu.PrefetchScalarGridSpec(
            num_scalar_prefetch=1,
            grid=(1,),
            in_specs=[pl.BlockSpec(item.shape, lambda i, m: (0, 0)) for item in operands]
            + [pl.BlockSpec(memory_space=pl.ANY)] * len(after),
            out_specs=[pl.BlockSpec(shape, lambda i, m: (0, 0)) for shape, _ in shapes],
        ),
        out_shape=[jax.ShapeDtypeStruct(shape, kind) for shape, kind in shapes],
        compiler_params=pltpu.CompilerParams(vmem_limit_bytes=VMEM_LIMIT, dimension_semantics=("arbitrary",)),
        cost_estimate=cost(flops=0, bytes_accessed=4000000, transcendentals=0),
        name="conv_grad_rows",
    )(meta, *operands, *after)


def weight_kernel(tasks, out_count, meta, *refs):
    refs = list(refs)
    step = pl.program_id(0)
    inputs = []
    for task in tasks:
        inputs.append([refs.pop(0) for _ in range(5 if task["add"] is not None else 4)])
    outs = refs[-out_count:]
    begin = 0
    for task, ins in zip(tasks, inputs):
        rows, columns = task["rows"], task["columns"]

        def store(where, values, at, task=task):
            index, column = where
            size = values.shape[0]
            span = pl.ds(pl.multiple_of(at * size, size), size)
            outs[index][span, column : column + values.shape[1]] = values.astype(jnp.bfloat16)

        @pl.when(jnp.logical_and(step >= begin, step < begin + task["blocks"]))
        def _(task=task, ins=ins, begin=begin, store=store, rows=rows, columns=columns):
            total = rows_dot(ins[0][...], ins[2][...]) + rows_dot(ins[1][...], ins[3][...])
            if task["add"] is not None:
                total = total + ins[4][...].astype(jnp.float32)
            at = step - begin + task["place"]
            if task["split"] is None:
                store(task["outs"][0], total, at)
                return
            if task["split"] == "columns":
                first, second = total[:, : columns // 2], total[:, columns // 2 :]
            else:
                blocks = total.reshape(-1, 2, task["unit"], columns)
                first, second = (blocks[:, k].reshape(rows // 2, columns) for k in range(2))
            bit = task["bit"](meta)
            store(task["outs"][0], jnp.where(bit == 0, second, first), at)
            store(task["outs"][1], jnp.where(bit == 0, first, second), at)

        begin = begin + task["blocks"]


def weight_task(
    outs, left, right, rows, blocks, row_of, columns, column_of, add=None, add_of=None, split=None, bit=None, unit=0, place=0
):
    return dict(
        outs=outs, left=left, right=right, rows=rows, blocks=blocks, row_of=row_of, columns=columns,
        column_of=column_of, add=add, add_of=add_of, split=split, bit=bit, unit=unit, place=place,
    )


def weight_parts(meta, tasks, shapes, name, after):
    in_specs, operands = [], []
    begin, flops, moved = 0, 0, 0
    for task in tasks:
        rows, columns, blocks = task["rows"], task["columns"], task["blocks"]
        tokens = task["left"][0][0].shape[0]

        def local(i, begin=begin, blocks=blocks):
            return jnp.clip(i - begin, 0, blocks - 1)

        for array, base in task["left"]:
            in_specs.append(
                pl.BlockSpec(
                    (tokens, rows), lambda i, m, t=task, local=local, base=base: (0, base // t["rows"] + t["row_of"](local(i), m))
                )
            )
            operands.append(array)
        for array, base in task["right"]:
            in_specs.append(
                pl.BlockSpec((tokens, columns), lambda i, m, t=task, base=base: (0, base // t["columns"] + t["column_of"](m)))
            )
            operands.append(array)
        if task["add"] is not None:
            in_specs.append(pl.BlockSpec((rows, columns), lambda i, m, t=task, local=local: t["add_of"](local(i), m)))
            operands.append(task["add"])
        begin += blocks
        flops += 4 * tokens * rows * blocks * columns
        moved += 2 * rows * blocks * columns + 4 * tokens * (rows * blocks + columns)
    in_specs += [pl.BlockSpec(memory_space=pl.ANY)] * len(after)
    operands += list(after)
    return pl.pallas_call(
        partial(weight_kernel, tasks, len(shapes)),
        grid_spec=pltpu.PrefetchScalarGridSpec(
            num_scalar_prefetch=1,
            grid=(begin,),
            in_specs=in_specs,
            out_specs=[pl.BlockSpec(shape, lambda i, m: (0, 0)) for shape in shapes],
        ),
        out_shape=[jax.ShapeDtypeStruct(shape, jnp.bfloat16) for shape in shapes],
        compiler_params=pltpu.CompilerParams(vmem_limit_bytes=VMEM_LIMIT, dimension_semantics=("arbitrary",)),
        cost_estimate=cost(flops=flops, bytes_accessed=moved, transcendentals=0),
        name=name,
    )(meta, *operands)


def flip_kernel(meta, own_ref, got_ref, out_ref):
    source = jnp.where(pl.program_id(0) < 4, own_ref[0], got_ref[0])
    out_ref[...] = source.astype(jnp.float32).T


def flip_columns(meta, own, got):
    _, width, rows = own.shape
    count = 8

    def column(i, m):
        return 4 * (m[0] ^ (i >> 2)) + 2 * (i & 1) + (m[1] ^ ((i >> 1) & 1))

    return pl.pallas_call(
        flip_kernel,
        grid_spec=pltpu.PrefetchScalarGridSpec(
            num_scalar_prefetch=1,
            grid=(count,),
            in_specs=[
                pl.BlockSpec((1, width, rows), lambda i, m: (jnp.minimum(i, 3), 0, 0)),
                pl.BlockSpec((1, width, rows), lambda i, m: (jnp.maximum(i - 4, 0), 0, 0)),
            ],
            out_specs=pl.BlockSpec((rows, width), lambda i, m: (0, column(i, m))),
        ),
        out_shape=jax.ShapeDtypeStruct((rows, count * width), jnp.float32),
        compiler_params=pltpu.CompilerParams(vmem_limit_bytes=VMEM_LIMIT, dimension_semantics=("arbitrary",)),
        cost_estimate=cost(flops=0, bytes_accessed=6 * count * width * rows, transcendentals=0),
        name="flip_columns",
    )(meta, own, got)


def small_kernel(meta, head_ref, mid_ref, first_ref, conv_ref, ours_ref, got_ref, up_ref, last_ref, *refs):
    out_ref = refs[-1]
    core = meta[0]
    half = conv_ref.shape[1]
    zero = jnp.zeros((1, half), jnp.float32)

    def wide(left, right):
        return jnp.concatenate([left, right], axis=1)

    def halves(part):
        ours = ours_ref[0:1, part * half : (part + 1) * half]
        got = got_ref[0:1, part * half : (part + 1) * half]
        return wide(jnp.where(core == 0, ours, got), jnp.where(core == 0, got, ours))

    conv = conv_ref[0:1, :]
    rows = jnp.concatenate(
        [
            mid_ref[0:4, :],
            first_ref[0:2, :],
            wide(jnp.where(core == 0, conv, zero), jnp.where(core == 0, zero, conv)),
            halves(0),
            halves(2),
        ],
        axis=0,
    )
    unit = out_ref.shape[2]
    for j in range(8):
        span = slice(j * unit, (j + 1) * unit)
        out_ref[j, 0:VOCAB, :] = head_ref[:, span]
        out_ref[j, VOCAB : VOCAB + 9, :] = rows[:, span]
        for r in range(4):
            out_ref[j, VOCAB + 9 + r : VOCAB + 10 + r, :] = up_ref[j, 0:1, r * unit : (r + 1) * unit]
        out_ref[j, VOCAB + 13 : VOCAB + 15, :] = last_ref[0:2, :]
        out_ref[j, VOCAB + 15 : VOCAB + 16, :] = last_ref[2:3, :]


def small_sums(meta, head, mid, first, conv, ours, got, up, last, after):
    operands = (head, mid, first, conv, ours, got, up, last)
    return pl.pallas_call(
        small_kernel,
        grid_spec=pltpu.PrefetchScalarGridSpec(
            num_scalar_prefetch=1,
            grid=(1,),
            in_specs=[pl.BlockSpec(item.shape, lambda i, m, n=item.ndim: (0,) * n) for item in operands]
            + [pl.BlockSpec(memory_space=pl.ANY)] * len(after),
            out_specs=pl.BlockSpec((8, 48, 128), lambda i, m: (0, 0, 0)),
        ),
        out_shape=jax.ShapeDtypeStruct((8, 48, 128), jnp.float32),
        compiler_params=pltpu.CompilerParams(vmem_limit_bytes=VMEM_LIMIT, dimension_semantics=("arbitrary",)),
        cost_estimate=cost(flops=0, bytes_accessed=400000, transcendentals=0),
        name="small_sums",
    )(meta, *operands, *after)


def tile_lists(seg_ext, rise):
    row_count = seg_ext.shape[0]
    frames = seg_ext.shape[1] - KERNEL
    tiles = frames // 64
    center = seg_ext[:, KERNEL // 2 : KERNEL // 2 + frames].reshape(row_count, tiles, 64)
    first = center[:, :, 0].reshape(-1)
    counts = (center[:, :, 63].reshape(-1) - first + 1).astype(jnp.int32)
    ends = jnp.cumsum(counts)
    slots = row_count * (tiles + rise)
    slot = jnp.arange(slots, dtype=jnp.int32)
    tile = jnp.sum((slot[:, None] >= ends[None, :]).astype(jnp.int32), axis=1)
    used = tile < row_count * tiles
    tile = jnp.minimum(tile, row_count * tiles - 1)
    onehot = tile[:, None] == jnp.arange(row_count * tiles, dtype=jnp.int32)[None, :]
    begin = jnp.sum(jnp.where(onehot, (ends - counts)[None, :], 0), axis=1)
    number = jnp.sum(jnp.where(onehot, first[None, :], 0), axis=1) + slot - begin
    number = jnp.where(used, number, -2)
    in_block = tile + (tile // tiles) * (KERNEL // 64)
    return in_block.astype(jnp.int32), tile.astype(jnp.int32), number.astype(jnp.int32)


def lane_low(rows):
    return lax.broadcasted_iota(jnp.int32, (rows, 128), 1) < 64


def half_roll(block):
    return pltpu.roll(block, 64, 1)


def quad_rows(src, rows, side):
    low = lane_low(rows)
    parts = [src[pl.ds(j, rows, stride=4), :] for j in range(4)]
    halves = []
    for a, b in ((0, 1), (2, 3)):
        if side == 0:
            halves.append(jnp.where(low, parts[a], half_roll(parts[b])))
        else:
            halves.append(jnp.where(low, half_roll(parts[a]), parts[b]))
    return halves


def conv_setup(meta, slots, seg_ref, flat, shifts, masks):
    rows4 = seg_ref.shape[0]
    blocks = rows4 // 16
    one, zero = jnp.ones((16, 256), jnp.bfloat16), jnp.zeros((16, 256), jnp.bfloat16)
    flat[0:rows4, :] = seg_ref[...]
    flat[rows4:, :] = jnp.zeros((16, 256), jnp.float32)
    for p in range(16):
        shifts[p] = flat[pl.ds(p, rows4), :].astype(jnp.bfloat16).reshape(blocks, 16, 256)

    @pl.loop(0, slots)
    def _(v):
        at = meta[1 + v]
        number = jnp.full((16, 256), meta[1 + 2 * slots + v].astype(jnp.float32), jnp.float32).astype(jnp.bfloat16)
        row = pl.multiple_of(v * 16, 16)
        for b in range(TAP_BLOCKS):
            ids = shifts[b % 16, at + b // 16]
            masks[pl.ds(row, 16), b * 256 : (b + 1) * 256] = jnp.where(ids == number, one, zero)


def conv_shifts(wide, side, flat, shifts):
    rows4 = shifts.shape[1] * 16
    halves = quad_rows(wide, rows4, side)
    flat[0:rows4, 0:128] = halves[0]
    flat[0:rows4, 128:256] = halves[1]
    for p in range(16):
        shifts[p] = flat[pl.ds(p, rows4), :].astype(jnp.bfloat16).reshape(rows4 // 16, 16, 256)


def conv_patch(places, b, shifts, masks):
    span = slice(b * 256, (b + 1) * 256)
    pieces = [
        shifts[b % 16, at + b // 16] * masks[v * 16 : (v + 1) * 16, span] for v, at in enumerate(places)
    ]
    return jnp.concatenate(pieces, axis=0)


def conv_taps(w_ref, side, b, taps):
    rows = 256
    low = lane_low(rows)
    depth = w_ref.shape[0]
    zero = jnp.zeros((64, 128), jnp.bfloat16)
    if b == 0:
        here, before = w_ref[0:rows, :], jnp.concatenate([zero, w_ref[0 : rows - 64, :]], axis=0)
    elif b * rows < depth:
        here, before = w_ref[b * rows : (b + 1) * rows, :], w_ref[b * rows - 64 : (b + 1) * rows - 64, :]
    else:
        here, before = jnp.concatenate([zero] * 4, axis=0), jnp.concatenate([w_ref[depth - 64 :, :]] + [zero] * 3, axis=0)
    block = jnp.where(low, here, half_roll(before)) if side == 0 else jnp.where(low, half_roll(here), before)
    taps[128 + b * rows : 128 + (b + 1) * rows, :] = block
    return jnp.concatenate([block, taps[b * rows : (b + 1) * rows, :]], axis=1)


def conv_kernel(slots, backward, meta, x_ref, seg_ref, w_ref, extra_ref, *refs):
    if backward:
        o_ref, *refs = refs[-8:]
    else:
        o_ref, *refs = refs[-9:]
    if backward:
        wide, flat, shifts, masks, taps, sums, outs = refs
    else:
        slope_ref, wide, flat, shifts, masks, taps, sums, outs = refs

    @pl.when(pl.program_id(0) == 0)
    def _():
        conv_setup(meta, slots, seg_ref, flat, shifts, masks)

    wide[...] = x_ref[...].astype(jnp.float32)
    taps[0:128, :] = jnp.zeros((128, 128), jnp.bfloat16)
    out_rows = o_ref.shape[0] // 4
    places = [meta[1 + v] for v in range(slots)]
    for side in range(2):
        conv_shifts(wide, side, flat, shifts)
        total = jnp.zeros((256, slots * 16) if backward else (slots * 16, 256), jnp.float32)
        for b in range(TAP_BLOCKS):
            weight = conv_taps(w_ref, side, b, taps)
            if backward:
                total = total + lanes_dot(weight, conv_patch(places, TAP_BLOCKS - 1 - b, shifts, masks))
            else:
                total = total + jnp.dot(
                    conv_patch(places, b, shifts, masks), weight, preferred_element_type=jnp.float32
                )
        sums[...] = total.T if backward else total

        @pl.loop(0, slots)
        def _(v):
            to = pl.ds(pl.multiple_of(meta[1 + slots + v] * 16, 16), 16)
            row = pl.ds(pl.multiple_of(v * 16, 16), 16)
            keep = masks[row, 16 * 256 : 17 * 256].astype(jnp.float32) > 0.5
            outs[side, to, :] = jnp.where(keep, sums[row, :], outs[side, to, :])

    low = lane_low(out_rows)
    for half in range(2):
        zero_side = outs[0, :, half * 128 : (half + 1) * 128]
        one_side = outs[1, :, half * 128 : (half + 1) * 128]
        wide[pl.ds(2 * half, out_rows, stride=4), :] = jnp.where(low, zero_side, half_roll(one_side))
        wide[pl.ds(2 * half + 1, out_rows, stride=4), :] = jnp.where(low, half_roll(zero_side), one_side)
    result = wide[0 : 4 * out_rows, :]
    if backward:
        o_ref[...] = (extra_ref[...] + result).astype(o_ref.dtype)
    else:
        result = result + extra_ref[...]
        below, density = phi_parts(result)
        center = x_ref[KERNEL // 2 : KERNEL // 2 + 4 * out_rows, :].astype(jnp.float32)
        o_ref[...] = center + result * below
        slope_ref[...] = below + result * density


def seg_quads(seg_ext):
    quads = seg_ext.astype(jnp.float32).reshape(-1, 4)
    return jnp.repeat(quads, 64, axis=1)


def grouped_conv(x_ext, seg_ext, weight, extra, first_pair, rise, backward, begin=0, pairs=None, after=()):
    row_count, length, width = x_ext.shape
    frames = length - KERNEL
    pairs = width // 128 if pairs is None else pairs
    in_block, tile, number = tile_lists(seg_ext, rise)
    slots = in_block.shape[0]
    meta = jnp.concatenate([jnp.reshape(first_pair, (1,)).astype(jnp.int32), in_block, tile, number])
    rows4 = row_count * length // 4
    out4 = row_count * frames // 4
    depth = TAP_BLOCKS * 256
    return pl.pallas_call(
        partial(conv_kernel, slots, backward),
        grid_spec=pltpu.PrefetchScalarGridSpec(
            num_scalar_prefetch=1,
            grid=(pairs,),
            in_specs=[
                pl.BlockSpec((row_count * length, 128), lambda p, meta: (0, begin + p)),
                pl.BlockSpec((rows4, 256), lambda p, meta: (0, 0)),
                pl.BlockSpec((weight.shape[0], 128), lambda p, meta: (0, meta[0] + begin + p)),
                pl.BlockSpec((extra.shape[0], 128), lambda p, meta: (0, begin + p)),
            ]
            + [pl.BlockSpec(memory_space=pl.ANY)] * len(after),
            out_specs=[pl.BlockSpec((row_count * frames, 128), lambda p, meta: (0, p))] * (1 if backward else 2),
            scratch_shapes=[
                pltpu.VMEM((row_count * length, 128), jnp.float32),
                pltpu.VMEM((rows4 + 16, 256), jnp.float32),
                pltpu.VMEM((16, rows4 // 16, 16, 256), jnp.bfloat16),
                pltpu.VMEM((slots * 16, depth), jnp.bfloat16),
                pltpu.VMEM((128 + depth, 128), jnp.bfloat16),
                pltpu.VMEM((slots * 16, 256), jnp.float32),
                pltpu.VMEM((2, out4, 256), jnp.float32),
            ],
        ),
        out_shape=[jax.ShapeDtypeStruct((row_count * frames, 128 * pairs), jnp.bfloat16 if backward else jnp.float32)]
        * (1 if backward else 2),
        compiler_params=pltpu.CompilerParams(vmem_limit_bytes=VMEM_LIMIT, dimension_semantics=("arbitrary",)),
        cost_estimate=cost(
            flops=2 * pairs * 2 * slots * 16 * 256 * depth, bytes_accessed=pairs * weight.shape[0] * 256, transcendentals=0
        ),
        name="conv_back" if backward else "conv_forth",
    )(meta, x_ext.reshape(row_count * length, width), seg_quads(seg_ext), weight, extra, *after)


def at_block(b):
    return pl.ds(b * 256, 256) if isinstance(b, int) else pl.ds(pl.multiple_of(b * 256, 256), 256)


def id_block(number):
    return jnp.full((16, 256), number, jnp.float32).astype(jnp.bfloat16)


def conv_ids(seg_ref, flat, ids):
    rows4 = seg_ref.shape[0]
    flat[0:rows4, :] = seg_ref[...]
    flat[rows4:, :] = jnp.zeros((16, 256), jnp.float32)
    for p in range(16):
        ids[p] = flat[pl.ds(p, rows4), :].astype(jnp.bfloat16).reshape(rows4 // 16, 16, 256)


def conv_cut(places, numbers, b, shifts, ids):
    nothing = jnp.zeros((16, 256), jnp.bfloat16)
    pieces = []
    for at, number in zip(places, numbers):
        same = ids[b & 15, at + (b >> 4)] == id_block(number)
        pieces.append(jnp.where(same, shifts[b & 15, at + (b >> 4)], nothing))
    return jnp.concatenate(pieces, axis=0)


def conv_weight_kernel(slots, meta, x_ref, seg_ref, g_ref, *refs):
    send_ref, keep_ref, wide, wide_g, flat, shifts, masks, quads, picks, sums = refs[-10:]
    @pl.when(pl.program_id(0) == 0)
    def _():
        conv_ids(seg_ref, flat, masks)

    wide[...] = x_ref[...].astype(jnp.float32)
    wide_g[...] = g_ref[...].astype(jnp.float32)
    out_rows = g_ref.shape[0] // 4
    low = lane_low(64)
    places = [meta[1 + v] for v in range(slots)]
    numbers = [meta[1 + 2 * slots + v].astype(jnp.float32) for v in range(slots)]
    nothing = jnp.zeros((16, 256), jnp.bfloat16)
    for side in range(2):
        conv_shifts(wide, side, flat, shifts)
        halves = quad_rows(wide_g, out_rows, side)
        quads[:, 0:128] = halves[0].astype(jnp.bfloat16)
        quads[:, 128:256] = halves[1].astype(jnp.bfloat16)

        for v in range(slots):
            at = pl.ds(pl.multiple_of(meta[1 + slots + v] * 16, 16), 16)
            same = masks[0, places[v] + 1] == id_block(numbers[v])
            picks[v * 16 : (v + 1) * 16, :] = jnp.where(same, quads[at, :], nothing)

        turned = picks[...].T

        @pl.loop(0, TAP_BLOCKS, unroll=DW_UNROLL)
        def _(b):
            sums[:, at_block(b)] = jnp.dot(
                turned, conv_cut(places, numbers, b, shifts, masks), preferred_element_type=jnp.float32
            )

        def piece(j, q):
            return sums[j * 64 : (j + 1) * 64, q * 128 : (q + 1) * 128]

        def odd(q):
            return half_roll(piece(1, q) + piece(3, q + 1))

        def emit(block, ref):
            left = odd(16 * block)
            for q in range(16 * block, 16 * block + 16):
                right = odd(q + 1)
                part = piece(0, q) + piece(2, q + 1) + jnp.where(low, left, right)
                first = (q // 8 % 2) * 128 + side * 64
                ref[block // 2, first : first + 64, q % 8 * 128 : (q % 8 + 1) * 128] = part.astype(ref.dtype)
                left = right

        for block in range(4):
            pl.when((meta[0] & 1) == (block & 1))(partial(emit, block, keep_ref))
            pl.when((meta[0] & 1) != (block & 1))(partial(emit, block, send_ref))


def grouped_conv_weight(x_ext, seg_ext, grad, rise, place, after):
    row_count, length, width = x_ext.shape
    frames = length - KERNEL
    pairs = width // 128
    in_block, tile, number = tile_lists(seg_ext, rise)
    slots = in_block.shape[0]
    meta = jnp.concatenate([jnp.reshape(place, (1,)).astype(jnp.int32), in_block, tile, number])
    rows4 = row_count * length // 4
    out4 = row_count * frames // 4
    depth = TAP_BLOCKS * 256
    return pl.pallas_call(
        partial(conv_weight_kernel, slots),
        grid_spec=pltpu.PrefetchScalarGridSpec(
            num_scalar_prefetch=1,
            grid=(pairs,),
            in_specs=[
                pl.BlockSpec((row_count * length, 128), lambda p, meta: (0, p)),
                pl.BlockSpec((rows4, 256), lambda p, meta: (0, 0)),
                pl.BlockSpec((row_count * frames, 128), lambda p, meta: (0, p)),
            ]
            + [pl.BlockSpec(memory_space=pl.ANY)] * len(after),
            out_specs=[pl.BlockSpec((2, 256, KERNEL * 8), lambda p, meta: (0, 0, 0))] * 2,
            scratch_shapes=[
                pltpu.VMEM((row_count * length, 128), jnp.float32),
                pltpu.VMEM((row_count * frames, 128), jnp.float32),
                pltpu.VMEM((rows4 + 16, 256), jnp.float32),
                pltpu.VMEM((16, rows4 // 16, 16, 256), jnp.bfloat16),
                pltpu.VMEM((16, rows4 // 16, 16, 256), jnp.bfloat16),
                pltpu.VMEM((out4, 256), jnp.bfloat16),
                pltpu.VMEM((slots * 16, 256), jnp.bfloat16),
                pltpu.VMEM((256, depth), jnp.float32),
            ],
        ),
        out_shape=[jax.ShapeDtypeStruct((2, 256, KERNEL * 8), jnp.bfloat16)] * 2,
        compiler_params=pltpu.CompilerParams(vmem_limit_bytes=VMEM_LIMIT, dimension_semantics=("arbitrary",)),
        cost_estimate=cost(
            flops=2 * pairs * 2 * slots * 16 * 256 * depth, bytes_accessed=width * KERNEL * 128, transcendentals=0
        ),
        name="conv_weight_grad",
    )(meta, x_ext.reshape(row_count * length, width), seg_quads(seg_ext), grad, *after)


def fold_kernel(items, outs_count, meta, *refs):
    refs = list(refs)
    outs = refs[-outs_count:]
    for item in items:
        kept = refs.pop(0)
        gots = [refs.pop(0) for _ in item["gots"]]
        place = item["place"]
        shape = kept.shape
        bit = item["bit"](meta)
        for side, where in ((1 - bit, item["send"]), (bit, item["keep"])):
            buffer, column, lanes = where
            out = outs[buffer]
            if place is None:
                width = shape[3] // 2
                span = pl.ds(pl.multiple_of(side * width, width), width)
                for other in range(shape[0]):
                    total = kept[other, 0, :, span].astype(jnp.float32) + gots[0][other, 0, :, span].astype(jnp.float32)
                    out[other, :, column : column + width] = total.astype(out.dtype)
                continue
            for other in range(shape[1 - place]):
                at = (side, other) if place == 0 else (other, side)
                begin = 0
                for got in gots:
                    width = got.shape[3]
                    total = kept[at[0], at[1], :, begin : begin + width].astype(jnp.float32)
                    total = (total + got[at[0], at[1]].astype(jnp.float32)).astype(out.dtype)
                    rows = shape[2] // lanes
                    for k in range(lanes):
                        first = column + begin + k * shape[3]
                        out[other, :, first : first + width] = total[k * rows : (k + 1) * rows, :]
                    begin += width


def fold_item(kept, gots, place, bit, send, keep):
    return dict(kept=kept, gots=gots, place=place, bit=bit, send=send, keep=keep)


def folds(meta, items, shapes, name, after=()):
    operands = []
    for item in items:
        operands += [item["kept"]] + list(item["gots"])
    described = [dict(item, kept=None, gots=[None] * len(item["gots"])) for item in items]
    return pl.pallas_call(
        partial(fold_kernel, described, len(shapes)),
        grid_spec=pltpu.PrefetchScalarGridSpec(
            num_scalar_prefetch=1,
            grid=(1,),
            in_specs=[pl.BlockSpec(item.shape, lambda i, m: (0, 0, 0, 0)) for item in operands]
            + [pl.BlockSpec(memory_space=pl.ANY)] * len(after),
            out_specs=[pl.BlockSpec(shape, lambda i, m: (0, 0, 0)) for shape in shapes],
        ),
        out_shape=[jax.ShapeDtypeStruct(shape, jnp.bfloat16) for shape in shapes],
        compiler_params=pltpu.CompilerParams(vmem_limit_bytes=VMEM_LIMIT, dimension_semantics=("arbitrary",)),
        cost_estimate=cost(flops=0, bytes_accessed=sum(2 * item.size for item in operands), transcendentals=0),
        name=name,
    )(meta, *operands, *after)


def chosen(meta, own_ref, got_ref):
    return jnp.where(pl.program_id(0) // 2 == meta[0], own_ref[0], got_ref[0])


def finish_pair_kernel(meta, own_ref, got_ref, *refs):
    up_ref, down_ref = refs[-2:]
    source = chosen(meta, own_ref, got_ref)
    width = up_ref.shape[1]
    up_ref[...] = source[:, :width].astype(jnp.float32)
    unit = source.shape[0]
    columns = down_ref.shape[1]
    for k in range(down_ref.shape[0] // unit):
        piece = source[:, width + k * columns : width + (k + 1) * columns]
        down_ref[k * unit : (k + 1) * unit, :] = piece.astype(jnp.float32)


def finish_pair(meta, own, got, rows, after):
    unit, total = own.shape[1:]
    width = total // 2
    columns = width * unit // rows
    place = lambda i, m: (0, 2 * (i // 2) + i % 2)
    return pl.pallas_call(
        finish_pair_kernel,
        grid_spec=pltpu.PrefetchScalarGridSpec(
            num_scalar_prefetch=1,
            grid=(4,),
            in_specs=[pl.BlockSpec((1, unit, total), lambda i, m: ((i % 2) ^ m[1], 0, 0))] * 2
            + [pl.BlockSpec(memory_space=pl.ANY)] * len(after),
            out_specs=[pl.BlockSpec((unit, width), place), pl.BlockSpec((rows, columns), place)],
        ),
        out_shape=[
            jax.ShapeDtypeStruct((unit, 4 * width), jnp.float32),
            jax.ShapeDtypeStruct((rows, 4 * columns), jnp.float32),
        ],
        compiler_params=pltpu.CompilerParams(vmem_limit_bytes=VMEM_LIMIT, dimension_semantics=("arbitrary",)),
        cost_estimate=cost(flops=0, bytes_accessed=12 * own.size, transcendentals=0),
        name="finish_up_down",
    )(meta, own, got, *after)


def finish_qkv_kernel(eighth, half, meta, own_ref, got_ref, *refs):
    qkv_ref, out_ref = refs[-2:]
    step = pl.program_id(0)
    source = chosen(meta, own_ref, got_ref)
    core, y = step // 2, step % 2
    units = eighth // 128
    per_part = half // 128
    for begin, base in ((0, 0), (eighth, 2 * units)):
        for u in range(units):
            at = base + y * units + u
            at = (at // per_part) * 2 * per_part + core * per_part + at % per_part
            piece = source[:, begin + u * 128 : begin + (u + 1) * 128]
            qkv_ref[:, pl.ds(pl.multiple_of(at * 128, 128), 128)] = piece.astype(jnp.float32)
    quarter = half // 2
    first = pl.multiple_of(step * quarter, quarter)
    out_ref[:, pl.ds(first, quarter)] = source[:, 2 * eighth : 2 * eighth + quarter].astype(jnp.float32)


def finish_qkv(meta, own, got, half, after):
    unit, total = own.shape[1:]
    eighth = 3 * half // 4
    return pl.pallas_call(
        partial(finish_qkv_kernel, eighth, half),
        grid_spec=pltpu.PrefetchScalarGridSpec(
            num_scalar_prefetch=1,
            grid=(4,),
            in_specs=[pl.BlockSpec((1, unit, total), lambda i, m: ((i % 2) ^ m[1], 0, 0))] * 2
            + [pl.BlockSpec(memory_space=pl.ANY)] * len(after),
            out_specs=[
                pl.BlockSpec((unit, 6 * half), lambda i, m: (0, 0)),
                pl.BlockSpec((unit, 2 * half), lambda i, m: (0, 0)),
            ],
        ),
        out_shape=[
            jax.ShapeDtypeStruct((unit, 6 * half), jnp.float32),
            jax.ShapeDtypeStruct((unit, 2 * half), jnp.float32),
        ],
        compiler_params=pltpu.CompilerParams(vmem_limit_bytes=VMEM_LIMIT, dimension_semantics=("arbitrary",)),
        cost_estimate=cost(flops=0, bytes_accessed=12 * own.size, transcendentals=0),
        name="finish_qkv_out",
    )(meta, own, got, *after)


AXES = ("y", "c", "z", "x")


def device_pairs(place):
    pairs = []
    for y in range(2):
        for c in range(2):
            for z in range(4):
                for x in range(2):
                    ty, tc, tz, tx = place(y, c, z, x)
                    pairs.append((((y * 2 + c) * 4 + z) * 2 + x, ((ty * 2 + tc) * 4 + tz) * 2 + tx))
    return pairs


def move(values, place):
    return lax.ppermute(values, AXES, device_pairs(place))


def swap_core(values):
    return lax.ppermute(values, "c", [(0, 1), (1, 0)])


def swap_x(values):
    return lax.ppermute(values, "x", [(0, 1), (1, 0)])


def swap_y(values):
    return lax.ppermute(values, "y", [(0, 1), (1, 0)])


def swap_xy(values):
    return lax.ppermute(values, ("y", "x"), [(0, 3), (3, 0), (1, 2), (2, 1)])


def swap_z1(values):
    return lax.ppermute(values, "z", [(0, 1), (1, 0), (2, 3), (3, 2)])


def swap_z2(values):
    return lax.ppermute(values, "z", [(0, 2), (2, 0), (1, 3), (3, 1)])


def take(values, index, size, axis):
    return lax.dynamic_slice_in_dim(values, index * size, size, axis)


def once(values, *earlier):
    return lax.optimization_barrier((values,) + earlier)[0]


def ordered(index, mine, other, axis):
    first = jnp.where(index == 0, mine, other)
    second = jnp.where(index == 0, other, mine)
    return jnp.concatenate([first, second], axis=axis)


def to_rows(blocks, x, z):
    got = []
    for turn in range(2):
        mine = lax.dynamic_index_in_dim(blocks, x ^ turn, 0, keepdims=False)
        got.append(move(mine, lambda y, c, z, x: (y, z & 1, 2 * c + (x ^ turn), z >> 1)))
    flip = (z & 1) == 0
    return jnp.where(flip, got[0], got[1]), jnp.where(flip, got[1], got[0])


def from_rows(frames, z):
    half = frames.shape[0] // 2
    got = []
    for turn in range(2):
        mine = take(frames, (z & 1) ^ turn, half, 0)
        got.append(move(mine, lambda y, c, z, x: (y, z >> 1, 2 * x + c, (z & 1) ^ turn)))
    return got


def split_body(
    feats, segments, labels, conv_weight, w_qkv, w_out, w_up, w_down, head_w, head_b, gains, biases, up_bias
):
    y, c, z, x = (lax.axis_index(name) for name in AXES)
    block, features = feats.shape[1:]
    half = features // 2
    frames = 2 * block
    chip_frames = 2 * frames
    tokens = frames
    rim = KERNEL // 2
    rise = lax.axis_size("z") * lax.axis_size("x") // 2
    meta = jnp.stack([c, y, x, z]).astype(jnp.int32)

    label_rows = jnp.pad(labels.astype(jnp.bfloat16)[:, None, :], ((0, 0), (0, 15), (0, features - block)))
    first_block, second_block = to_rows(jnp.concatenate([feats, label_rows], axis=1), x, z)
    feats_own = jnp.concatenate([first_block[:block], second_block[:block]], axis=0)
    labels_own = jnp.concatenate([first_block[block, :block], second_block[block, :block]]).astype(jnp.int32)
    seg_rows = ordered(c, segments, swap_core(segments), 0)
    seg_row = lax.dynamic_index_in_dim(seg_rows, z, 0, keepdims=False)
    seg_halves = seg_row.reshape(2, 2, frames)
    seg_near = lax.dynamic_index_in_dim(seg_halves, x, 0, keepdims=False)
    seg_far = lax.dynamic_index_in_dim(seg_halves, 1 - x, 0, keepdims=False)
    seg_near, seg_far = (jnp.where(c == 0, item, item[::-1]).reshape(-1) for item in (seg_near, seg_far))
    seg_wide = jnp.pad(seg_row, (rim, rim), constant_values=-1)
    seg_ext = lax.dynamic_slice_in_dim(seg_wide, x * chip_frames, chip_frames + 2 * rim, 0)[None]

    def to_chip(values):
        return ordered(c, take(values, c, half, 1), swap_core(take(values, 1 - c, half, 1)), 0)

    def rimmed(values, edge):
        empty = jnp.zeros_like(edge)
        before = jnp.where(x == 0, empty, edge)
        after = jnp.where(x == 0, edge, empty)
        return jnp.concatenate([before, values, after], axis=0)[None]

    def with_rim(values):
        return rimmed(values, swap_x(jnp.where(x == 0, values[chip_frames - rim :], values[:rim])))

    def grouped(own, got_x, got_y, got_xy):
        return ordered(y, ordered(x, own, got_x, 0)[None], ordered(x, got_y, got_xy, 0)[None], 0)

    def to_groups(values):
        def part(yy, xx):
            return lax.dynamic_slice_in_dim(values, 256 * xx + 128 * yy, 128, 1)

        return grouped(
            part(y, x), swap_x(part(y, 1 - x)), swap_y(part(1 - y, x)), swap_xy(part(1 - y, 1 - x))
        )

    shift_bias = biases.T
    qkv_bias = jnp.concatenate([shift_bias[2], jnp.zeros((features,), jnp.float32), shift_bias[3]])[None]
    gain_rows = gains.T
    feats_chip = to_chip(feats_own)
    feats_group = jnp.pad(to_groups(feats_chip), ((0, 0), (rim, rim), (0, 0)))
    seg_pair = ordered(y, seg_row[None], swap_y(seg_row)[None], 0)
    seg_pair = jnp.pad(seg_pair, ((0, 0), (rim, rim)), constant_values=-1)
    position_chip, slope = grouped_conv(
        with_rim(feats_chip), seg_ext, conv_weight, take(shift_bias[0:1], c, half, 1), 4 * c, rise, False
    )
    theirs, ours, normed, position = mix_rows(
        meta,
        (
            take(position_chip, c, frames, 0),
            swap_core(take(position_chip, 1 - c, frames, 0)),
            gain_rows[0:1],
            shift_bias[1:2],
        ),
        w_qkv,
        qkv_bias,
        1,
        2,
        (seg_pair,),
    )
    near = jnp.concatenate([ours, swap_core(theirs)], axis=0)
    got_normed = swap_core(normed)
    far = swap_x(near)
    theirs, ours = mix_rows(meta, (normed,), w_qkv, qkv_bias, 0, 1, (feats_group,))
    queries = jnp.concatenate([ours, swap_core(theirs)], axis=0)
    mixed, state = attend_near(queries, near, seg_near, seg_near)
    attended, attended_ours, attended_away, lse = attend_far(queries, far, seg_near, seg_far, mixed, state)
    zero_row = jnp.zeros((features,), jnp.float32)
    rows = jnp.stack([gain_rows[1], shift_bias[5], shift_bias[4], shift_bias[6]] + [zero_row] * 4)
    (
        pack, output_low, out_ours, up_ours, branch_ours, att_ours, att_theirs, grad_resid, mid_sums, up_sums,
        grad_head_w, last,
    ) = middle(
        meta,
        attended_ours,
        swap_core(attended_away),
        position,
        w_out,
        w_up,
        w_down,
        up_bias[None],
        head_w,
        head_b[None],
        labels_own[:, None],
        rows,
    )

    grad_heads = jnp.concatenate([att_ours, swap_core(att_theirs)], axis=0)
    dq_far, dkv_far = attend_back(queries, far, grad_heads, attended, lse, seg_near, seg_far, jnp.bfloat16, att_ours)
    got_kv = swap_x(dkv_far)

    C, Y, X, Z = 0, 1, 2, 3
    places = pack_places(features, w_up.shape[1])
    got_pack = swap_core(once(pack, grad_heads))
    up_pair = ((up_ours, 0), (got_pack, places["up"]))
    down_pair = ((out_ours, 0), (got_pack, places["out"]))
    branch_pair = ((branch_ours, 0), (got_pack, places["branch"]))
    second_pair, active_pair, attended_pair = (
        ((pack, places[name]), (got_pack, places[name])) for name in ("second", "active", "attended")
    )
    unit = features // 8
    down_rows = w_down.shape[0] // 4
    up_wide = w_up.shape[1] // 4
    quarter = half // 2
    eighth = 3 * half // 4
    up_low, up_high, down_away, down_home = weight_parts(
        meta,
        [
            weight_task([(0, 0)], second_pair, up_pair, half, 1, lambda i, m: 0, up_wide, lambda m: 1 - m[Y]),
            weight_task(
                [(2, 0)], active_pair, down_pair, down_rows, 1,
                lambda i, m: 2 * (1 - (m[Z] >> 1)) + 1 - (m[Z] & 1), half, lambda m: 0,
            ),
            weight_task([(1, 0)], second_pair, up_pair, half, 1, lambda i, m: 1, up_wide, lambda m: 1 - m[Y]),
            weight_task(
                [(3, 0)], active_pair, down_pair, down_rows, 1,
                lambda i, m: 2 * (m[Z] >> 1) + 1 - (m[Z] & 1), half, lambda m: 0,
            ),
        ],
        [(half, up_wide), (half, up_wide), (down_rows, half), (down_rows, half)],
        "weight_first",
        (dkv_far,),
    )
    got_up_low, got_down_away = swap_y(up_low), swap_z1(down_away)
    got_up_high, got_down_home = swap_y(up_high), swap_z1(down_home)
    dq, dkv = attend_back(queries, near, grad_heads, attended, lse, seg_near, seg_near, jnp.float32, down_home)

    def mixed_grad(part):
        piece = slice(part * frames, (part + 1) * frames)
        return jnp.concatenate(
            [
                dq[piece] + dq_far[piece],
                dkv[0, piece] + got_kv[0, piece].astype(jnp.float32),
                dkv[1, piece] + got_kv[1, piece].astype(jnp.float32),
            ],
            axis=1,
        ).astype(jnp.bfloat16)

    grad_theirs = mixed_grad(1)
    grad_got = swap_core(grad_theirs)
    grad_ours = mixed_grad(0)
    position_ours, position_theirs, first_sums = unmix_rows(
        meta, grad_ours, grad_got, w_qkv, position, grad_resid, gain_rows[0:1], (got_up_low, got_down_away)
    )
    grad_position, grad_conv, edge, own_part, to_x, to_y, to_xy, conv_bias = conv_grad_rows(
        meta, position_ours, swap_core(position_theirs), slope, (got_up_high, got_down_home)
    )
    grad_rim = rimmed(grad_conv, swap_x(edge))
    grad_group = grouped(own_part, swap_x(to_x), swap_y(to_y), swap_xy(to_xy))

    x_bit, y_bit = (lambda m: m[X]), (lambda m: m[Y])
    own_sums, got_sums = (jnp.sum(item.astype(jnp.float32), axis=0, keepdims=True) for item in (grad_ours, grad_got))
    total = small_sums(
        meta, grad_head_w, mid_sums, first_sums, conv_bias, own_sums, got_sums, up_sums, last, (grad_conv,)
    )
    total = (total + swap_core(total)).reshape(2, 2, 2, -1, unit)

    def half_sum(values, axis, bit, swap):
        mine = lax.dynamic_index_in_dim(values, bit, axis, keepdims=False)
        return mine + swap(lax.dynamic_index_in_dim(values, 1 - bit, axis, keepdims=False))

    normed_pair = ((normed, 0), (got_normed, 0))
    qkv_pair = ((grad_ours, 0), (grad_theirs, 0))
    a_first, b_first = weight_parts(
        meta,
        [
            weight_task([(0, 0)], normed_pair, qkv_pair, features, 1, lambda i, m: 0, eighth, lambda m: 1 - m[Y]),
            weight_task([(1, 0)], normed_pair, qkv_pair, unit, 4, lambda i, m: 2 * i + 1 - m[X], 2 * eighth, lambda m: 1),
            weight_task(
                [(1, 2 * eighth)], attended_pair, branch_pair, unit, 4, lambda i, m: 2 * i + 1 - m[X], half, lambda m: 0
            ),
        ],
        [(features, eighth), (half, 2 * eighth + half)],
        "weight_qkv_first",
        (grad_conv, total),
    )
    total = half_sum(total, 1, z & 1, swap_z1)
    total = half_sum(total, 0, z >> 1, swap_z2)
    got_a, got_b = swap_y(a_first), swap_x(b_first)
    conv_send, conv_kept = grouped_conv_weight(
        feats_group, seg_pair, grad_group.reshape(-1, 128), rise, z, (a_first, grad_rim, total)
    )
    conv_got = swap_z1(conv_send)
    up_send, up_kept, down_send, down_kept = weight_parts(
        meta,
        [
            weight_task(
                [(0, 0), (1, 0)], second_pair, up_pair, half, 1, lambda i, m: 0, up_wide, lambda m: m[Y],
                got_up_low, lambda i, m: (0, 0), "rows", lambda m: m[Z] & 1, 2 * unit,
            ),
            weight_task(
                [(0, 0), (1, 0)], second_pair, up_pair, half, 1, lambda i, m: 1, up_wide, lambda m: m[Y],
                got_up_high, lambda i, m: (0, 0), "rows", lambda m: m[Z] & 1, 2 * unit, 1,
            ),
            weight_task(
                [(2, 0), (3, 0)], active_pair, down_pair, down_rows, 1,
                lambda i, m: 2 * (1 - (m[Z] >> 1)) + (m[Z] & 1), half, lambda m: 0, got_down_away, lambda i, m: (0, 0),
                "rows", x_bit, down_rows // 2,
            ),
            weight_task(
                [(2, 0), (3, 0)], active_pair, down_pair, down_rows, 1,
                lambda i, m: 2 * (m[Z] >> 1) + (m[Z] & 1), half, lambda m: 0, got_down_home, lambda i, m: (0, 0),
                "rows", x_bit, down_rows // 2, 1,
            ),
        ],
        [(half, up_wide), (half, up_wide), (down_rows, half), (down_rows, half)],
        "weight_second",
        (conv_send, got_a),
    )
    up_got, down_got = swap_z1(up_send), swap_x(down_send)
    low_z, high_z = (lambda m: m[Z] & 1), (lambda m: m[Z] >> 1)

    def view(values, *lead):
        return values.reshape(lead + (-1, values.shape[-1]))

    conv_left = grouped_conv(grad_rim, seg_ext, conv_weight, grad_position, 4 * c, rise, True, 0, 2, (up_kept,))[0]

    conv_send, conv_kept = folds(
        meta,
        [fold_item(conv_kept[:, None], [conv_got[:, None]], 0, high_z, (0, 0, 1), (1, 0, 1))],
        [(1, 256, KERNEL * 8)] * 2,
        "fold_taps",
        (conv_left,),
    )
    conv_got = swap_z2(conv_send)
    a_send, b_send, qkv_kept = weight_parts(
        meta,
        [
            weight_task(
                [(0, 0), (2, 0)], normed_pair, qkv_pair, features, 1, lambda i, m: 0, eighth, lambda m: m[Y],
                got_a, lambda i, m: (0, 0), "rows", x_bit, unit,
            ),
            weight_task(
                [(1, 0), (2, eighth)], normed_pair, qkv_pair, unit, 4, lambda i, m: 2 * i + m[X], 2 * eighth, lambda m: 1,
                got_b[:, : 2 * eighth], lambda i, m: (i, 0), "columns", y_bit,
            ),
            weight_task(
                [(1, eighth), (2, 2 * eighth)], attended_pair, branch_pair, unit, 4, lambda i, m: 2 * i + m[X], half,
                lambda m: 0, got_b[:, 2 * eighth :], lambda i, m: (i, 0), "columns", y_bit,
            ),
        ],
        [(half, eighth), (half, eighth + quarter), (half, 2 * eighth + quarter)],
        "weight_qkv_second",
        (conv_kept,),
    )
    a_got, b_got = swap_x(a_send), swap_y(b_send)
    conv_right = grouped_conv(
        grad_rim, seg_ext, conv_weight, grad_position, 4 * c, rise, True, 2, 2, (qkv_kept,)
    )[0]
    wide = 2 * eighth + quarter
    up_send, up_kept, qkv_kept, down_send, down_kept, conv_send, conv_kept, qkv_send = folds(
        meta,
        [
            fold_item(view(up_kept, 2, 2), [view(up_got, 2, 2)], 1, x_bit, (0, 0, 1), (1, 0, 1)),
            fold_item(view(qkv_kept, 2, 2), [view(a_got, 2, 2), view(b_got, 2, 2)], 1, low_z, (7, 0, 1), (2, 0, 1)),
            fold_item(view(down_kept, 2, 1), [view(down_got, 2, 1)], None, y_bit, (3, 0, 1), (4, 0, 1)),
            fold_item(view(conv_kept, 2, 1), [view(conv_got, 2, 1)], 0, x_bit, (5, 0, 1), (6, 0, 1)),
        ],
        [(2, unit, up_wide)] * 2 + [(2, unit, wide)] + [(2, down_rows // 2, quarter)] * 2
        + [(1, 128, KERNEL * 8)] * 2 + [(2, unit, wide)],
        "fold_first",
        (conv_right,),
    )
    qkv_got, up_got, down_got, conv_got = swap_z1(qkv_send), swap_x(up_send), swap_y(down_send), swap_x(conv_send)
    conv_input = jnp.concatenate([once(conv_left, up_send), conv_right], axis=1)
    away = swap_core(take(conv_input, 1 - c, frames, 0))
    back = from_rows(jnp.concatenate([ordered(c, take(conv_input, c, frames, 0), away, 1), output_low], axis=1), z)
    qkv_send, qkv_kept, pair_send, pair_kept = folds(
        meta,
        [
            fold_item(qkv_kept[:, None], [qkv_got[:, None]], 0, high_z, (0, 0, 1), (1, 0, 1)),
            fold_item(up_kept[:, None], [up_got[:, None]], 0, high_z, (2, 0, 1), (3, 0, 1)),
            fold_item(down_kept[:, None], [down_got[:, None]], 0, lambda m: 1, (2, up_wide, 4), (3, up_wide, 4)),
        ],
        [(1, unit, wide)] * 2 + [(1, unit, 2 * up_wide)] * 2,
        "fold_second",
        (),
    )
    qkv_got, pair_got = swap_z2(qkv_send), swap_z2(pair_send)
    total = half_sum(once(total, pair_send), 0, x, swap_x)
    total = total + swap_y(total)
    shard = ordered(x, conv_kept, conv_got, 0)
    shard = jnp.concatenate([shard, swap_y(shard)], axis=0)
    grad_conv_weight = flip_columns(meta, shard, swap_core(shard))

    def spread(kept, got):
        shard = (kept.astype(jnp.float32) + got.astype(jnp.float32)).astype(jnp.bfloat16)
        shard = jnp.concatenate([shard, swap_y(shard)], axis=0)
        return shard, swap_core(shard)

    grad_w_qkv, grad_w_out = finish_qkv(meta, *spread(qkv_kept, qkv_got), half, (grad_conv_weight,))
    grad_w_up, grad_w_down = finish_pair(
        meta, *spread(pair_kept, pair_got), w_down.shape[0] // 8, (grad_conv_weight,)
    )
    back = [once(item, grad_w_up, grad_w_qkv)[None] for item in back]
    back = ordered(x, back[0], back[1], 0)
    grad_feats, layer_out = back[:, :, :features], back[:, :, features:]
    v = VOCAB
    loss = total[v + 14, 0] / (tokens * 32)
    gain_part = jnp.stack([total[v + 4], total[v]], axis=1)
    bias_part = jnp.stack(
        [total[v + 6], total[v + 5], total[v + 7], total[v + 8], total[v + 1], total[v + 2], total[v + 3]], axis=1
    )
    return (
        layer_out,
        loss,
        grad_feats.astype(jnp.float32),
        grad_conv_weight,
        grad_w_qkv,
        grad_w_out,
        grad_w_up,
        grad_w_down,
        total[:v].T,
        total[v + 13, :v],
        gain_part,
        bias_part,
        total[v + 9 : v + 13].reshape(-1),
    )


def split_solution(mesh):
    fine = Mesh(mesh.devices.reshape(2, 2, 4, 2), AXES)
    rows, parts = ("y", "c"), ("z", "x")
    return jax.shard_map(
        split_body,
        mesh=fine,
        in_specs=(P(rows, parts, None), P(rows, None), P(rows, parts)) + (P(),) * 10,
        out_specs=(
            P(rows, parts, None),
            P(),
            P(rows, parts, None),
            P(parts, None),
            P(parts, None),
            P(parts, None),
            P(parts, None),
            P(parts, None),
            P(parts, None),
            P(),
            P(parts, None),
            P(parts, None),
            P(parts),
        ),
        check_vma=False,
    )


def solution(mesh):
    if mesh.shape["dp"] == 4 and mesh.shape["seq"] == 8:
        return split_solution(mesh)
    return whole_solution(mesh)
```

```python
from functools import partial
import math

import jax
import jax.numpy as jnp
from jax import lax
from jax.experimental import pallas as pl
from jax.experimental.pallas import tpu as pltpu
from jax.sharding import Mesh, PartitionSpec as P

HEADS = 16
GROUPS = 16
KERNEL = 128
VOCAB = 32
TAP_BLOCKS = 33
VMEM_LIMIT = 56 * 1024 * 1024
DW_UNROLL = 11
IN_ORDER = ("arbitrary",)
COST_SHARE = 0.001


epsilon = 1e-05
masked_score = -1e30
tap_group = 8


def extended(cells, sides, width):
    for axis, dim in sides:
        count = lax.axis_size(axis)
        ends = count - 1
        head = lax.slice_in_dim(cells, 0, width, axis=dim)
        tail = lax.slice_in_dim(cells, cells.shape[dim] - width, cells.shape[dim], axis=dim)
        cells = jnp.concatenate(
            [
                lax.ppermute(tail, axis, [(i, (i + 1) % count) for i in range(ends)]),
                cells,
                lax.ppermute(head, axis, [((i + 1) % count, i) for i in range(ends)]),
            ],
            axis=dim,
        )
    return cells


def layer_norm(values, gain_row, shift_row):
    center = values - jnp.mean(values, axis=-1, keepdims=True)
    spread = jnp.mean(center * center, axis=-1, keepdims=True)
    return center * lax.rsqrt(spread + epsilon) * gain_row + shift_row


def gelu_exact(values):
    return jax.nn.gelu(values, approximate=False)


def outer_sum(left_side, right_side):
    return lax.dot_general(
        left_side, right_side, (((0,), (0,)), ((), ())), preferred_element_type=jnp.float32
    )


def back_product(grad_rows, weight):
    return lax.dot_general(
        grad_rows, weight, (((1,), (1,)), ((), ())), preferred_element_type=jnp.float32
    )


def masked_windows(source, seg_padded, seg_local, offsets, frames):
    windows = []
    for offset in offsets:
        window = lax.dynamic_slice_in_dim(source, offset, frames, 1)
        near_ids = lax.dynamic_slice_in_dim(seg_padded, offset, frames, 1)
        keep_mask = (near_ids == seg_local)[:, :, None]
        windows.append(jnp.where(keep_mask, window, jnp.zeros_like(window)))
    return jnp.stack(windows, axis=2)


def conv_forward(feats_rim, seg_padded, seg_local, conv_weight):
    row_count, frames = seg_local.shape
    features = feats_rim.shape[2]
    group_width = features // GROUPS
    tap_count = conv_weight.shape[0] // group_width
    grouped = conv_weight.reshape(tap_count, group_width, GROUPS, group_width)

    def one_block(tap_block, running):
        offsets = [tap_block * tap_group + tap_inner for tap_inner in range(tap_group)]
        stacked = masked_windows(feats_rim, seg_padded, seg_local, offsets, frames)
        stacked = stacked.reshape(row_count, frames, tap_group, GROUPS, group_width)
        weight_part = lax.dynamic_slice_in_dim(grouped, tap_block * tap_group, tap_group, 0)
        return running + jnp.einsum(
            "rtkgi,kigo->rtgo", stacked, weight_part, preferred_element_type=jnp.float32
        )

    start_sum = jnp.zeros((row_count, frames, GROUPS, group_width), jnp.float32)
    running = lax.fori_loop(0, tap_count // tap_group, one_block, start_sum)
    return running.reshape(row_count, frames, features)


def conv_weight_grad(feats_rim, seg_padded, seg_local, grad_conv_low, tap_count):
    row_count, frames = seg_local.shape
    features = feats_rim.shape[2]
    group_width = features // GROUPS
    grad_grouped = grad_conv_low.reshape(row_count, frames, GROUPS, group_width)

    def one_block(tap_block, running):
        offsets = [tap_block * tap_group + tap_inner for tap_inner in range(tap_group)]
        stacked = masked_windows(feats_rim, seg_padded, seg_local, offsets, frames)
        stacked = stacked.reshape(row_count, frames, tap_group, GROUPS, group_width)
        block_grad = jnp.einsum(
            "rtkgi,rtgo->kigo", stacked, grad_grouped, preferred_element_type=jnp.float32
        )
        return lax.dynamic_update_slice_in_dim(running, block_grad, tap_block * tap_group, 0)

    start_sum = jnp.zeros((tap_count, group_width, GROUPS, group_width), jnp.float32)
    running = lax.fori_loop(0, tap_count // tap_group, one_block, start_sum)
    return running.reshape(tap_count * group_width, features)


def conv_input_grad(grad_rim, seg_padded, seg_local, conv_weight):
    row_count, frames = seg_local.shape
    features = grad_rim.shape[2]
    group_width = features // GROUPS
    tap_count = conv_weight.shape[0] // group_width
    grouped = conv_weight.reshape(tap_count, group_width, GROUPS, group_width)

    def one_block(tap_block, running):
        offsets = [
            tap_count - (tap_block * tap_group + tap_inner) for tap_inner in range(tap_group)
        ]
        stacked = masked_windows(grad_rim, seg_padded, seg_local, offsets, frames)
        stacked = stacked.reshape(row_count, frames, tap_group, GROUPS, group_width)
        weight_part = lax.dynamic_slice_in_dim(grouped, tap_block * tap_group, tap_group, 0)
        return running + jnp.einsum(
            "rtkgo,kigo->rtgi", stacked, weight_part, preferred_element_type=jnp.float32
        )

    start_sum = jnp.zeros((row_count, frames, GROUPS, group_width), jnp.float32)
    running = lax.fori_loop(0, tap_count // tap_group, one_block, start_sum)
    return running.reshape(row_count, frames, features)


def span_size(piece_rows, frames):
    return math.gcd(piece_rows, 8 * frames)


def attend_row(row_state, query_row, key_row, value_row, seg_query, seg_key, score_scale):
    running_max, running_sum, weighted = row_state
    scores = score_scale * jnp.einsum(
        "qhe,khe->qhk", query_row, key_row, preferred_element_type=jnp.float32
    )
    allowed = (seg_query[:, None] == seg_key[None, :])[:, None, :]
    scores = jnp.where(allowed, scores, masked_score)
    new_max = jnp.maximum(running_max, jnp.max(scores, axis=-1))
    rescale = jnp.exp(running_max - new_max)
    weights = jnp.where(allowed, jnp.exp(scores - new_max[:, :, None]), 0.0)
    running_sum = running_sum * rescale + jnp.sum(weights, axis=-1)
    weighted = weighted * rescale[:, :, None] + jnp.einsum(
        "qhk,khe->qhe", weights.astype(jnp.bfloat16), value_row, preferred_element_type=jnp.float32
    )
    return (new_max, running_sum, weighted)


def query_grad_row(
    grad_query,
    query_row,
    key_row,
    value_row,
    seg_query,
    seg_key,
    lse_row,
    dots_row,
    grad_row,
    score_scale,
):
    scores = score_scale * jnp.einsum(
        "qhe,khe->qhk", query_row, key_row, preferred_element_type=jnp.float32
    )
    allowed = (seg_query[:, None] == seg_key[None, :])[:, None, :]
    probs = jnp.where(allowed, jnp.exp(scores - lse_row[:, :, None]), 0.0)
    grad_probs = jnp.einsum("qhe,khe->qhk", grad_row, value_row, preferred_element_type=jnp.float32)
    grad_scores = (probs * (grad_probs - dots_row[:, :, None])).astype(jnp.bfloat16)
    return grad_query + score_scale * jnp.einsum(
        "qhk,khe->qhe", grad_scores, key_row, preferred_element_type=jnp.float32
    )


def key_grad_row(
    grads_pair,
    key_row,
    value_row,
    query_row,
    grad_row,
    lse_row,
    dots_row,
    seg_query,
    seg_key,
    score_scale,
):
    scores = score_scale * jnp.einsum(
        "qhe,khe->qhk", query_row, key_row, preferred_element_type=jnp.float32
    )
    allowed = (seg_query[:, None] == seg_key[None, :])[:, None, :]
    probs = jnp.where(allowed, jnp.exp(scores - lse_row[:, :, None]), 0.0)
    grad_value = jnp.einsum(
        "qhk,qhe->khe", probs.astype(jnp.bfloat16), grad_row, preferred_element_type=jnp.float32
    )
    grad_probs = jnp.einsum("qhe,khe->qhk", grad_row, value_row, preferred_element_type=jnp.float32)
    grad_scores = (probs * (grad_probs - dots_row[:, :, None])).astype(jnp.bfloat16)
    grad_key = score_scale * jnp.einsum(
        "qhk,qhe->khe", grad_scores, query_row, preferred_element_type=jnp.float32
    )
    return (grad_key, grad_value)


def body(
    feats,
    segments,
    labels,
    conv_weight,
    w_qkv,
    w_out,
    w_up,
    w_down,
    head_w,
    head_b,
    gains,
    biases,
    up_bias,
):
    row_count, frames, features = feats.shape
    head_count = HEADS
    head_width = features // head_count
    score_scale = head_width ** (-0.5)
    tokens = row_count * frames
    tap_count = KERNEL
    rim_width = tap_count // 2
    own_first = lax.axis_index("seq") * frames
    seg_local = lax.dynamic_slice_in_dim(segments, own_first, frames, 1)
    seg_wide = jnp.pad(segments, ((0, 0), (rim_width, rim_width)), constant_values=-1)
    seg_padded = lax.dynamic_slice_in_dim(seg_wide, own_first, frames + 2 * rim_width, 1)
    feats_rim = extended(feats, (("seq", 1),), rim_width)
    conv_sum = conv_forward(feats_rim, seg_padded, seg_local, conv_weight) + biases[:, 0]
    activated, conv_pull = jax.vjp(gelu_exact, conv_sum)
    position = feats.astype(jnp.float32) + activated
    normed, first_pull = jax.vjp(layer_norm, position, gains[:, 0], biases[:, 1])
    normed_low = normed.astype(jnp.bfloat16).reshape(tokens, features)
    qkv_bias = jnp.concatenate([biases[:, 2], jnp.zeros((features,), jnp.float32), biases[:, 3]])
    mixed = (jnp.dot(normed_low, w_qkv, preferred_element_type=jnp.float32) + qkv_bias).astype(
        jnp.bfloat16
    )
    queries = mixed[:, :features].reshape(row_count, frames, head_count, head_width)
    keys = mixed[:, features : 2 * features].reshape(row_count, frames, features)
    values = mixed[:, 2 * features :].reshape(row_count, frames, features)
    start_state = (
        jnp.full((row_count, frames, head_count), masked_score, jnp.float32),
        jnp.zeros((row_count, frames, head_count), jnp.float32),
        jnp.zeros((row_count, frames, head_count, head_width), jnp.float32),
    )
    key_shard = lax.all_gather(keys, "seq", axis=1, tiled=True)
    value_shard = lax.all_gather(values, "seq", axis=1, tiled=True)
    piece_rows = key_shard.shape[1]
    span = span_size(piece_rows, frames)

    def forward_one_span(span_index, state):
        offset = span_index * span
        key_part = lax.dynamic_slice_in_dim(key_shard, offset, span, 1)
        value_part = lax.dynamic_slice_in_dim(value_shard, offset, span, 1)
        seg_keys = lax.dynamic_slice_in_dim(segments, offset, span, 1)
        results = []
        for row_index in range(row_count):
            action = partial(
                attend_row,
                query_row=queries[row_index],
                key_row=key_part[row_index].reshape(span, head_count, head_width),
                value_row=value_part[row_index].reshape(span, head_count, head_width),
                seg_query=seg_local[row_index],
                seg_key=seg_keys[row_index],
                score_scale=score_scale,
            )
            row_state = (state[0][row_index], state[1][row_index], state[2][row_index])
            results.append(action(row_state))
        return (
            jnp.stack([item[0] for item in results]),
            jnp.stack([item[1] for item in results]),
            jnp.stack([item[2] for item in results]),
        )

    running_max, running_sum, weighted = lax.fori_loop(
        0, piece_rows // span, forward_one_span, start_state
    )
    attended = weighted / running_sum[:, :, :, None]
    log_total = running_max + jnp.log(running_sum)
    attended_low = attended.reshape(tokens, features).astype(jnp.bfloat16)
    resid = (
        position.reshape(tokens, features)
        + jnp.dot(attended_low, w_out, preferred_element_type=jnp.float32)
        + biases[:, 4]
    )
    normed_second, second_pull = jax.vjp(layer_norm, resid, gains[:, 1], biases[:, 5])
    second_low = normed_second.astype(jnp.bfloat16)
    up_sum = jnp.dot(second_low, w_up, preferred_element_type=jnp.float32) + up_bias
    up_active, up_pull = jax.vjp(gelu_exact, up_sum)
    active_low = up_active.astype(jnp.bfloat16)
    output = resid + jnp.dot(active_low, w_down, preferred_element_type=jnp.float32) + biases[:, 6]
    output_low = output.astype(jnp.bfloat16)
    logits = jnp.dot(output_low, head_w, preferred_element_type=jnp.float32) + head_b
    row_top = jnp.max(logits, axis=-1, keepdims=True)
    shifted = jnp.exp(logits - row_top)
    exp_sums = jnp.sum(shifted, axis=-1, keepdims=True)
    onehot = labels.reshape(tokens)[:, None] == jnp.arange(VOCAB, dtype=jnp.int32)[None, :]
    picked = jnp.sum(jnp.where(onehot, logits, 0.0), axis=-1)
    local_loss = jnp.sum(row_top[:, 0] + jnp.log(exp_sums[:, 0]) - picked)
    grad_logits = (shifted / exp_sums - onehot.astype(jnp.float32)).astype(jnp.bfloat16)
    grad_head_w = outer_sum(output_low, grad_logits)
    grad_head_b = jnp.sum(grad_logits.astype(jnp.float32), axis=0)
    grad_output = back_product(grad_logits, head_w)
    grad_output_low = grad_output.astype(jnp.bfloat16)
    grad_w_down = outer_sum(active_low, grad_output_low)
    grad_down_bias = jnp.sum(grad_output_low.astype(jnp.float32), axis=0)
    grad_active = back_product(grad_output_low, w_down)
    grad_up_low = up_pull(grad_active)[0].astype(jnp.bfloat16)
    grad_w_up = outer_sum(second_low, grad_up_low)
    grad_up_bias = jnp.sum(grad_up_low.astype(jnp.float32), axis=0)
    grad_second = back_product(grad_up_low, w_up)
    grad_resid_part, grad_gain_second, grad_shift_second = second_pull(grad_second)
    grad_resid = grad_output + grad_resid_part
    grad_branch_low = grad_resid.astype(jnp.bfloat16)
    grad_w_out = outer_sum(attended_low, grad_branch_low)
    grad_out_bias = jnp.sum(grad_branch_low.astype(jnp.float32), axis=0)
    grad_attended = back_product(grad_branch_low, w_out).astype(jnp.bfloat16)
    grad_heads = grad_attended.reshape(row_count, frames, head_count, head_width)
    head_dots = jnp.sum(grad_heads.astype(jnp.float32) * attended, axis=-1)
    zero_grads = jnp.zeros((row_count, frames, head_count, head_width), jnp.float32)
    all_keys, all_values = (
        lax.all_gather(keys, "seq", axis=1, tiled=True),
        lax.all_gather(values, "seq", axis=1, tiled=True),
    )
    length = all_keys.shape[1]
    key_span = 8 * frames

    def query_block(block_index, grad_query):
        first_row = block_index * key_span
        key_block = lax.dynamic_slice_in_dim(all_keys, first_row, key_span, 1)
        value_block = lax.dynamic_slice_in_dim(all_values, first_row, key_span, 1)
        seg_keys = lax.dynamic_slice_in_dim(segments, first_row, key_span, 1)
        results = []
        for row_index in range(row_count):
            action = partial(
                query_grad_row,
                query_row=queries[row_index],
                key_row=key_block[row_index].reshape(key_span, head_count, head_width),
                value_row=value_block[row_index].reshape(key_span, head_count, head_width),
                seg_query=seg_local[row_index],
                seg_key=seg_keys[row_index],
                lse_row=log_total[row_index],
                dots_row=head_dots[row_index],
                grad_row=grad_heads[row_index],
                score_scale=score_scale,
            )
            results.append(action(grad_query[row_index]))
        return jnp.stack(results)

    grad_queries = lax.fori_loop(0, length // key_span, query_block, zero_grads)

    def key_term(piece_rows):
        span = math.gcd(piece_rows, key_span)

        def key_one_span(span_index, gathered_terms):
            offset = span_index * span
            key_block = lax.dynamic_slice_in_dim(all_keys, offset, span, 1)
            value_block = lax.dynamic_slice_in_dim(all_values, offset, span, 1)
            seg_keys = lax.dynamic_slice_in_dim(segments, offset, span, 1)
            empty_row = jnp.zeros((span, head_count, head_width), jnp.float32)
            results = []
            for row_index in range(row_count):
                action = partial(
                    key_grad_row,
                    key_row=key_block[row_index].reshape(span, head_count, head_width),
                    value_row=value_block[row_index].reshape(span, head_count, head_width),
                    query_row=queries[row_index],
                    grad_row=grad_heads[row_index],
                    lse_row=log_total[row_index],
                    dots_row=head_dots[row_index],
                    seg_query=seg_local[row_index],
                    seg_key=seg_keys[row_index],
                    score_scale=score_scale,
                )
                results.append(action((empty_row, empty_row)))
            key_part = jnp.stack([item[0] for item in results], axis=1).reshape(
                span, row_count, features
            )
            value_part = jnp.stack([item[1] for item in results], axis=1).reshape(
                span, row_count, features
            )
            both_parts = jnp.concatenate([key_part, value_part], axis=2)
            return lax.dynamic_update_slice_in_dim(gathered_terms, both_parts, offset, 0)

        empty_terms = jnp.zeros((piece_rows, row_count, 2 * features), jnp.float32)
        return lax.fori_loop(0, piece_rows // span, key_one_span, empty_terms)

    both_grads = lax.psum_scatter(
        key_term(frames * lax.axis_size("seq")), "seq", scatter_dimension=0, tiled=True
    )
    grad_keys = jnp.transpose(both_grads[:, :, :features], (1, 0, 2)).reshape(
        row_count, frames, head_count, head_width
    )
    grad_values = jnp.transpose(both_grads[:, :, features:], (1, 0, 2)).reshape(
        row_count, frames, head_count, head_width
    )
    grad_mixed = jnp.concatenate(
        [
            grad_queries.reshape(tokens, features),
            grad_keys.reshape(tokens, features),
            grad_values.reshape(tokens, features),
        ],
        axis=1,
    ).astype(jnp.bfloat16)
    grad_w_qkv = outer_sum(normed_low, grad_mixed)
    mixed_sums = jnp.sum(grad_mixed.astype(jnp.float32), axis=0)
    grad_normed = back_product(grad_mixed, w_qkv).reshape(row_count, frames, features)
    grad_position_part, grad_gain_first, grad_shift_first = first_pull(grad_normed)
    grad_position = grad_resid.reshape(row_count, frames, features) + grad_position_part
    grad_conv_low = conv_pull(grad_position)[0].astype(jnp.bfloat16)
    grad_conv_bias = jnp.sum(grad_conv_low.astype(jnp.float32), axis=(0, 1))
    grad_conv_weight = conv_weight_grad(feats_rim, seg_padded, seg_local, grad_conv_low, tap_count)
    grad_rim = extended(grad_conv_low, (("seq", 1),), rim_width)
    grad_feats = grad_position + conv_input_grad(grad_rim, seg_padded, seg_local, conv_weight)
    grad_gains = jnp.stack([grad_gain_first, grad_gain_second], axis=1)
    grad_biases = jnp.stack(
        [
            grad_conv_bias,
            grad_shift_first,
            mixed_sums[:features],
            mixed_sums[2 * features :],
            grad_out_bias,
            grad_shift_second,
            grad_down_bias,
        ],
        axis=1,
    )
    shared = (
        lax.psum_scatter(grad_conv_weight, "seq", scatter_dimension=0, tiled=True),
        lax.psum_scatter(grad_w_qkv, "seq", scatter_dimension=0, tiled=True),
        lax.psum_scatter(grad_w_out, "seq", scatter_dimension=0, tiled=True),
        lax.psum_scatter(grad_w_up, "seq", scatter_dimension=0, tiled=True),
        lax.psum_scatter(grad_w_down, "seq", scatter_dimension=0, tiled=True),
        lax.psum_scatter(grad_head_w, "seq", scatter_dimension=0, tiled=True),
        lax.psum_scatter(grad_gains, "seq", scatter_dimension=0, tiled=True),
        lax.psum_scatter(grad_biases, "seq", scatter_dimension=0, tiled=True),
        lax.psum_scatter(grad_up_bias, "seq", scatter_dimension=0, tiled=True),
    )
    summed = (
        lax.psum(shared[0].astype(jnp.bfloat16), "dp").astype(jnp.float32),
        lax.psum(shared[1].astype(jnp.bfloat16), "dp").astype(jnp.float32),
        lax.psum(shared[2].astype(jnp.bfloat16), "dp").astype(jnp.float32),
        lax.psum(shared[3].astype(jnp.bfloat16), "dp").astype(jnp.float32),
        lax.psum(shared[4].astype(jnp.bfloat16), "dp").astype(jnp.float32),
        lax.psum(shared[5].astype(jnp.bfloat16), "dp").astype(jnp.float32),
        lax.psum(shared[6].astype(jnp.bfloat16), "dp").astype(jnp.float32),
        lax.psum(shared[7].astype(jnp.bfloat16), "dp").astype(jnp.float32),
        lax.psum(shared[8].astype(jnp.bfloat16), "dp").astype(jnp.float32),
    )
    loss_total, head_bias_total = lax.psum((local_loss, grad_head_b), ("dp", "seq"))
    loss = loss_total / (tokens * lax.axis_size("dp") * lax.axis_size("seq"))
    layer_out = output_low.reshape(row_count, frames, features)
    return (
        layer_out,
        loss,
        grad_feats,
        summed[0],
        summed[1],
        summed[2],
        summed[3],
        summed[4],
        summed[5],
        head_bias_total,
        summed[6],
        summed[7],
        summed[8],
    )


def whole_solution(mesh):
    placed = (
        P("dp", "seq", None),
        P("dp", None),
        P("dp", "seq"),
        P(),
        P(),
        P(),
        P(),
        P(),
        P(),
        P(),
        P(),
        P(),
        P(),
    )
    return jax.shard_map(
        body,
        mesh=mesh,
        in_specs=placed,
        out_specs=(
            P("dp", "seq", None),
            P(),
            P("dp", "seq", None),
            P("seq", None),
            P("seq", None),
            P("seq", None),
            P("seq", None),
            P("seq", None),
            P("seq", None),
            P(),
            P("seq", None),
            P("seq", None),
            P("seq"),
        ),
        check_vma=False,
    )


def cost(flops, bytes_accessed, transcendentals):
    return pl.CostEstimate(
        flops=int(flops * COST_SHARE), bytes_accessed=int(bytes_accessed * COST_SHARE), transcendentals=int(transcendentals * COST_SHARE)
    )


def lanes_dot(a, b):
    return lax.dot_general(a, b, (((1,), (1,)), ((), ())), preferred_element_type=jnp.float32)


def rows_dot(a, b):
    return lax.dot_general(a, b, (((0,), (0,)), ((), ())), preferred_element_type=jnp.float32)


def attend_parts(side, queries, keys, values, allowed, low):
    mine = low if side == 0 else jnp.logical_not(low)
    scores = lanes_dot(jnp.where(mine, keys, jnp.zeros_like(keys)), queries)
    scores = jnp.where(allowed, scores, masked_score)
    top = jnp.max(scores, axis=0, keepdims=True)
    return scores, top


def attend_kernel(seg_q_ref, seg_k_ref, q_ref, k_ref, v_ref, mixed_ref, state_ref):
    queries = q_ref[...] * jnp.bfloat16(0.125)
    low = lax.broadcasted_iota(jnp.int32, k_ref.shape, 1) < 64
    allowed = seg_k_ref[...] == seg_q_ref[...]
    for side in range(2):
        scores, top = attend_parts(side, queries, k_ref[...], None, allowed, low)
        weights = jnp.exp(scores - top)
        state_ref[0, side : side + 1, :] = top
        state_ref[0, side + 2 : side + 3, :] = jnp.sum(weights, axis=0, keepdims=True)
        mixed = rows_dot(v_ref[...], weights.astype(jnp.bfloat16))
        mixed_ref[side * 64 : (side + 1) * 64, :] = mixed[side * 64 : (side + 1) * 64, :]


def attend_far_kernel(seg_q_ref, seg_k_ref, q_ref, k_ref, v_ref, mixed_ref, state_ref, out_ref, low_ref, away_ref, lse_ref):
    queries = q_ref[...] * jnp.bfloat16(0.125)
    low = lax.broadcasted_iota(jnp.int32, k_ref.shape, 1) < 64
    allowed = seg_k_ref[...] == seg_q_ref[...]
    pieces = []
    for side in range(2):
        scores, top = attend_parts(side, queries, k_ref[...], None, allowed, low)
        near_top = state_ref[0, side : side + 1, :]
        top = jnp.maximum(top, near_top)
        weights = jnp.exp(scores - top)
        rescale = jnp.exp(near_top - top)
        total = state_ref[0, side + 2 : side + 3, :] * rescale + jnp.sum(weights, axis=0, keepdims=True)
        mixed = rows_dot(v_ref[...], weights.astype(jnp.bfloat16))[side * 64 : (side + 1) * 64, :]
        pieces.append((mixed + mixed_ref[side * 64 : (side + 1) * 64, :] * rescale) / total)
        lse_ref[0, side : side + 1, :] = top + jnp.log(total)
    attended = jnp.concatenate(pieces, axis=0).T
    own = low_ref.shape[0]
    out_ref[...] = attended
    low_ref[...] = attended[:own, :].astype(jnp.bfloat16)
    away_ref[...] = attended[own:, :].astype(jnp.bfloat16)


def attend_specs(frames, length, pairs):
    return [
        pl.BlockSpec((1, frames), lambda p: (0, 0)),
        pl.BlockSpec((length, 1), lambda p: (0, 0)),
        pl.BlockSpec((frames, 128), lambda p: (0, p)),
        pl.BlockSpec((length, 128), lambda p: (0, p)),
        pl.BlockSpec((length, 128), lambda p: (0, pairs + p)),
    ]


def attend_cost(frames, length, pairs, products):
    return cost(
        flops=4 * products * pairs * frames * length * 128,
        bytes_accessed=16 * frames * pairs * 128,
        transcendentals=2 * pairs * frames * length,
    )


def attend_near(queries, pair, seg_q, seg_k):
    frames, width = queries.shape
    length = pair.shape[0]
    pairs = width // 128
    return pl.pallas_call(
        attend_kernel,
        grid=(pairs,),
        in_specs=attend_specs(frames, length, pairs),
        out_specs=[
            pl.BlockSpec((128, frames), lambda p: (p, 0)),
            pl.BlockSpec((1, 8, frames), lambda p: (p, 0, 0)),
        ],
        out_shape=[
            jax.ShapeDtypeStruct((width, frames), jnp.float32),
            jax.ShapeDtypeStruct((pairs, 8, frames), jnp.float32),
        ],
        compiler_params=pltpu.CompilerParams(vmem_limit_bytes=VMEM_LIMIT),
        cost_estimate=attend_cost(frames, length, pairs, 2),
        name="attend_near",
    )(seg_q.reshape(1, -1), seg_k.reshape(-1, 1), queries, pair, pair)


def attend_far(queries, pair, seg_q, seg_k, mixed, state):
    frames, width = queries.shape
    length = pair.shape[0]
    pairs = width // 128
    return pl.pallas_call(
        attend_far_kernel,
        grid=(pairs,),
        in_specs=attend_specs(frames, length, pairs)
        + [
            pl.BlockSpec((128, frames), lambda p: (p, 0)),
            pl.BlockSpec((1, 8, frames), lambda p: (p, 0, 0)),
        ],
        out_specs=[
            pl.BlockSpec((frames, 128), lambda p: (0, p)),
            pl.BlockSpec((frames // 2, 128), lambda p: (0, p)),
            pl.BlockSpec((frames // 2, 128), lambda p: (0, p)),
            pl.BlockSpec((1, 8, frames), lambda p: (p, 0, 0)),
        ],
        out_shape=[
            jax.ShapeDtypeStruct((frames, width), jnp.float32),
            jax.ShapeDtypeStruct((frames // 2, width), jnp.bfloat16),
            jax.ShapeDtypeStruct((frames // 2, width), jnp.bfloat16),
            jax.ShapeDtypeStruct((pairs, 8, frames), jnp.float32),
        ],
        compiler_params=pltpu.CompilerParams(vmem_limit_bytes=VMEM_LIMIT),
        cost_estimate=attend_cost(frames, length, pairs, 2),
        name="attend_far",
    )(seg_q.reshape(1, -1), seg_k.reshape(-1, 1), queries, pair, pair, mixed, state)


def attend_back_kernel(seg_q_ref, seg_k_ref, q_ref, k_ref, v_ref, g_ref, a_ref, lse_ref, after_ref, dq_ref, dkv_ref):
    queries = q_ref[...] * jnp.bfloat16(0.125)
    key_count = k_ref.shape[0]
    low = lax.broadcasted_iota(jnp.int32, (key_count, 128), 1) < 64
    keys, values, grads = k_ref[...], v_ref[...], g_ref[...]
    allowed = seg_k_ref[...] == seg_q_ref[...]
    products = (grads.astype(jnp.float32) * a_ref[...]).T
    dq, dk, dv = [], [], []
    for side in range(2):
        mine = low if side == 0 else jnp.logical_not(low)
        zero = jnp.zeros_like(keys)
        scores = lanes_dot(jnp.where(mine, keys, zero), queries)
        probs = jnp.where(allowed, jnp.exp(scores - lse_ref[0, side : side + 1, :]), 0.0)
        dots = jnp.sum(products[side * 64 : (side + 1) * 64, :], axis=0, keepdims=True)
        dv.append(jnp.dot(probs.astype(jnp.bfloat16), grads, preferred_element_type=jnp.float32))
        grad_probs = lanes_dot(jnp.where(mine, values, zero), grads)
        grad_scores = (probs * (grad_probs - dots)).astype(jnp.bfloat16)
        dk.append(jnp.dot(grad_scores, queries, preferred_element_type=jnp.float32))
        dq.append(rows_dot(keys, grad_scores)[side * 64 : (side + 1) * 64, :])
    dq_ref[...] = 0.125 * jnp.concatenate(dq, axis=0).T
    dkv_ref[0] = jnp.where(low, dk[0], dk[1]).astype(dkv_ref.dtype)
    dkv_ref[1] = jnp.where(low, dv[0], dv[1]).astype(dkv_ref.dtype)


def attend_back(queries, pair, grads, attended, lse, seg_q, seg_k, kind, after):
    frames, width = queries.shape
    length = pair.shape[0]
    pairs = width // 128
    return pl.pallas_call(
        attend_back_kernel,
        grid=(pairs,),
        in_specs=attend_specs(frames, length, pairs)
        + [
            pl.BlockSpec((frames, 128), lambda p: (0, p)),
            pl.BlockSpec((frames, 128), lambda p: (0, p)),
            pl.BlockSpec((1, 8, frames), lambda p: (p, 0, 0)),
            pl.BlockSpec(memory_space=pl.ANY),
        ],
        out_specs=[
            pl.BlockSpec((frames, 128), lambda p: (0, p)),
            pl.BlockSpec((2, length, 128), lambda p: (0, 0, p)),
        ],
        out_shape=[
            jax.ShapeDtypeStruct((frames, width), jnp.float32),
            jax.ShapeDtypeStruct((2, length, width), kind),
        ],
        compiler_params=pltpu.CompilerParams(vmem_limit_bytes=VMEM_LIMIT),
        cost_estimate=attend_cost(frames, length, pairs, 5),
        name="attend_back",
    )(seg_q.reshape(1, -1), seg_k.reshape(-1, 1), queries, pair, pair, grads, attended, lse, after)


def phi_parts(values):
    below = 0.5 * (1.0 + lax.erf(values * (0.5**0.5)))
    density = jnp.exp(-0.5 * values * values) * (1.0 / math.sqrt(2.0 * math.pi))
    return below, density


def norm_parts(values):
    center = values - jnp.mean(values, axis=-1, keepdims=True)
    scale = lax.rsqrt(jnp.mean(center * center, axis=-1, keepdims=True) + epsilon)
    return center * scale, scale


def norm_back(grad, hat, scale, gain):
    inner = grad * gain
    mean_inner = jnp.mean(inner, axis=-1, keepdims=True)
    mean_hat = jnp.mean(inner * hat, axis=-1, keepdims=True)
    return (inner - mean_inner - hat * mean_hat) * scale


def column_sum(values):
    return jnp.sum(values, axis=0, keepdims=True)


def by_core(core, mine, other):
    return jnp.where(core == 0, mine, other), jnp.where(core == 0, other, mine)


def mix_kernel(first, meta, *refs):
    if first:
        mine_ref, other_ref, gain_ref, shift_ref, w_ref, bias_ref = refs[:6]
        theirs_ref, ours_ref, normed_ref, position_ref = refs[-4:]
    else:
        normed_ref, w_ref, bias_ref = refs[:3]
        theirs_ref, ours_ref = refs[-2:]
    step = pl.program_id(0)
    half = w_ref.shape[1]
    if first:

        @pl.when(step == 0)
        def _():
            left, right = by_core(meta[0], mine_ref[...], other_ref[...])
            position_ref[:, :half] = left
            position_ref[:, half:] = right
            hat, _ = norm_parts(position_ref[...])
            normed_ref[...] = (hat * gain_ref[...] + shift_ref[...]).astype(jnp.bfloat16)

    block = jnp.dot(normed_ref[...], w_ref[...], preferred_element_type=jnp.float32) + bias_ref[...]
    block = block.astype(jnp.bfloat16)
    parts = theirs_ref.shape[1] // half

    @pl.when(step < parts)
    def _():
        theirs_ref[:, pl.ds(pl.multiple_of(step * half, half), half)] = block

    @pl.when(step >= parts)
    def _():
        ours_ref[:, pl.ds(pl.multiple_of((step - parts) * half, half), half)] = block


def mix_rows(core, sources, weight, bias, begin, parts, after=()):
    first = len(sources) > 1
    tokens = sources[0].shape[0]
    features = weight.shape[0]
    half = features // 2

    def column(i, meta):
        return 2 * (begin + i % parts) + jnp.where(i < parts, 1 - meta[0], meta[0])

    whole = lambda shape: pl.BlockSpec(shape, lambda i, meta: (0, 0))
    out_specs = [whole((tokens, parts * half))] * 2
    out_shape = [jax.ShapeDtypeStruct((tokens, parts * half), jnp.bfloat16)] * 2
    if first:
        out_specs = out_specs + [whole((tokens, features))] * 2
        out_shape = out_shape + [jax.ShapeDtypeStruct((tokens, features), kind) for kind in (jnp.bfloat16, jnp.float32)]
    return pl.pallas_call(
        partial(mix_kernel, first),
        grid_spec=pltpu.PrefetchScalarGridSpec(
            num_scalar_prefetch=1,
            grid=(2 * parts,),
            in_specs=[whole(item.shape) for item in sources]
            + [
                pl.BlockSpec((features, half), lambda i, meta: (0, column(i, meta))),
                pl.BlockSpec((1, half), lambda i, meta: (0, column(i, meta))),
            ]
            + [pl.BlockSpec(memory_space=pl.ANY)] * len(after),
            out_specs=out_specs,
        ),
        out_shape=out_shape,
        compiler_params=pltpu.CompilerParams(vmem_limit_bytes=VMEM_LIMIT, dimension_semantics=IN_ORDER),
        cost_estimate=cost(
            flops=4 * parts * tokens * half * features, bytes_accessed=4 * parts * half * features, transcendentals=0
        ),
        name="norm_keys_values" if first else "queries",
    )(core, *sources, weight, bias, *after)


def unmix_kernel(
    meta, mine_ref, other_ref, w_ref, position_ref, resid_ref, gain_ref, *refs
):
    ours_ref, theirs_ref, sums_ref, total = refs[-4:]
    step = pl.program_id(0)
    half = theirs_ref.shape[1]

    @pl.when(step == 0)
    def _():
        total[...] = jnp.zeros_like(total)

    block = jnp.where(step < 3, mine_ref[...], other_ref[...])
    total[...] += lanes_dot(block, w_ref[...])

    @pl.when(step == 5)
    def _():
        grad = total[...]
        hat, scale = norm_parts(position_ref[...])
        sums_ref[0:1, :] = column_sum(grad * hat)
        sums_ref[1:2, :] = column_sum(grad)
        sums_ref[2:8, :] = jnp.zeros((6, 2 * half), jnp.float32)
        result = resid_ref[...] + norm_back(grad, hat, scale, gain_ref[...])
        low_half, high_half = result[:, :half], result[:, half:]
        ours_ref[...] = jnp.where(meta[0] == 0, low_half, high_half)
        theirs_ref[...] = jnp.where(meta[0] == 0, high_half, low_half)


def unmix_rows(core, mine, other, weight, position, grad_resid, gain, after):
    tokens, features = position.shape
    half = features // 2

    def column(i, meta):
        return 2 * (i % 3) + jnp.where(i < 3, meta[0], 1 - meta[0])

    whole = lambda shape: pl.BlockSpec(shape, lambda i, meta: (0, 0))
    return pl.pallas_call(
        unmix_kernel,
        grid_spec=pltpu.PrefetchScalarGridSpec(
            num_scalar_prefetch=1,
            grid=(6,),
            in_specs=[
                pl.BlockSpec((tokens, half), lambda i, meta: (0, i % 3)),
                pl.BlockSpec((tokens, half), lambda i, meta: (0, i % 3)),
                pl.BlockSpec((features, half), lambda i, meta: (0, column(i, meta))),
                whole((tokens, features)),
                whole((tokens, features)),
                whole((1, features)),
            ]
            + [pl.BlockSpec(memory_space=pl.ANY)] * len(after),
            out_specs=[whole((tokens, half)), whole((tokens, half)), whole((8, features))],
            scratch_shapes=[pltpu.VMEM((tokens, features), jnp.float32)],
        ),
        out_shape=[
            jax.ShapeDtypeStruct((tokens, half), jnp.float32),
            jax.ShapeDtypeStruct((tokens, half), jnp.float32),
            jax.ShapeDtypeStruct((8, features), jnp.float32),
        ],
        compiler_params=pltpu.CompilerParams(vmem_limit_bytes=VMEM_LIMIT, dimension_semantics=IN_ORDER),
        cost_estimate=cost(flops=12 * tokens * half * features, bytes_accessed=14 * half * features, transcendentals=0),
        name="qkv_and_norm_back",
    )(core, mine, other, weight, position, grad_resid, gain, *after)


def pack_places(features, width):
    places, at = {}, 0
    for name, size in (
        ("active", width), ("second", features), ("attended", features), ("up", width // 2),
        ("out", features // 2), ("branch", features // 2),
    ):
        places[name] = at
        at += size
    places["all"] = at
    return places


def middle_kernel(
    meta, mine_ref, other_ref, position_ref, w_out_ref, w_up_ref, w_down_ref, up_bias_ref, head_w_ref, head_b_ref,
    labels_ref, rows_ref,
    pack_ref, output_ref, out_low_ours, up_ours, branch_ours, att_ours, att_theirs, resid_grad_ref, sums_ref,
    up_sums_ref, head_ref, last_ref,
    resid, total, slope, grad_out, grad_low,
):
    step = pl.program_id(0)
    chunks = slope.shape[0]
    core = meta[0]
    half = mine_ref.shape[1]
    features = 2 * half
    chunk_width = slope.shape[2]
    places = pack_places(features, chunks * chunk_width)

    def at(name, size):
        return slice(places[name], places[name] + size)

    second_at, attended_at = at("second", features), at("attended", features)

    def store_halves(ours, theirs, values):
        low_half, high_half = values[:, :half], values[:, half:]
        ours[...] = jnp.where(core == 0, low_half, high_half)
        theirs[...] = jnp.where(core == 0, high_half, low_half)

    @pl.when(step == 0)
    def _():
        left, right = by_core(core, mine_ref[...].astype(jnp.float32), other_ref[...].astype(jnp.float32))
        pack_ref[:, places["attended"] : places["attended"] + half] = left.astype(jnp.bfloat16)
        pack_ref[:, places["attended"] + half : places["attended"] + features] = right.astype(jnp.bfloat16)
        resid[...] = (
            position_ref[...]
            + jnp.dot(pack_ref[:, attended_at], w_out_ref[...], preferred_element_type=jnp.float32)
            + rows_ref[2:3, :]
        )
        hat, _ = norm_parts(resid[...])
        pack_ref[:, second_at] = (hat * rows_ref[0:1, :] + rows_ref[1:2, :]).astype(jnp.bfloat16)
        total[...] = jnp.zeros_like(total)

    @pl.when(step < chunks)
    def _():
        raised = jnp.dot(pack_ref[:, second_at], w_up_ref[...], preferred_element_type=jnp.float32) + up_bias_ref[...]
        below, density = phi_parts(raised)
        slope[step] = below + raised * density
        active = (raised * below).astype(jnp.bfloat16)
        pack_ref[:, pl.ds(pl.multiple_of(places["active"] + step * chunk_width, chunk_width), chunk_width)] = active
        total[...] += jnp.dot(active, w_down_ref[...], preferred_element_type=jnp.float32)

    @pl.when(step == chunks - 1)
    def _():
        low = (resid[...] + total[...] + rows_ref[3:4, :]).astype(jnp.bfloat16)
        output_ref[...] = low
        logits = jnp.dot(low, head_w_ref[...], preferred_element_type=jnp.float32) + head_b_ref[...]
        top = jnp.max(logits, axis=-1, keepdims=True)
        shifted = jnp.exp(logits - top)
        sums = jnp.sum(shifted, axis=-1, keepdims=True)
        onehot = labels_ref[...] == lax.broadcasted_iota(jnp.int32, logits.shape, 1)
        picked = jnp.sum(jnp.where(onehot, logits, 0.0), axis=-1, keepdims=True)
        loss = jnp.sum(top + jnp.log(sums) - picked)
        grad_logits = (shifted / sums - onehot.astype(jnp.float32)).astype(jnp.bfloat16)
        head_ref[...] = rows_dot(grad_logits, low)
        last_ref[...] = jnp.zeros_like(last_ref)
        last_ref[0:1, 0:VOCAB] = column_sum(grad_logits.astype(jnp.float32))
        last_ref[1:2, :] = jnp.full((1, 128), loss, jnp.float32)
        grad = lanes_dot(grad_logits, head_w_ref[...])
        grad_out[...] = grad
        grad_low[...] = grad.astype(jnp.bfloat16)
        store_halves(out_low_ours, pack_ref.at[:, at("out", half)], grad_low[...])
        sums_ref[3:4, :] = column_sum(grad_low[...].astype(jnp.float32))
        sums_ref[4:8, :] = jnp.zeros((4, 2 * half), jnp.float32)
        total[...] = jnp.zeros_like(total)

    @pl.when(step >= chunks)
    def _():
        chunk = 2 * chunks - 1 - step
        grad = lanes_dot(grad_low[...], w_down_ref[...]) * slope[chunk]
        low = grad.astype(jnp.bfloat16)
        up_sums_ref[0] = jnp.broadcast_to(column_sum(low.astype(jnp.float32)), up_sums_ref.shape[1:])
        total[...] += lanes_dot(low, w_up_ref[...])
        ours = (chunk >= chunks // 2) == (core == 1)

        @pl.when(ours)
        def _():
            up_ours[...] = low

        @pl.when(jnp.logical_not(ours))
        def _():
            place = places["up"] + (chunk & (chunks // 2 - 1)) * chunk_width
            pack_ref[:, pl.ds(pl.multiple_of(place, chunk_width), chunk_width)] = low

    @pl.when(step == 2 * chunks - 1)
    def _():
        hat, scale = norm_parts(resid[...])
        grad = total[...]
        sums_ref[0:1, :] = column_sum(grad * hat)
        sums_ref[2:3, :] = column_sum(grad)
        result = grad_out[...] + norm_back(grad, hat, scale, rows_ref[0:1, :])
        resid_grad_ref[...] = result
        branch = result.astype(jnp.bfloat16)
        store_halves(branch_ours, pack_ref.at[:, at("branch", half)], branch)
        sums_ref[1:2, :] = column_sum(branch.astype(jnp.float32))
        store_halves(att_ours, att_theirs, lanes_dot(branch, w_out_ref[...]).astype(jnp.bfloat16))


def middle(core, mine, other, position, w_out, w_up, w_down, up_bias, head_w, head_b, labels, rows):
    tokens, features = position.shape
    half = features // 2
    width = w_up.shape[1]
    chunks = 8
    chunk = width // chunks
    vocab = head_w.shape[1]
    last = 2 * chunks - 1

    def part(i):
        return jnp.where(i < chunks, i, last - i)

    def own_up(i, meta):
        back = part(jnp.maximum(i, chunks))
        return jnp.where(meta[0] == 0, jnp.minimum(back, chunks // 2 - 1), jnp.maximum(back - chunks // 2, 0))

    whole = lambda shape: pl.BlockSpec(shape, lambda i, meta: tuple(0 for _ in shape))
    low = lambda *shape: jax.ShapeDtypeStruct(shape, jnp.bfloat16)
    full = lambda *shape: jax.ShapeDtypeStruct(shape, jnp.float32)
    return pl.pallas_call(
        middle_kernel,
        grid_spec=pltpu.PrefetchScalarGridSpec(
            num_scalar_prefetch=1,
            grid=(2 * chunks,),
            in_specs=[
                whole((tokens, half)),
                whole((tokens, half)),
                whole((tokens, features)),
                whole((features, features)),
                pl.BlockSpec((features, chunk), lambda i, meta: (0, part(i))),
                pl.BlockSpec((chunk, features), lambda i, meta: (part(i), 0)),
                pl.BlockSpec((1, chunk), lambda i, meta: (0, part(i))),
                whole((features, vocab)),
                whole((1, vocab)),
                whole((tokens, 1)),
                whole((8, features)),
            ],
            out_specs=[
                whole((tokens, pack_places(features, width)["all"])),
                whole((tokens, features)),
                whole((tokens, half)),
                pl.BlockSpec((tokens, chunk), lambda i, meta: (0, own_up(i, meta))),
                whole((tokens, half)),
                whole((tokens, half)),
                whole((tokens, half)),
                whole((tokens, features)),
                whole((8, features)),
                pl.BlockSpec((1, 8, chunk), lambda i, meta: (part(jnp.maximum(i, chunks)), 0, 0)),
                whole((vocab, features)),
                whole((8, 128)),
            ],
            scratch_shapes=[
                pltpu.VMEM((tokens, features), jnp.float32),
                pltpu.VMEM((tokens, features), jnp.float32),
                pltpu.VMEM((chunks, tokens, chunk), jnp.float32),
                pltpu.VMEM((tokens, features), jnp.float32),
                pltpu.VMEM((tokens, features), jnp.bfloat16),
            ],
        ),
        out_shape=[
            low(tokens, pack_places(features, width)["all"]),
            low(tokens, features),
            low(tokens, half),
            low(tokens, width // 2),
            low(tokens, half),
            low(tokens, half),
            low(tokens, half),
            full(tokens, features),
            full(8, features),
            full(chunks, 8, chunk),
            full(vocab, features),
            full(8, 128),
        ],
        compiler_params=pltpu.CompilerParams(vmem_limit_bytes=VMEM_LIMIT, dimension_semantics=IN_ORDER),
        cost_estimate=cost(
            flops=8 * tokens * features * width, bytes_accessed=8 * features * width, transcendentals=2 * tokens * width
        ),
        name="middle",
    )(core, mine, other, position, w_out, w_up, w_down, up_bias, head_w, head_b, labels, rows)


def conv_grad_kernel(meta, ours_ref, got_ref, slope_ref, *refs):
    position_ref, grad_ref, edge_ref, own_ref, to_x_ref, to_y_ref, to_xy_ref, sums_ref = refs[-8:]
    core, y, x = meta[0], meta[1], meta[2]
    frames = ours_ref.shape[0]
    rim = edge_ref.shape[0]
    ours, got = ours_ref[...], got_ref[...]
    position_ref[0:frames, :] = jnp.where(core == 0, ours, got)
    position_ref[frames:, :] = jnp.where(core == 0, got, ours)
    grad_ref[...] = (position_ref[...] * slope_ref[...]).astype(jnp.bfloat16)
    side = x ^ (meta[3] & 1)
    edge_ref[...] = jnp.where(side == 0, grad_ref[2 * frames - rim :, :], grad_ref[0:rim, :])
    sums_ref[...] = jnp.broadcast_to(column_sum(grad_ref[...].astype(jnp.float32)), sums_ref.shape)
    for ref, yy, xx in ((own_ref, y, x), (to_x_ref, y, 1 - x), (to_y_ref, 1 - y, x), (to_xy_ref, 1 - y, 1 - x)):
        ref[...] = grad_ref[:, pl.ds(pl.multiple_of(256 * xx + 128 * yy, 128), 128)]


def conv_grad_rows(meta, ours, got, slope, after):
    frames, half = ours.shape
    operands = (ours, got, slope)
    shapes = [((2 * frames, half), jnp.float32), ((2 * frames, half), jnp.bfloat16), ((KERNEL // 2, half), jnp.bfloat16)]
    shapes += [((2 * frames, 128), jnp.bfloat16)] * 4 + [((8, half), jnp.float32)]
    return pl.pallas_call(
        conv_grad_kernel,
        grid_spec=pltpu.PrefetchScalarGridSpec(
            num_scalar_prefetch=1,
            grid=(1,),
            in_specs=[pl.BlockSpec(item.shape, lambda i, m: (0, 0)) for item in operands]
            + [pl.BlockSpec(memory_space=pl.ANY)] * len(after),
            out_specs=[pl.BlockSpec(shape, lambda i, m: (0, 0)) for shape, _ in shapes],
        ),
        out_shape=[jax.ShapeDtypeStruct(shape, kind) for shape, kind in shapes],
        compiler_params=pltpu.CompilerParams(vmem_limit_bytes=VMEM_LIMIT, dimension_semantics=IN_ORDER),
        cost_estimate=cost(flops=0, bytes_accessed=4000000, transcendentals=0),
        name="conv_grad_rows",
    )(meta, *operands, *after)


def weight_kernel(tasks, out_count, meta, *refs):
    refs = list(refs)
    step = pl.program_id(0)
    inputs = []
    for task in tasks:
        count = 1 if task["right"] is None else 4
        inputs.append([refs.pop(0) for _ in range(count + (task["add"] is not None))])
    outs = refs[-out_count:]
    begin = 0
    for task, ins in zip(tasks, inputs):
        rows, columns = task["rows"], task["columns"]

        def store(where, values, at, task=task):
            index, column = where
            size = values.shape[0]
            span = pl.ds(pl.multiple_of(at * size, size), size)
            outs[index][span, column : column + values.shape[1]] = values.astype(jnp.bfloat16)

        @pl.when(jnp.logical_and(step >= begin, step < begin + task["blocks"]))
        def _(task=task, ins=ins, begin=begin, store=store, rows=rows, columns=columns):
            if task["right"] is None:
                total = ins[0][...].astype(jnp.float32)
            else:
                total = rows_dot(ins[0][...], ins[2][...]) + rows_dot(ins[1][...], ins[3][...])
            if task["add"] is not None:
                total = total + ins[-1][...].astype(jnp.float32)
            at = step - begin + task["place"]
            if task["split"] is None:
                for where in task["outs"]:
                    store(where, total, at)
                return
            if task["split"] == "columns":
                first, second = total[:, : columns // 2], total[:, columns // 2 :]
            else:
                blocks = total.reshape(-1, 2, task["unit"], columns)
                first, second = (blocks[:, k].reshape(rows // 2, columns) for k in range(2))
            bit = task["bit"](meta)
            store(task["outs"][0], jnp.where(bit == 0, second, first), at)
            store(task["outs"][1], jnp.where(bit == 0, first, second), at)

        begin = begin + task["blocks"]


def weight_task(
    outs, left, right, rows, blocks, row_of, columns, column_of, add=None, add_of=None, split=None, bit=None, unit=0, place=0
):
    return dict(
        outs=outs, left=left, right=right, rows=rows, blocks=blocks, row_of=row_of, columns=columns,
        column_of=column_of, add=add, add_of=add_of, split=split, bit=bit, unit=unit, place=place,
    )


def weight_parts(meta, tasks, shapes, name, after):
    in_specs, operands = [], []
    begin, flops, moved = 0, 0, 0
    for task in tasks:
        rows, columns, blocks = task["rows"], task["columns"], task["blocks"]
        tokens = task["left"][0][0].shape[0]
        if task["right"] is None:
            in_specs.append(
                pl.BlockSpec((rows, columns), lambda i, m, t=task, begin=begin, blocks=blocks: (t["row_of"](jnp.clip(i - begin, 0, blocks - 1), m), 0))
            )
            operands.append(task["left"][0][0])

        def local(i, begin=begin, blocks=blocks):
            return jnp.clip(i - begin, 0, blocks - 1)

        for array, base in task["left"] if task["right"] is not None else ():
            in_specs.append(
                pl.BlockSpec(
                    (tokens, rows), lambda i, m, t=task, local=local, base=base: (0, base // t["rows"] + t["row_of"](local(i), m))
                )
            )
            operands.append(array)
        for array, base in task["right"] or ():
            in_specs.append(
                pl.BlockSpec((tokens, columns), lambda i, m, t=task, base=base: (0, base // t["columns"] + t["column_of"](m)))
            )
            operands.append(array)
        if task["add"] is not None:
            in_specs.append(pl.BlockSpec((rows, columns), lambda i, m, t=task, local=local: t["add_of"](local(i), m)))
            operands.append(task["add"])
        begin += blocks
        flops += 4 * tokens * rows * blocks * columns
        moved += 2 * rows * blocks * columns + 4 * tokens * (rows * blocks + columns)
    in_specs += [pl.BlockSpec(memory_space=pl.ANY)] * len(after)
    operands += list(after)
    return pl.pallas_call(
        partial(weight_kernel, tasks, len(shapes)),
        grid_spec=pltpu.PrefetchScalarGridSpec(
            num_scalar_prefetch=1,
            grid=(begin,),
            in_specs=in_specs,
            out_specs=[pl.BlockSpec(shape, lambda i, m: (0, 0)) for shape in shapes],
        ),
        out_shape=[jax.ShapeDtypeStruct(shape, jnp.bfloat16) for shape in shapes],
        compiler_params=pltpu.CompilerParams(vmem_limit_bytes=VMEM_LIMIT, dimension_semantics=IN_ORDER),
        cost_estimate=cost(flops=flops, bytes_accessed=moved, transcendentals=0),
        name=name,
    )(meta, *operands)


def flip_kernel(meta, own_ref, got_ref, out_ref):
    source = jnp.where(pl.program_id(0) < 4, own_ref[0], got_ref[0])
    out_ref[...] = source.astype(jnp.float32).T


def flip_columns(meta, own, got):
    _, width, rows = own.shape
    count = 8

    def column(i, m):
        return 4 * (m[0] ^ (i >> 2)) + 2 * (i & 1) + (m[1] ^ ((i >> 1) & 1))

    return pl.pallas_call(
        flip_kernel,
        grid_spec=pltpu.PrefetchScalarGridSpec(
            num_scalar_prefetch=1,
            grid=(count,),
            in_specs=[
                pl.BlockSpec((1, width, rows), lambda i, m: (jnp.minimum(i, 3), 0, 0)),
                pl.BlockSpec((1, width, rows), lambda i, m: (jnp.maximum(i - 4, 0), 0, 0)),
            ],
            out_specs=pl.BlockSpec((rows, width), lambda i, m: (0, column(i, m))),
        ),
        out_shape=jax.ShapeDtypeStruct((rows, count * width), jnp.float32),
        compiler_params=pltpu.CompilerParams(vmem_limit_bytes=VMEM_LIMIT, dimension_semantics=IN_ORDER),
        cost_estimate=cost(flops=0, bytes_accessed=6 * count * width * rows, transcendentals=0),
        name="flip_columns",
    )(meta, own, got)


def small_kernel(meta, head_ref, mid_ref, first_ref, conv_ref, ours_ref, got_ref, up_ref, last_ref, *refs):
    out_ref = refs[-1]
    core = meta[0]
    half = conv_ref.shape[1]
    zero = jnp.zeros((1, half), jnp.float32)
    wide = lambda *parts: jnp.concatenate(parts, axis=1)

    def halves(part):
        ours = ours_ref[0:1, part * half : (part + 1) * half]
        got = got_ref[0:1, part * half : (part + 1) * half]
        return wide(jnp.where(core == 0, ours, got), jnp.where(core == 0, got, ours))

    conv = conv_ref[0:1, :]
    unit = last_ref.shape[1]
    rows = [
        head_ref[...],
        mid_ref[0:4, :],
        first_ref[0:2, :],
        wide(jnp.where(core == 0, conv, zero), jnp.where(core == 0, zero, conv)),
        halves(0),
        halves(2),
    ]
    rows += [wide(*(up_ref[j, 0:1, r * unit : (r + 1) * unit] for j in range(8))) for r in range(4)]
    rows += [wide(*([last_ref[...]] * 8)), jnp.zeros((128 - VOCAB - 14, 2 * half), jnp.float32)]
    out_ref[...] = jnp.concatenate(rows, axis=0).T.astype(out_ref.dtype)


def small_sums(meta, head, mid, first, conv, ours, got, up, last):
    operands = (head, mid, first, conv, ours, got, up, last)
    features = head.shape[1]
    return pl.pallas_call(
        small_kernel,
        grid_spec=pltpu.PrefetchScalarGridSpec(
            num_scalar_prefetch=1,
            grid=(1,),
            in_specs=[pl.BlockSpec(item.shape, lambda i, m, n=item.ndim: (0,) * n) for item in operands],
            out_specs=pl.BlockSpec((features, 128), lambda i, m: (0, 0)),
        ),
        out_shape=jax.ShapeDtypeStruct((features, 128), jnp.bfloat16),
        compiler_params=pltpu.CompilerParams(vmem_limit_bytes=VMEM_LIMIT, dimension_semantics=IN_ORDER),
        cost_estimate=cost(flops=0, bytes_accessed=400000, transcendentals=0),
        name="small_sums",
    )(meta, *operands)


def tile_lists(seg_ext, rise):
    row_count = seg_ext.shape[0]
    frames = seg_ext.shape[1] - KERNEL
    tiles = frames // 64
    center = seg_ext[:, KERNEL // 2 : KERNEL // 2 + frames].reshape(row_count, tiles, 64)
    first = center[:, :, 0].reshape(-1)
    counts = (center[:, :, 63].reshape(-1) - first + 1).astype(jnp.int32)
    ends = jnp.cumsum(counts)
    slots = row_count * (tiles + rise)
    slot = jnp.arange(slots, dtype=jnp.int32)
    tile = jnp.sum((slot[:, None] >= ends[None, :]).astype(jnp.int32), axis=1)
    used = tile < row_count * tiles
    tile = jnp.minimum(tile, row_count * tiles - 1)
    onehot = tile[:, None] == jnp.arange(row_count * tiles, dtype=jnp.int32)[None, :]
    begin = jnp.sum(jnp.where(onehot, (ends - counts)[None, :], 0), axis=1)
    number = jnp.sum(jnp.where(onehot, first[None, :], 0), axis=1) + slot - begin
    number = jnp.where(used, number, -2)
    in_block = tile + (tile // tiles) * (KERNEL // 64)
    return in_block.astype(jnp.int32), tile.astype(jnp.int32), number.astype(jnp.int32)


def lane_low(rows):
    return lax.broadcasted_iota(jnp.int32, (rows, 128), 1) < 64


def half_roll(block):
    return pltpu.roll(block, 64, 1)


def quad_rows(src, rows, side):
    low = lane_low(rows)
    parts = [src[pl.ds(j, rows, stride=4), :] for j in range(4)]
    halves = []
    for a, b in ((0, 1), (2, 3)):
        if side == 0:
            halves.append(jnp.where(low, parts[a], half_roll(parts[b])))
        else:
            halves.append(jnp.where(low, half_roll(parts[a]), parts[b]))
    return halves


def conv_setup(meta, slots, seg_ref, flat, shifts, masks):
    rows4 = seg_ref.shape[0]
    blocks = rows4 // 16
    one, zero = jnp.ones((16, 256), jnp.bfloat16), jnp.zeros((16, 256), jnp.bfloat16)
    flat[0:rows4, :] = seg_ref[...]
    flat[rows4:, :] = jnp.zeros((16, 256), jnp.float32)
    for p in range(16):
        shifts[p] = flat[pl.ds(p, rows4), :].astype(jnp.bfloat16).reshape(blocks, 16, 256)

    @pl.loop(0, slots)
    def _(v):
        at = meta[1 + v]
        number = jnp.full((16, 256), meta[1 + 2 * slots + v].astype(jnp.float32), jnp.float32).astype(jnp.bfloat16)
        row = pl.multiple_of(v * 16, 16)
        for b in range(TAP_BLOCKS):
            ids = shifts[b % 16, at + b // 16]
            masks[pl.ds(row, 16), b * 256 : (b + 1) * 256] = jnp.where(ids == number, one, zero)


def conv_shifts(wide, side, flat, shifts):
    rows4 = shifts.shape[1] * 16
    halves = quad_rows(wide, rows4, side)
    flat[0:rows4, 0:128] = halves[0]
    flat[0:rows4, 128:256] = halves[1]
    for p in range(16):
        shifts[p] = flat[pl.ds(p, rows4), :].astype(jnp.bfloat16).reshape(rows4 // 16, 16, 256)


def conv_patch(places, b, shifts, masks):
    span = slice(b * 256, (b + 1) * 256)
    pieces = [
        shifts[b % 16, at + b // 16] * masks[v * 16 : (v + 1) * 16, span] for v, at in enumerate(places)
    ]
    return jnp.concatenate(pieces, axis=0)


def conv_taps(w_ref, side, b, taps):
    rows = 256
    low = lane_low(rows)
    depth = w_ref.shape[0]
    zero = jnp.zeros((64, 128), jnp.bfloat16)
    if b == 0:
        here, before = w_ref[0:rows, :], jnp.concatenate([zero, w_ref[0 : rows - 64, :]], axis=0)
    elif b * rows < depth:
        here, before = w_ref[b * rows : (b + 1) * rows, :], w_ref[b * rows - 64 : (b + 1) * rows - 64, :]
    else:
        here, before = jnp.concatenate([zero] * 4, axis=0), jnp.concatenate([w_ref[depth - 64 :, :]] + [zero] * 3, axis=0)
    block = jnp.where(low, here, half_roll(before)) if side == 0 else jnp.where(low, half_roll(here), before)
    taps[128 + b * rows : 128 + (b + 1) * rows, :] = block
    return jnp.concatenate([block, taps[b * rows : (b + 1) * rows, :]], axis=1)


def conv_kernel(slots, backward, meta, x_ref, seg_ref, w_ref, extra_ref, *refs):
    if backward:
        o_ref, *refs = refs[-8:]
    else:
        o_ref, *refs = refs[-9:]
    if backward:
        wide, flat, shifts, masks, taps, sums, outs = refs
    else:
        slope_ref, wide, flat, shifts, masks, taps, sums, outs = refs

    @pl.when(pl.program_id(0) == 0)
    def _():
        conv_setup(meta, slots, seg_ref, flat, shifts, masks)

    wide[...] = x_ref[...].astype(jnp.float32)
    taps[0:128, :] = jnp.zeros((128, 128), jnp.bfloat16)
    out_rows = o_ref.shape[0] // 4
    places = [meta[1 + v] for v in range(slots)]
    for side in range(2):
        conv_shifts(wide, side, flat, shifts)
        total = jnp.zeros((256, slots * 16) if backward else (slots * 16, 256), jnp.float32)
        for b in range(TAP_BLOCKS):
            weight = conv_taps(w_ref, side, b, taps)
            if backward:
                total = total + lanes_dot(weight, conv_patch(places, TAP_BLOCKS - 1 - b, shifts, masks))
            else:
                total = total + jnp.dot(
                    conv_patch(places, b, shifts, masks), weight, preferred_element_type=jnp.float32
                )
        sums[...] = total.T if backward else total

        @pl.loop(0, slots)
        def _(v):
            to = pl.ds(pl.multiple_of(meta[1 + slots + v] * 16, 16), 16)
            row = pl.ds(pl.multiple_of(v * 16, 16), 16)
            keep = masks[row, 16 * 256 : 17 * 256].astype(jnp.float32) > 0.5
            outs[side, to, :] = jnp.where(keep, sums[row, :], outs[side, to, :])

    low = lane_low(out_rows)
    for half in range(2):
        zero_side = outs[0, :, half * 128 : (half + 1) * 128]
        one_side = outs[1, :, half * 128 : (half + 1) * 128]
        wide[pl.ds(2 * half, out_rows, stride=4), :] = jnp.where(low, zero_side, half_roll(one_side))
        wide[pl.ds(2 * half + 1, out_rows, stride=4), :] = jnp.where(low, half_roll(zero_side), one_side)
    result = wide[0 : 4 * out_rows, :]
    if backward:
        o_ref[...] = (extra_ref[...] + result).astype(o_ref.dtype)
    else:
        result = result + extra_ref[...]
        below, density = phi_parts(result)
        center = x_ref[KERNEL // 2 : KERNEL // 2 + 4 * out_rows, :].astype(jnp.float32)
        o_ref[...] = center + result * below
        slope_ref[...] = below + result * density


def seg_quads(seg_ext):
    quads = seg_ext.astype(jnp.float32).reshape(-1, 4)
    return jnp.repeat(quads, 64, axis=1)


def grouped_conv(x_ext, seg_ext, weight, extra, first_pair, rise, backward, begin=0, pairs=None, after=()):
    row_count, length, width = x_ext.shape
    frames = length - KERNEL
    pairs = width // 128 if pairs is None else pairs
    in_block, tile, number = tile_lists(seg_ext, rise)
    slots = in_block.shape[0]
    meta = jnp.concatenate([jnp.reshape(first_pair, (1,)).astype(jnp.int32), in_block, tile, number])
    rows4 = row_count * length // 4
    out4 = row_count * frames // 4
    depth = TAP_BLOCKS * 256
    return pl.pallas_call(
        partial(conv_kernel, slots, backward),
        grid_spec=pltpu.PrefetchScalarGridSpec(
            num_scalar_prefetch=1,
            grid=(pairs,),
            in_specs=[
                pl.BlockSpec((row_count * length, 128), lambda p, meta: (0, begin + p)),
                pl.BlockSpec((rows4, 256), lambda p, meta: (0, 0)),
                pl.BlockSpec((weight.shape[0], 128), lambda p, meta: (0, meta[0] + begin + p)),
                pl.BlockSpec((extra.shape[0], 128), lambda p, meta: (0, begin + p)),
            ]
            + [pl.BlockSpec(memory_space=pl.ANY)] * len(after),
            out_specs=[pl.BlockSpec((row_count * frames, 128), lambda p, meta: (0, p))] * (1 if backward else 2),
            scratch_shapes=[
                pltpu.VMEM((row_count * length, 128), jnp.float32),
                pltpu.VMEM((rows4 + 16, 256), jnp.float32),
                pltpu.VMEM((16, rows4 // 16, 16, 256), jnp.bfloat16),
                pltpu.VMEM((slots * 16, depth), jnp.bfloat16),
                pltpu.VMEM((128 + depth, 128), jnp.bfloat16),
                pltpu.VMEM((slots * 16, 256), jnp.float32),
                pltpu.VMEM((2, out4, 256), jnp.float32),
            ],
        ),
        out_shape=[jax.ShapeDtypeStruct((row_count * frames, 128 * pairs), jnp.bfloat16 if backward else jnp.float32)]
        * (1 if backward else 2),
        compiler_params=pltpu.CompilerParams(vmem_limit_bytes=VMEM_LIMIT, dimension_semantics=IN_ORDER),
        cost_estimate=cost(
            flops=2 * pairs * 2 * slots * 16 * 256 * depth, bytes_accessed=pairs * weight.shape[0] * 256, transcendentals=0
        ),
        name="conv_back" if backward else "conv_forth",
    )(meta, x_ext.reshape(row_count * length, width), seg_quads(seg_ext), weight, extra, *after)


def at_block(b):
    return pl.ds(b * 256, 256) if isinstance(b, int) else pl.ds(pl.multiple_of(b * 256, 256), 256)


def id_block(number):
    return jnp.full((16, 256), number, jnp.float32).astype(jnp.bfloat16)


def conv_ids(seg_ref, flat, ids):
    rows4 = seg_ref.shape[0]
    flat[0:rows4, :] = seg_ref[...]
    flat[rows4:, :] = jnp.zeros((16, 256), jnp.float32)
    for p in range(16):
        ids[p] = flat[pl.ds(p, rows4), :].astype(jnp.bfloat16).reshape(rows4 // 16, 16, 256)


def conv_cut(places, numbers, b, shifts, ids):
    nothing = jnp.zeros((16, 256), jnp.bfloat16)
    pieces = []
    for at, number in zip(places, numbers):
        same = ids[b & 15, at + (b >> 4)] == id_block(number)
        pieces.append(jnp.where(same, shifts[b & 15, at + (b >> 4)], nothing))
    return jnp.concatenate(pieces, axis=0)


def conv_weight_kernel(slots, meta, x_ref, seg_ref, g_ref, *refs):
    send_ref, keep_ref, wide, wide_g, flat, shifts, masks, quads, picks, sums = refs[-10:]
    @pl.when(pl.program_id(0) == 0)
    def _():
        conv_ids(seg_ref, flat, masks)

    wide[...] = x_ref[...].astype(jnp.float32)
    wide_g[...] = g_ref[...].astype(jnp.float32)
    out_rows = g_ref.shape[0] // 4
    low = lane_low(64)
    places = [meta[1 + v] for v in range(slots)]
    numbers = [meta[1 + 2 * slots + v].astype(jnp.float32) for v in range(slots)]
    nothing = jnp.zeros((16, 256), jnp.bfloat16)
    for side in range(2):
        conv_shifts(wide, side, flat, shifts)
        halves = quad_rows(wide_g, out_rows, side)
        quads[:, 0:128] = halves[0].astype(jnp.bfloat16)
        quads[:, 128:256] = halves[1].astype(jnp.bfloat16)

        for v in range(slots):
            at = pl.ds(pl.multiple_of(meta[1 + slots + v] * 16, 16), 16)
            same = masks[0, places[v] + 1] == id_block(numbers[v])
            picks[v * 16 : (v + 1) * 16, :] = jnp.where(same, quads[at, :], nothing)

        turned = picks[...].T

        @pl.loop(0, TAP_BLOCKS, unroll=DW_UNROLL)
        def _(b):
            sums[:, at_block(b)] = jnp.dot(
                turned, conv_cut(places, numbers, b, shifts, masks), preferred_element_type=jnp.float32
            )

        def piece(j, q):
            return sums[j * 64 : (j + 1) * 64, q * 128 : (q + 1) * 128]

        def odd(q):
            return half_roll(piece(1, q) + piece(3, q + 1))

        def emit(block, ref):
            left = odd(16 * block)
            for q in range(16 * block, 16 * block + 16):
                right = odd(q + 1)
                part = piece(0, q) + piece(2, q + 1) + jnp.where(low, left, right)
                first = (q // 8 % 2) * 128 + side * 64
                ref[block // 2, first : first + 64, q % 8 * 128 : (q % 8 + 1) * 128] = part.astype(ref.dtype)
                left = right

        for block in range(4):
            pl.when((meta[0] & 1) == (block & 1))(partial(emit, block, keep_ref))
            pl.when((meta[0] & 1) != (block & 1))(partial(emit, block, send_ref))


def grouped_conv_weight(x_ext, seg_ext, grad, rise, place, after):
    row_count, length, width = x_ext.shape
    frames = length - KERNEL
    pairs = width // 128
    in_block, tile, number = tile_lists(seg_ext, rise)
    slots = in_block.shape[0]
    meta = jnp.concatenate([jnp.reshape(place, (1,)).astype(jnp.int32), in_block, tile, number])
    rows4 = row_count * length // 4
    out4 = row_count * frames // 4
    depth = TAP_BLOCKS * 256
    return pl.pallas_call(
        partial(conv_weight_kernel, slots),
        grid_spec=pltpu.PrefetchScalarGridSpec(
            num_scalar_prefetch=1,
            grid=(pairs,),
            in_specs=[
                pl.BlockSpec((row_count * length, 128), lambda p, meta: (0, p)),
                pl.BlockSpec((rows4, 256), lambda p, meta: (0, 0)),
                pl.BlockSpec((row_count * frames, 128), lambda p, meta: (0, p)),
            ]
            + [pl.BlockSpec(memory_space=pl.ANY)] * len(after),
            out_specs=[pl.BlockSpec((2, 256, KERNEL * 8), lambda p, meta: (0, 0, 0))] * 2,
            scratch_shapes=[
                pltpu.VMEM((row_count * length, 128), jnp.float32),
                pltpu.VMEM((row_count * frames, 128), jnp.float32),
                pltpu.VMEM((rows4 + 16, 256), jnp.float32),
                pltpu.VMEM((16, rows4 // 16, 16, 256), jnp.bfloat16),
                pltpu.VMEM((16, rows4 // 16, 16, 256), jnp.bfloat16),
                pltpu.VMEM((out4, 256), jnp.bfloat16),
                pltpu.VMEM((slots * 16, 256), jnp.bfloat16),
                pltpu.VMEM((256, depth), jnp.float32),
            ],
        ),
        out_shape=[jax.ShapeDtypeStruct((2, 256, KERNEL * 8), jnp.bfloat16)] * 2,
        compiler_params=pltpu.CompilerParams(vmem_limit_bytes=VMEM_LIMIT, dimension_semantics=IN_ORDER),
        cost_estimate=cost(
            flops=2 * pairs * 2 * slots * 16 * 256 * depth, bytes_accessed=width * KERNEL * 128, transcendentals=0
        ),
        name="conv_weight_grad",
    )(meta, x_ext.reshape(row_count * length, width), seg_quads(seg_ext), grad, *after)


def fold_kernel(items, outs_count, meta, *refs):
    refs = list(refs)
    outs = refs[-outs_count:]
    for item in items:
        kept = refs.pop(0)
        gots = [refs.pop(0) for _ in item["gots"]]
        place = item["place"]
        shape = kept.shape
        bit = item["bit"](meta)
        for side, where in ((1 - bit, item["send"]), (bit, item["keep"])):
            buffer, column, lanes = where
            out = outs[buffer]
            if place is None:
                width = shape[3] // 2
                span = pl.ds(pl.multiple_of(side * width, width), width)
                for other in range(shape[0]):
                    total = kept[other, 0, :, span].astype(jnp.float32) + gots[0][other, 0, :, span].astype(jnp.float32)
                    out[other, :, column : column + width] = total.astype(out.dtype)
                continue
            for other in range(shape[1 - place]):
                at = (side, other) if place == 0 else (other, side)
                begin = 0
                for got in gots:
                    width = got.shape[3]
                    total = kept[at[0], at[1], :, begin : begin + width].astype(jnp.float32)
                    total = (total + got[at[0], at[1]].astype(jnp.float32)).astype(out.dtype)
                    rows = shape[2] // lanes
                    for k in range(lanes):
                        first = column + begin + k * shape[3]
                        out[other, :, first : first + width] = total[k * rows : (k + 1) * rows, :]
                    begin += width


def fold_item(kept, gots, place, bit, send, keep):
    return dict(kept=kept, gots=gots, place=place, bit=bit, send=send, keep=keep)


def folds(meta, items, shapes, name, after=()):
    operands = []
    for item in items:
        operands += [item["kept"]] + list(item["gots"])
    described = [dict(item, kept=None, gots=[None] * len(item["gots"])) for item in items]
    return pl.pallas_call(
        partial(fold_kernel, described, len(shapes)),
        grid_spec=pltpu.PrefetchScalarGridSpec(
            num_scalar_prefetch=1,
            grid=(1,),
            in_specs=[pl.BlockSpec(item.shape, lambda i, m: (0, 0, 0, 0)) for item in operands]
            + [pl.BlockSpec(memory_space=pl.ANY)] * len(after),
            out_specs=[pl.BlockSpec(shape, lambda i, m: (0, 0, 0)) for shape in shapes],
        ),
        out_shape=[jax.ShapeDtypeStruct(shape, jnp.bfloat16) for shape in shapes],
        compiler_params=pltpu.CompilerParams(vmem_limit_bytes=VMEM_LIMIT, dimension_semantics=IN_ORDER),
        cost_estimate=cost(flops=0, bytes_accessed=sum(2 * item.size for item in operands), transcendentals=0),
        name=name,
    )(meta, *operands, *after)


def chosen(meta, own_ref, got_ref):
    return jnp.where(pl.program_id(0) // 2 == meta[0], own_ref[0], got_ref[0])


def finish_pair_kernel(meta, own_ref, got_ref, *refs):
    up_ref, down_ref = refs[-2:]
    source = chosen(meta, own_ref, got_ref)
    width = up_ref.shape[1]
    up_ref[...] = source[:, :width].astype(jnp.float32)
    unit = source.shape[0]
    columns = down_ref.shape[1]
    for k in range(down_ref.shape[0] // unit):
        piece = source[:, width + k * columns : width + (k + 1) * columns]
        down_ref[k * unit : (k + 1) * unit, :] = piece.astype(jnp.float32)


def finish_pair(meta, own, got, rows, after):
    unit, total = own.shape[1:]
    width = total // 2
    columns = width * unit // rows
    place = lambda i, m: (0, 2 * (i // 2) + i % 2)
    return pl.pallas_call(
        finish_pair_kernel,
        grid_spec=pltpu.PrefetchScalarGridSpec(
            num_scalar_prefetch=1,
            grid=(4,),
            in_specs=[pl.BlockSpec((1, unit, total), lambda i, m: ((i % 2) ^ m[1], 0, 0))] * 2
            + [pl.BlockSpec(memory_space=pl.ANY)] * len(after),
            out_specs=[pl.BlockSpec((unit, width), place), pl.BlockSpec((rows, columns), place)],
        ),
        out_shape=[
            jax.ShapeDtypeStruct((unit, 4 * width), jnp.float32),
            jax.ShapeDtypeStruct((rows, 4 * columns), jnp.float32),
        ],
        compiler_params=pltpu.CompilerParams(vmem_limit_bytes=VMEM_LIMIT, dimension_semantics=IN_ORDER),
        cost_estimate=cost(flops=0, bytes_accessed=12 * own.size, transcendentals=0),
        name="finish_up_down",
    )(meta, own, got, *after)


def finish_qkv_kernel(eighth, half, meta, own_ref, got_ref, *refs):
    qkv_ref, out_ref = refs[-2:]
    step = pl.program_id(0)
    source = chosen(meta, own_ref, got_ref)
    core, y = step // 2, step % 2
    units = eighth // 128
    per_part = half // 128
    for begin, base in ((0, 0), (eighth, 2 * units)):
        for u in range(units):
            at = base + y * units + u
            at = (at // per_part) * 2 * per_part + core * per_part + at % per_part
            piece = source[:, begin + u * 128 : begin + (u + 1) * 128]
            qkv_ref[:, pl.ds(pl.multiple_of(at * 128, 128), 128)] = piece.astype(jnp.float32)
    quarter = half // 2
    first = pl.multiple_of(step * quarter, quarter)
    out_ref[:, pl.ds(first, quarter)] = source[:, 2 * eighth : 2 * eighth + quarter].astype(jnp.float32)


def finish_qkv(meta, own, got, half, after):
    unit, total = own.shape[1:]
    eighth = 3 * half // 4
    return pl.pallas_call(
        partial(finish_qkv_kernel, eighth, half),
        grid_spec=pltpu.PrefetchScalarGridSpec(
            num_scalar_prefetch=1,
            grid=(4,),
            in_specs=[pl.BlockSpec((1, unit, total), lambda i, m: ((i % 2) ^ m[1], 0, 0))] * 2
            + [pl.BlockSpec(memory_space=pl.ANY)] * len(after),
            out_specs=[
                pl.BlockSpec((unit, 6 * half), lambda i, m: (0, 0)),
                pl.BlockSpec((unit, 2 * half), lambda i, m: (0, 0)),
            ],
        ),
        out_shape=[
            jax.ShapeDtypeStruct((unit, 6 * half), jnp.float32),
            jax.ShapeDtypeStruct((unit, 2 * half), jnp.float32),
        ],
        compiler_params=pltpu.CompilerParams(vmem_limit_bytes=VMEM_LIMIT, dimension_semantics=IN_ORDER),
        cost_estimate=cost(flops=0, bytes_accessed=12 * own.size, transcendentals=0),
        name="finish_qkv_out",
    )(meta, own, got, *after)


AXES = ("y", "c", "z", "x")
LOSS_POWERS = (8, 7, 6, 5, 4, 3, 2, 1)


def device_pairs(place):
    pairs = []
    for y in range(2):
        for c in range(2):
            for z in range(4):
                for x in range(2):
                    ty, tc, tz, tx = place(y, c, z, x)
                    pairs.append((((y * 2 + c) * 4 + z) * 2 + x, ((ty * 2 + tc) * 4 + tz) * 2 + tx))
    return pairs


def move(values, place):
    return lax.ppermute(values, AXES, device_pairs(place))


def swap_core(values):
    return lax.ppermute(values, "c", [(0, 1), (1, 0)])


def swap_x(values):
    return lax.ppermute(values, "x", [(0, 1), (1, 0)])


def swap_y(values):
    return lax.ppermute(values, "y", [(0, 1), (1, 0)])


def swap_xy(values):
    return lax.ppermute(values, ("y", "x"), [(0, 3), (3, 0), (1, 2), (2, 1)])


def swap_z1(values):
    return lax.ppermute(values, "z", [(0, 1), (1, 0), (2, 3), (3, 2)])


def swap_z2(values):
    return lax.ppermute(values, "z", [(0, 2), (2, 0), (1, 3), (3, 1)])


def take(values, index, size, axis):
    return lax.dynamic_slice_in_dim(values, index * size, size, axis)


def once(values, *earlier):
    return lax.optimization_barrier((values,) + earlier)[0]


def ordered(index, mine, other, axis):
    first = jnp.where(index == 0, mine, other)
    second = jnp.where(index == 0, other, mine)
    return jnp.concatenate([first, second], axis=axis)


def to_rows(blocks, x, z):
    got = []
    for turn in range(2):
        mine = lax.dynamic_index_in_dim(blocks, x ^ turn, 0, keepdims=False)
        got.append(move(mine, lambda y, c, z, x: (y, z & 1, 2 * c + (x ^ turn), (z >> 1) ^ x ^ turn)))
    flip = (z & 1) == 0
    return jnp.where(flip, got[0], got[1]), jnp.where(flip, got[1], got[0])


def from_rows(frames, z):
    half = frames.shape[0] // 2
    got = []
    for turn in range(2):
        mine = take(frames, (z & 1) ^ turn, half, 0)
        got.append(move(mine, lambda y, c, z, x: (y, z >> 1, 2 * (x ^ (z & 1)) + c, (z & 1) ^ turn)))
    return got


def split_body(
    feats, segments, labels, conv_weight, w_qkv, w_out, w_up, w_down, head_w, head_b, gains, biases, up_bias
):
    y, c, z, x = (lax.axis_index(name) for name in AXES)
    block, features = feats.shape[1:]
    half = features // 2
    frames = 2 * block
    chip_frames = 2 * frames
    tokens = frames
    rim = KERNEL // 2
    rise = lax.axis_size("z") * lax.axis_size("x") // 2
    meta = jnp.stack([c, y, x, z]).astype(jnp.int32)
    side = x ^ (z & 1)

    label_rows = jnp.pad(labels.astype(jnp.bfloat16)[:, None, :], ((0, 0), (0, 15), (0, features - block)))
    first_block, second_block = to_rows(jnp.concatenate([feats, label_rows], axis=1), x, z)
    feats_own = jnp.concatenate([first_block[:block], second_block[:block]], axis=0)
    labels_own = jnp.concatenate([first_block[block, :block], second_block[block, :block]]).astype(jnp.int32)
    seg_rows = ordered(c, segments, swap_core(segments), 0)
    seg_row = lax.dynamic_index_in_dim(seg_rows, z, 0, keepdims=False)
    seg_halves = seg_row.reshape(2, 2, frames)
    seg_near = lax.dynamic_index_in_dim(seg_halves, side, 0, keepdims=False)
    seg_far = lax.dynamic_index_in_dim(seg_halves, 1 - side, 0, keepdims=False)
    seg_near, seg_far = (jnp.where(c == 0, item, item[::-1]).reshape(-1) for item in (seg_near, seg_far))
    seg_wide = jnp.pad(seg_row, (rim, rim), constant_values=-1)
    seg_ext = lax.dynamic_slice_in_dim(seg_wide, side * chip_frames, chip_frames + 2 * rim, 0)[None]

    def to_chip(values):
        return ordered(c, take(values, c, half, 1), swap_core(take(values, 1 - c, half, 1)), 0)

    def rimmed(values, edge):
        empty = jnp.zeros_like(edge)
        before = jnp.where(side == 0, empty, edge)
        after = jnp.where(side == 0, edge, empty)
        return jnp.concatenate([before, values, after], axis=0)[None]

    def with_rim(values):
        return rimmed(values, swap_x(jnp.where(side == 0, values[chip_frames - rim :], values[:rim])))

    def grouped(own, got_x, got_y, got_xy):
        return ordered(y, ordered(side, own, got_x, 0)[None], ordered(side, got_y, got_xy, 0)[None], 0)

    def to_groups(values):
        def part(yy, xx):
            return lax.dynamic_slice_in_dim(values, 256 * xx + 128 * yy, 128, 1)

        return grouped(
            part(y, x), swap_x(part(y, 1 - x)), swap_y(part(1 - y, x)), swap_xy(part(1 - y, 1 - x))
        )

    shift_bias = biases.T
    qkv_bias = jnp.concatenate([shift_bias[2], jnp.zeros((features,), jnp.float32), shift_bias[3]])[None]
    gain_rows = gains.T
    feats_chip = to_chip(feats_own)
    feats_group = jnp.pad(to_groups(feats_chip), ((0, 0), (rim, rim), (0, 0)))
    seg_pair = ordered(y, seg_row[None], swap_y(seg_row)[None], 0)
    seg_pair = jnp.pad(seg_pair, ((0, 0), (rim, rim)), constant_values=-1)
    position_chip, slope = grouped_conv(
        with_rim(feats_chip), seg_ext, conv_weight, take(shift_bias[0:1], c, half, 1), 4 * c, rise, False
    )
    theirs, ours, normed, position = mix_rows(
        meta,
        (
            take(position_chip, c, frames, 0),
            swap_core(take(position_chip, 1 - c, frames, 0)),
            gain_rows[0:1],
            shift_bias[1:2],
        ),
        w_qkv,
        qkv_bias,
        1,
        2,
        (seg_pair,),
    )
    near = jnp.concatenate([ours, swap_core(theirs)], axis=0)
    got_normed = swap_core(normed)
    far = swap_x(near)
    theirs, ours = mix_rows(meta, (normed,), w_qkv, qkv_bias, 0, 1, (feats_group,))
    queries = jnp.concatenate([ours, swap_core(theirs)], axis=0)
    mixed, state = attend_near(queries, near, seg_near, seg_near)
    attended, attended_ours, attended_away, lse = attend_far(queries, far, seg_near, seg_far, mixed, state)
    zero_row = jnp.zeros((features,), jnp.float32)
    rows = jnp.stack([gain_rows[1], shift_bias[5], shift_bias[4], shift_bias[6]] + [zero_row] * 4)
    (
        pack, output_low, out_ours, up_ours, branch_ours, att_ours, att_theirs, grad_resid, mid_sums, up_sums,
        grad_head_w, last,
    ) = middle(
        meta,
        attended_ours,
        swap_core(attended_away),
        position,
        w_out,
        w_up,
        w_down,
        up_bias[None],
        head_w,
        head_b[None],
        labels_own[:, None],
        rows,
    )

    grad_heads = jnp.concatenate([att_ours, swap_core(att_theirs)], axis=0)
    dq_far, dkv_far = attend_back(queries, far, grad_heads, attended, lse, seg_near, seg_far, jnp.bfloat16, att_ours)
    got_kv = swap_x(dkv_far)

    C, Y, X, Z = 0, 1, 2, 3
    places = pack_places(features, w_up.shape[1])
    got_pack = swap_core(once(pack, grad_heads))
    up_pair = ((up_ours, 0), (got_pack, places["up"]))
    down_pair = ((out_ours, 0), (got_pack, places["out"]))
    branch_pair = ((branch_ours, 0), (got_pack, places["branch"]))
    second_pair, active_pair, attended_pair = (
        ((pack, places[name]), (got_pack, places[name])) for name in ("second", "active", "attended")
    )
    unit = features // 8
    down_rows = w_down.shape[0] // 4
    up_wide = w_up.shape[1] // 4
    quarter = half // 2
    eighth = 3 * half // 4
    up_low, up_high, down_away, down_home = weight_parts(
        meta,
        [
            weight_task([(0, 0)], second_pair, up_pair, half, 1, lambda i, m: 0, up_wide, lambda m: 1 - m[Y]),
            weight_task(
                [(2, 0)], active_pair, down_pair, down_rows, 1,
                lambda i, m: 2 * (1 - (m[Z] >> 1)) + 1 - (m[Z] & 1), half, lambda m: 0,
            ),
            weight_task([(1, 0)], second_pair, up_pair, half, 1, lambda i, m: 1, up_wide, lambda m: 1 - m[Y]),
            weight_task(
                [(3, 0)], active_pair, down_pair, down_rows, 1,
                lambda i, m: 2 * (m[Z] >> 1) + 1 - (m[Z] & 1), half, lambda m: 0,
            ),
        ],
        [(half, up_wide), (half, up_wide), (down_rows, half), (down_rows, half)],
        "weight_first",
        (dkv_far,),
    )
    got_up_low, got_down_away = swap_y(up_low), swap_z1(down_away)
    got_up_high, got_down_home = swap_y(up_high), swap_z1(down_home)
    dq, dkv = attend_back(queries, near, grad_heads, attended, lse, seg_near, seg_near, jnp.float32, down_home)

    def mixed_grad(part):
        piece = slice(part * frames, (part + 1) * frames)
        return jnp.concatenate(
            [
                dq[piece] + dq_far[piece],
                dkv[0, piece] + got_kv[0, piece].astype(jnp.float32),
                dkv[1, piece] + got_kv[1, piece].astype(jnp.float32),
            ],
            axis=1,
        ).astype(jnp.bfloat16)

    grad_theirs = mixed_grad(1)
    grad_got = swap_core(grad_theirs)
    grad_ours = mixed_grad(0)
    position_ours, position_theirs, first_sums = unmix_rows(
        meta, grad_ours, grad_got, w_qkv, position, grad_resid, gain_rows[0:1], (got_up_low, got_down_away)
    )
    grad_position, grad_conv, edge, own_part, to_x, to_y, to_xy, conv_bias = conv_grad_rows(
        meta, position_ours, swap_core(position_theirs), slope, (got_up_high, got_down_home)
    )
    grad_rim = rimmed(grad_conv, swap_x(edge))
    grad_group = grouped(own_part, swap_x(to_x), swap_y(to_y), swap_xy(to_xy))

    x_bit, y_bit = (lambda m: m[X]), (lambda m: m[Y])
    own_sums, got_sums = (jnp.sum(item.astype(jnp.float32), axis=0, keepdims=True) for item in (grad_ours, grad_got))
    rest_loss, digits = last[1, 0], []
    for power in LOSS_POWERS:
        digit = jnp.floor(rest_loss / 8.0**power)
        digits.append(digit)
        rest_loss = rest_loss - digit * 8.0**power
    digits.append(rest_loss)
    final = jnp.concatenate(
        [last[0, :VOCAB], jnp.stack(digits), jnp.zeros((unit - VOCAB - len(digits),), jnp.float32)]
    )
    small = small_sums(
        meta, grad_head_w, mid_sums, first_sums, conv_bias, own_sums, got_sums, up_sums, final[None]
    )

    normed_pair = ((normed, 0), (got_normed, 0))
    qkv_pair = ((grad_ours, 0), (grad_theirs, 0))
    a_first, b_first = weight_parts(
        meta,
        [
            weight_task([(0, 0)], normed_pair, qkv_pair, features, 1, lambda i, m: 0, eighth, lambda m: 1 - m[Y]),
            weight_task(
                [(1, 2 * eighth)], normed_pair, qkv_pair, unit, 4, lambda i, m: 2 * i + 1 - m[X], 2 * eighth, lambda m: 1
            ),
            weight_task([(1, 0)], attended_pair, branch_pair, unit, 4, lambda i, m: 2 * i + 1 - m[X], half, lambda m: 0),
            weight_task([(1, half)], ((small, 0),), None, unit, 4, lambda i, m: 2 * i + 1 - m[X], 128, None),
        ],
        [(features, eighth), (half, 4 * eighth)],
        "weight_qkv_first",
        (grad_conv,),
    )
    got_a, got_b = swap_y(a_first), swap_x(b_first)
    conv_send, conv_kept = grouped_conv_weight(
        feats_group, seg_pair, grad_group.reshape(-1, 128), rise, z, (a_first, grad_rim)
    )
    conv_got = swap_z1(conv_send)
    up_send, up_kept, down_send, down_kept = weight_parts(
        meta,
        [
            weight_task(
                [(0, 0), (1, 0)], second_pair, up_pair, half, 1, lambda i, m: 0, up_wide, lambda m: m[Y],
                got_up_low, lambda i, m: (0, 0), "rows", lambda m: m[Z] & 1, 2 * unit,
            ),
            weight_task(
                [(0, 0), (1, 0)], second_pair, up_pair, half, 1, lambda i, m: 1, up_wide, lambda m: m[Y],
                got_up_high, lambda i, m: (0, 0), "rows", lambda m: m[Z] & 1, 2 * unit, 1,
            ),
            weight_task(
                [(2, 0), (3, 0)], active_pair, down_pair, down_rows, 1,
                lambda i, m: 2 * (1 - (m[Z] >> 1)) + (m[Z] & 1), half, lambda m: 0, got_down_away, lambda i, m: (0, 0),
                "rows", x_bit, down_rows // 2,
            ),
            weight_task(
                [(2, 0), (3, 0)], active_pair, down_pair, down_rows, 1,
                lambda i, m: 2 * (m[Z] >> 1) + (m[Z] & 1), half, lambda m: 0, got_down_home, lambda i, m: (0, 0),
                "rows", x_bit, down_rows // 2, 1,
            ),
        ],
        [(half, up_wide), (half, up_wide), (down_rows, half), (down_rows, half)],
        "weight_second",
        (conv_send,),
    )
    up_got, down_got = swap_z1(up_send), swap_x(down_send)
    low_z, high_z = (lambda m: m[Z] & 1), (lambda m: m[Z] >> 1)

    def view(values, *lead):
        return values.reshape(lead + (-1, values.shape[-1]))

    conv_left = grouped_conv(grad_rim, seg_ext, conv_weight, grad_position, 4 * c, rise, True, 0, 2, (up_kept,))[0]

    conv_send, conv_kept = folds(
        meta,
        [fold_item(conv_kept[:, None], [conv_got[:, None]], 0, high_z, (0, 0, 1), (1, 0, 1))],
        [(1, 256, KERNEL * 8)] * 2,
        "fold_taps",
        (conv_left,),
    )
    conv_got = swap_z2(conv_send)
    a_send, b_send, qkv_kept = weight_parts(
        meta,
        [
            weight_task(
                [(0, 0), (2, 0)], normed_pair, qkv_pair, features, 1, lambda i, m: 0, eighth, lambda m: m[Y],
                got_a, lambda i, m: (0, 0), "rows", x_bit, unit,
            ),
            weight_task(
                [(1, 0), (2, eighth)], normed_pair, qkv_pair, unit, 4, lambda i, m: 2 * i + m[X], 2 * eighth, lambda m: 1,
                got_b, lambda i, m: (i, 1), "columns", y_bit,
            ),
            weight_task(
                [(1, eighth), (2, 2 * eighth)], attended_pair, branch_pair, unit, 4, lambda i, m: 2 * i + m[X], half,
                lambda m: 0, got_b, lambda i, m: (i, 0), "columns", y_bit,
            ),
            weight_task(
                [(1, eighth + quarter), (2, 2 * eighth + quarter)], ((small, 0),), None, unit, 4,
                lambda i, m: 2 * i + m[X], 128, None, got_b, lambda i, m: (i, half // 128),
            ),
        ],
        [(half, eighth), (half, eighth + quarter + 128), (half, 2 * eighth + quarter + 128)],
        "weight_qkv_second",
        (conv_kept,),
    )
    a_got, b_got = swap_x(a_send), swap_y(b_send)
    conv_right = grouped_conv(
        grad_rim, seg_ext, conv_weight, grad_position, 4 * c, rise, True, 2, 2, (qkv_kept,)
    )[0]
    wide = 2 * eighth + quarter + 128
    x_send, up_kept, qkv_kept, down_send, down_kept, conv_send, conv_kept, qkv_send = folds(
        meta,
        [
            fold_item(view(up_kept, 2, 2), [view(up_got, 2, 2)], 1, x_bit, (0, 0, 1), (1, 0, 1)),
            fold_item(view(qkv_kept, 2, 2), [view(a_got, 2, 2), view(b_got, 2, 2)], 1, low_z, (7, 0, 1), (2, 0, 1)),
            fold_item(view(down_kept, 2, 1), [view(down_got, 2, 1)], None, y_bit, (3, 0, 1), (4, 0, 1)),
            fold_item(view(conv_kept, 2, 1), [view(conv_got, 2, 1)], 0, x_bit, (5, 0, 1), (6, 0, 1)),
        ],
        [(2, unit, up_wide)] * 2 + [(2, unit, wide)] + [(2, down_rows // 2, quarter)] * 2
        + [(1, 128, KERNEL * 8)] * 2 + [(2, unit, wide)],
        "fold_first",
        (conv_right,),
    )
    qkv_got, up_got, down_got, conv_got = swap_z1(qkv_send), swap_x(x_send), swap_y(down_send), swap_x(conv_send)
    shard = ordered(x, conv_kept, conv_got, 0)
    shard = jnp.concatenate([shard, swap_y(shard)], axis=0)
    conv_input = jnp.concatenate([once(conv_left, x_send), conv_right], axis=1)
    away = swap_core(take(conv_input, 1 - c, frames, 0))
    back = jnp.concatenate([ordered(c, take(conv_input, c, frames, 0), away, 1), output_low], axis=1)
    qkv_send, qkv_kept, pair_send, pair_kept = folds(
        meta,
        [
            fold_item(qkv_kept[:, None], [qkv_got[:, None]], 0, high_z, (0, 0, 1), (1, 0, 1)),
            fold_item(up_kept[:, None], [up_got[:, None]], 0, high_z, (2, 0, 1), (3, 0, 1)),
            fold_item(down_kept[:, None], [down_got[:, None]], 0, lambda m: 1, (2, up_wide, 4), (3, up_wide, 4)),
        ],
        [(1, unit, wide)] * 2 + [(1, unit, 2 * up_wide)] * 2,
        "fold_second",
        (),
    )
    qkv_got, pair_got = swap_z2(qkv_send), swap_z2(pair_send)
    grad_conv_weight = flip_columns(meta, shard, swap_core(shard))

    def add(kept, got):
        return (kept.astype(jnp.float32) + got.astype(jnp.float32)).astype(jnp.bfloat16)

    def spread(shard, *earlier):
        shard = jnp.concatenate([shard, once(swap_y(shard), *earlier)], axis=0)
        return shard, swap_core(shard)

    pair_sum, qkv_sum = add(pair_kept, pair_got), add(qkv_kept, qkv_got)
    back = from_rows(once(back, pair_sum, qkv_sum), z)
    grad_w_up, grad_w_down = finish_pair(meta, *spread(pair_sum, grad_conv_weight), w_down.shape[0] // 8, ())
    qkv_own, qkv_other = spread(qkv_sum)
    grad_w_qkv, grad_w_out = finish_qkv(meta, qkv_own, qkv_other, half, (grad_w_up,))
    total = qkv_own[0, :, wide - 128 :].astype(jnp.float32) + qkv_other[0, :, wide - 128 :].astype(jnp.float32)
    back = [once(item, grad_w_up, grad_w_qkv)[None] for item in back]
    back = ordered(x, back[0], back[1], 0)
    grad_feats, layer_out = back[:, :, :features], back[:, :, features:]
    v = VOCAB
    powers = jnp.array([8.0**power for power in LOSS_POWERS] + [1.0], jnp.float32)
    loss = jnp.sum(total[v : v + len(LOSS_POWERS) + 1, v + 13] * powers) / (tokens * 32)
    gain_part = jnp.stack([total[:, v + 4], total[:, v]], axis=1)
    bias_part = jnp.stack([total[:, v + k] for k in (6, 5, 7, 8, 1, 2, 3)], axis=1)
    return (
        layer_out,
        loss,
        grad_feats.astype(jnp.float32),
        grad_conv_weight,
        grad_w_qkv,
        grad_w_out,
        grad_w_up,
        grad_w_down,
        total[:, :v],
        total[:v, v + 13],
        gain_part,
        bias_part,
        total[:, v + 9 : v + 13].T.reshape(-1),
    )


def split_solution(mesh):
    fine = Mesh(mesh.devices.reshape(2, 2, 4, 2), AXES)
    rows, parts = ("y", "c"), ("z", "x")
    return jax.shard_map(
        split_body,
        mesh=fine,
        in_specs=(P(rows, parts, None), P(rows, None), P(rows, parts)) + (P(),) * 10,
        out_specs=(
            P(rows, parts, None),
            P(),
            P(rows, parts, None),
            P(parts, None),
            P(parts, None),
            P(parts, None),
            P(parts, None),
            P(parts, None),
            P(parts, None),
            P(),
            P(parts, None),
            P(parts, None),
            P(parts),
        ),
        check_vma=False,
    )


def solution(mesh):
    if mesh.shape["dp"] == 4 and mesh.shape["seq"] == 8:
        return split_solution(mesh)
    return whole_solution(mesh)
```

```python
from functools import partial
import math

import jax
import jax.numpy as jnp
from jax import lax
from jax.experimental import pallas as pl
from jax.experimental.pallas import tpu as pltpu
from jax.sharding import Mesh, PartitionSpec as P

HEADS = 16
GROUPS = 16
KERNEL = 128
VOCAB = 32
TAP_BLOCKS = 33
VMEM_LIMIT = 56 * 1024 * 1024
DW_UNROLL = 11
IN_ORDER = ("arbitrary",)
COST_SHARE = 0.001


epsilon = 1e-05
masked_score = -1e30
tap_group = 8


def extended(cells, sides, width):
    for axis, dim in sides:
        count = lax.axis_size(axis)
        ends = count - 1
        head = lax.slice_in_dim(cells, 0, width, axis=dim)
        tail = lax.slice_in_dim(cells, cells.shape[dim] - width, cells.shape[dim], axis=dim)
        cells = jnp.concatenate(
            [
                lax.ppermute(tail, axis, [(i, (i + 1) % count) for i in range(ends)]),
                cells,
                lax.ppermute(head, axis, [((i + 1) % count, i) for i in range(ends)]),
            ],
            axis=dim,
        )
    return cells


def layer_norm(values, gain_row, shift_row):
    center = values - jnp.mean(values, axis=-1, keepdims=True)
    spread = jnp.mean(center * center, axis=-1, keepdims=True)
    return center * lax.rsqrt(spread + epsilon) * gain_row + shift_row


def gelu_exact(values):
    return jax.nn.gelu(values, approximate=False)


def outer_sum(left_side, right_side):
    return lax.dot_general(
        left_side, right_side, (((0,), (0,)), ((), ())), preferred_element_type=jnp.float32
    )


def back_product(grad_rows, weight):
    return lax.dot_general(
        grad_rows, weight, (((1,), (1,)), ((), ())), preferred_element_type=jnp.float32
    )


def masked_windows(source, seg_padded, seg_local, offsets, frames):
    windows = []
    for offset in offsets:
        window = lax.dynamic_slice_in_dim(source, offset, frames, 1)
        near_ids = lax.dynamic_slice_in_dim(seg_padded, offset, frames, 1)
        keep_mask = (near_ids == seg_local)[:, :, None]
        windows.append(jnp.where(keep_mask, window, jnp.zeros_like(window)))
    return jnp.stack(windows, axis=2)


def conv_forward(feats_rim, seg_padded, seg_local, conv_weight):
    row_count, frames = seg_local.shape
    features = feats_rim.shape[2]
    group_width = features // GROUPS
    tap_count = conv_weight.shape[0] // group_width
    grouped = conv_weight.reshape(tap_count, group_width, GROUPS, group_width)

    def one_block(tap_block, running):
        offsets = [tap_block * tap_group + tap_inner for tap_inner in range(tap_group)]
        stacked = masked_windows(feats_rim, seg_padded, seg_local, offsets, frames)
        stacked = stacked.reshape(row_count, frames, tap_group, GROUPS, group_width)
        weight_part = lax.dynamic_slice_in_dim(grouped, tap_block * tap_group, tap_group, 0)
        return running + jnp.einsum(
            "rtkgi,kigo->rtgo", stacked, weight_part, preferred_element_type=jnp.float32
        )

    start_sum = jnp.zeros((row_count, frames, GROUPS, group_width), jnp.float32)
    running = lax.fori_loop(0, tap_count // tap_group, one_block, start_sum)
    return running.reshape(row_count, frames, features)


def conv_weight_grad(feats_rim, seg_padded, seg_local, grad_conv_low, tap_count):
    row_count, frames = seg_local.shape
    features = feats_rim.shape[2]
    group_width = features // GROUPS
    grad_grouped = grad_conv_low.reshape(row_count, frames, GROUPS, group_width)

    def one_block(tap_block, running):
        offsets = [tap_block * tap_group + tap_inner for tap_inner in range(tap_group)]
        stacked = masked_windows(feats_rim, seg_padded, seg_local, offsets, frames)
        stacked = stacked.reshape(row_count, frames, tap_group, GROUPS, group_width)
        block_grad = jnp.einsum(
            "rtkgi,rtgo->kigo", stacked, grad_grouped, preferred_element_type=jnp.float32
        )
        return lax.dynamic_update_slice_in_dim(running, block_grad, tap_block * tap_group, 0)

    start_sum = jnp.zeros((tap_count, group_width, GROUPS, group_width), jnp.float32)
    running = lax.fori_loop(0, tap_count // tap_group, one_block, start_sum)
    return running.reshape(tap_count * group_width, features)


def conv_input_grad(grad_rim, seg_padded, seg_local, conv_weight):
    row_count, frames = seg_local.shape
    features = grad_rim.shape[2]
    group_width = features // GROUPS
    tap_count = conv_weight.shape[0] // group_width
    grouped = conv_weight.reshape(tap_count, group_width, GROUPS, group_width)

    def one_block(tap_block, running):
        offsets = [
            tap_count - (tap_block * tap_group + tap_inner) for tap_inner in range(tap_group)
        ]
        stacked = masked_windows(grad_rim, seg_padded, seg_local, offsets, frames)
        stacked = stacked.reshape(row_count, frames, tap_group, GROUPS, group_width)
        weight_part = lax.dynamic_slice_in_dim(grouped, tap_block * tap_group, tap_group, 0)
        return running + jnp.einsum(
            "rtkgo,kigo->rtgi", stacked, weight_part, preferred_element_type=jnp.float32
        )

    start_sum = jnp.zeros((row_count, frames, GROUPS, group_width), jnp.float32)
    running = lax.fori_loop(0, tap_count // tap_group, one_block, start_sum)
    return running.reshape(row_count, frames, features)


def span_size(piece_rows, frames):
    return math.gcd(piece_rows, 8 * frames)


def attend_row(row_state, query_row, key_row, value_row, seg_query, seg_key, score_scale):
    running_max, running_sum, weighted = row_state
    scores = score_scale * jnp.einsum(
        "qhe,khe->qhk", query_row, key_row, preferred_element_type=jnp.float32
    )
    allowed = (seg_query[:, None] == seg_key[None, :])[:, None, :]
    scores = jnp.where(allowed, scores, masked_score)
    new_max = jnp.maximum(running_max, jnp.max(scores, axis=-1))
    rescale = jnp.exp(running_max - new_max)
    weights = jnp.where(allowed, jnp.exp(scores - new_max[:, :, None]), 0.0)
    running_sum = running_sum * rescale + jnp.sum(weights, axis=-1)
    weighted = weighted * rescale[:, :, None] + jnp.einsum(
        "qhk,khe->qhe", weights.astype(jnp.bfloat16), value_row, preferred_element_type=jnp.float32
    )
    return (new_max, running_sum, weighted)


def query_grad_row(
    grad_query,
    query_row,
    key_row,
    value_row,
    seg_query,
    seg_key,
    lse_row,
    dots_row,
    grad_row,
    score_scale,
):
    scores = score_scale * jnp.einsum(
        "qhe,khe->qhk", query_row, key_row, preferred_element_type=jnp.float32
    )
    allowed = (seg_query[:, None] == seg_key[None, :])[:, None, :]
    probs = jnp.where(allowed, jnp.exp(scores - lse_row[:, :, None]), 0.0)
    grad_probs = jnp.einsum("qhe,khe->qhk", grad_row, value_row, preferred_element_type=jnp.float32)
    grad_scores = (probs * (grad_probs - dots_row[:, :, None])).astype(jnp.bfloat16)
    return grad_query + score_scale * jnp.einsum(
        "qhk,khe->qhe", grad_scores, key_row, preferred_element_type=jnp.float32
    )


def key_grad_row(
    grads_pair,
    key_row,
    value_row,
    query_row,
    grad_row,
    lse_row,
    dots_row,
    seg_query,
    seg_key,
    score_scale,
):
    scores = score_scale * jnp.einsum(
        "qhe,khe->qhk", query_row, key_row, preferred_element_type=jnp.float32
    )
    allowed = (seg_query[:, None] == seg_key[None, :])[:, None, :]
    probs = jnp.where(allowed, jnp.exp(scores - lse_row[:, :, None]), 0.0)
    grad_value = jnp.einsum(
        "qhk,qhe->khe", probs.astype(jnp.bfloat16), grad_row, preferred_element_type=jnp.float32
    )
    grad_probs = jnp.einsum("qhe,khe->qhk", grad_row, value_row, preferred_element_type=jnp.float32)
    grad_scores = (probs * (grad_probs - dots_row[:, :, None])).astype(jnp.bfloat16)
    grad_key = score_scale * jnp.einsum(
        "qhk,qhe->khe", grad_scores, query_row, preferred_element_type=jnp.float32
    )
    return (grad_key, grad_value)


def body(
    feats,
    segments,
    labels,
    conv_weight,
    w_qkv,
    w_out,
    w_up,
    w_down,
    head_w,
    head_b,
    gains,
    biases,
    up_bias,
):
    row_count, frames, features = feats.shape
    head_count = HEADS
    head_width = features // head_count
    score_scale = head_width ** (-0.5)
    tokens = row_count * frames
    tap_count = KERNEL
    rim_width = tap_count // 2
    own_first = lax.axis_index("seq") * frames
    seg_local = lax.dynamic_slice_in_dim(segments, own_first, frames, 1)
    seg_wide = jnp.pad(segments, ((0, 0), (rim_width, rim_width)), constant_values=-1)
    seg_padded = lax.dynamic_slice_in_dim(seg_wide, own_first, frames + 2 * rim_width, 1)
    feats_rim = extended(feats, (("seq", 1),), rim_width)
    conv_sum = conv_forward(feats_rim, seg_padded, seg_local, conv_weight) + biases[:, 0]
    activated, conv_pull = jax.vjp(gelu_exact, conv_sum)
    position = feats.astype(jnp.float32) + activated
    normed, first_pull = jax.vjp(layer_norm, position, gains[:, 0], biases[:, 1])
    normed_low = normed.astype(jnp.bfloat16).reshape(tokens, features)
    qkv_bias = jnp.concatenate([biases[:, 2], jnp.zeros((features,), jnp.float32), biases[:, 3]])
    mixed = (jnp.dot(normed_low, w_qkv, preferred_element_type=jnp.float32) + qkv_bias).astype(
        jnp.bfloat16
    )
    queries = mixed[:, :features].reshape(row_count, frames, head_count, head_width)
    keys = mixed[:, features : 2 * features].reshape(row_count, frames, features)
    values = mixed[:, 2 * features :].reshape(row_count, frames, features)
    start_state = (
        jnp.full((row_count, frames, head_count), masked_score, jnp.float32),
        jnp.zeros((row_count, frames, head_count), jnp.float32),
        jnp.zeros((row_count, frames, head_count, head_width), jnp.float32),
    )
    key_shard = lax.all_gather(keys, "seq", axis=1, tiled=True)
    value_shard = lax.all_gather(values, "seq", axis=1, tiled=True)
    piece_rows = key_shard.shape[1]
    span = span_size(piece_rows, frames)

    def forward_one_span(span_index, state):
        offset = span_index * span
        key_part = lax.dynamic_slice_in_dim(key_shard, offset, span, 1)
        value_part = lax.dynamic_slice_in_dim(value_shard, offset, span, 1)
        seg_keys = lax.dynamic_slice_in_dim(segments, offset, span, 1)
        results = []
        for row_index in range(row_count):
            action = partial(
                attend_row,
                query_row=queries[row_index],
                key_row=key_part[row_index].reshape(span, head_count, head_width),
                value_row=value_part[row_index].reshape(span, head_count, head_width),
                seg_query=seg_local[row_index],
                seg_key=seg_keys[row_index],
                score_scale=score_scale,
            )
            row_state = (state[0][row_index], state[1][row_index], state[2][row_index])
            results.append(action(row_state))
        return (
            jnp.stack([item[0] for item in results]),
            jnp.stack([item[1] for item in results]),
            jnp.stack([item[2] for item in results]),
        )

    running_max, running_sum, weighted = lax.fori_loop(
        0, piece_rows // span, forward_one_span, start_state
    )
    attended = weighted / running_sum[:, :, :, None]
    log_total = running_max + jnp.log(running_sum)
    attended_low = attended.reshape(tokens, features).astype(jnp.bfloat16)
    resid = (
        position.reshape(tokens, features)
        + jnp.dot(attended_low, w_out, preferred_element_type=jnp.float32)
        + biases[:, 4]
    )
    normed_second, second_pull = jax.vjp(layer_norm, resid, gains[:, 1], biases[:, 5])
    second_low = normed_second.astype(jnp.bfloat16)
    up_sum = jnp.dot(second_low, w_up, preferred_element_type=jnp.float32) + up_bias
    up_active, up_pull = jax.vjp(gelu_exact, up_sum)
    active_low = up_active.astype(jnp.bfloat16)
    output = resid + jnp.dot(active_low, w_down, preferred_element_type=jnp.float32) + biases[:, 6]
    output_low = output.astype(jnp.bfloat16)
    logits = jnp.dot(output_low, head_w, preferred_element_type=jnp.float32) + head_b
    row_top = jnp.max(logits, axis=-1, keepdims=True)
    shifted = jnp.exp(logits - row_top)
    exp_sums = jnp.sum(shifted, axis=-1, keepdims=True)
    onehot = labels.reshape(tokens)[:, None] == jnp.arange(VOCAB, dtype=jnp.int32)[None, :]
    picked = jnp.sum(jnp.where(onehot, logits, 0.0), axis=-1)
    local_loss = jnp.sum(row_top[:, 0] + jnp.log(exp_sums[:, 0]) - picked)
    grad_logits = (shifted / exp_sums - onehot.astype(jnp.float32)).astype(jnp.bfloat16)
    grad_head_w = outer_sum(output_low, grad_logits)
    grad_head_b = jnp.sum(grad_logits.astype(jnp.float32), axis=0)
    grad_output = back_product(grad_logits, head_w)
    grad_output_low = grad_output.astype(jnp.bfloat16)
    grad_w_down = outer_sum(active_low, grad_output_low)
    grad_down_bias = jnp.sum(grad_output_low.astype(jnp.float32), axis=0)
    grad_active = back_product(grad_output_low, w_down)
    grad_up_low = up_pull(grad_active)[0].astype(jnp.bfloat16)
    grad_w_up = outer_sum(second_low, grad_up_low)
    grad_up_bias = jnp.sum(grad_up_low.astype(jnp.float32), axis=0)
    grad_second = back_product(grad_up_low, w_up)
    grad_resid_part, grad_gain_second, grad_shift_second = second_pull(grad_second)
    grad_resid = grad_output + grad_resid_part
    grad_branch_low = grad_resid.astype(jnp.bfloat16)
    grad_w_out = outer_sum(attended_low, grad_branch_low)
    grad_out_bias = jnp.sum(grad_branch_low.astype(jnp.float32), axis=0)
    grad_attended = back_product(grad_branch_low, w_out).astype(jnp.bfloat16)
    grad_heads = grad_attended.reshape(row_count, frames, head_count, head_width)
    head_dots = jnp.sum(grad_heads.astype(jnp.float32) * attended, axis=-1)
    zero_grads = jnp.zeros((row_count, frames, head_count, head_width), jnp.float32)
    all_keys, all_values = (
        lax.all_gather(keys, "seq", axis=1, tiled=True),
        lax.all_gather(values, "seq", axis=1, tiled=True),
    )
    length = all_keys.shape[1]
    key_span = 8 * frames

    def query_block(block_index, grad_query):
        first_row = block_index * key_span
        key_block = lax.dynamic_slice_in_dim(all_keys, first_row, key_span, 1)
        value_block = lax.dynamic_slice_in_dim(all_values, first_row, key_span, 1)
        seg_keys = lax.dynamic_slice_in_dim(segments, first_row, key_span, 1)
        results = []
        for row_index in range(row_count):
            action = partial(
                query_grad_row,
                query_row=queries[row_index],
                key_row=key_block[row_index].reshape(key_span, head_count, head_width),
                value_row=value_block[row_index].reshape(key_span, head_count, head_width),
                seg_query=seg_local[row_index],
                seg_key=seg_keys[row_index],
                lse_row=log_total[row_index],
                dots_row=head_dots[row_index],
                grad_row=grad_heads[row_index],
                score_scale=score_scale,
            )
            results.append(action(grad_query[row_index]))
        return jnp.stack(results)

    grad_queries = lax.fori_loop(0, length // key_span, query_block, zero_grads)

    def key_term(piece_rows):
        span = math.gcd(piece_rows, key_span)

        def key_one_span(span_index, gathered_terms):
            offset = span_index * span
            key_block = lax.dynamic_slice_in_dim(all_keys, offset, span, 1)
            value_block = lax.dynamic_slice_in_dim(all_values, offset, span, 1)
            seg_keys = lax.dynamic_slice_in_dim(segments, offset, span, 1)
            empty_row = jnp.zeros((span, head_count, head_width), jnp.float32)
            results = []
            for row_index in range(row_count):
                action = partial(
                    key_grad_row,
                    key_row=key_block[row_index].reshape(span, head_count, head_width),
                    value_row=value_block[row_index].reshape(span, head_count, head_width),
                    query_row=queries[row_index],
                    grad_row=grad_heads[row_index],
                    lse_row=log_total[row_index],
                    dots_row=head_dots[row_index],
                    seg_query=seg_local[row_index],
                    seg_key=seg_keys[row_index],
                    score_scale=score_scale,
                )
                results.append(action((empty_row, empty_row)))
            key_part = jnp.stack([item[0] for item in results], axis=1).reshape(
                span, row_count, features
            )
            value_part = jnp.stack([item[1] for item in results], axis=1).reshape(
                span, row_count, features
            )
            both_parts = jnp.concatenate([key_part, value_part], axis=2)
            return lax.dynamic_update_slice_in_dim(gathered_terms, both_parts, offset, 0)

        empty_terms = jnp.zeros((piece_rows, row_count, 2 * features), jnp.float32)
        return lax.fori_loop(0, piece_rows // span, key_one_span, empty_terms)

    both_grads = lax.psum_scatter(
        key_term(frames * lax.axis_size("seq")), "seq", scatter_dimension=0, tiled=True
    )
    grad_keys = jnp.transpose(both_grads[:, :, :features], (1, 0, 2)).reshape(
        row_count, frames, head_count, head_width
    )
    grad_values = jnp.transpose(both_grads[:, :, features:], (1, 0, 2)).reshape(
        row_count, frames, head_count, head_width
    )
    grad_mixed = jnp.concatenate(
        [
            grad_queries.reshape(tokens, features),
            grad_keys.reshape(tokens, features),
            grad_values.reshape(tokens, features),
        ],
        axis=1,
    ).astype(jnp.bfloat16)
    grad_w_qkv = outer_sum(normed_low, grad_mixed)
    mixed_sums = jnp.sum(grad_mixed.astype(jnp.float32), axis=0)
    grad_normed = back_product(grad_mixed, w_qkv).reshape(row_count, frames, features)
    grad_position_part, grad_gain_first, grad_shift_first = first_pull(grad_normed)
    grad_position = grad_resid.reshape(row_count, frames, features) + grad_position_part
    grad_conv_low = conv_pull(grad_position)[0].astype(jnp.bfloat16)
    grad_conv_bias = jnp.sum(grad_conv_low.astype(jnp.float32), axis=(0, 1))
    grad_conv_weight = conv_weight_grad(feats_rim, seg_padded, seg_local, grad_conv_low, tap_count)
    grad_rim = extended(grad_conv_low, (("seq", 1),), rim_width)
    grad_feats = grad_position + conv_input_grad(grad_rim, seg_padded, seg_local, conv_weight)
    grad_gains = jnp.stack([grad_gain_first, grad_gain_second], axis=1)
    grad_biases = jnp.stack(
        [
            grad_conv_bias,
            grad_shift_first,
            mixed_sums[:features],
            mixed_sums[2 * features :],
            grad_out_bias,
            grad_shift_second,
            grad_down_bias,
        ],
        axis=1,
    )
    shared = (
        lax.psum_scatter(grad_conv_weight, "seq", scatter_dimension=0, tiled=True),
        lax.psum_scatter(grad_w_qkv, "seq", scatter_dimension=0, tiled=True),
        lax.psum_scatter(grad_w_out, "seq", scatter_dimension=0, tiled=True),
        lax.psum_scatter(grad_w_up, "seq", scatter_dimension=0, tiled=True),
        lax.psum_scatter(grad_w_down, "seq", scatter_dimension=0, tiled=True),
        lax.psum_scatter(grad_head_w, "seq", scatter_dimension=0, tiled=True),
        lax.psum_scatter(grad_gains, "seq", scatter_dimension=0, tiled=True),
        lax.psum_scatter(grad_biases, "seq", scatter_dimension=0, tiled=True),
        lax.psum_scatter(grad_up_bias, "seq", scatter_dimension=0, tiled=True),
    )
    summed = (
        lax.psum(shared[0].astype(jnp.bfloat16), "dp").astype(jnp.float32),
        lax.psum(shared[1].astype(jnp.bfloat16), "dp").astype(jnp.float32),
        lax.psum(shared[2].astype(jnp.bfloat16), "dp").astype(jnp.float32),
        lax.psum(shared[3].astype(jnp.bfloat16), "dp").astype(jnp.float32),
        lax.psum(shared[4].astype(jnp.bfloat16), "dp").astype(jnp.float32),
        lax.psum(shared[5].astype(jnp.bfloat16), "dp").astype(jnp.float32),
        lax.psum(shared[6].astype(jnp.bfloat16), "dp").astype(jnp.float32),
        lax.psum(shared[7].astype(jnp.bfloat16), "dp").astype(jnp.float32),
        lax.psum(shared[8].astype(jnp.bfloat16), "dp").astype(jnp.float32),
    )
    loss_total, head_bias_total = lax.psum((local_loss, grad_head_b), ("dp", "seq"))
    loss = loss_total / (tokens * lax.axis_size("dp") * lax.axis_size("seq"))
    layer_out = output_low.reshape(row_count, frames, features)
    return (
        layer_out,
        loss,
        grad_feats,
        summed[0],
        summed[1],
        summed[2],
        summed[3],
        summed[4],
        summed[5],
        head_bias_total,
        summed[6],
        summed[7],
        summed[8],
    )


def whole_solution(mesh):
    placed = (
        P("dp", "seq", None),
        P("dp", None),
        P("dp", "seq"),
        P(),
        P(),
        P(),
        P(),
        P(),
        P(),
        P(),
        P(),
        P(),
        P(),
    )
    return jax.shard_map(
        body,
        mesh=mesh,
        in_specs=placed,
        out_specs=(
            P("dp", "seq", None),
            P(),
            P("dp", "seq", None),
            P("seq", None),
            P("seq", None),
            P("seq", None),
            P("seq", None),
            P("seq", None),
            P("seq", None),
            P(),
            P("seq", None),
            P("seq", None),
            P("seq"),
        ),
        check_vma=False,
    )


def cost(flops, bytes_accessed, transcendentals):
    return pl.CostEstimate(
        flops=int(flops * COST_SHARE), bytes_accessed=int(bytes_accessed * COST_SHARE), transcendentals=int(transcendentals * COST_SHARE)
    )


def lanes_dot(a, b):
    return lax.dot_general(a, b, (((1,), (1,)), ((), ())), preferred_element_type=jnp.float32)


def rows_dot(a, b):
    return lax.dot_general(a, b, (((0,), (0,)), ((), ())), preferred_element_type=jnp.float32)


def attend_parts(side, queries, keys, values, allowed, low):
    mine = low if side == 0 else jnp.logical_not(low)
    scores = lanes_dot(jnp.where(mine, keys, jnp.zeros_like(keys)), queries)
    scores = jnp.where(allowed, scores, masked_score)
    top = jnp.max(scores, axis=0, keepdims=True)
    return scores, top


def attend_kernel(seg_q_ref, seg_k_ref, q_ref, k_ref, v_ref, mixed_ref, state_ref):
    queries = q_ref[...] * jnp.bfloat16(0.125)
    low = lax.broadcasted_iota(jnp.int32, k_ref.shape, 1) < 64
    allowed = seg_k_ref[...] == seg_q_ref[...]
    for side in range(2):
        scores, top = attend_parts(side, queries, k_ref[...], None, allowed, low)
        weights = jnp.exp(scores - top)
        state_ref[0, side : side + 1, :] = top
        state_ref[0, side + 2 : side + 3, :] = jnp.sum(weights, axis=0, keepdims=True)
        mixed = rows_dot(v_ref[...], weights.astype(jnp.bfloat16))
        mixed_ref[side * 64 : (side + 1) * 64, :] = mixed[side * 64 : (side + 1) * 64, :]


def attend_far_kernel(seg_q_ref, seg_k_ref, q_ref, k_ref, v_ref, mixed_ref, state_ref, out_ref, low_ref, away_ref, lse_ref):
    queries = q_ref[...] * jnp.bfloat16(0.125)
    low = lax.broadcasted_iota(jnp.int32, k_ref.shape, 1) < 64
    allowed = seg_k_ref[...] == seg_q_ref[...]
    pieces = []
    for side in range(2):
        scores, top = attend_parts(side, queries, k_ref[...], None, allowed, low)
        near_top = state_ref[0, side : side + 1, :]
        top = jnp.maximum(top, near_top)
        weights = jnp.exp(scores - top)
        rescale = jnp.exp(near_top - top)
        total = state_ref[0, side + 2 : side + 3, :] * rescale + jnp.sum(weights, axis=0, keepdims=True)
        mixed = rows_dot(v_ref[...], weights.astype(jnp.bfloat16))[side * 64 : (side + 1) * 64, :]
        pieces.append((mixed + mixed_ref[side * 64 : (side + 1) * 64, :] * rescale) / total)
        lse_ref[0, side : side + 1, :] = top + jnp.log(total)
    attended = jnp.concatenate(pieces, axis=0).T
    own = low_ref.shape[0]
    out_ref[...] = attended
    low_ref[...] = attended[:own, :].astype(jnp.bfloat16)
    away_ref[...] = attended[own:, :].astype(jnp.bfloat16)


def attend_specs(frames, length, pairs):
    return [
        pl.BlockSpec((1, frames), lambda p: (0, 0)),
        pl.BlockSpec((length, 1), lambda p: (0, 0)),
        pl.BlockSpec((frames, 128), lambda p: (0, p)),
        pl.BlockSpec((length, 128), lambda p: (0, p)),
        pl.BlockSpec((length, 128), lambda p: (0, pairs + p)),
    ]


def attend_cost(frames, length, pairs, products):
    return cost(
        flops=4 * products * pairs * frames * length * 128,
        bytes_accessed=16 * frames * pairs * 128,
        transcendentals=2 * pairs * frames * length,
    )


def attend_near(queries, pair, seg_q, seg_k):
    frames, width = queries.shape
    length = pair.shape[0]
    pairs = width // 128
    return pl.pallas_call(
        attend_kernel,
        grid=(pairs,),
        in_specs=attend_specs(frames, length, pairs),
        out_specs=[
            pl.BlockSpec((128, frames), lambda p: (p, 0)),
            pl.BlockSpec((1, 8, frames), lambda p: (p, 0, 0)),
        ],
        out_shape=[
            jax.ShapeDtypeStruct((width, frames), jnp.float32),
            jax.ShapeDtypeStruct((pairs, 8, frames), jnp.float32),
        ],
        compiler_params=pltpu.CompilerParams(vmem_limit_bytes=VMEM_LIMIT),
        cost_estimate=attend_cost(frames, length, pairs, 2),
        name="attend_near",
    )(seg_q.reshape(1, -1), seg_k.reshape(-1, 1), queries, pair, pair)


def attend_far(queries, pair, seg_q, seg_k, mixed, state):
    frames, width = queries.shape
    length = pair.shape[0]
    pairs = width // 128
    return pl.pallas_call(
        attend_far_kernel,
        grid=(pairs,),
        in_specs=attend_specs(frames, length, pairs)
        + [
            pl.BlockSpec((128, frames), lambda p: (p, 0)),
            pl.BlockSpec((1, 8, frames), lambda p: (p, 0, 0)),
        ],
        out_specs=[
            pl.BlockSpec((frames, 128), lambda p: (0, p)),
            pl.BlockSpec((frames // 2, 128), lambda p: (0, p)),
            pl.BlockSpec((frames // 2, 128), lambda p: (0, p)),
            pl.BlockSpec((1, 8, frames), lambda p: (p, 0, 0)),
        ],
        out_shape=[
            jax.ShapeDtypeStruct((frames, width), jnp.float32),
            jax.ShapeDtypeStruct((frames // 2, width), jnp.bfloat16),
            jax.ShapeDtypeStruct((frames // 2, width), jnp.bfloat16),
            jax.ShapeDtypeStruct((pairs, 8, frames), jnp.float32),
        ],
        compiler_params=pltpu.CompilerParams(vmem_limit_bytes=VMEM_LIMIT),
        cost_estimate=attend_cost(frames, length, pairs, 2),
        name="attend_far",
    )(seg_q.reshape(1, -1), seg_k.reshape(-1, 1), queries, pair, pair, mixed, state)


def attend_back_kernel(seg_q_ref, seg_k_ref, q_ref, k_ref, v_ref, g_ref, a_ref, lse_ref, after_ref, dq_ref, dkv_ref):
    queries = q_ref[...] * jnp.bfloat16(0.125)
    key_count = k_ref.shape[0]
    low = lax.broadcasted_iota(jnp.int32, (key_count, 128), 1) < 64
    keys, values, grads = k_ref[...], v_ref[...], g_ref[...]
    allowed = seg_k_ref[...] == seg_q_ref[...]
    products = (grads.astype(jnp.float32) * a_ref[...]).T
    dq, dk, dv = [], [], []
    for side in range(2):
        mine = low if side == 0 else jnp.logical_not(low)
        zero = jnp.zeros_like(keys)
        scores = lanes_dot(jnp.where(mine, keys, zero), queries)
        probs = jnp.where(allowed, jnp.exp(scores - lse_ref[0, side : side + 1, :]), 0.0)
        dots = jnp.sum(products[side * 64 : (side + 1) * 64, :], axis=0, keepdims=True)
        dv.append(jnp.dot(probs.astype(jnp.bfloat16), grads, preferred_element_type=jnp.float32))
        grad_probs = lanes_dot(jnp.where(mine, values, zero), grads)
        grad_scores = (probs * (grad_probs - dots)).astype(jnp.bfloat16)
        dk.append(jnp.dot(grad_scores, queries, preferred_element_type=jnp.float32))
        dq.append(rows_dot(keys, grad_scores)[side * 64 : (side + 1) * 64, :])
    dq_ref[...] = 0.125 * jnp.concatenate(dq, axis=0).T
    dkv_ref[0] = jnp.where(low, dk[0], dk[1]).astype(dkv_ref.dtype)
    dkv_ref[1] = jnp.where(low, dv[0], dv[1]).astype(dkv_ref.dtype)


def attend_back(queries, pair, grads, attended, lse, seg_q, seg_k, kind, after):
    frames, width = queries.shape
    length = pair.shape[0]
    pairs = width // 128
    return pl.pallas_call(
        attend_back_kernel,
        grid=(pairs,),
        in_specs=attend_specs(frames, length, pairs)
        + [
            pl.BlockSpec((frames, 128), lambda p: (0, p)),
            pl.BlockSpec((frames, 128), lambda p: (0, p)),
            pl.BlockSpec((1, 8, frames), lambda p: (p, 0, 0)),
            pl.BlockSpec(memory_space=pl.ANY),
        ],
        out_specs=[
            pl.BlockSpec((frames, 128), lambda p: (0, p)),
            pl.BlockSpec((2, length, 128), lambda p: (0, 0, p)),
        ],
        out_shape=[
            jax.ShapeDtypeStruct((frames, width), jnp.float32),
            jax.ShapeDtypeStruct((2, length, width), kind),
        ],
        compiler_params=pltpu.CompilerParams(vmem_limit_bytes=VMEM_LIMIT),
        cost_estimate=attend_cost(frames, length, pairs, 5),
        name="attend_back",
    )(seg_q.reshape(1, -1), seg_k.reshape(-1, 1), queries, pair, pair, grads, attended, lse, after)


def phi_parts(values):
    below = 0.5 * (1.0 + lax.erf(values * (0.5**0.5)))
    density = jnp.exp(-0.5 * values * values) * (1.0 / math.sqrt(2.0 * math.pi))
    return below, density


def norm_parts(values):
    center = values - jnp.mean(values, axis=-1, keepdims=True)
    scale = lax.rsqrt(jnp.mean(center * center, axis=-1, keepdims=True) + epsilon)
    return center * scale, scale


def norm_back(grad, hat, scale, gain):
    inner = grad * gain
    mean_inner = jnp.mean(inner, axis=-1, keepdims=True)
    mean_hat = jnp.mean(inner * hat, axis=-1, keepdims=True)
    return (inner - mean_inner - hat * mean_hat) * scale


def column_sum(values):
    return jnp.sum(values, axis=0, keepdims=True)


def by_core(core, mine, other):
    return jnp.where(core == 0, mine, other), jnp.where(core == 0, other, mine)


def mix_kernel(first, meta, *refs):
    if first:
        mine_ref, other_ref, gain_ref, shift_ref, w_ref, bias_ref = refs[:6]
        theirs_ref, ours_ref, normed_ref, position_ref = refs[-4:]
    else:
        normed_ref, w_ref, bias_ref = refs[:3]
        theirs_ref, ours_ref = refs[-2:]
    step = pl.program_id(0)
    half = w_ref.shape[1]
    if first:

        @pl.when(step == 0)
        def _():
            left, right = by_core(meta[0], mine_ref[...], other_ref[...])
            position_ref[:, :half] = left
            position_ref[:, half:] = right
            hat, _ = norm_parts(position_ref[...])
            normed_ref[...] = (hat * gain_ref[...] + shift_ref[...]).astype(jnp.bfloat16)

    block = jnp.dot(normed_ref[...], w_ref[...], preferred_element_type=jnp.float32) + bias_ref[...]
    block = block.astype(jnp.bfloat16)
    parts = theirs_ref.shape[1] // half

    @pl.when(step < parts)
    def _():
        theirs_ref[:, pl.ds(pl.multiple_of(step * half, half), half)] = block

    @pl.when(step >= parts)
    def _():
        ours_ref[:, pl.ds(pl.multiple_of((step - parts) * half, half), half)] = block


def mix_rows(core, sources, weight, bias, begin, parts, after=()):
    first = len(sources) > 1
    tokens = sources[0].shape[0]
    features = weight.shape[0]
    half = features // 2

    def column(i, meta):
        return 2 * (begin + i % parts) + jnp.where(i < parts, 1 - meta[0], meta[0])

    whole = lambda shape: pl.BlockSpec(shape, lambda i, meta: (0, 0))
    out_specs = [whole((tokens, parts * half))] * 2
    out_shape = [jax.ShapeDtypeStruct((tokens, parts * half), jnp.bfloat16)] * 2
    if first:
        out_specs = out_specs + [whole((tokens, features))] * 2
        out_shape = out_shape + [jax.ShapeDtypeStruct((tokens, features), kind) for kind in (jnp.bfloat16, jnp.float32)]
    return pl.pallas_call(
        partial(mix_kernel, first),
        grid_spec=pltpu.PrefetchScalarGridSpec(
            num_scalar_prefetch=1,
            grid=(2 * parts,),
            in_specs=[whole(item.shape) for item in sources]
            + [
                pl.BlockSpec((features, half), lambda i, meta: (0, column(i, meta))),
                pl.BlockSpec((1, half), lambda i, meta: (0, column(i, meta))),
            ]
            + [pl.BlockSpec(memory_space=pl.ANY)] * len(after),
            out_specs=out_specs,
        ),
        out_shape=out_shape,
        compiler_params=pltpu.CompilerParams(vmem_limit_bytes=VMEM_LIMIT, dimension_semantics=IN_ORDER),
        cost_estimate=cost(
            flops=4 * parts * tokens * half * features, bytes_accessed=4 * parts * half * features, transcendentals=0
        ),
        name="norm_keys_values" if first else "queries",
    )(core, *sources, weight, bias, *after)


def unmix_kernel(
    meta, mine_ref, other_ref, w_ref, position_ref, resid_ref, gain_ref, *refs
):
    ours_ref, theirs_ref, sums_ref, total = refs[-4:]
    step = pl.program_id(0)
    half = theirs_ref.shape[1]

    @pl.when(step == 0)
    def _():
        total[...] = jnp.zeros_like(total)

    block = jnp.where(step < 3, mine_ref[...], other_ref[...])
    total[...] += lanes_dot(block, w_ref[...])

    @pl.when(step == 5)
    def _():
        grad = total[...]
        hat, scale = norm_parts(position_ref[...])
        sums_ref[0:1, :] = column_sum(grad * hat)
        sums_ref[1:2, :] = column_sum(grad)
        sums_ref[2:8, :] = jnp.zeros((6, 2 * half), jnp.float32)
        result = resid_ref[...] + norm_back(grad, hat, scale, gain_ref[...])
        low_half, high_half = result[:, :half], result[:, half:]
        ours_ref[...] = jnp.where(meta[0] == 0, low_half, high_half)
        theirs_ref[...] = jnp.where(meta[0] == 0, high_half, low_half)


def unmix_rows(core, mine, other, weight, position, grad_resid, gain, after):
    tokens, features = position.shape
    half = features // 2

    def column(i, meta):
        return 2 * (i % 3) + jnp.where(i < 3, meta[0], 1 - meta[0])

    whole = lambda shape: pl.BlockSpec(shape, lambda i, meta: (0, 0))
    return pl.pallas_call(
        unmix_kernel,
        grid_spec=pltpu.PrefetchScalarGridSpec(
            num_scalar_prefetch=1,
            grid=(6,),
            in_specs=[
                pl.BlockSpec((tokens, half), lambda i, meta: (0, i % 3)),
                pl.BlockSpec((tokens, half), lambda i, meta: (0, i % 3)),
                pl.BlockSpec((features, half), lambda i, meta: (0, column(i, meta))),
                whole((tokens, features)),
                whole((tokens, features)),
                whole((1, features)),
            ]
            + [pl.BlockSpec(memory_space=pl.ANY)] * len(after),
            out_specs=[whole((tokens, half)), whole((tokens, half)), whole((8, features))],
            scratch_shapes=[pltpu.VMEM((tokens, features), jnp.float32)],
        ),
        out_shape=[
            jax.ShapeDtypeStruct((tokens, half), jnp.float32),
            jax.ShapeDtypeStruct((tokens, half), jnp.float32),
            jax.ShapeDtypeStruct((8, features), jnp.float32),
        ],
        compiler_params=pltpu.CompilerParams(vmem_limit_bytes=VMEM_LIMIT, dimension_semantics=IN_ORDER),
        cost_estimate=cost(flops=12 * tokens * half * features, bytes_accessed=14 * half * features, transcendentals=0),
        name="qkv_and_norm_back",
    )(core, mine, other, weight, position, grad_resid, gain, *after)


def pack_places(features, width):
    places, at = {}, 0
    for name, size in (
        ("active", width), ("second", features), ("attended", features), ("up", width // 2),
        ("out", features // 2), ("branch", features // 2),
    ):
        places[name] = at
        at += size
    places["all"] = at
    return places


def middle_kernel(
    meta, mine_ref, other_ref, position_ref, w_out_ref, w_up_ref, w_down_ref, up_bias_ref, head_w_ref, head_b_ref,
    labels_ref, rows_ref,
    pack_ref, output_ref, out_low_ours, up_ours, branch_ours, att_ours, att_theirs, resid_grad_ref, sums_ref,
    up_sums_ref, head_ref, last_ref,
    resid, total, slope, grad_out, grad_low,
):
    step = pl.program_id(0)
    chunks = slope.shape[0]
    core = meta[0]
    half = mine_ref.shape[1]
    features = 2 * half
    chunk_width = slope.shape[2]
    places = pack_places(features, chunks * chunk_width)

    def at(name, size):
        return slice(places[name], places[name] + size)

    second_at, attended_at = at("second", features), at("attended", features)

    def store_halves(ours, theirs, values):
        low_half, high_half = values[:, :half], values[:, half:]
        ours[...] = jnp.where(core == 0, low_half, high_half)
        theirs[...] = jnp.where(core == 0, high_half, low_half)

    @pl.when(step == 0)
    def _():
        left, right = by_core(core, mine_ref[...].astype(jnp.float32), other_ref[...].astype(jnp.float32))
        pack_ref[:, places["attended"] : places["attended"] + half] = left.astype(jnp.bfloat16)
        pack_ref[:, places["attended"] + half : places["attended"] + features] = right.astype(jnp.bfloat16)
        resid[...] = (
            position_ref[...]
            + jnp.dot(pack_ref[:, attended_at], w_out_ref[...], preferred_element_type=jnp.float32)
            + rows_ref[2:3, :]
        )
        hat, _ = norm_parts(resid[...])
        pack_ref[:, second_at] = (hat * rows_ref[0:1, :] + rows_ref[1:2, :]).astype(jnp.bfloat16)
        total[...] = jnp.zeros_like(total)

    @pl.when(step < chunks)
    def _():
        raised = jnp.dot(pack_ref[:, second_at], w_up_ref[...], preferred_element_type=jnp.float32) + up_bias_ref[...]
        below, density = phi_parts(raised)
        slope[step] = below + raised * density
        active = (raised * below).astype(jnp.bfloat16)
        pack_ref[:, pl.ds(pl.multiple_of(places["active"] + step * chunk_width, chunk_width), chunk_width)] = active
        total[...] += jnp.dot(active, w_down_ref[...], preferred_element_type=jnp.float32)

    @pl.when(step == chunks - 1)
    def _():
        low = (resid[...] + total[...] + rows_ref[3:4, :]).astype(jnp.bfloat16)
        output_ref[...] = low
        logits = jnp.dot(low, head_w_ref[...], preferred_element_type=jnp.float32) + head_b_ref[...]
        top = jnp.max(logits, axis=-1, keepdims=True)
        shifted = jnp.exp(logits - top)
        sums = jnp.sum(shifted, axis=-1, keepdims=True)
        onehot = labels_ref[...] == lax.broadcasted_iota(jnp.int32, logits.shape, 1)
        picked = jnp.sum(jnp.where(onehot, logits, 0.0), axis=-1, keepdims=True)
        loss = jnp.sum(top + jnp.log(sums) - picked)
        grad_logits = (shifted / sums - onehot.astype(jnp.float32)).astype(jnp.bfloat16)
        head_ref[...] = rows_dot(grad_logits, low)
        last_ref[...] = jnp.zeros_like(last_ref)
        last_ref[0:1, 0:VOCAB] = column_sum(grad_logits.astype(jnp.float32))
        last_ref[1:2, :] = jnp.full((1, 128), loss, jnp.float32)
        grad = lanes_dot(grad_logits, head_w_ref[...])
        grad_out[...] = grad
        grad_low[...] = grad.astype(jnp.bfloat16)
        store_halves(out_low_ours, pack_ref.at[:, at("out", half)], grad_low[...])
        sums_ref[3:4, :] = column_sum(grad_low[...].astype(jnp.float32))
        sums_ref[4:8, :] = jnp.zeros((4, 2 * half), jnp.float32)
        total[...] = jnp.zeros_like(total)

    @pl.when(step >= chunks)
    def _():
        chunk = 2 * chunks - 1 - step
        grad = lanes_dot(grad_low[...], w_down_ref[...]) * slope[chunk]
        low = grad.astype(jnp.bfloat16)
        up_sums_ref[0] = jnp.broadcast_to(column_sum(low.astype(jnp.float32)), up_sums_ref.shape[1:])
        total[...] += lanes_dot(low, w_up_ref[...])
        ours = (chunk >= chunks // 2) == (core == 1)

        @pl.when(ours)
        def _():
            up_ours[...] = low

        @pl.when(jnp.logical_not(ours))
        def _():
            place = places["up"] + (chunk & (chunks // 2 - 1)) * chunk_width
            pack_ref[:, pl.ds(pl.multiple_of(place, chunk_width), chunk_width)] = low

    @pl.when(step == 2 * chunks - 1)
    def _():
        hat, scale = norm_parts(resid[...])
        grad = total[...]
        sums_ref[0:1, :] = column_sum(grad * hat)
        sums_ref[2:3, :] = column_sum(grad)
        result = grad_out[...] + norm_back(grad, hat, scale, rows_ref[0:1, :])
        resid_grad_ref[...] = result
        branch = result.astype(jnp.bfloat16)
        store_halves(branch_ours, pack_ref.at[:, at("branch", half)], branch)
        sums_ref[1:2, :] = column_sum(branch.astype(jnp.float32))
        store_halves(att_ours, att_theirs, lanes_dot(branch, w_out_ref[...]).astype(jnp.bfloat16))


def middle(core, mine, other, position, w_out, w_up, w_down, up_bias, head_w, head_b, labels, rows):
    tokens, features = position.shape
    half = features // 2
    width = w_up.shape[1]
    chunks = 4
    chunk = width // chunks
    vocab = head_w.shape[1]
    last = 2 * chunks - 1

    def part(i):
        return jnp.where(i < chunks, i, last - i)

    def own_up(i, meta):
        back = part(jnp.maximum(i, chunks))
        return jnp.where(meta[0] == 0, jnp.minimum(back, chunks // 2 - 1), jnp.maximum(back - chunks // 2, 0))

    whole = lambda shape: pl.BlockSpec(shape, lambda i, meta: tuple(0 for _ in shape))
    low = lambda *shape: jax.ShapeDtypeStruct(shape, jnp.bfloat16)
    full = lambda *shape: jax.ShapeDtypeStruct(shape, jnp.float32)
    return pl.pallas_call(
        middle_kernel,
        grid_spec=pltpu.PrefetchScalarGridSpec(
            num_scalar_prefetch=1,
            grid=(2 * chunks,),
            in_specs=[
                whole((tokens, half)),
                whole((tokens, half)),
                whole((tokens, features)),
                whole((features, features)),
                pl.BlockSpec((features, chunk), lambda i, meta: (0, part(i))),
                pl.BlockSpec((chunk, features), lambda i, meta: (part(i), 0)),
                pl.BlockSpec((1, chunk), lambda i, meta: (0, part(i))),
                whole((features, vocab)),
                whole((1, vocab)),
                whole((tokens, 1)),
                whole((8, features)),
            ],
            out_specs=[
                whole((tokens, pack_places(features, width)["all"])),
                whole((tokens, features)),
                whole((tokens, half)),
                pl.BlockSpec((tokens, chunk), lambda i, meta: (0, own_up(i, meta))),
                whole((tokens, half)),
                whole((tokens, half)),
                whole((tokens, half)),
                whole((tokens, features)),
                whole((8, features)),
                pl.BlockSpec((1, 8, chunk), lambda i, meta: (part(jnp.maximum(i, chunks)), 0, 0)),
                whole((vocab, features)),
                whole((8, 128)),
            ],
            scratch_shapes=[
                pltpu.VMEM((tokens, features), jnp.float32),
                pltpu.VMEM((tokens, features), jnp.float32),
                pltpu.VMEM((chunks, tokens, chunk), jnp.float32),
                pltpu.VMEM((tokens, features), jnp.float32),
                pltpu.VMEM((tokens, features), jnp.bfloat16),
            ],
        ),
        out_shape=[
            low(tokens, pack_places(features, width)["all"]),
            low(tokens, features),
            low(tokens, half),
            low(tokens, width // 2),
            low(tokens, half),
            low(tokens, half),
            low(tokens, half),
            full(tokens, features),
            full(8, features),
            full(chunks, 8, chunk),
            full(vocab, features),
            full(8, 128),
        ],
        compiler_params=pltpu.CompilerParams(vmem_limit_bytes=VMEM_LIMIT, dimension_semantics=IN_ORDER),
        cost_estimate=cost(
            flops=8 * tokens * features * width, bytes_accessed=8 * features * width, transcendentals=2 * tokens * width
        ),
        name="middle",
    )(core, mine, other, position, w_out, w_up, w_down, up_bias, head_w, head_b, labels, rows)


def conv_grad_kernel(meta, ours_ref, got_ref, slope_ref, *refs):
    position_ref, grad_ref, edge_ref, own_ref, to_x_ref, to_y_ref, to_xy_ref, sums_ref = refs[-8:]
    core, y, x = meta[0], meta[1], meta[2]
    frames = ours_ref.shape[0]
    rim = edge_ref.shape[0]
    ours, got = ours_ref[...], got_ref[...]
    position_ref[0:frames, :] = jnp.where(core == 0, ours, got)
    position_ref[frames:, :] = jnp.where(core == 0, got, ours)
    grad_ref[...] = (position_ref[...] * slope_ref[...]).astype(jnp.bfloat16)
    side = x ^ (meta[3] & 1)
    edge_ref[...] = jnp.where(side == 0, grad_ref[2 * frames - rim :, :], grad_ref[0:rim, :])
    sums_ref[...] = jnp.broadcast_to(column_sum(grad_ref[...].astype(jnp.float32)), sums_ref.shape)
    for ref, yy, xx in ((own_ref, y, x), (to_x_ref, y, 1 - x), (to_y_ref, 1 - y, x), (to_xy_ref, 1 - y, 1 - x)):
        ref[...] = grad_ref[:, pl.ds(pl.multiple_of(256 * xx + 128 * yy, 128), 128)]


def conv_grad_rows(meta, ours, got, slope, after):
    frames, half = ours.shape
    operands = (ours, got, slope)
    shapes = [((2 * frames, half), jnp.float32), ((2 * frames, half), jnp.bfloat16), ((KERNEL // 2, half), jnp.bfloat16)]
    shapes += [((2 * frames, 128), jnp.bfloat16)] * 4 + [((8, half), jnp.float32)]
    return pl.pallas_call(
        conv_grad_kernel,
        grid_spec=pltpu.PrefetchScalarGridSpec(
            num_scalar_prefetch=1,
            grid=(1,),
            in_specs=[pl.BlockSpec(item.shape, lambda i, m: (0, 0)) for item in operands]
            + [pl.BlockSpec(memory_space=pl.ANY)] * len(after),
            out_specs=[pl.BlockSpec(shape, lambda i, m: (0, 0)) for shape, _ in shapes],
        ),
        out_shape=[jax.ShapeDtypeStruct(shape, kind) for shape, kind in shapes],
        compiler_params=pltpu.CompilerParams(vmem_limit_bytes=VMEM_LIMIT, dimension_semantics=IN_ORDER),
        cost_estimate=cost(flops=0, bytes_accessed=4000000, transcendentals=0),
        name="conv_grad_rows",
    )(meta, *operands, *after)


def weight_kernel(tasks, out_count, meta, *refs):
    refs = list(refs)
    step = pl.program_id(0)
    inputs = []
    for task in tasks:
        count = 1 if task["right"] is None else 4
        inputs.append([refs.pop(0) for _ in range(count + (task["add"] is not None))])
    outs = refs[-out_count:]
    begin = 0
    for task, ins in zip(tasks, inputs):
        if task["joint"]:
            begin = begin - task["blocks"]
        rows, columns = task["rows"], task["columns"]

        def store(where, values, at, task=task):
            index, column = where
            size = values.shape[0]
            span = pl.ds(pl.multiple_of(at * size, size), size)
            outs[index][span, column : column + values.shape[1]] = values.astype(jnp.bfloat16)

        @pl.when(jnp.logical_and(step >= begin, step < begin + task["blocks"]))
        def _(task=task, ins=ins, begin=begin, store=store, rows=rows, columns=columns):
            if task["right"] is None:
                total = ins[0][...].astype(jnp.float32)
            else:
                total = rows_dot(ins[0][...], ins[2][...]) + rows_dot(ins[1][...], ins[3][...])
            if task["add"] is not None:
                total = total + ins[-1][...].astype(jnp.float32)
            at = step - begin + task["place"]
            if task["split"] is None:
                for where in task["outs"]:
                    store(where, total, at)
                return
            if task["split"] == "columns":
                first, second = total[:, : columns // 2], total[:, columns // 2 :]
            else:
                blocks = total.reshape(-1, 2, task["unit"], columns)
                first, second = (blocks[:, k].reshape(rows // 2, columns) for k in range(2))
            bit = task["bit"](meta)
            store(task["outs"][0], jnp.where(bit == 0, second, first), at)
            store(task["outs"][1], jnp.where(bit == 0, first, second), at)

        begin = begin + task["blocks"]


def weight_task(
    outs, left, right, rows, blocks, row_of, columns, column_of, add=None, add_of=None, split=None, bit=None, unit=0, place=0,
    joint=False,
):
    return dict(
        outs=outs, left=left, right=right, rows=rows, blocks=blocks, row_of=row_of, columns=columns,
        column_of=column_of, add=add, add_of=add_of, split=split, bit=bit, unit=unit, place=place,
        joint=joint,
    )


def weight_parts(meta, tasks, shapes, name, after):
    in_specs, operands = [], []
    begin, flops, moved = 0, 0, 0
    for task in tasks:
        rows, columns, blocks = task["rows"], task["columns"], task["blocks"]
        if task["joint"]:
            begin -= blocks
        tokens = task["left"][0][0].shape[0]
        if task["right"] is None:
            in_specs.append(
                pl.BlockSpec((rows, columns), lambda i, m, t=task, begin=begin, blocks=blocks: (t["row_of"](jnp.clip(i - begin, 0, blocks - 1), m), 0))
            )
            operands.append(task["left"][0][0])

        def local(i, begin=begin, blocks=blocks):
            return jnp.clip(i - begin, 0, blocks - 1)

        for array, base in task["left"] if task["right"] is not None else ():
            in_specs.append(
                pl.BlockSpec(
                    (tokens, rows), lambda i, m, t=task, local=local, base=base: (0, base // t["rows"] + t["row_of"](local(i), m))
                )
            )
            operands.append(array)
        for array, base in task["right"] or ():
            in_specs.append(
                pl.BlockSpec((tokens, columns), lambda i, m, t=task, base=base: (0, base // t["columns"] + t["column_of"](m)))
            )
            operands.append(array)
        if task["add"] is not None:
            in_specs.append(pl.BlockSpec((rows, columns), lambda i, m, t=task, local=local: t["add_of"](local(i), m)))
            operands.append(task["add"])
        begin += blocks
        flops += 4 * tokens * rows * blocks * columns
        moved += 2 * rows * blocks * columns + 4 * tokens * (rows * blocks + columns)
    in_specs += [pl.BlockSpec(memory_space=pl.ANY)] * len(after)
    operands += list(after)
    return pl.pallas_call(
        partial(weight_kernel, tasks, len(shapes)),
        grid_spec=pltpu.PrefetchScalarGridSpec(
            num_scalar_prefetch=1,
            grid=(begin,),
            in_specs=in_specs,
            out_specs=[pl.BlockSpec(shape, lambda i, m: (0, 0)) for shape in shapes],
        ),
        out_shape=[jax.ShapeDtypeStruct(shape, jnp.bfloat16) for shape in shapes],
        compiler_params=pltpu.CompilerParams(vmem_limit_bytes=VMEM_LIMIT, dimension_semantics=IN_ORDER),
        cost_estimate=cost(flops=flops, bytes_accessed=moved, transcendentals=0),
        name=name,
    )(meta, *operands)


def flip_kernel(meta, own_ref, got_ref, out_ref):
    source = jnp.where(pl.program_id(0) < 4, own_ref[0], got_ref[0])
    out_ref[...] = source.astype(jnp.float32).T


def flip_columns(meta, own, got):
    _, width, rows = own.shape
    count = 8

    def column(i, m):
        return 4 * (m[0] ^ (i >> 2)) + 2 * (i & 1) + (m[1] ^ ((i >> 1) & 1))

    return pl.pallas_call(
        flip_kernel,
        grid_spec=pltpu.PrefetchScalarGridSpec(
            num_scalar_prefetch=1,
            grid=(count,),
            in_specs=[
                pl.BlockSpec((1, width, rows), lambda i, m: (jnp.minimum(i, 3), 0, 0)),
                pl.BlockSpec((1, width, rows), lambda i, m: (jnp.maximum(i - 4, 0), 0, 0)),
            ],
            out_specs=pl.BlockSpec((rows, width), lambda i, m: (0, column(i, m))),
        ),
        out_shape=jax.ShapeDtypeStruct((rows, count * width), jnp.float32),
        compiler_params=pltpu.CompilerParams(vmem_limit_bytes=VMEM_LIMIT, dimension_semantics=IN_ORDER),
        cost_estimate=cost(flops=0, bytes_accessed=6 * count * width * rows, transcendentals=0),
        name="flip_columns",
    )(meta, own, got)


def small_kernel(meta, head_ref, mid_ref, first_ref, conv_ref, ours_ref, got_ref, up_ref, last_ref, *refs):
    out_ref = refs[-1]
    core = meta[0]
    half = conv_ref.shape[1]
    zero = jnp.zeros((1, half), jnp.float32)
    wide = lambda *parts: jnp.concatenate(parts, axis=1)

    def halves(part):
        ours = ours_ref[0:1, part * half : (part + 1) * half]
        got = got_ref[0:1, part * half : (part + 1) * half]
        return wide(jnp.where(core == 0, ours, got), jnp.where(core == 0, got, ours))

    conv = conv_ref[0:1, :]
    unit = last_ref.shape[1]
    rows = [
        head_ref[...],
        mid_ref[0:4, :],
        first_ref[0:2, :],
        wide(jnp.where(core == 0, conv, zero), jnp.where(core == 0, zero, conv)),
        halves(0),
        halves(2),
    ]
    rows += [wide(*(up_ref[j, 0:1, r * unit : (r + 1) * unit] for j in range(8))) for r in range(4)]
    rows += [wide(*([last_ref[...]] * 8)), jnp.zeros((128 - VOCAB - 14, 2 * half), jnp.float32)]
    out_ref[...] = jnp.concatenate(rows, axis=0).T.astype(out_ref.dtype)


def small_sums(meta, head, mid, first, conv, ours, got, up, last):
    operands = (head, mid, first, conv, ours, got, up, last)
    features = head.shape[1]
    return pl.pallas_call(
        small_kernel,
        grid_spec=pltpu.PrefetchScalarGridSpec(
            num_scalar_prefetch=1,
            grid=(1,),
            in_specs=[pl.BlockSpec(item.shape, lambda i, m, n=item.ndim: (0,) * n) for item in operands],
            out_specs=pl.BlockSpec((features, 128), lambda i, m: (0, 0)),
        ),
        out_shape=jax.ShapeDtypeStruct((features, 128), jnp.bfloat16),
        compiler_params=pltpu.CompilerParams(vmem_limit_bytes=VMEM_LIMIT, dimension_semantics=IN_ORDER),
        cost_estimate=cost(flops=0, bytes_accessed=400000, transcendentals=0),
        name="small_sums",
    )(meta, *operands)


def tile_lists(seg_ext, rise):
    row_count = seg_ext.shape[0]
    frames = seg_ext.shape[1] - KERNEL
    tiles = frames // 64
    center = seg_ext[:, KERNEL // 2 : KERNEL // 2 + frames].reshape(row_count, tiles, 64)
    first = center[:, :, 0].reshape(-1)
    counts = (center[:, :, 63].reshape(-1) - first + 1).astype(jnp.int32)
    ends = jnp.cumsum(counts)
    slots = row_count * (tiles + rise)
    slot = jnp.arange(slots, dtype=jnp.int32)
    tile = jnp.sum((slot[:, None] >= ends[None, :]).astype(jnp.int32), axis=1)
    used = tile < row_count * tiles
    tile = jnp.minimum(tile, row_count * tiles - 1)
    onehot = tile[:, None] == jnp.arange(row_count * tiles, dtype=jnp.int32)[None, :]
    begin = jnp.sum(jnp.where(onehot, (ends - counts)[None, :], 0), axis=1)
    number = jnp.sum(jnp.where(onehot, first[None, :], 0), axis=1) + slot - begin
    number = jnp.where(used, number, -2)
    in_block = tile + (tile // tiles) * (KERNEL // 64)
    return in_block.astype(jnp.int32), tile.astype(jnp.int32), number.astype(jnp.int32)


def lane_low(rows):
    return lax.broadcasted_iota(jnp.int32, (rows, 128), 1) < 64


def half_roll(block):
    return pltpu.roll(block, 64, 1)


def quad_rows(src, rows, side):
    low = lane_low(rows)
    parts = [src[pl.ds(j, rows, stride=4), :] for j in range(4)]
    halves = []
    for a, b in ((0, 1), (2, 3)):
        if side == 0:
            halves.append(jnp.where(low, parts[a], half_roll(parts[b])))
        else:
            halves.append(jnp.where(low, half_roll(parts[a]), parts[b]))
    return halves


def conv_setup(meta, slots, seg_ref, flat, shifts, masks):
    rows4 = seg_ref.shape[0]
    blocks = rows4 // 16
    one, zero = jnp.ones((16, 256), jnp.bfloat16), jnp.zeros((16, 256), jnp.bfloat16)
    flat[0:rows4, :] = seg_ref[...]
    flat[rows4:, :] = jnp.zeros((16, 256), jnp.float32)
    for p in range(16):
        shifts[p] = flat[pl.ds(p, rows4), :].astype(jnp.bfloat16).reshape(blocks, 16, 256)

    @pl.loop(0, slots)
    def _(v):
        at = meta[1 + v]
        number = jnp.full((16, 256), meta[1 + 2 * slots + v].astype(jnp.float32), jnp.float32).astype(jnp.bfloat16)
        row = pl.multiple_of(v * 16, 16)
        for b in range(TAP_BLOCKS):
            ids = shifts[b % 16, at + b // 16]
            masks[pl.ds(row, 16), b * 256 : (b + 1) * 256] = jnp.where(ids == number, one, zero)


def conv_shifts(wide, side, flat, shifts):
    rows4 = shifts.shape[1] * 16
    halves = quad_rows(wide, rows4, side)
    flat[0:rows4, 0:128] = halves[0]
    flat[0:rows4, 128:256] = halves[1]
    for p in range(16):
        shifts[p] = flat[pl.ds(p, rows4), :].astype(jnp.bfloat16).reshape(rows4 // 16, 16, 256)


def conv_patch(places, b, shifts, masks):
    span = slice(b * 256, (b + 1) * 256)
    pieces = [
        shifts[b % 16, at + b // 16] * masks[v * 16 : (v + 1) * 16, span] for v, at in enumerate(places)
    ]
    return jnp.concatenate(pieces, axis=0)


def conv_taps(w_ref, side, b, taps):
    rows = 256
    low = lane_low(rows)
    depth = w_ref.shape[0]
    zero = jnp.zeros((64, 128), jnp.bfloat16)
    if b == 0:
        here, before = w_ref[0:rows, :], jnp.concatenate([zero, w_ref[0 : rows - 64, :]], axis=0)
    elif b * rows < depth:
        here, before = w_ref[b * rows : (b + 1) * rows, :], w_ref[b * rows - 64 : (b + 1) * rows - 64, :]
    else:
        here, before = jnp.concatenate([zero] * 4, axis=0), jnp.concatenate([w_ref[depth - 64 :, :]] + [zero] * 3, axis=0)
    block = jnp.where(low, here, half_roll(before)) if side == 0 else jnp.where(low, half_roll(here), before)
    taps[128 + b * rows : 128 + (b + 1) * rows, :] = block
    return jnp.concatenate([block, taps[b * rows : (b + 1) * rows, :]], axis=1)


def conv_kernel(slots, backward, meta, x_ref, seg_ref, w_ref, extra_ref, *refs):
    if backward:
        o_ref, *refs = refs[-8:]
    else:
        o_ref, *refs = refs[-9:]
    if backward:
        wide, flat, shifts, masks, taps, sums, outs = refs
    else:
        slope_ref, wide, flat, shifts, masks, taps, sums, outs = refs

    @pl.when(pl.program_id(0) == 0)
    def _():
        conv_setup(meta, slots, seg_ref, flat, shifts, masks)

    wide[...] = x_ref[...].astype(jnp.float32)
    taps[0:128, :] = jnp.zeros((128, 128), jnp.bfloat16)
    out_rows = o_ref.shape[0] // 4
    places = [meta[1 + v] for v in range(slots)]
    for side in range(2):
        conv_shifts(wide, side, flat, shifts)
        total = jnp.zeros((256, slots * 16) if backward else (slots * 16, 256), jnp.float32)
        for b in range(TAP_BLOCKS):
            weight = conv_taps(w_ref, side, b, taps)
            if backward:
                total = total + lanes_dot(weight, conv_patch(places, TAP_BLOCKS - 1 - b, shifts, masks))
            else:
                total = total + jnp.dot(
                    conv_patch(places, b, shifts, masks), weight, preferred_element_type=jnp.float32
                )
        sums[...] = total.T if backward else total

        @pl.loop(0, slots)
        def _(v):
            to = pl.ds(pl.multiple_of(meta[1 + slots + v] * 16, 16), 16)
            row = pl.ds(pl.multiple_of(v * 16, 16), 16)
            keep = masks[row, 16 * 256 : 17 * 256].astype(jnp.float32) > 0.5
            outs[side, to, :] = jnp.where(keep, sums[row, :], outs[side, to, :])

    low = lane_low(out_rows)
    for half in range(2):
        zero_side = outs[0, :, half * 128 : (half + 1) * 128]
        one_side = outs[1, :, half * 128 : (half + 1) * 128]
        wide[pl.ds(2 * half, out_rows, stride=4), :] = jnp.where(low, zero_side, half_roll(one_side))
        wide[pl.ds(2 * half + 1, out_rows, stride=4), :] = jnp.where(low, half_roll(zero_side), one_side)
    result = wide[0 : 4 * out_rows, :]
    if backward:
        o_ref[...] = (extra_ref[...] + result).astype(o_ref.dtype)
    else:
        result = result + extra_ref[...]
        below, density = phi_parts(result)
        center = x_ref[KERNEL // 2 : KERNEL // 2 + 4 * out_rows, :].astype(jnp.float32)
        o_ref[...] = center + result * below
        slope_ref[...] = below + result * density


def seg_quads(seg_ext):
    quads = seg_ext.astype(jnp.float32).reshape(-1, 4)
    return jnp.repeat(quads, 64, axis=1)


def grouped_conv(x_ext, seg_ext, weight, extra, first_pair, rise, backward, begin=0, pairs=None, after=()):
    row_count, length, width = x_ext.shape
    frames = length - KERNEL
    pairs = width // 128 if pairs is None else pairs
    in_block, tile, number = tile_lists(seg_ext, rise)
    slots = in_block.shape[0]
    meta = jnp.concatenate([jnp.reshape(first_pair, (1,)).astype(jnp.int32), in_block, tile, number])
    rows4 = row_count * length // 4
    out4 = row_count * frames // 4
    depth = TAP_BLOCKS * 256
    return pl.pallas_call(
        partial(conv_kernel, slots, backward),
        grid_spec=pltpu.PrefetchScalarGridSpec(
            num_scalar_prefetch=1,
            grid=(pairs,),
            in_specs=[
                pl.BlockSpec((row_count * length, 128), lambda p, meta: (0, begin + p)),
                pl.BlockSpec((rows4, 256), lambda p, meta: (0, 0)),
                pl.BlockSpec((weight.shape[0], 128), lambda p, meta: (0, meta[0] + begin + p)),
                pl.BlockSpec((extra.shape[0], 128), lambda p, meta: (0, begin + p)),
            ]
            + [pl.BlockSpec(memory_space=pl.ANY)] * len(after),
            out_specs=[pl.BlockSpec((row_count * frames, 128), lambda p, meta: (0, p))] * (1 if backward else 2),
            scratch_shapes=[
                pltpu.VMEM((row_count * length, 128), jnp.float32),
                pltpu.VMEM((rows4 + 16, 256), jnp.float32),
                pltpu.VMEM((16, rows4 // 16, 16, 256), jnp.bfloat16),
                pltpu.VMEM((slots * 16, depth), jnp.bfloat16),
                pltpu.VMEM((128 + depth, 128), jnp.bfloat16),
                pltpu.VMEM((slots * 16, 256), jnp.float32),
                pltpu.VMEM((2, out4, 256), jnp.float32),
            ],
        ),
        out_shape=[jax.ShapeDtypeStruct((row_count * frames, 128 * pairs), jnp.bfloat16 if backward else jnp.float32)]
        * (1 if backward else 2),
        compiler_params=pltpu.CompilerParams(vmem_limit_bytes=VMEM_LIMIT, dimension_semantics=IN_ORDER),
        cost_estimate=cost(
            flops=2 * pairs * 2 * slots * 16 * 256 * depth, bytes_accessed=pairs * weight.shape[0] * 256, transcendentals=0
        ),
        name="conv_back" if backward else "conv_forth",
    )(meta, x_ext.reshape(row_count * length, width), seg_quads(seg_ext), weight, extra, *after)


def at_block(b):
    return pl.ds(b * 256, 256) if isinstance(b, int) else pl.ds(pl.multiple_of(b * 256, 256), 256)


def id_block(number):
    return jnp.full((16, 256), number, jnp.float32).astype(jnp.bfloat16)


def conv_ids(seg_ref, flat, ids):
    rows4 = seg_ref.shape[0]
    flat[0:rows4, :] = seg_ref[...]
    flat[rows4:, :] = jnp.zeros((16, 256), jnp.float32)
    for p in range(16):
        ids[p] = flat[pl.ds(p, rows4), :].astype(jnp.bfloat16).reshape(rows4 // 16, 16, 256)


def conv_cut(places, numbers, b, shifts, ids):
    nothing = jnp.zeros((16, 256), jnp.bfloat16)
    pieces = []
    for at, number in zip(places, numbers):
        same = ids[b & 15, at + (b >> 4)] == id_block(number)
        pieces.append(jnp.where(same, shifts[b & 15, at + (b >> 4)], nothing))
    return jnp.concatenate(pieces, axis=0)


def conv_weight_kernel(slots, meta, x_ref, seg_ref, g_ref, *refs):
    send_ref, keep_ref, wide, wide_g, flat, shifts, masks, quads, picks, sums = refs[-10:]
    @pl.when(pl.program_id(0) == 0)
    def _():
        conv_ids(seg_ref, flat, masks)

    wide[...] = x_ref[...].astype(jnp.float32)
    wide_g[...] = g_ref[...].astype(jnp.float32)
    out_rows = g_ref.shape[0] // 4
    low = lane_low(64)
    places = [meta[1 + v] for v in range(slots)]
    numbers = [meta[1 + 2 * slots + v].astype(jnp.float32) for v in range(slots)]
    nothing = jnp.zeros((16, 256), jnp.bfloat16)
    for side in range(2):
        conv_shifts(wide, side, flat, shifts)
        halves = quad_rows(wide_g, out_rows, side)
        quads[:, 0:128] = halves[0].astype(jnp.bfloat16)
        quads[:, 128:256] = halves[1].astype(jnp.bfloat16)

        for v in range(slots):
            at = pl.ds(pl.multiple_of(meta[1 + slots + v] * 16, 16), 16)
            same = masks[0, places[v] + 1] == id_block(numbers[v])
            picks[v * 16 : (v + 1) * 16, :] = jnp.where(same, quads[at, :], nothing)

        turned = picks[...].T

        @pl.loop(0, TAP_BLOCKS, unroll=DW_UNROLL)
        def _(b):
            sums[:, at_block(b)] = jnp.dot(
                turned, conv_cut(places, numbers, b, shifts, masks), preferred_element_type=jnp.float32
            )

        def piece(j, q):
            return sums[j * 64 : (j + 1) * 64, q * 128 : (q + 1) * 128]

        def odd(q):
            return half_roll(piece(1, q) + piece(3, q + 1))

        def emit(block, ref):
            left = odd(16 * block)
            for q in range(16 * block, 16 * block + 16):
                right = odd(q + 1)
                part = piece(0, q) + piece(2, q + 1) + jnp.where(low, left, right)
                first = (q // 8 % 2) * 128 + side * 64
                ref[block // 2, first : first + 64, q % 8 * 128 : (q % 8 + 1) * 128] = part.astype(ref.dtype)
                left = right

        for block in range(4):
            pl.when((meta[0] & 1) == (block & 1))(partial(emit, block, keep_ref))
            pl.when((meta[0] & 1) != (block & 1))(partial(emit, block, send_ref))


def grouped_conv_weight(x_ext, seg_ext, grad, rise, place, after):
    row_count, length, width = x_ext.shape
    frames = length - KERNEL
    pairs = width // 128
    in_block, tile, number = tile_lists(seg_ext, rise)
    slots = in_block.shape[0]
    meta = jnp.concatenate([jnp.reshape(place, (1,)).astype(jnp.int32), in_block, tile, number])
    rows4 = row_count * length // 4
    out4 = row_count * frames // 4
    depth = TAP_BLOCKS * 256
    return pl.pallas_call(
        partial(conv_weight_kernel, slots),
        grid_spec=pltpu.PrefetchScalarGridSpec(
            num_scalar_prefetch=1,
            grid=(pairs,),
            in_specs=[
                pl.BlockSpec((row_count * length, 128), lambda p, meta: (0, p)),
                pl.BlockSpec((rows4, 256), lambda p, meta: (0, 0)),
                pl.BlockSpec((row_count * frames, 128), lambda p, meta: (0, p)),
            ]
            + [pl.BlockSpec(memory_space=pl.ANY)] * len(after),
            out_specs=[pl.BlockSpec((2, 256, KERNEL * 8), lambda p, meta: (0, 0, 0))] * 2,
            scratch_shapes=[
                pltpu.VMEM((row_count * length, 128), jnp.float32),
                pltpu.VMEM((row_count * frames, 128), jnp.float32),
                pltpu.VMEM((rows4 + 16, 256), jnp.float32),
                pltpu.VMEM((16, rows4 // 16, 16, 256), jnp.bfloat16),
                pltpu.VMEM((16, rows4 // 16, 16, 256), jnp.bfloat16),
                pltpu.VMEM((out4, 256), jnp.bfloat16),
                pltpu.VMEM((slots * 16, 256), jnp.bfloat16),
                pltpu.VMEM((256, depth), jnp.float32),
            ],
        ),
        out_shape=[jax.ShapeDtypeStruct((2, 256, KERNEL * 8), jnp.bfloat16)] * 2,
        compiler_params=pltpu.CompilerParams(vmem_limit_bytes=VMEM_LIMIT, dimension_semantics=IN_ORDER),
        cost_estimate=cost(
            flops=2 * pairs * 2 * slots * 16 * 256 * depth, bytes_accessed=width * KERNEL * 128, transcendentals=0
        ),
        name="conv_weight_grad",
    )(meta, x_ext.reshape(row_count * length, width), seg_quads(seg_ext), grad, *after)


def fold_kernel(items, outs_count, meta, *refs):
    refs = list(refs)
    outs = refs[-outs_count:]
    for item in items:
        kept = refs.pop(0)
        gots = [refs.pop(0) for _ in item["gots"]]
        place = item["place"]
        shape = kept.shape
        bit = item["bit"](meta)
        for side, where in ((1 - bit, item["send"]), (bit, item["keep"])):
            buffer, column, lanes = where
            out = outs[buffer]
            if place is None:
                width = shape[3] // 2
                span = pl.ds(pl.multiple_of(side * width, width), width)
                for other in range(shape[0]):
                    total = kept[other, 0, :, span].astype(jnp.float32) + gots[0][other, 0, :, span].astype(jnp.float32)
                    out[other, :, column : column + width] = total.astype(out.dtype)
                continue
            for other in range(shape[1 - place]):
                at = (side, other) if place == 0 else (other, side)
                begin = 0
                for got in gots:
                    width = got.shape[3]
                    total = kept[at[0], at[1], :, begin : begin + width].astype(jnp.float32)
                    total = (total + got[at[0], at[1]].astype(jnp.float32)).astype(out.dtype)
                    rows = shape[2] // lanes
                    for k in range(lanes):
                        first = column + begin + k * shape[3]
                        out[other, :, first : first + width] = total[k * rows : (k + 1) * rows, :]
                    begin += width


def fold_item(kept, gots, place, bit, send, keep):
    return dict(kept=kept, gots=gots, place=place, bit=bit, send=send, keep=keep)


def folds(meta, items, shapes, name, after=()):
    operands = []
    for item in items:
        operands += [item["kept"]] + list(item["gots"])
    described = [dict(item, kept=None, gots=[None] * len(item["gots"])) for item in items]
    return pl.pallas_call(
        partial(fold_kernel, described, len(shapes)),
        grid_spec=pltpu.PrefetchScalarGridSpec(
            num_scalar_prefetch=1,
            grid=(1,),
            in_specs=[pl.BlockSpec(item.shape, lambda i, m: (0, 0, 0, 0)) for item in operands]
            + [pl.BlockSpec(memory_space=pl.ANY)] * len(after),
            out_specs=[pl.BlockSpec(shape, lambda i, m: (0, 0, 0)) for shape in shapes],
        ),
        out_shape=[jax.ShapeDtypeStruct(shape, jnp.bfloat16) for shape in shapes],
        compiler_params=pltpu.CompilerParams(vmem_limit_bytes=VMEM_LIMIT, dimension_semantics=IN_ORDER),
        cost_estimate=cost(flops=0, bytes_accessed=sum(2 * item.size for item in operands), transcendentals=0),
        name=name,
    )(meta, *operands, *after)


def chosen(meta, own_ref, got_ref):
    return jnp.where(pl.program_id(0) // 2 == meta[0], own_ref[0], got_ref[0])


def finish_pair_kernel(meta, own_ref, got_ref, *refs):
    up_ref, down_ref = refs[-2:]
    source = chosen(meta, own_ref, got_ref)
    width = up_ref.shape[1]
    up_ref[...] = source[:, :width].astype(jnp.float32)
    unit = source.shape[0]
    columns = down_ref.shape[1]
    for k in range(down_ref.shape[0] // unit):
        piece = source[:, width + k * columns : width + (k + 1) * columns]
        down_ref[k * unit : (k + 1) * unit, :] = piece.astype(jnp.float32)


def finish_pair(meta, own, got, rows, after):
    unit, total = own.shape[1:]
    width = total // 2
    columns = width * unit // rows
    place = lambda i, m: (0, 2 * (i // 2) + i % 2)
    return pl.pallas_call(
        finish_pair_kernel,
        grid_spec=pltpu.PrefetchScalarGridSpec(
            num_scalar_prefetch=1,
            grid=(4,),
            in_specs=[pl.BlockSpec((1, unit, total), lambda i, m: ((i % 2) ^ m[1], 0, 0))] * 2
            + [pl.BlockSpec(memory_space=pl.ANY)] * len(after),
            out_specs=[pl.BlockSpec((unit, width), place), pl.BlockSpec((rows, columns), place)],
        ),
        out_shape=[
            jax.ShapeDtypeStruct((unit, 4 * width), jnp.float32),
            jax.ShapeDtypeStruct((rows, 4 * columns), jnp.float32),
        ],
        compiler_params=pltpu.CompilerParams(vmem_limit_bytes=VMEM_LIMIT, dimension_semantics=IN_ORDER),
        cost_estimate=cost(flops=0, bytes_accessed=12 * own.size, transcendentals=0),
        name="finish_up_down",
    )(meta, own, got, *after)


def finish_qkv_kernel(eighth, half, meta, own_ref, got_ref, *refs):
    qkv_ref, out_ref = refs[-2:]
    step = pl.program_id(0)
    source = chosen(meta, own_ref, got_ref)
    core, y = step // 2, step % 2
    units = eighth // 128
    per_part = half // 128
    for begin, base in ((0, 0), (eighth, 2 * units)):
        for u in range(units):
            at = base + y * units + u
            at = (at // per_part) * 2 * per_part + core * per_part + at % per_part
            piece = source[:, begin + u * 128 : begin + (u + 1) * 128]
            qkv_ref[:, pl.ds(pl.multiple_of(at * 128, 128), 128)] = piece.astype(jnp.float32)
    quarter = half // 2
    first = pl.multiple_of(step * quarter, quarter)
    out_ref[:, pl.ds(first, quarter)] = source[:, 2 * eighth : 2 * eighth + quarter].astype(jnp.float32)


def finish_qkv(meta, own, got, half, after):
    unit, total = own.shape[1:]
    eighth = 3 * half // 4
    return pl.pallas_call(
        partial(finish_qkv_kernel, eighth, half),
        grid_spec=pltpu.PrefetchScalarGridSpec(
            num_scalar_prefetch=1,
            grid=(4,),
            in_specs=[pl.BlockSpec((1, unit, total), lambda i, m: ((i % 2) ^ m[1], 0, 0))] * 2
            + [pl.BlockSpec(memory_space=pl.ANY)] * len(after),
            out_specs=[
                pl.BlockSpec((unit, 6 * half), lambda i, m: (0, 0)),
                pl.BlockSpec((unit, 2 * half), lambda i, m: (0, 0)),
            ],
        ),
        out_shape=[
            jax.ShapeDtypeStruct((unit, 6 * half), jnp.float32),
            jax.ShapeDtypeStruct((unit, 2 * half), jnp.float32),
        ],
        compiler_params=pltpu.CompilerParams(vmem_limit_bytes=VMEM_LIMIT, dimension_semantics=IN_ORDER),
        cost_estimate=cost(flops=0, bytes_accessed=12 * own.size, transcendentals=0),
        name="finish_qkv_out",
    )(meta, own, got, *after)


AXES = ("y", "c", "z", "x")
LOSS_POWERS = (8, 7, 6, 5, 4, 3, 2, 1)


def device_pairs(place):
    pairs = []
    for y in range(2):
        for c in range(2):
            for z in range(4):
                for x in range(2):
                    ty, tc, tz, tx = place(y, c, z, x)
                    pairs.append((((y * 2 + c) * 4 + z) * 2 + x, ((ty * 2 + tc) * 4 + tz) * 2 + tx))
    return pairs


def move(values, place):
    return lax.ppermute(values, AXES, device_pairs(place))


def swap_core(values):
    return lax.ppermute(values, "c", [(0, 1), (1, 0)])


def swap_x(values):
    return lax.ppermute(values, "x", [(0, 1), (1, 0)])


def swap_y(values):
    return lax.ppermute(values, "y", [(0, 1), (1, 0)])


def swap_xy(values):
    return lax.ppermute(values, ("y", "x"), [(0, 3), (3, 0), (1, 2), (2, 1)])


def swap_z1(values):
    return lax.ppermute(values, "z", [(0, 1), (1, 0), (2, 3), (3, 2)])


def swap_z2(values):
    return lax.ppermute(values, "z", [(0, 2), (2, 0), (1, 3), (3, 1)])


def take(values, index, size, axis):
    return lax.dynamic_slice_in_dim(values, index * size, size, axis)


def once(values, *earlier):
    return lax.optimization_barrier((values,) + earlier)[0]


def ordered(index, mine, other, axis):
    first = jnp.where(index == 0, mine, other)
    second = jnp.where(index == 0, other, mine)
    return jnp.concatenate([first, second], axis=axis)


def to_rows(blocks, x, z):
    got = []
    for turn in range(2):
        mine = lax.dynamic_index_in_dim(blocks, x ^ turn, 0, keepdims=False)
        got.append(move(mine, lambda y, c, z, x: (y, z & 1, 2 * c + (x ^ turn), (z >> 1) ^ x ^ turn)))
    flip = (z & 1) == 0
    return jnp.where(flip, got[0], got[1]), jnp.where(flip, got[1], got[0])


def from_rows(frames, z):
    half = frames.shape[0] // 2
    got = []
    for turn in range(2):
        mine = take(frames, (z & 1) ^ turn, half, 0)
        got.append(move(mine, lambda y, c, z, x: (y, z >> 1, 2 * (x ^ (z & 1)) + c, (z & 1) ^ turn)))
    return got


def split_body(
    feats, segments, labels, conv_weight, w_qkv, w_out, w_up, w_down, head_w, head_b, gains, biases, up_bias
):
    y, c, z, x = (lax.axis_index(name) for name in AXES)
    block, features = feats.shape[1:]
    half = features // 2
    frames = 2 * block
    chip_frames = 2 * frames
    tokens = frames
    rim = KERNEL // 2
    rise = lax.axis_size("z") * lax.axis_size("x") // 2
    meta = jnp.stack([c, y, x, z]).astype(jnp.int32)
    side = x ^ (z & 1)

    label_rows = jnp.pad(labels.astype(jnp.bfloat16)[:, None, :], ((0, 0), (0, 15), (0, features - block)))
    first_block, second_block = to_rows(jnp.concatenate([feats, label_rows], axis=1), x, z)
    feats_own = jnp.concatenate([first_block[:block], second_block[:block]], axis=0)
    labels_own = jnp.concatenate([first_block[block, :block], second_block[block, :block]]).astype(jnp.int32)
    seg_rows = ordered(c, segments, swap_core(segments), 0)
    seg_row = lax.dynamic_index_in_dim(seg_rows, z, 0, keepdims=False)
    seg_halves = seg_row.reshape(2, 2, frames)
    seg_near = lax.dynamic_index_in_dim(seg_halves, side, 0, keepdims=False)
    seg_far = lax.dynamic_index_in_dim(seg_halves, 1 - side, 0, keepdims=False)
    seg_near, seg_far = (jnp.where(c == 0, item, item[::-1]).reshape(-1) for item in (seg_near, seg_far))
    seg_wide = jnp.pad(seg_row, (rim, rim), constant_values=-1)
    seg_ext = lax.dynamic_slice_in_dim(seg_wide, side * chip_frames, chip_frames + 2 * rim, 0)[None]

    def to_chip(values):
        return ordered(c, take(values, c, half, 1), swap_core(take(values, 1 - c, half, 1)), 0)

    def rimmed(values, edge):
        empty = jnp.zeros_like(edge)
        before = jnp.where(side == 0, empty, edge)
        after = jnp.where(side == 0, edge, empty)
        return jnp.concatenate([before, values, after], axis=0)[None]

    def with_rim(values):
        return rimmed(values, swap_x(jnp.where(side == 0, values[chip_frames - rim :], values[:rim])))

    def grouped(own, got_x, got_y, got_xy):
        return ordered(y, ordered(side, own, got_x, 0)[None], ordered(side, got_y, got_xy, 0)[None], 0)

    def to_groups(values):
        def part(yy, xx):
            return lax.dynamic_slice_in_dim(values, 256 * xx + 128 * yy, 128, 1)

        return grouped(
            part(y, x), swap_x(part(y, 1 - x)), swap_y(part(1 - y, x)), swap_xy(part(1 - y, 1 - x))
        )

    shift_bias = biases.T
    qkv_bias = jnp.concatenate([shift_bias[2], jnp.zeros((features,), jnp.float32), shift_bias[3]])[None]
    gain_rows = gains.T
    feats_chip = to_chip(feats_own)
    feats_group = jnp.pad(to_groups(feats_chip), ((0, 0), (rim, rim), (0, 0)))
    seg_pair = ordered(y, seg_row[None], swap_y(seg_row)[None], 0)
    seg_pair = jnp.pad(seg_pair, ((0, 0), (rim, rim)), constant_values=-1)
    position_chip, slope = grouped_conv(
        with_rim(feats_chip), seg_ext, conv_weight, take(shift_bias[0:1], c, half, 1), 4 * c, rise, False
    )
    theirs, ours, normed, position = mix_rows(
        meta,
        (
            take(position_chip, c, frames, 0),
            swap_core(take(position_chip, 1 - c, frames, 0)),
            gain_rows[0:1],
            shift_bias[1:2],
        ),
        w_qkv,
        qkv_bias,
        1,
        2,
        (seg_pair,),
    )
    near = jnp.concatenate([ours, swap_core(theirs)], axis=0)
    got_normed = swap_core(normed)
    far = swap_x(near)
    theirs, ours = mix_rows(meta, (normed,), w_qkv, qkv_bias, 0, 1, (feats_group,))
    queries = jnp.concatenate([ours, swap_core(theirs)], axis=0)
    mixed, state = attend_near(queries, near, seg_near, seg_near)
    attended, attended_ours, attended_away, lse = attend_far(queries, far, seg_near, seg_far, mixed, state)
    zero_row = jnp.zeros((features,), jnp.float32)
    rows = jnp.stack([gain_rows[1], shift_bias[5], shift_bias[4], shift_bias[6]] + [zero_row] * 4)
    (
        pack, output_low, out_ours, up_ours, branch_ours, att_ours, att_theirs, grad_resid, mid_sums, up_sums,
        grad_head_w, last,
    ) = middle(
        meta,
        attended_ours,
        swap_core(attended_away),
        position,
        w_out,
        w_up,
        w_down,
        up_bias[None],
        head_w,
        head_b[None],
        labels_own[:, None],
        rows,
    )

    grad_heads = jnp.concatenate([att_ours, swap_core(att_theirs)], axis=0)
    dq_far, dkv_far = attend_back(queries, far, grad_heads, attended, lse, seg_near, seg_far, jnp.bfloat16, att_ours)
    got_kv = swap_x(dkv_far)

    C, Y, X, Z = 0, 1, 2, 3
    places = pack_places(features, w_up.shape[1])
    got_pack = swap_core(once(pack, grad_heads))
    up_pair = ((up_ours, 0), (got_pack, places["up"]))
    down_pair = ((out_ours, 0), (got_pack, places["out"]))
    branch_pair = ((branch_ours, 0), (got_pack, places["branch"]))
    second_pair, active_pair, attended_pair = (
        ((pack, places[name]), (got_pack, places[name])) for name in ("second", "active", "attended")
    )
    unit = features // 8
    down_rows = w_down.shape[0] // 4
    up_wide = w_up.shape[1] // 4
    quarter = half // 2
    eighth = 3 * half // 4
    first_pieces, before = [], dkv_far
    for piece in range(2):
        up_piece, down_piece = weight_parts(
            meta,
            [
                weight_task(
                    [(0, 0)], second_pair, up_pair, half, 1, lambda i, m, k=piece: k, up_wide, lambda m: 1 - m[Y]
                ),
                weight_task(
                    [(1, 0)], active_pair, down_pair, down_rows, 1,
                    lambda i, m, k=piece: 2 * ((m[Z] >> 1) ^ (1 - k)) + 1 - (m[Z] & 1), half, lambda m: 0,
                ),
            ],
            [(half, up_wide), (down_rows, half)],
            "weight_first",
            (before,),
        )
        first_pieces.append((up_piece, down_piece))
        before = down_piece
    (up_low, down_away), (up_high, down_home) = first_pieces
    got_up_low, got_down_away = swap_y(up_low), swap_z1(down_away)
    got_up_high, got_down_home = swap_y(up_high), swap_z1(down_home)
    dq, dkv = attend_back(queries, near, grad_heads, attended, lse, seg_near, seg_near, jnp.float32, down_home)

    def mixed_grad(part):
        piece = slice(part * frames, (part + 1) * frames)
        return jnp.concatenate(
            [
                dq[piece] + dq_far[piece],
                dkv[0, piece] + got_kv[0, piece].astype(jnp.float32),
                dkv[1, piece] + got_kv[1, piece].astype(jnp.float32),
            ],
            axis=1,
        ).astype(jnp.bfloat16)

    grad_theirs = mixed_grad(1)
    grad_got = swap_core(grad_theirs)
    grad_ours = mixed_grad(0)
    position_ours, position_theirs, first_sums = unmix_rows(
        meta, grad_ours, grad_got, w_qkv, position, grad_resid, gain_rows[0:1], (got_up_low, got_down_away)
    )
    grad_position, grad_conv, edge, own_part, to_x, to_y, to_xy, conv_bias = conv_grad_rows(
        meta, position_ours, swap_core(position_theirs), slope, (got_up_high, got_down_home)
    )
    grad_rim = rimmed(grad_conv, swap_x(edge))
    grad_group = grouped(own_part, swap_x(to_x), swap_y(to_y), swap_xy(to_xy))

    x_bit, y_bit = (lambda m: m[X]), (lambda m: m[Y])
    own_sums, got_sums = (jnp.sum(item.astype(jnp.float32), axis=0, keepdims=True) for item in (grad_ours, grad_got))
    rest_loss, digits = last[1, 0], []
    for power in LOSS_POWERS:
        digit = jnp.floor(rest_loss / 8.0**power)
        digits.append(digit)
        rest_loss = rest_loss - digit * 8.0**power
    digits.append(rest_loss)
    final = jnp.concatenate(
        [last[0, :VOCAB], jnp.stack(digits), jnp.zeros((unit - VOCAB - len(digits),), jnp.float32)]
    )
    small = small_sums(
        meta, grad_head_w, mid_sums, first_sums, conv_bias, own_sums, got_sums, up_sums[:, 0].reshape(8, 1, -1), final[None]
    )

    normed_pair = ((normed, 0), (got_normed, 0))
    qkv_pair = ((grad_ours, 0), (grad_theirs, 0))
    a_first, b_first = weight_parts(
        meta,
        [
            weight_task([(0, 0)], normed_pair, qkv_pair, features, 1, lambda i, m: 0, eighth, lambda m: 1 - m[Y]),
            weight_task(
                [(1, 2 * eighth)], normed_pair, qkv_pair, unit, 4, lambda i, m: 2 * i + 1 - m[X], 2 * eighth, lambda m: 1
            ),
            weight_task(
                [(1, 0)], attended_pair, branch_pair, unit, 4, lambda i, m: 2 * i + 1 - m[X], half, lambda m: 0, joint=True
            ),
            weight_task([(1, half)], ((small, 0),), None, unit, 4, lambda i, m: 2 * i + 1 - m[X], 128, None, joint=True),
        ],
        [(features, eighth), (half, 4 * eighth)],
        "weight_qkv_first",
        (grad_conv,),
    )
    got_a, got_b = swap_y(a_first), swap_x(b_first)
    conv_send, conv_kept = grouped_conv_weight(
        feats_group, seg_pair, grad_group.reshape(-1, 128), rise, z, (a_first, grad_rim)
    )
    conv_got = swap_z1(conv_send)
    up_send, up_kept, down_send, down_kept = weight_parts(
        meta,
        [
            weight_task(
                [(0, 0), (1, 0)], second_pair, up_pair, half, 1, lambda i, m: 0, up_wide, lambda m: m[Y],
                got_up_low, lambda i, m: (0, 0), "rows", lambda m: m[Z] & 1, 2 * unit,
            ),
            weight_task(
                [(0, 0), (1, 0)], second_pair, up_pair, half, 1, lambda i, m: 1, up_wide, lambda m: m[Y],
                got_up_high, lambda i, m: (0, 0), "rows", lambda m: m[Z] & 1, 2 * unit, 1,
            ),
            weight_task(
                [(2, 0), (3, 0)], active_pair, down_pair, down_rows, 1,
                lambda i, m: 2 * (1 - (m[Z] >> 1)) + (m[Z] & 1), half, lambda m: 0, got_down_away, lambda i, m: (0, 0),
                "rows", x_bit, down_rows // 2,
            ),
            weight_task(
                [(2, 0), (3, 0)], active_pair, down_pair, down_rows, 1,
                lambda i, m: 2 * (m[Z] >> 1) + (m[Z] & 1), half, lambda m: 0, got_down_home, lambda i, m: (0, 0),
                "rows", x_bit, down_rows // 2, 1,
            ),
        ],
        [(half, up_wide), (half, up_wide), (down_rows, half), (down_rows, half)],
        "weight_second",
        (conv_send,),
    )
    up_got, down_got = swap_z1(up_send), swap_x(down_send)
    low_z, high_z = (lambda m: m[Z] & 1), (lambda m: m[Z] >> 1)

    def view(values, *lead):
        return values.reshape(lead + (-1, values.shape[-1]))

    conv_left = grouped_conv(grad_rim, seg_ext, conv_weight, grad_position, 4 * c, rise, True, 0, 2, (up_kept,))[0]

    conv_send, conv_kept = folds(
        meta,
        [fold_item(conv_kept[:, None], [conv_got[:, None]], 0, high_z, (0, 0, 1), (1, 0, 1))],
        [(1, 256, KERNEL * 8)] * 2,
        "fold_taps",
        (conv_left,),
    )
    conv_got = swap_z2(conv_send)
    a_send, b_send, qkv_kept = weight_parts(
        meta,
        [
            weight_task(
                [(0, 0), (2, 0)], normed_pair, qkv_pair, features, 1, lambda i, m: 0, eighth, lambda m: m[Y],
                got_a, lambda i, m: (0, 0), "rows", x_bit, unit,
            ),
            weight_task(
                [(1, 0), (2, eighth)], normed_pair, qkv_pair, unit, 4, lambda i, m: 2 * i + m[X], 2 * eighth, lambda m: 1,
                got_b, lambda i, m: (i, 1), "columns", y_bit,
            ),
            weight_task(
                [(1, eighth), (2, 2 * eighth)], attended_pair, branch_pair, unit, 4, lambda i, m: 2 * i + m[X], half,
                lambda m: 0, got_b, lambda i, m: (i, 0), "columns", y_bit, joint=True,
            ),
            weight_task(
                [(1, eighth + quarter), (2, 2 * eighth + quarter)], ((small, 0),), None, unit, 4,
                lambda i, m: 2 * i + m[X], 128, None, got_b, lambda i, m: (i, half // 128), joint=True,
            ),
        ],
        [(half, eighth), (half, eighth + quarter + 128), (half, 2 * eighth + quarter + 128)],
        "weight_qkv_second",
        (conv_kept,),
    )
    a_got, b_got = swap_x(a_send), swap_y(b_send)
    conv_right = grouped_conv(
        grad_rim, seg_ext, conv_weight, grad_position, 4 * c, rise, True, 2, 2, (qkv_kept,)
    )[0]
    wide = 2 * eighth + quarter + 128
    x_send, up_kept, qkv_kept, down_send, down_kept, conv_send, conv_kept, qkv_send = folds(
        meta,
        [
            fold_item(view(up_kept, 2, 2), [view(up_got, 2, 2)], 1, x_bit, (0, 0, 1), (1, 0, 1)),
            fold_item(view(qkv_kept, 2, 2), [view(a_got, 2, 2), view(b_got, 2, 2)], 1, low_z, (7, 0, 1), (2, 0, 1)),
            fold_item(view(down_kept, 2, 1), [view(down_got, 2, 1)], None, y_bit, (3, 0, 1), (4, 0, 1)),
            fold_item(view(conv_kept, 2, 1), [view(conv_got, 2, 1)], 0, x_bit, (5, 0, 1), (6, 0, 1)),
        ],
        [(2, unit, up_wide)] * 2 + [(2, unit, wide)] + [(2, down_rows // 2, quarter)] * 2
        + [(1, 128, KERNEL * 8)] * 2 + [(2, unit, wide)],
        "fold_first",
        (conv_right,),
    )
    qkv_got, up_got, down_got, conv_got = swap_z1(qkv_send), swap_x(x_send), swap_y(down_send), swap_x(conv_send)
    shard = ordered(x, conv_kept, conv_got, 0)
    shard = jnp.concatenate([shard, swap_y(shard)], axis=0)
    conv_input = jnp.concatenate([once(conv_left, x_send), conv_right], axis=1)
    away = swap_core(take(conv_input, 1 - c, frames, 0))
    back = jnp.concatenate([ordered(c, take(conv_input, c, frames, 0), away, 1), output_low], axis=1)
    qkv_send, qkv_kept, pair_send, pair_kept = folds(
        meta,
        [
            fold_item(qkv_kept[:, None], [qkv_got[:, None]], 0, high_z, (0, 0, 1), (1, 0, 1)),
            fold_item(up_kept[:, None], [up_got[:, None]], 0, high_z, (2, 0, 1), (3, 0, 1)),
            fold_item(down_kept[:, None], [down_got[:, None]], 0, lambda m: 1, (2, up_wide, 4), (3, up_wide, 4)),
        ],
        [(1, unit, wide)] * 2 + [(1, unit, 2 * up_wide)] * 2,
        "fold_second",
        (),
    )
    qkv_got, pair_got = swap_z2(qkv_send), swap_z2(pair_send)
    grad_conv_weight = flip_columns(meta, shard, swap_core(shard))

    def add(kept, got):
        return (kept.astype(jnp.float32) + got.astype(jnp.float32)).astype(jnp.bfloat16)

    def spread(shard, *earlier):
        shard = jnp.concatenate([shard, once(swap_y(shard), *earlier)], axis=0)
        return shard, swap_core(shard)

    pair_sum, qkv_sum = add(pair_kept, pair_got), add(qkv_kept, qkv_got)
    back = from_rows(once(back, pair_sum, qkv_sum), z)
    grad_w_up, grad_w_down = finish_pair(meta, *spread(pair_sum, grad_conv_weight), w_down.shape[0] // 8, ())
    qkv_own, qkv_other = spread(qkv_sum)
    grad_w_qkv, grad_w_out = finish_qkv(meta, qkv_own, qkv_other, half, (grad_w_up,))
    total = qkv_own[0, :, wide - 128 :].astype(jnp.float32) + qkv_other[0, :, wide - 128 :].astype(jnp.float32)
    back = [once(item, grad_w_up, grad_w_qkv)[None] for item in back]
    back = ordered(x, back[0], back[1], 0)
    grad_feats, layer_out = back[:, :, :features], back[:, :, features:]
    v = VOCAB
    powers = jnp.array([8.0**power for power in LOSS_POWERS] + [1.0], jnp.float32)
    loss = jnp.sum(total[v : v + len(LOSS_POWERS) + 1, v + 13] * powers) / (tokens * 32)
    gain_part = jnp.stack([total[:, v + 4], total[:, v]], axis=1)
    bias_part = jnp.stack([total[:, v + k] for k in (6, 5, 7, 8, 1, 2, 3)], axis=1)
    return (
        layer_out,
        loss,
        grad_feats.astype(jnp.float32),
        grad_conv_weight,
        grad_w_qkv,
        grad_w_out,
        grad_w_up,
        grad_w_down,
        total[:, :v],
        total[:v, v + 13],
        gain_part,
        bias_part,
        total[:, v + 9 : v + 13].T.reshape(-1),
    )


def split_solution(mesh):
    fine = Mesh(mesh.devices.reshape(2, 2, 4, 2), AXES)
    rows, parts = ("y", "c"), ("z", "x")
    return jax.shard_map(
        split_body,
        mesh=fine,
        in_specs=(P(rows, parts, None), P(rows, None), P(rows, parts)) + (P(),) * 10,
        out_specs=(
            P(rows, parts, None),
            P(),
            P(rows, parts, None),
            P(parts, None),
            P(parts, None),
            P(parts, None),
            P(parts, None),
            P(parts, None),
            P(parts, None),
            P(),
            P(parts, None),
            P(parts, None),
            P(parts),
        ),
        check_vma=False,
    )


def solution(mesh):
    if mesh.shape["dp"] == 4 and mesh.shape["seq"] == 8:
        return split_solution(mesh)
    return whole_solution(mesh)
```

```python
from functools import partial
import math

import jax
import jax.numpy as jnp
from jax import lax
from jax.experimental import pallas as pl
from jax.experimental.pallas import tpu as pltpu
from jax.sharding import Mesh, PartitionSpec as P

HEADS = 16
GROUPS = 16
KERNEL = 128
VOCAB = 32
TAP_BLOCKS = 33
VMEM_LIMIT = 56 * 1024 * 1024
DW_UNROLL = 11
IN_ORDER = ("arbitrary",)
COST_SHARE = 0.001


epsilon = 1e-05
masked_score = -1e30
tap_group = 8


def extended(cells, sides, width):
    for axis, dim in sides:
        count = lax.axis_size(axis)
        ends = count - 1
        head = lax.slice_in_dim(cells, 0, width, axis=dim)
        tail = lax.slice_in_dim(cells, cells.shape[dim] - width, cells.shape[dim], axis=dim)
        cells = jnp.concatenate(
            [
                lax.ppermute(tail, axis, [(i, (i + 1) % count) for i in range(ends)]),
                cells,
                lax.ppermute(head, axis, [((i + 1) % count, i) for i in range(ends)]),
            ],
            axis=dim,
        )
    return cells


def layer_norm(values, gain_row, shift_row):
    center = values - jnp.mean(values, axis=-1, keepdims=True)
    spread = jnp.mean(center * center, axis=-1, keepdims=True)
    return center * lax.rsqrt(spread + epsilon) * gain_row + shift_row


def gelu_exact(values):
    return jax.nn.gelu(values, approximate=False)


def outer_sum(left_side, right_side):
    return lax.dot_general(
        left_side, right_side, (((0,), (0,)), ((), ())), preferred_element_type=jnp.float32
    )


def back_product(grad_rows, weight):
    return lax.dot_general(
        grad_rows, weight, (((1,), (1,)), ((), ())), preferred_element_type=jnp.float32
    )


def masked_windows(source, seg_padded, seg_local, offsets, frames):
    windows = []
    for offset in offsets:
        window = lax.dynamic_slice_in_dim(source, offset, frames, 1)
        near_ids = lax.dynamic_slice_in_dim(seg_padded, offset, frames, 1)
        keep_mask = (near_ids == seg_local)[:, :, None]
        windows.append(jnp.where(keep_mask, window, jnp.zeros_like(window)))
    return jnp.stack(windows, axis=2)


def conv_forward(feats_rim, seg_padded, seg_local, conv_weight):
    row_count, frames = seg_local.shape
    features = feats_rim.shape[2]
    group_width = features // GROUPS
    tap_count = conv_weight.shape[0] // group_width
    grouped = conv_weight.reshape(tap_count, group_width, GROUPS, group_width)

    def one_block(tap_block, running):
        offsets = [tap_block * tap_group + tap_inner for tap_inner in range(tap_group)]
        stacked = masked_windows(feats_rim, seg_padded, seg_local, offsets, frames)
        stacked = stacked.reshape(row_count, frames, tap_group, GROUPS, group_width)
        weight_part = lax.dynamic_slice_in_dim(grouped, tap_block * tap_group, tap_group, 0)
        return running + jnp.einsum(
            "rtkgi,kigo->rtgo", stacked, weight_part, preferred_element_type=jnp.float32
        )

    start_sum = jnp.zeros((row_count, frames, GROUPS, group_width), jnp.float32)
    running = lax.fori_loop(0, tap_count // tap_group, one_block, start_sum)
    return running.reshape(row_count, frames, features)


def conv_weight_grad(feats_rim, seg_padded, seg_local, grad_conv_low, tap_count):
    row_count, frames = seg_local.shape
    features = feats_rim.shape[2]
    group_width = features // GROUPS
    grad_grouped = grad_conv_low.reshape(row_count, frames, GROUPS, group_width)

    def one_block(tap_block, running):
        offsets = [tap_block * tap_group + tap_inner for tap_inner in range(tap_group)]
        stacked = masked_windows(feats_rim, seg_padded, seg_local, offsets, frames)
        stacked = stacked.reshape(row_count, frames, tap_group, GROUPS, group_width)
        block_grad = jnp.einsum(
            "rtkgi,rtgo->kigo", stacked, grad_grouped, preferred_element_type=jnp.float32
        )
        return lax.dynamic_update_slice_in_dim(running, block_grad, tap_block * tap_group, 0)

    start_sum = jnp.zeros((tap_count, group_width, GROUPS, group_width), jnp.float32)
    running = lax.fori_loop(0, tap_count // tap_group, one_block, start_sum)
    return running.reshape(tap_count * group_width, features)


def conv_input_grad(grad_rim, seg_padded, seg_local, conv_weight):
    row_count, frames = seg_local.shape
    features = grad_rim.shape[2]
    group_width = features // GROUPS
    tap_count = conv_weight.shape[0] // group_width
    grouped = conv_weight.reshape(tap_count, group_width, GROUPS, group_width)

    def one_block(tap_block, running):
        offsets = [
            tap_count - (tap_block * tap_group + tap_inner) for tap_inner in range(tap_group)
        ]
        stacked = masked_windows(grad_rim, seg_padded, seg_local, offsets, frames)
        stacked = stacked.reshape(row_count, frames, tap_group, GROUPS, group_width)
        weight_part = lax.dynamic_slice_in_dim(grouped, tap_block * tap_group, tap_group, 0)
        return running + jnp.einsum(
            "rtkgo,kigo->rtgi", stacked, weight_part, preferred_element_type=jnp.float32
        )

    start_sum = jnp.zeros((row_count, frames, GROUPS, group_width), jnp.float32)
    running = lax.fori_loop(0, tap_count // tap_group, one_block, start_sum)
    return running.reshape(row_count, frames, features)


def span_size(piece_rows, frames):
    return math.gcd(piece_rows, 8 * frames)


def attend_row(row_state, query_row, key_row, value_row, seg_query, seg_key, score_scale):
    running_max, running_sum, weighted = row_state
    scores = score_scale * jnp.einsum(
        "qhe,khe->qhk", query_row, key_row, preferred_element_type=jnp.float32
    )
    allowed = (seg_query[:, None] == seg_key[None, :])[:, None, :]
    scores = jnp.where(allowed, scores, masked_score)
    new_max = jnp.maximum(running_max, jnp.max(scores, axis=-1))
    rescale = jnp.exp(running_max - new_max)
    weights = jnp.where(allowed, jnp.exp(scores - new_max[:, :, None]), 0.0)
    running_sum = running_sum * rescale + jnp.sum(weights, axis=-1)
    weighted = weighted * rescale[:, :, None] + jnp.einsum(
        "qhk,khe->qhe", weights.astype(jnp.bfloat16), value_row, preferred_element_type=jnp.float32
    )
    return (new_max, running_sum, weighted)


def query_grad_row(
    grad_query,
    query_row,
    key_row,
    value_row,
    seg_query,
    seg_key,
    lse_row,
    dots_row,
    grad_row,
    score_scale,
):
    scores = score_scale * jnp.einsum(
        "qhe,khe->qhk", query_row, key_row, preferred_element_type=jnp.float32
    )
    allowed = (seg_query[:, None] == seg_key[None, :])[:, None, :]
    probs = jnp.where(allowed, jnp.exp(scores - lse_row[:, :, None]), 0.0)
    grad_probs = jnp.einsum("qhe,khe->qhk", grad_row, value_row, preferred_element_type=jnp.float32)
    grad_scores = (probs * (grad_probs - dots_row[:, :, None])).astype(jnp.bfloat16)
    return grad_query + score_scale * jnp.einsum(
        "qhk,khe->qhe", grad_scores, key_row, preferred_element_type=jnp.float32
    )


def key_grad_row(
    grads_pair,
    key_row,
    value_row,
    query_row,
    grad_row,
    lse_row,
    dots_row,
    seg_query,
    seg_key,
    score_scale,
):
    scores = score_scale * jnp.einsum(
        "qhe,khe->qhk", query_row, key_row, preferred_element_type=jnp.float32
    )
    allowed = (seg_query[:, None] == seg_key[None, :])[:, None, :]
    probs = jnp.where(allowed, jnp.exp(scores - lse_row[:, :, None]), 0.0)
    grad_value = jnp.einsum(
        "qhk,qhe->khe", probs.astype(jnp.bfloat16), grad_row, preferred_element_type=jnp.float32
    )
    grad_probs = jnp.einsum("qhe,khe->qhk", grad_row, value_row, preferred_element_type=jnp.float32)
    grad_scores = (probs * (grad_probs - dots_row[:, :, None])).astype(jnp.bfloat16)
    grad_key = score_scale * jnp.einsum(
        "qhk,qhe->khe", grad_scores, query_row, preferred_element_type=jnp.float32
    )
    return (grad_key, grad_value)


def body(
    feats,
    segments,
    labels,
    conv_weight,
    w_qkv,
    w_out,
    w_up,
    w_down,
    head_w,
    head_b,
    gains,
    biases,
    up_bias,
):
    row_count, frames, features = feats.shape
    head_count = HEADS
    head_width = features // head_count
    score_scale = head_width ** (-0.5)
    tokens = row_count * frames
    tap_count = KERNEL
    rim_width = tap_count // 2
    own_first = lax.axis_index("seq") * frames
    seg_local = lax.dynamic_slice_in_dim(segments, own_first, frames, 1)
    seg_wide = jnp.pad(segments, ((0, 0), (rim_width, rim_width)), constant_values=-1)
    seg_padded = lax.dynamic_slice_in_dim(seg_wide, own_first, frames + 2 * rim_width, 1)
    feats_rim = extended(feats, (("seq", 1),), rim_width)
    conv_sum = conv_forward(feats_rim, seg_padded, seg_local, conv_weight) + biases[:, 0]
    activated, conv_pull = jax.vjp(gelu_exact, conv_sum)
    position = feats.astype(jnp.float32) + activated
    normed, first_pull = jax.vjp(layer_norm, position, gains[:, 0], biases[:, 1])
    normed_low = normed.astype(jnp.bfloat16).reshape(tokens, features)
    qkv_bias = jnp.concatenate([biases[:, 2], jnp.zeros((features,), jnp.float32), biases[:, 3]])
    mixed = (jnp.dot(normed_low, w_qkv, preferred_element_type=jnp.float32) + qkv_bias).astype(
        jnp.bfloat16
    )
    queries = mixed[:, :features].reshape(row_count, frames, head_count, head_width)
    keys = mixed[:, features : 2 * features].reshape(row_count, frames, features)
    values = mixed[:, 2 * features :].reshape(row_count, frames, features)
    start_state = (
        jnp.full((row_count, frames, head_count), masked_score, jnp.float32),
        jnp.zeros((row_count, frames, head_count), jnp.float32),
        jnp.zeros((row_count, frames, head_count, head_width), jnp.float32),
    )
    key_shard = lax.all_gather(keys, "seq", axis=1, tiled=True)
    value_shard = lax.all_gather(values, "seq", axis=1, tiled=True)
    piece_rows = key_shard.shape[1]
    span = span_size(piece_rows, frames)

    def forward_one_span(span_index, state):
        offset = span_index * span
        key_part = lax.dynamic_slice_in_dim(key_shard, offset, span, 1)
        value_part = lax.dynamic_slice_in_dim(value_shard, offset, span, 1)
        seg_keys = lax.dynamic_slice_in_dim(segments, offset, span, 1)
        results = []
        for row_index in range(row_count):
            action = partial(
                attend_row,
                query_row=queries[row_index],
                key_row=key_part[row_index].reshape(span, head_count, head_width),
                value_row=value_part[row_index].reshape(span, head_count, head_width),
                seg_query=seg_local[row_index],
                seg_key=seg_keys[row_index],
                score_scale=score_scale,
            )
            row_state = (state[0][row_index], state[1][row_index], state[2][row_index])
            results.append(action(row_state))
        return (
            jnp.stack([item[0] for item in results]),
            jnp.stack([item[1] for item in results]),
            jnp.stack([item[2] for item in results]),
        )

    running_max, running_sum, weighted = lax.fori_loop(
        0, piece_rows // span, forward_one_span, start_state
    )
    attended = weighted / running_sum[:, :, :, None]
    log_total = running_max + jnp.log(running_sum)
    attended_low = attended.reshape(tokens, features).astype(jnp.bfloat16)
    resid = (
        position.reshape(tokens, features)
        + jnp.dot(attended_low, w_out, preferred_element_type=jnp.float32)
        + biases[:, 4]
    )
    normed_second, second_pull = jax.vjp(layer_norm, resid, gains[:, 1], biases[:, 5])
    second_low = normed_second.astype(jnp.bfloat16)
    up_sum = jnp.dot(second_low, w_up, preferred_element_type=jnp.float32) + up_bias
    up_active, up_pull = jax.vjp(gelu_exact, up_sum)
    active_low = up_active.astype(jnp.bfloat16)
    output = resid + jnp.dot(active_low, w_down, preferred_element_type=jnp.float32) + biases[:, 6]
    output_low = output.astype(jnp.bfloat16)
    logits = jnp.dot(output_low, head_w, preferred_element_type=jnp.float32) + head_b
    row_top = jnp.max(logits, axis=-1, keepdims=True)
    shifted = jnp.exp(logits - row_top)
    exp_sums = jnp.sum(shifted, axis=-1, keepdims=True)
    onehot = labels.reshape(tokens)[:, None] == jnp.arange(VOCAB, dtype=jnp.int32)[None, :]
    picked = jnp.sum(jnp.where(onehot, logits, 0.0), axis=-1)
    local_loss = jnp.sum(row_top[:, 0] + jnp.log(exp_sums[:, 0]) - picked)
    grad_logits = (shifted / exp_sums - onehot.astype(jnp.float32)).astype(jnp.bfloat16)
    grad_head_w = outer_sum(output_low, grad_logits)
    grad_head_b = jnp.sum(grad_logits.astype(jnp.float32), axis=0)
    grad_output = back_product(grad_logits, head_w)
    grad_output_low = grad_output.astype(jnp.bfloat16)
    grad_w_down = outer_sum(active_low, grad_output_low)
    grad_down_bias = jnp.sum(grad_output_low.astype(jnp.float32), axis=0)
    grad_active = back_product(grad_output_low, w_down)
    grad_up_low = up_pull(grad_active)[0].astype(jnp.bfloat16)
    grad_w_up = outer_sum(second_low, grad_up_low)
    grad_up_bias = jnp.sum(grad_up_low.astype(jnp.float32), axis=0)
    grad_second = back_product(grad_up_low, w_up)
    grad_resid_part, grad_gain_second, grad_shift_second = second_pull(grad_second)
    grad_resid = grad_output + grad_resid_part
    grad_branch_low = grad_resid.astype(jnp.bfloat16)
    grad_w_out = outer_sum(attended_low, grad_branch_low)
    grad_out_bias = jnp.sum(grad_branch_low.astype(jnp.float32), axis=0)
    grad_attended = back_product(grad_branch_low, w_out).astype(jnp.bfloat16)
    grad_heads = grad_attended.reshape(row_count, frames, head_count, head_width)
    head_dots = jnp.sum(grad_heads.astype(jnp.float32) * attended, axis=-1)
    zero_grads = jnp.zeros((row_count, frames, head_count, head_width), jnp.float32)
    all_keys, all_values = (
        lax.all_gather(keys, "seq", axis=1, tiled=True),
        lax.all_gather(values, "seq", axis=1, tiled=True),
    )
    length = all_keys.shape[1]
    key_span = 8 * frames

    def query_block(block_index, grad_query):
        first_row = block_index * key_span
        key_block = lax.dynamic_slice_in_dim(all_keys, first_row, key_span, 1)
        value_block = lax.dynamic_slice_in_dim(all_values, first_row, key_span, 1)
        seg_keys = lax.dynamic_slice_in_dim(segments, first_row, key_span, 1)
        results = []
        for row_index in range(row_count):
            action = partial(
                query_grad_row,
                query_row=queries[row_index],
                key_row=key_block[row_index].reshape(key_span, head_count, head_width),
                value_row=value_block[row_index].reshape(key_span, head_count, head_width),
                seg_query=seg_local[row_index],
                seg_key=seg_keys[row_index],
                lse_row=log_total[row_index],
                dots_row=head_dots[row_index],
                grad_row=grad_heads[row_index],
                score_scale=score_scale,
            )
            results.append(action(grad_query[row_index]))
        return jnp.stack(results)

    grad_queries = lax.fori_loop(0, length // key_span, query_block, zero_grads)

    def key_term(piece_rows):
        span = math.gcd(piece_rows, key_span)

        def key_one_span(span_index, gathered_terms):
            offset = span_index * span
            key_block = lax.dynamic_slice_in_dim(all_keys, offset, span, 1)
            value_block = lax.dynamic_slice_in_dim(all_values, offset, span, 1)
            seg_keys = lax.dynamic_slice_in_dim(segments, offset, span, 1)
            empty_row = jnp.zeros((span, head_count, head_width), jnp.float32)
            results = []
            for row_index in range(row_count):
                action = partial(
                    key_grad_row,
                    key_row=key_block[row_index].reshape(span, head_count, head_width),
                    value_row=value_block[row_index].reshape(span, head_count, head_width),
                    query_row=queries[row_index],
                    grad_row=grad_heads[row_index],
                    lse_row=log_total[row_index],
                    dots_row=head_dots[row_index],
                    seg_query=seg_local[row_index],
                    seg_key=seg_keys[row_index],
                    score_scale=score_scale,
                )
                results.append(action((empty_row, empty_row)))
            key_part = jnp.stack([item[0] for item in results], axis=1).reshape(
                span, row_count, features
            )
            value_part = jnp.stack([item[1] for item in results], axis=1).reshape(
                span, row_count, features
            )
            both_parts = jnp.concatenate([key_part, value_part], axis=2)
            return lax.dynamic_update_slice_in_dim(gathered_terms, both_parts, offset, 0)

        empty_terms = jnp.zeros((piece_rows, row_count, 2 * features), jnp.float32)
        return lax.fori_loop(0, piece_rows // span, key_one_span, empty_terms)

    both_grads = lax.psum_scatter(
        key_term(frames * lax.axis_size("seq")), "seq", scatter_dimension=0, tiled=True
    )
    grad_keys = jnp.transpose(both_grads[:, :, :features], (1, 0, 2)).reshape(
        row_count, frames, head_count, head_width
    )
    grad_values = jnp.transpose(both_grads[:, :, features:], (1, 0, 2)).reshape(
        row_count, frames, head_count, head_width
    )
    grad_mixed = jnp.concatenate(
        [
            grad_queries.reshape(tokens, features),
            grad_keys.reshape(tokens, features),
            grad_values.reshape(tokens, features),
        ],
        axis=1,
    ).astype(jnp.bfloat16)
    grad_w_qkv = outer_sum(normed_low, grad_mixed)
    mixed_sums = jnp.sum(grad_mixed.astype(jnp.float32), axis=0)
    grad_normed = back_product(grad_mixed, w_qkv).reshape(row_count, frames, features)
    grad_position_part, grad_gain_first, grad_shift_first = first_pull(grad_normed)
    grad_position = grad_resid.reshape(row_count, frames, features) + grad_position_part
    grad_conv_low = conv_pull(grad_position)[0].astype(jnp.bfloat16)
    grad_conv_bias = jnp.sum(grad_conv_low.astype(jnp.float32), axis=(0, 1))
    grad_conv_weight = conv_weight_grad(feats_rim, seg_padded, seg_local, grad_conv_low, tap_count)
    grad_rim = extended(grad_conv_low, (("seq", 1),), rim_width)
    grad_feats = grad_position + conv_input_grad(grad_rim, seg_padded, seg_local, conv_weight)
    grad_gains = jnp.stack([grad_gain_first, grad_gain_second], axis=1)
    grad_biases = jnp.stack(
        [
            grad_conv_bias,
            grad_shift_first,
            mixed_sums[:features],
            mixed_sums[2 * features :],
            grad_out_bias,
            grad_shift_second,
            grad_down_bias,
        ],
        axis=1,
    )
    shared = (
        lax.psum_scatter(grad_conv_weight, "seq", scatter_dimension=0, tiled=True),
        lax.psum_scatter(grad_w_qkv, "seq", scatter_dimension=0, tiled=True),
        lax.psum_scatter(grad_w_out, "seq", scatter_dimension=0, tiled=True),
        lax.psum_scatter(grad_w_up, "seq", scatter_dimension=0, tiled=True),
        lax.psum_scatter(grad_w_down, "seq", scatter_dimension=0, tiled=True),
        lax.psum_scatter(grad_head_w, "seq", scatter_dimension=0, tiled=True),
        lax.psum_scatter(grad_gains, "seq", scatter_dimension=0, tiled=True),
        lax.psum_scatter(grad_biases, "seq", scatter_dimension=0, tiled=True),
        lax.psum_scatter(grad_up_bias, "seq", scatter_dimension=0, tiled=True),
    )
    summed = (
        lax.psum(shared[0].astype(jnp.bfloat16), "dp").astype(jnp.float32),
        lax.psum(shared[1].astype(jnp.bfloat16), "dp").astype(jnp.float32),
        lax.psum(shared[2].astype(jnp.bfloat16), "dp").astype(jnp.float32),
        lax.psum(shared[3].astype(jnp.bfloat16), "dp").astype(jnp.float32),
        lax.psum(shared[4].astype(jnp.bfloat16), "dp").astype(jnp.float32),
        lax.psum(shared[5].astype(jnp.bfloat16), "dp").astype(jnp.float32),
        lax.psum(shared[6].astype(jnp.bfloat16), "dp").astype(jnp.float32),
        lax.psum(shared[7].astype(jnp.bfloat16), "dp").astype(jnp.float32),
        lax.psum(shared[8].astype(jnp.bfloat16), "dp").astype(jnp.float32),
    )
    loss_total, head_bias_total = lax.psum((local_loss, grad_head_b), ("dp", "seq"))
    loss = loss_total / (tokens * lax.axis_size("dp") * lax.axis_size("seq"))
    layer_out = output_low.reshape(row_count, frames, features)
    return (
        layer_out,
        loss,
        grad_feats,
        summed[0],
        summed[1],
        summed[2],
        summed[3],
        summed[4],
        summed[5],
        head_bias_total,
        summed[6],
        summed[7],
        summed[8],
    )


def whole_solution(mesh):
    placed = (
        P("dp", "seq", None),
        P("dp", None),
        P("dp", "seq"),
        P(),
        P(),
        P(),
        P(),
        P(),
        P(),
        P(),
        P(),
        P(),
        P(),
    )
    return jax.shard_map(
        body,
        mesh=mesh,
        in_specs=placed,
        out_specs=(
            P("dp", "seq", None),
            P(),
            P("dp", "seq", None),
            P("seq", None),
            P("seq", None),
            P("seq", None),
            P("seq", None),
            P("seq", None),
            P("seq", None),
            P(),
            P("seq", None),
            P("seq", None),
            P("seq"),
        ),
        check_vma=False,
    )


def cost(flops, bytes_accessed, transcendentals):
    return pl.CostEstimate(
        flops=int(flops * COST_SHARE), bytes_accessed=int(bytes_accessed * COST_SHARE), transcendentals=int(transcendentals * COST_SHARE)
    )


def lanes_dot(a, b):
    return lax.dot_general(a, b, (((1,), (1,)), ((), ())), preferred_element_type=jnp.float32)


def rows_dot(a, b):
    return lax.dot_general(a, b, (((0,), (0,)), ((), ())), preferred_element_type=jnp.float32)


def attend_parts(side, queries, keys, values, allowed, low):
    mine = low if side == 0 else jnp.logical_not(low)
    scores = lanes_dot(jnp.where(mine, keys, jnp.zeros_like(keys)), queries)
    scores = jnp.where(allowed, scores, masked_score)
    top = jnp.max(scores, axis=0, keepdims=True)
    return scores, top


def attend_kernel(seg_q_ref, seg_k_ref, q_ref, k_ref, v_ref, mixed_ref, state_ref):
    queries = q_ref[...] * jnp.bfloat16(0.125)
    low = lax.broadcasted_iota(jnp.int32, k_ref.shape, 1) < 64
    allowed = seg_k_ref[...] == seg_q_ref[...]
    for side in range(2):
        scores, top = attend_parts(side, queries, k_ref[...], None, allowed, low)
        weights = jnp.exp(scores - top)
        state_ref[0, side : side + 1, :] = top
        state_ref[0, side + 2 : side + 3, :] = jnp.sum(weights, axis=0, keepdims=True)
        mixed = rows_dot(v_ref[...], weights.astype(jnp.bfloat16))
        mixed_ref[side * 64 : (side + 1) * 64, :] = mixed[side * 64 : (side + 1) * 64, :]


def attend_far_kernel(seg_q_ref, seg_k_ref, q_ref, k_ref, v_ref, mixed_ref, state_ref, out_ref, low_ref, away_ref, lse_ref):
    queries = q_ref[...] * jnp.bfloat16(0.125)
    low = lax.broadcasted_iota(jnp.int32, k_ref.shape, 1) < 64
    allowed = seg_k_ref[...] == seg_q_ref[...]
    pieces = []
    for side in range(2):
        scores, top = attend_parts(side, queries, k_ref[...], None, allowed, low)
        near_top = state_ref[0, side : side + 1, :]
        top = jnp.maximum(top, near_top)
        weights = jnp.exp(scores - top)
        rescale = jnp.exp(near_top - top)
        total = state_ref[0, side + 2 : side + 3, :] * rescale + jnp.sum(weights, axis=0, keepdims=True)
        mixed = rows_dot(v_ref[...], weights.astype(jnp.bfloat16))[side * 64 : (side + 1) * 64, :]
        pieces.append((mixed + mixed_ref[side * 64 : (side + 1) * 64, :] * rescale) / total)
        lse_ref[0, side : side + 1, :] = top + jnp.log(total)
    attended = jnp.concatenate(pieces, axis=0).T
    own = low_ref.shape[0]
    out_ref[...] = attended
    low_ref[...] = attended[:own, :].astype(jnp.bfloat16)
    away_ref[...] = attended[own:, :].astype(jnp.bfloat16)


def attend_specs(frames, length, pairs):
    return [
        pl.BlockSpec((1, frames), lambda p: (0, 0)),
        pl.BlockSpec((length, 1), lambda p: (0, 0)),
        pl.BlockSpec((frames, 128), lambda p: (0, p)),
        pl.BlockSpec((length, 128), lambda p: (0, p)),
        pl.BlockSpec((length, 128), lambda p: (0, pairs + p)),
    ]


def attend_cost(frames, length, pairs, products):
    return cost(
        flops=4 * products * pairs * frames * length * 128,
        bytes_accessed=16 * frames * pairs * 128,
        transcendentals=2 * pairs * frames * length,
    )


def attend_near(queries, pair, seg_q, seg_k):
    frames, width = queries.shape
    length = pair.shape[0]
    pairs = width // 128
    return pl.pallas_call(
        attend_kernel,
        grid=(pairs,),
        in_specs=attend_specs(frames, length, pairs),
        out_specs=[
            pl.BlockSpec((128, frames), lambda p: (p, 0)),
            pl.BlockSpec((1, 8, frames), lambda p: (p, 0, 0)),
        ],
        out_shape=[
            jax.ShapeDtypeStruct((width, frames), jnp.float32),
            jax.ShapeDtypeStruct((pairs, 8, frames), jnp.float32),
        ],
        compiler_params=pltpu.CompilerParams(vmem_limit_bytes=VMEM_LIMIT),
        cost_estimate=attend_cost(frames, length, pairs, 2),
        name="attend_near",
    )(seg_q.reshape(1, -1), seg_k.reshape(-1, 1), queries, pair, pair)


def attend_far(queries, pair, seg_q, seg_k, mixed, state):
    frames, width = queries.shape
    length = pair.shape[0]
    pairs = width // 128
    return pl.pallas_call(
        attend_far_kernel,
        grid=(pairs,),
        in_specs=attend_specs(frames, length, pairs)
        + [
            pl.BlockSpec((128, frames), lambda p: (p, 0)),
            pl.BlockSpec((1, 8, frames), lambda p: (p, 0, 0)),
        ],
        out_specs=[
            pl.BlockSpec((frames, 128), lambda p: (0, p)),
            pl.BlockSpec((frames // 2, 128), lambda p: (0, p)),
            pl.BlockSpec((frames // 2, 128), lambda p: (0, p)),
            pl.BlockSpec((1, 8, frames), lambda p: (p, 0, 0)),
        ],
        out_shape=[
            jax.ShapeDtypeStruct((frames, width), jnp.float32),
            jax.ShapeDtypeStruct((frames // 2, width), jnp.bfloat16),
            jax.ShapeDtypeStruct((frames // 2, width), jnp.bfloat16),
            jax.ShapeDtypeStruct((pairs, 8, frames), jnp.float32),
        ],
        compiler_params=pltpu.CompilerParams(vmem_limit_bytes=VMEM_LIMIT),
        cost_estimate=attend_cost(frames, length, pairs, 2),
        name="attend_far",
    )(seg_q.reshape(1, -1), seg_k.reshape(-1, 1), queries, pair, pair, mixed, state)


def attend_back_kernel(seg_q_ref, seg_k_ref, q_ref, k_ref, v_ref, g_ref, a_ref, lse_ref, after_ref, dq_ref, dkv_ref):
    queries = q_ref[...] * jnp.bfloat16(0.125)
    key_count = k_ref.shape[0]
    low = lax.broadcasted_iota(jnp.int32, (key_count, 128), 1) < 64
    keys, values, grads = k_ref[...], v_ref[...], g_ref[...]
    allowed = seg_k_ref[...] == seg_q_ref[...]
    products = (grads.astype(jnp.float32) * a_ref[...]).T
    dq, dk, dv = [], [], []
    for side in range(2):
        mine = low if side == 0 else jnp.logical_not(low)
        zero = jnp.zeros_like(keys)
        scores = lanes_dot(jnp.where(mine, keys, zero), queries)
        probs = jnp.where(allowed, jnp.exp(scores - lse_ref[0, side : side + 1, :]), 0.0)
        dots = jnp.sum(products[side * 64 : (side + 1) * 64, :], axis=0, keepdims=True)
        dv.append(jnp.dot(probs.astype(jnp.bfloat16), grads, preferred_element_type=jnp.float32))
        grad_probs = lanes_dot(jnp.where(mine, values, zero), grads)
        grad_scores = (probs * (grad_probs - dots)).astype(jnp.bfloat16)
        dk.append(jnp.dot(grad_scores, queries, preferred_element_type=jnp.float32))
        dq.append(rows_dot(keys, grad_scores)[side * 64 : (side + 1) * 64, :])
    dq_ref[...] = 0.125 * jnp.concatenate(dq, axis=0).T
    dkv_ref[0] = jnp.where(low, dk[0], dk[1]).astype(dkv_ref.dtype)
    dkv_ref[1] = jnp.where(low, dv[0], dv[1]).astype(dkv_ref.dtype)


def attend_back(queries, pair, grads, attended, lse, seg_q, seg_k, kind, after):
    frames, width = queries.shape
    length = pair.shape[0]
    pairs = width // 128
    return pl.pallas_call(
        attend_back_kernel,
        grid=(pairs,),
        in_specs=attend_specs(frames, length, pairs)
        + [
            pl.BlockSpec((frames, 128), lambda p: (0, p)),
            pl.BlockSpec((frames, 128), lambda p: (0, p)),
            pl.BlockSpec((1, 8, frames), lambda p: (p, 0, 0)),
            pl.BlockSpec(memory_space=pl.ANY),
        ],
        out_specs=[
            pl.BlockSpec((frames, 128), lambda p: (0, p)),
            pl.BlockSpec((2, length, 128), lambda p: (0, 0, p)),
        ],
        out_shape=[
            jax.ShapeDtypeStruct((frames, width), jnp.float32),
            jax.ShapeDtypeStruct((2, length, width), kind),
        ],
        compiler_params=pltpu.CompilerParams(vmem_limit_bytes=VMEM_LIMIT),
        cost_estimate=attend_cost(frames, length, pairs, 5),
        name="attend_back",
    )(seg_q.reshape(1, -1), seg_k.reshape(-1, 1), queries, pair, pair, grads, attended, lse, after)


def phi_parts(values):
    below = 0.5 * (1.0 + lax.erf(values * (0.5**0.5)))
    density = jnp.exp(-0.5 * values * values) * (1.0 / math.sqrt(2.0 * math.pi))
    return below, density


def norm_parts(values):
    center = values - jnp.mean(values, axis=-1, keepdims=True)
    scale = lax.rsqrt(jnp.mean(center * center, axis=-1, keepdims=True) + epsilon)
    return center * scale, scale


def norm_back(grad, hat, scale, gain):
    inner = grad * gain
    mean_inner = jnp.mean(inner, axis=-1, keepdims=True)
    mean_hat = jnp.mean(inner * hat, axis=-1, keepdims=True)
    return (inner - mean_inner - hat * mean_hat) * scale


def column_sum(values):
    return jnp.sum(values, axis=0, keepdims=True)


def by_core(core, mine, other):
    return jnp.where(core == 0, mine, other), jnp.where(core == 0, other, mine)


def mix_kernel(first, meta, *refs):
    if first:
        mine_ref, other_ref, gain_ref, shift_ref, away_w_ref, away_bias_ref, w_ref, bias_ref = refs[:8]
        theirs_ref, ours_ref, normed_ref, position_ref = refs[-4:]
    else:
        normed_ref, away_w_ref, away_bias_ref, w_ref, bias_ref = refs[:5]
        theirs_ref, ours_ref = refs[-2:]
    step = pl.program_id(0)
    half = w_ref.shape[1]
    if first:

        @pl.when(step == 0)
        def _():
            left, right = by_core(meta[0], mine_ref[...], other_ref[...])
            position_ref[:, :half] = left
            position_ref[:, half:] = right
            hat, _ = norm_parts(position_ref[...])
            normed_ref[...] = (hat * gain_ref[...] + shift_ref[...]).astype(jnp.bfloat16)

    span = pl.ds(pl.multiple_of(step * half, half), half)
    for out_ref, weight_ref, shift in ((theirs_ref, away_w_ref, away_bias_ref), (ours_ref, w_ref, bias_ref)):
        block = jnp.dot(normed_ref[...], weight_ref[...], preferred_element_type=jnp.float32) + shift[...]
        out_ref[:, span] = block.astype(jnp.bfloat16)


def mix_rows(core, sources, weight, bias, begin, parts, after=()):
    first = len(sources) > 1
    tokens = sources[0].shape[0]
    features = weight.shape[0]
    half = features // 2

    def columns(flip):
        def at(i, meta):
            return (0, 2 * (begin + i) + (1 - meta[0] if flip else meta[0]))

        return [pl.BlockSpec((features, half), at), pl.BlockSpec((1, half), at)]

    whole = lambda shape: pl.BlockSpec(shape, lambda i, meta: (0, 0))
    out_specs = [whole((tokens, parts * half))] * 2
    out_shape = [jax.ShapeDtypeStruct((tokens, parts * half), jnp.bfloat16)] * 2
    if first:
        out_specs = out_specs + [whole((tokens, features))] * 2
        out_shape = out_shape + [jax.ShapeDtypeStruct((tokens, features), kind) for kind in (jnp.bfloat16, jnp.float32)]
    return pl.pallas_call(
        partial(mix_kernel, first),
        grid_spec=pltpu.PrefetchScalarGridSpec(
            num_scalar_prefetch=1,
            grid=(parts,),
            in_specs=[whole(item.shape) for item in sources]
            + columns(True)
            + columns(False)
            + [pl.BlockSpec(memory_space=pl.ANY)] * len(after),
            out_specs=out_specs,
        ),
        out_shape=out_shape,
        compiler_params=pltpu.CompilerParams(vmem_limit_bytes=VMEM_LIMIT, dimension_semantics=IN_ORDER),
        cost_estimate=cost(
            flops=4 * parts * tokens * half * features, bytes_accessed=4 * parts * half * features, transcendentals=0
        ),
        name="norm_keys_values" if first else "queries",
    )(core, *sources, weight, bias, weight, bias, *after)


def unmix_kernel(
    meta, mine_ref, other_ref, w_ref, away_w_ref, position_ref, resid_ref, gain_ref, *refs
):
    ours_ref, theirs_ref, sums_ref, total = refs[-4:]
    step = pl.program_id(0)
    half = theirs_ref.shape[1]

    @pl.when(step == 0)
    def _():
        total[...] = jnp.zeros_like(total)

    total[...] += lanes_dot(mine_ref[...], w_ref[...]) + lanes_dot(other_ref[...], away_w_ref[...])

    @pl.when(step == 2)
    def _():
        grad = total[...]
        hat, scale = norm_parts(position_ref[...])
        sums_ref[0:1, :] = column_sum(grad * hat)
        sums_ref[1:2, :] = column_sum(grad)
        sums_ref[2:8, :] = jnp.zeros((6, 2 * half), jnp.float32)
        result = resid_ref[...] + norm_back(grad, hat, scale, gain_ref[...])
        low_half, high_half = result[:, :half], result[:, half:]
        ours_ref[...] = jnp.where(meta[0] == 0, low_half, high_half)
        theirs_ref[...] = jnp.where(meta[0] == 0, high_half, low_half)


def unmix_rows(core, mine, other, weight, position, grad_resid, gain, after):
    tokens, features = position.shape
    half = features // 2

    whole = lambda shape: pl.BlockSpec(shape, lambda i, meta: (0, 0))
    return pl.pallas_call(
        unmix_kernel,
        grid_spec=pltpu.PrefetchScalarGridSpec(
            num_scalar_prefetch=1,
            grid=(3,),
            in_specs=[
                pl.BlockSpec((tokens, half), lambda i, meta: (0, i)),
                pl.BlockSpec((tokens, half), lambda i, meta: (0, i)),
                pl.BlockSpec((features, half), lambda i, meta: (0, 2 * i + meta[0])),
                pl.BlockSpec((features, half), lambda i, meta: (0, 2 * i + 1 - meta[0])),
                whole((tokens, features)),
                whole((tokens, features)),
                whole((1, features)),
            ]
            + [pl.BlockSpec(memory_space=pl.ANY)] * len(after),
            out_specs=[whole((tokens, half)), whole((tokens, half)), whole((8, features))],
            scratch_shapes=[pltpu.VMEM((tokens, features), jnp.float32)],
        ),
        out_shape=[
            jax.ShapeDtypeStruct((tokens, half), jnp.float32),
            jax.ShapeDtypeStruct((tokens, half), jnp.float32),
            jax.ShapeDtypeStruct((8, features), jnp.float32),
        ],
        compiler_params=pltpu.CompilerParams(vmem_limit_bytes=VMEM_LIMIT, dimension_semantics=IN_ORDER),
        cost_estimate=cost(flops=12 * tokens * half * features, bytes_accessed=14 * half * features, transcendentals=0),
        name="qkv_and_norm_back",
    )(core, mine, other, weight, weight, position, grad_resid, gain, *after)


def pack_places(features, width):
    places, at = {}, 0
    for name, size in (
        ("active", width), ("second", features), ("attended", features), ("up", width // 2),
        ("out", features // 2), ("branch", features // 2),
    ):
        places[name] = at
        at += size
    places["all"] = at
    return places


def middle_kernel(
    meta, mine_ref, other_ref, position_ref, w_out_ref, w_up_ref, w_down_ref, up_bias_ref, head_w_ref, head_b_ref,
    labels_ref, rows_ref,
    pack_ref, output_ref, out_low_ours, up_ours, branch_ours, att_ours, att_theirs, resid_grad_ref, sums_ref,
    up_sums_ref, head_ref, last_ref,
    resid, total, slope, grad_out, grad_low,
):
    step = pl.program_id(0)
    chunks = slope.shape[0]
    core = meta[0]
    half = mine_ref.shape[1]
    features = 2 * half
    chunk_width = slope.shape[2]
    places = pack_places(features, chunks * chunk_width)

    def at(name, size):
        return slice(places[name], places[name] + size)

    second_at, attended_at = at("second", features), at("attended", features)

    def store_halves(ours, theirs, values):
        low_half, high_half = values[:, :half], values[:, half:]
        ours[...] = jnp.where(core == 0, low_half, high_half)
        theirs[...] = jnp.where(core == 0, high_half, low_half)

    @pl.when(step == 0)
    def _():
        left, right = by_core(core, mine_ref[...].astype(jnp.float32), other_ref[...].astype(jnp.float32))
        pack_ref[:, places["attended"] : places["attended"] + half] = left.astype(jnp.bfloat16)
        pack_ref[:, places["attended"] + half : places["attended"] + features] = right.astype(jnp.bfloat16)
        resid[...] = (
            position_ref[...]
            + jnp.dot(pack_ref[:, attended_at], w_out_ref[...], preferred_element_type=jnp.float32)
            + rows_ref[2:3, :]
        )
        hat, _ = norm_parts(resid[...])
        pack_ref[:, second_at] = (hat * rows_ref[0:1, :] + rows_ref[1:2, :]).astype(jnp.bfloat16)
        total[...] = jnp.zeros_like(total)

    @pl.when(step < chunks)
    def _():
        raised = jnp.dot(pack_ref[:, second_at], w_up_ref[...], preferred_element_type=jnp.float32) + up_bias_ref[...]
        below, density = phi_parts(raised)
        slope[step] = below + raised * density
        active = (raised * below).astype(jnp.bfloat16)
        pack_ref[:, pl.ds(pl.multiple_of(places["active"] + step * chunk_width, chunk_width), chunk_width)] = active
        total[...] += jnp.dot(active, w_down_ref[...], preferred_element_type=jnp.float32)

    @pl.when(step == chunks - 1)
    def _():
        low = (resid[...] + total[...] + rows_ref[3:4, :]).astype(jnp.bfloat16)
        output_ref[...] = low
        logits = jnp.dot(low, head_w_ref[...], preferred_element_type=jnp.float32) + head_b_ref[...]
        top = jnp.max(logits, axis=-1, keepdims=True)
        shifted = jnp.exp(logits - top)
        sums = jnp.sum(shifted, axis=-1, keepdims=True)
        onehot = labels_ref[...] == lax.broadcasted_iota(jnp.int32, logits.shape, 1)
        picked = jnp.sum(jnp.where(onehot, logits, 0.0), axis=-1, keepdims=True)
        loss = jnp.sum(top + jnp.log(sums) - picked)
        grad_logits = (shifted / sums - onehot.astype(jnp.float32)).astype(jnp.bfloat16)
        head_ref[...] = rows_dot(grad_logits, low)
        last_ref[...] = jnp.zeros_like(last_ref)
        last_ref[0:1, 0:VOCAB] = column_sum(grad_logits.astype(jnp.float32))
        last_ref[1:2, :] = jnp.full((1, 128), loss, jnp.float32)
        grad = lanes_dot(grad_logits, head_w_ref[...])
        grad_out[...] = grad
        grad_low[...] = grad.astype(jnp.bfloat16)
        store_halves(out_low_ours, pack_ref.at[:, at("out", half)], grad_low[...])
        sums_ref[3:4, :] = column_sum(grad_low[...].astype(jnp.float32))
        sums_ref[4:8, :] = jnp.zeros((4, 2 * half), jnp.float32)
        total[...] = jnp.zeros_like(total)

    @pl.when(step >= chunks)
    def _():
        chunk = 2 * chunks - 1 - step
        grad = lanes_dot(grad_low[...], w_down_ref[...]) * slope[chunk]
        low = grad.astype(jnp.bfloat16)
        up_sums_ref[0] = jnp.broadcast_to(column_sum(low.astype(jnp.float32)), up_sums_ref.shape[1:])
        total[...] += lanes_dot(low, w_up_ref[...])
        ours = (chunk >= chunks // 2) == (core == 1)

        @pl.when(ours)
        def _():
            up_ours[...] = low

        @pl.when(jnp.logical_not(ours))
        def _():
            place = places["up"] + (chunk & (chunks // 2 - 1)) * chunk_width
            pack_ref[:, pl.ds(pl.multiple_of(place, chunk_width), chunk_width)] = low

    @pl.when(step == 2 * chunks - 1)
    def _():
        hat, scale = norm_parts(resid[...])
        grad = total[...]
        sums_ref[0:1, :] = column_sum(grad * hat)
        sums_ref[2:3, :] = column_sum(grad)
        result = grad_out[...] + norm_back(grad, hat, scale, rows_ref[0:1, :])
        resid_grad_ref[...] = result
        branch = result.astype(jnp.bfloat16)
        store_halves(branch_ours, pack_ref.at[:, at("branch", half)], branch)
        sums_ref[1:2, :] = column_sum(branch.astype(jnp.float32))
        store_halves(att_ours, att_theirs, lanes_dot(branch, w_out_ref[...]).astype(jnp.bfloat16))


def middle(core, mine, other, position, w_out, w_up, w_down, up_bias, head_w, head_b, labels, rows):
    tokens, features = position.shape
    half = features // 2
    width = w_up.shape[1]
    chunks = 2
    chunk = width // chunks
    vocab = head_w.shape[1]
    last = 2 * chunks - 1

    def part(i):
        return jnp.where(i < chunks, i, last - i)

    def own_up(i, meta):
        back = part(jnp.maximum(i, chunks))
        return jnp.where(meta[0] == 0, jnp.minimum(back, chunks // 2 - 1), jnp.maximum(back - chunks // 2, 0))

    whole = lambda shape: pl.BlockSpec(shape, lambda i, meta: tuple(0 for _ in shape))
    low = lambda *shape: jax.ShapeDtypeStruct(shape, jnp.bfloat16)
    full = lambda *shape: jax.ShapeDtypeStruct(shape, jnp.float32)
    return pl.pallas_call(
        middle_kernel,
        grid_spec=pltpu.PrefetchScalarGridSpec(
            num_scalar_prefetch=1,
            grid=(2 * chunks,),
            in_specs=[
                whole((tokens, half)),
                whole((tokens, half)),
                whole((tokens, features)),
                whole((features, features)),
                pl.BlockSpec((features, chunk), lambda i, meta: (0, part(i))),
                pl.BlockSpec((chunk, features), lambda i, meta: (part(i), 0)),
                pl.BlockSpec((1, chunk), lambda i, meta: (0, part(i))),
                whole((features, vocab)),
                whole((1, vocab)),
                whole((tokens, 1)),
                whole((8, features)),
            ],
            out_specs=[
                whole((tokens, pack_places(features, width)["all"])),
                whole((tokens, features)),
                whole((tokens, half)),
                pl.BlockSpec((tokens, chunk), lambda i, meta: (0, own_up(i, meta))),
                whole((tokens, half)),
                whole((tokens, half)),
                whole((tokens, half)),
                whole((tokens, features)),
                whole((8, features)),
                pl.BlockSpec((1, 8, chunk), lambda i, meta: (part(jnp.maximum(i, chunks)), 0, 0)),
                whole((vocab, features)),
                whole((8, 128)),
            ],
            scratch_shapes=[
                pltpu.VMEM((tokens, features), jnp.float32),
                pltpu.VMEM((tokens, features), jnp.float32),
                pltpu.VMEM((chunks, tokens, chunk), jnp.float32),
                pltpu.VMEM((tokens, features), jnp.float32),
                pltpu.VMEM((tokens, features), jnp.bfloat16),
            ],
        ),
        out_shape=[
            low(tokens, pack_places(features, width)["all"]),
            low(tokens, features),
            low(tokens, half),
            low(tokens, width // 2),
            low(tokens, half),
            low(tokens, half),
            low(tokens, half),
            full(tokens, features),
            full(8, features),
            full(chunks, 8, chunk),
            full(vocab, features),
            full(8, 128),
        ],
        compiler_params=pltpu.CompilerParams(vmem_limit_bytes=VMEM_LIMIT, dimension_semantics=IN_ORDER),
        cost_estimate=cost(
            flops=8 * tokens * features * width, bytes_accessed=8 * features * width, transcendentals=2 * tokens * width
        ),
        name="middle",
    )(core, mine, other, position, w_out, w_up, w_down, up_bias, head_w, head_b, labels, rows)


def conv_grad_kernel(meta, ours_ref, got_ref, slope_ref, *refs):
    position_ref, grad_ref, edge_ref, own_ref, to_x_ref, to_y_ref, to_xy_ref, sums_ref = refs[-8:]
    core, y, x = meta[0], meta[1], meta[2]
    frames = ours_ref.shape[0]
    rim = edge_ref.shape[0]
    ours, got = ours_ref[...], got_ref[...]
    position_ref[0:frames, :] = jnp.where(core == 0, ours, got)
    position_ref[frames:, :] = jnp.where(core == 0, got, ours)
    grad_ref[...] = (position_ref[...] * slope_ref[...]).astype(jnp.bfloat16)
    side = x ^ (meta[3] & 1)
    edge_ref[...] = jnp.where(side == 0, grad_ref[2 * frames - rim :, :], grad_ref[0:rim, :])
    sums_ref[...] = jnp.broadcast_to(column_sum(grad_ref[...].astype(jnp.float32)), sums_ref.shape)
    for ref, yy, xx in ((own_ref, y, x), (to_x_ref, y, 1 - x), (to_y_ref, 1 - y, x), (to_xy_ref, 1 - y, 1 - x)):
        ref[...] = grad_ref[:, pl.ds(pl.multiple_of(256 * xx + 128 * yy, 128), 128)]


def conv_grad_rows(meta, ours, got, slope, after):
    frames, half = ours.shape
    operands = (ours, got, slope)
    shapes = [((2 * frames, half), jnp.float32), ((2 * frames, half), jnp.bfloat16), ((KERNEL // 2, half), jnp.bfloat16)]
    shapes += [((2 * frames, 128), jnp.bfloat16)] * 4 + [((8, half), jnp.float32)]
    return pl.pallas_call(
        conv_grad_kernel,
        grid_spec=pltpu.PrefetchScalarGridSpec(
            num_scalar_prefetch=1,
            grid=(1,),
            in_specs=[pl.BlockSpec(item.shape, lambda i, m: (0, 0)) for item in operands]
            + [pl.BlockSpec(memory_space=pl.ANY)] * len(after),
            out_specs=[pl.BlockSpec(shape, lambda i, m: (0, 0)) for shape, _ in shapes],
        ),
        out_shape=[jax.ShapeDtypeStruct(shape, kind) for shape, kind in shapes],
        compiler_params=pltpu.CompilerParams(vmem_limit_bytes=VMEM_LIMIT, dimension_semantics=IN_ORDER),
        cost_estimate=cost(flops=0, bytes_accessed=4000000, transcendentals=0),
        name="conv_grad_rows",
    )(meta, *operands, *after)


def weight_kernel(tasks, out_count, meta, *refs):
    refs = list(refs)
    step = pl.program_id(0)
    inputs = []
    for task in tasks:
        count = 1 if task["right"] is None else 4
        inputs.append([refs.pop(0) for _ in range(count + (task["add"] is not None))])
    outs = refs[-out_count:]
    begin = 0
    for task, ins in zip(tasks, inputs):
        if task["joint"]:
            begin = begin - task["blocks"]
        rows, columns = task["rows"], task["columns"]

        def store(where, values, at, task=task):
            index, column = where
            size = values.shape[0]
            span = pl.ds(pl.multiple_of(at * size, size), size)
            outs[index][span, column : column + values.shape[1]] = values.astype(jnp.bfloat16)

        @pl.when(jnp.logical_and(step >= begin, step < begin + task["blocks"]))
        def _(task=task, ins=ins, begin=begin, store=store, rows=rows, columns=columns):
            if task["right"] is None:
                total = ins[0][...].astype(jnp.float32)
            else:
                total = rows_dot(ins[0][...], ins[2][...]) + rows_dot(ins[1][...], ins[3][...])
            if task["add"] is not None:
                total = total + ins[-1][...].astype(jnp.float32)
            at = step - begin + task["place"]
            if task["split"] is None:
                for where in task["outs"]:
                    store(where, total, at)
                return
            if task["split"] == "columns":
                first, second = total[:, : columns // 2], total[:, columns // 2 :]
            else:
                blocks = total.reshape(-1, 2, task["unit"], columns)
                first, second = (blocks[:, k].reshape(rows // 2, columns) for k in range(2))
            bit = task["bit"](meta)
            store(task["outs"][0], jnp.where(bit == 0, second, first), at)
            store(task["outs"][1], jnp.where(bit == 0, first, second), at)

        begin = begin + task["blocks"]


def weight_task(
    outs, left, right, rows, blocks, row_of, columns, column_of, add=None, add_of=None, split=None, bit=None, unit=0, place=0,
    joint=False,
):
    return dict(
        outs=outs, left=left, right=right, rows=rows, blocks=blocks, row_of=row_of, columns=columns,
        column_of=column_of, add=add, add_of=add_of, split=split, bit=bit, unit=unit, place=place,
        joint=joint,
    )


def weight_parts(meta, tasks, shapes, name, after):
    in_specs, operands = [], []
    begin, flops, moved = 0, 0, 0
    for task in tasks:
        rows, columns, blocks = task["rows"], task["columns"], task["blocks"]
        if task["joint"]:
            begin -= blocks
        tokens = task["left"][0][0].shape[0]
        if task["right"] is None:
            in_specs.append(
                pl.BlockSpec((rows, columns), lambda i, m, t=task, begin=begin, blocks=blocks: (t["row_of"](jnp.clip(i - begin, 0, blocks - 1), m), 0))
            )
            operands.append(task["left"][0][0])

        def local(i, begin=begin, blocks=blocks):
            return jnp.clip(i - begin, 0, blocks - 1)

        for array, base in task["left"] if task["right"] is not None else ():
            in_specs.append(
                pl.BlockSpec(
                    (tokens, rows), lambda i, m, t=task, local=local, base=base: (0, base // t["rows"] + t["row_of"](local(i), m))
                )
            )
            operands.append(array)
        for array, base in task["right"] or ():
            in_specs.append(
                pl.BlockSpec((tokens, columns), lambda i, m, t=task, base=base: (0, base // t["columns"] + t["column_of"](m)))
            )
            operands.append(array)
        if task["add"] is not None:
            in_specs.append(pl.BlockSpec((rows, columns), lambda i, m, t=task, local=local: t["add_of"](local(i), m)))
            operands.append(task["add"])
        begin += blocks
        flops += 4 * tokens * rows * blocks * columns
        moved += 2 * rows * blocks * columns + 4 * tokens * (rows * blocks + columns)
    in_specs += [pl.BlockSpec(memory_space=pl.ANY)] * len(after)
    operands += list(after)
    return pl.pallas_call(
        partial(weight_kernel, tasks, len(shapes)),
        grid_spec=pltpu.PrefetchScalarGridSpec(
            num_scalar_prefetch=1,
            grid=(begin,),
            in_specs=in_specs,
            out_specs=[pl.BlockSpec(shape, lambda i, m: (0, 0)) for shape in shapes],
        ),
        out_shape=[jax.ShapeDtypeStruct(shape, jnp.bfloat16) for shape in shapes],
        compiler_params=pltpu.CompilerParams(vmem_limit_bytes=VMEM_LIMIT, dimension_semantics=IN_ORDER),
        cost_estimate=cost(flops=flops, bytes_accessed=moved, transcendentals=0),
        name=name,
    )(meta, *operands)


def flip_kernel(meta, own_ref, got_ref, out_ref):
    source = jnp.where(pl.program_id(0) < 4, own_ref[0], got_ref[0])
    out_ref[...] = source.astype(jnp.float32).T


def flip_columns(meta, own, got):
    _, width, rows = own.shape
    count = 8

    def column(i, m):
        return 4 * (m[0] ^ (i >> 2)) + 2 * (i & 1) + (m[1] ^ ((i >> 1) & 1))

    return pl.pallas_call(
        flip_kernel,
        grid_spec=pltpu.PrefetchScalarGridSpec(
            num_scalar_prefetch=1,
            grid=(count,),
            in_specs=[
                pl.BlockSpec((1, width, rows), lambda i, m: (jnp.minimum(i, 3), 0, 0)),
                pl.BlockSpec((1, width, rows), lambda i, m: (jnp.maximum(i - 4, 0), 0, 0)),
            ],
            out_specs=pl.BlockSpec((rows, width), lambda i, m: (0, column(i, m))),
        ),
        out_shape=jax.ShapeDtypeStruct((rows, count * width), jnp.float32),
        compiler_params=pltpu.CompilerParams(vmem_limit_bytes=VMEM_LIMIT, dimension_semantics=IN_ORDER),
        cost_estimate=cost(flops=0, bytes_accessed=6 * count * width * rows, transcendentals=0),
        name="flip_columns",
    )(meta, own, got)


def small_kernel(meta, head_ref, mid_ref, first_ref, conv_ref, ours_ref, got_ref, up_ref, last_ref, *refs):
    out_ref = refs[-1]
    core = meta[0]
    half = conv_ref.shape[1]
    zero = jnp.zeros((1, half), jnp.float32)
    wide = lambda *parts: jnp.concatenate(parts, axis=1)

    def halves(part):
        ours = ours_ref[0:1, part * half : (part + 1) * half]
        got = got_ref[0:1, part * half : (part + 1) * half]
        return wide(jnp.where(core == 0, ours, got), jnp.where(core == 0, got, ours))

    conv = conv_ref[0:1, :]
    unit = last_ref.shape[1]
    rows = [
        head_ref[...],
        mid_ref[0:4, :],
        first_ref[0:2, :],
        wide(jnp.where(core == 0, conv, zero), jnp.where(core == 0, zero, conv)),
        halves(0),
        halves(2),
    ]
    rows += [wide(*(up_ref[j, 0:1, r * unit : (r + 1) * unit] for j in range(8))) for r in range(4)]
    rows += [wide(*([last_ref[...]] * 8)), jnp.zeros((128 - VOCAB - 14, 2 * half), jnp.float32)]
    out_ref[...] = jnp.concatenate(rows, axis=0).T.astype(out_ref.dtype)


def small_sums(meta, head, mid, first, conv, ours, got, up, last):
    operands = (head, mid, first, conv, ours, got, up, last)
    features = head.shape[1]
    return pl.pallas_call(
        small_kernel,
        grid_spec=pltpu.PrefetchScalarGridSpec(
            num_scalar_prefetch=1,
            grid=(1,),
            in_specs=[pl.BlockSpec(item.shape, lambda i, m, n=item.ndim: (0,) * n) for item in operands],
            out_specs=pl.BlockSpec((features, 128), lambda i, m: (0, 0)),
        ),
        out_shape=jax.ShapeDtypeStruct((features, 128), jnp.bfloat16),
        compiler_params=pltpu.CompilerParams(vmem_limit_bytes=VMEM_LIMIT, dimension_semantics=IN_ORDER),
        cost_estimate=cost(flops=0, bytes_accessed=400000, transcendentals=0),
        name="small_sums",
    )(meta, *operands)


def tile_lists(seg_ext, rise):
    row_count = seg_ext.shape[0]
    frames = seg_ext.shape[1] - KERNEL
    tiles = frames // 64
    center = seg_ext[:, KERNEL // 2 : KERNEL // 2 + frames].reshape(row_count, tiles, 64)
    first = center[:, :, 0].reshape(-1)
    counts = (center[:, :, 63].reshape(-1) - first + 1).astype(jnp.int32)
    ends = jnp.cumsum(counts)
    slots = row_count * (tiles + rise)
    slot = jnp.arange(slots, dtype=jnp.int32)
    tile = jnp.sum((slot[:, None] >= ends[None, :]).astype(jnp.int32), axis=1)
    used = tile < row_count * tiles
    tile = jnp.minimum(tile, row_count * tiles - 1)
    onehot = tile[:, None] == jnp.arange(row_count * tiles, dtype=jnp.int32)[None, :]
    begin = jnp.sum(jnp.where(onehot, (ends - counts)[None, :], 0), axis=1)
    number = jnp.sum(jnp.where(onehot, first[None, :], 0), axis=1) + slot - begin
    number = jnp.where(used, number, -2)
    in_block = tile + (tile // tiles) * (KERNEL // 64)
    return in_block.astype(jnp.int32), tile.astype(jnp.int32), number.astype(jnp.int32)


def lane_low(rows):
    return lax.broadcasted_iota(jnp.int32, (rows, 128), 1) < 64


def half_roll(block):
    return pltpu.roll(block, 64, 1)


def quad_rows(src, rows, side):
    low = lane_low(rows)
    parts = [src[pl.ds(j, rows, stride=4), :] for j in range(4)]
    halves = []
    for a, b in ((0, 1), (2, 3)):
        if side == 0:
            halves.append(jnp.where(low, parts[a], half_roll(parts[b])))
        else:
            halves.append(jnp.where(low, half_roll(parts[a]), parts[b]))
    return halves


def conv_setup(meta, slots, seg_ref, flat, shifts, masks):
    rows4 = seg_ref.shape[0]
    blocks = rows4 // 16
    one, zero = jnp.ones((16, 256), jnp.bfloat16), jnp.zeros((16, 256), jnp.bfloat16)
    flat[0:rows4, :] = seg_ref[...]
    flat[rows4:, :] = jnp.zeros((16, 256), jnp.float32)
    for p in range(16):
        shifts[p] = flat[pl.ds(p, rows4), :].astype(jnp.bfloat16).reshape(blocks, 16, 256)

    @pl.loop(0, slots)
    def _(v):
        at = meta[1 + v]
        number = jnp.full((16, 256), meta[1 + 2 * slots + v].astype(jnp.float32), jnp.float32).astype(jnp.bfloat16)
        row = pl.multiple_of(v * 16, 16)
        for b in range(TAP_BLOCKS):
            ids = shifts[b % 16, at + b // 16]
            masks[pl.ds(row, 16), b * 256 : (b + 1) * 256] = jnp.where(ids == number, one, zero)


def conv_shifts(wide, side, flat, shifts):
    rows4 = shifts.shape[1] * 16
    halves = quad_rows(wide, rows4, side)
    flat[0:rows4, 0:128] = halves[0]
    flat[0:rows4, 128:256] = halves[1]
    for p in range(16):
        shifts[p] = flat[pl.ds(p, rows4), :].astype(jnp.bfloat16).reshape(rows4 // 16, 16, 256)


def conv_patch(places, b, shifts, masks):
    span = slice(b * 256, (b + 1) * 256)
    pieces = [
        shifts[b % 16, at + b // 16] * masks[v * 16 : (v + 1) * 16, span] for v, at in enumerate(places)
    ]
    return jnp.concatenate(pieces, axis=0)


def conv_taps(w_ref, side, b, taps):
    rows = 256
    low = lane_low(rows)
    depth = w_ref.shape[0]
    zero = jnp.zeros((64, 128), jnp.bfloat16)
    if b == 0:
        here, before = w_ref[0:rows, :], jnp.concatenate([zero, w_ref[0 : rows - 64, :]], axis=0)
    elif b * rows < depth:
        here, before = w_ref[b * rows : (b + 1) * rows, :], w_ref[b * rows - 64 : (b + 1) * rows - 64, :]
    else:
        here, before = jnp.concatenate([zero] * 4, axis=0), jnp.concatenate([w_ref[depth - 64 :, :]] + [zero] * 3, axis=0)
    block = jnp.where(low, here, half_roll(before)) if side == 0 else jnp.where(low, half_roll(here), before)
    taps[128 + b * rows : 128 + (b + 1) * rows, :] = block
    return jnp.concatenate([block, taps[b * rows : (b + 1) * rows, :]], axis=1)


def conv_kernel(slots, backward, meta, x_ref, seg_ref, w_ref, extra_ref, *refs):
    if backward:
        o_ref, *refs = refs[-8:]
    else:
        o_ref, *refs = refs[-9:]
    if backward:
        wide, flat, shifts, masks, taps, sums, outs = refs
    else:
        slope_ref, wide, flat, shifts, masks, taps, sums, outs = refs

    @pl.when(pl.program_id(0) == 0)
    def _():
        conv_setup(meta, slots, seg_ref, flat, shifts, masks)

    wide[...] = x_ref[...].astype(jnp.float32)
    taps[0:128, :] = jnp.zeros((128, 128), jnp.bfloat16)
    out_rows = o_ref.shape[0] // 4
    places = [meta[1 + v] for v in range(slots)]
    for side in range(2):
        conv_shifts(wide, side, flat, shifts)
        total = jnp.zeros((256, slots * 16) if backward else (slots * 16, 256), jnp.float32)
        for b in range(TAP_BLOCKS):
            weight = conv_taps(w_ref, side, b, taps)
            if backward:
                total = total + lanes_dot(weight, conv_patch(places, TAP_BLOCKS - 1 - b, shifts, masks))
            else:
                total = total + jnp.dot(
                    conv_patch(places, b, shifts, masks), weight, preferred_element_type=jnp.float32
                )
        sums[...] = total.T if backward else total

        @pl.loop(0, slots)
        def _(v):
            to = pl.ds(pl.multiple_of(meta[1 + slots + v] * 16, 16), 16)
            row = pl.ds(pl.multiple_of(v * 16, 16), 16)
            keep = masks[row, 16 * 256 : 17 * 256].astype(jnp.float32) > 0.5
            outs[side, to, :] = jnp.where(keep, sums[row, :], outs[side, to, :])

    low = lane_low(out_rows)
    for half in range(2):
        zero_side = outs[0, :, half * 128 : (half + 1) * 128]
        one_side = outs[1, :, half * 128 : (half + 1) * 128]
        wide[pl.ds(2 * half, out_rows, stride=4), :] = jnp.where(low, zero_side, half_roll(one_side))
        wide[pl.ds(2 * half + 1, out_rows, stride=4), :] = jnp.where(low, half_roll(zero_side), one_side)
    result = wide[0 : 4 * out_rows, :]
    if backward:
        o_ref[...] = (extra_ref[...] + result).astype(o_ref.dtype)
    else:
        result = result + extra_ref[...]
        below, density = phi_parts(result)
        center = x_ref[KERNEL // 2 : KERNEL // 2 + 4 * out_rows, :].astype(jnp.float32)
        o_ref[...] = center + result * below
        slope_ref[...] = below + result * density


def seg_quads(seg_ext):
    quads = seg_ext.astype(jnp.float32).reshape(-1, 4)
    return jnp.repeat(quads, 64, axis=1)


def grouped_conv(x_ext, seg_ext, weight, extra, first_pair, rise, backward, begin=0, pairs=None, after=()):
    row_count, length, width = x_ext.shape
    frames = length - KERNEL
    pairs = width // 128 if pairs is None else pairs
    in_block, tile, number = tile_lists(seg_ext, rise)
    slots = in_block.shape[0]
    meta = jnp.concatenate([jnp.reshape(first_pair, (1,)).astype(jnp.int32), in_block, tile, number])
    rows4 = row_count * length // 4
    out4 = row_count * frames // 4
    depth = TAP_BLOCKS * 256
    return pl.pallas_call(
        partial(conv_kernel, slots, backward),
        grid_spec=pltpu.PrefetchScalarGridSpec(
            num_scalar_prefetch=1,
            grid=(pairs,),
            in_specs=[
                pl.BlockSpec((row_count * length, 128), lambda p, meta: (0, begin + p)),
                pl.BlockSpec((rows4, 256), lambda p, meta: (0, 0)),
                pl.BlockSpec((weight.shape[0], 128), lambda p, meta: (0, meta[0] + begin + p)),
                pl.BlockSpec((extra.shape[0], 128), lambda p, meta: (0, begin + p)),
            ]
            + [pl.BlockSpec(memory_space=pl.ANY)] * len(after),
            out_specs=[pl.BlockSpec((row_count * frames, 128), lambda p, meta: (0, p))] * (1 if backward else 2),
            scratch_shapes=[
                pltpu.VMEM((row_count * length, 128), jnp.float32),
                pltpu.VMEM((rows4 + 16, 256), jnp.float32),
                pltpu.VMEM((16, rows4 // 16, 16, 256), jnp.bfloat16),
                pltpu.VMEM((slots * 16, depth), jnp.bfloat16),
                pltpu.VMEM((128 + depth, 128), jnp.bfloat16),
                pltpu.VMEM((slots * 16, 256), jnp.float32),
                pltpu.VMEM((2, out4, 256), jnp.float32),
            ],
        ),
        out_shape=[jax.ShapeDtypeStruct((row_count * frames, 128 * pairs), jnp.bfloat16 if backward else jnp.float32)]
        * (1 if backward else 2),
        compiler_params=pltpu.CompilerParams(vmem_limit_bytes=VMEM_LIMIT, dimension_semantics=IN_ORDER),
        cost_estimate=cost(
            flops=2 * pairs * 2 * slots * 16 * 256 * depth, bytes_accessed=pairs * weight.shape[0] * 256, transcendentals=0
        ),
        name="conv_back" if backward else "conv_forth",
    )(meta, x_ext.reshape(row_count * length, width), seg_quads(seg_ext), weight, extra, *after)


def at_block(b):
    return pl.ds(b * 256, 256) if isinstance(b, int) else pl.ds(pl.multiple_of(b * 256, 256), 256)


def id_block(number):
    return jnp.full((16, 256), number, jnp.float32).astype(jnp.bfloat16)


def conv_ids(seg_ref, flat, ids):
    rows4 = seg_ref.shape[0]
    flat[0:rows4, :] = seg_ref[...]
    flat[rows4:, :] = jnp.zeros((16, 256), jnp.float32)
    for p in range(16):
        ids[p] = flat[pl.ds(p, rows4), :].astype(jnp.bfloat16).reshape(rows4 // 16, 16, 256)


def conv_cut(places, numbers, b, shifts, ids):
    nothing = jnp.zeros((16, 256), jnp.bfloat16)
    pieces = []
    for at, number in zip(places, numbers):
        same = ids[b & 15, at + (b >> 4)] == id_block(number)
        pieces.append(jnp.where(same, shifts[b & 15, at + (b >> 4)], nothing))
    return jnp.concatenate(pieces, axis=0)


def conv_weight_kernel(slots, meta, x_ref, seg_ref, g_ref, *refs):
    send_ref, keep_ref, wide, wide_g, flat, shifts, masks, quads, picks, sums = refs[-10:]
    @pl.when(pl.program_id(0) == 0)
    def _():
        conv_ids(seg_ref, flat, masks)

    wide[...] = x_ref[...].astype(jnp.float32)
    wide_g[...] = g_ref[...].astype(jnp.float32)
    out_rows = g_ref.shape[0] // 4
    low = lane_low(64)
    places = [meta[1 + v] for v in range(slots)]
    numbers = [meta[1 + 2 * slots + v].astype(jnp.float32) for v in range(slots)]
    nothing = jnp.zeros((16, 256), jnp.bfloat16)
    for side in range(2):
        conv_shifts(wide, side, flat, shifts)
        halves = quad_rows(wide_g, out_rows, side)
        quads[:, 0:128] = halves[0].astype(jnp.bfloat16)
        quads[:, 128:256] = halves[1].astype(jnp.bfloat16)

        for v in range(slots):
            at = pl.ds(pl.multiple_of(meta[1 + slots + v] * 16, 16), 16)
            same = masks[0, places[v] + 1] == id_block(numbers[v])
            picks[v * 16 : (v + 1) * 16, :] = jnp.where(same, quads[at, :], nothing)

        turned = picks[...].T

        @pl.loop(0, TAP_BLOCKS, unroll=DW_UNROLL)
        def _(b):
            sums[:, at_block(b)] = jnp.dot(
                turned, conv_cut(places, numbers, b, shifts, masks), preferred_element_type=jnp.float32
            )

        def piece(j, q):
            return sums[j * 64 : (j + 1) * 64, q * 128 : (q + 1) * 128]

        def odd(q):
            return half_roll(piece(1, q) + piece(3, q + 1))

        def emit(block, ref):
            left = odd(16 * block)
            for q in range(16 * block, 16 * block + 16):
                right = odd(q + 1)
                part = piece(0, q) + piece(2, q + 1) + jnp.where(low, left, right)
                first = (q // 8 % 2) * 128 + side * 64
                ref[block // 2, first : first + 64, q % 8 * 128 : (q % 8 + 1) * 128] = part.astype(ref.dtype)
                left = right

        for block in range(4):
            pl.when((meta[0] & 1) == (block & 1))(partial(emit, block, keep_ref))
            pl.when((meta[0] & 1) != (block & 1))(partial(emit, block, send_ref))


def grouped_conv_weight(x_ext, seg_ext, grad, rise, place, after):
    row_count, length, width = x_ext.shape
    frames = length - KERNEL
    pairs = width // 128
    in_block, tile, number = tile_lists(seg_ext, rise)
    slots = in_block.shape[0]
    meta = jnp.concatenate([jnp.reshape(place, (1,)).astype(jnp.int32), in_block, tile, number])
    rows4 = row_count * length // 4
    out4 = row_count * frames // 4
    depth = TAP_BLOCKS * 256
    return pl.pallas_call(
        partial(conv_weight_kernel, slots),
        grid_spec=pltpu.PrefetchScalarGridSpec(
            num_scalar_prefetch=1,
            grid=(pairs,),
            in_specs=[
                pl.BlockSpec((row_count * length, 128), lambda p, meta: (0, p)),
                pl.BlockSpec((rows4, 256), lambda p, meta: (0, 0)),
                pl.BlockSpec((row_count * frames, 128), lambda p, meta: (0, p)),
            ]
            + [pl.BlockSpec(memory_space=pl.ANY)] * len(after),
            out_specs=[pl.BlockSpec((2, 256, KERNEL * 8), lambda p, meta: (0, 0, 0))] * 2,
            scratch_shapes=[
                pltpu.VMEM((row_count * length, 128), jnp.float32),
                pltpu.VMEM((row_count * frames, 128), jnp.float32),
                pltpu.VMEM((rows4 + 16, 256), jnp.float32),
                pltpu.VMEM((16, rows4 // 16, 16, 256), jnp.bfloat16),
                pltpu.VMEM((16, rows4 // 16, 16, 256), jnp.bfloat16),
                pltpu.VMEM((out4, 256), jnp.bfloat16),
                pltpu.VMEM((slots * 16, 256), jnp.bfloat16),
                pltpu.VMEM((256, depth), jnp.float32),
            ],
        ),
        out_shape=[jax.ShapeDtypeStruct((2, 256, KERNEL * 8), jnp.bfloat16)] * 2,
        compiler_params=pltpu.CompilerParams(vmem_limit_bytes=VMEM_LIMIT, dimension_semantics=IN_ORDER),
        cost_estimate=cost(
            flops=2 * pairs * 2 * slots * 16 * 256 * depth, bytes_accessed=width * KERNEL * 128, transcendentals=0
        ),
        name="conv_weight_grad",
    )(meta, x_ext.reshape(row_count * length, width), seg_quads(seg_ext), grad, *after)


def fold_kernel(items, outs_count, meta, *refs):
    refs = list(refs)
    outs = refs[-outs_count:]
    for item in items:
        kept = refs.pop(0)
        gots = [refs.pop(0) for _ in item["gots"]]
        place = item["place"]
        shape = kept.shape
        bit = item["bit"](meta)
        for side, where in ((1 - bit, item["send"]), (bit, item["keep"])):
            buffer, column, lanes = where
            out = outs[buffer]
            if place is None:
                width = shape[3] // 2
                span = pl.ds(pl.multiple_of(side * width, width), width)
                for other in range(shape[0]):
                    total = kept[other, 0, :, span].astype(jnp.float32) + gots[0][other, 0, :, span].astype(jnp.float32)
                    out[other, :, column : column + width] = total.astype(out.dtype)
                continue
            for other in range(shape[1 - place]):
                at = (side, other) if place == 0 else (other, side)
                begin = 0
                for got in gots:
                    width = got.shape[3]
                    total = kept[at[0], at[1], :, begin : begin + width].astype(jnp.float32)
                    total = (total + got[at[0], at[1]].astype(jnp.float32)).astype(out.dtype)
                    rows = shape[2] // lanes
                    for k in range(lanes):
                        first = column + begin + k * shape[3]
                        out[other, :, first : first + width] = total[k * rows : (k + 1) * rows, :]
                    begin += width


def fold_item(kept, gots, place, bit, send, keep):
    return dict(kept=kept, gots=gots, place=place, bit=bit, send=send, keep=keep)


def folds(meta, items, shapes, name, after=()):
    operands = []
    for item in items:
        operands += [item["kept"]] + list(item["gots"])
    described = [dict(item, kept=None, gots=[None] * len(item["gots"])) for item in items]
    return pl.pallas_call(
        partial(fold_kernel, described, len(shapes)),
        grid_spec=pltpu.PrefetchScalarGridSpec(
            num_scalar_prefetch=1,
            grid=(1,),
            in_specs=[pl.BlockSpec(item.shape, lambda i, m: (0, 0, 0, 0)) for item in operands]
            + [pl.BlockSpec(memory_space=pl.ANY)] * len(after),
            out_specs=[pl.BlockSpec(shape, lambda i, m: (0, 0, 0)) for shape in shapes],
        ),
        out_shape=[jax.ShapeDtypeStruct(shape, jnp.bfloat16) for shape in shapes],
        compiler_params=pltpu.CompilerParams(vmem_limit_bytes=VMEM_LIMIT, dimension_semantics=IN_ORDER),
        cost_estimate=cost(flops=0, bytes_accessed=sum(2 * item.size for item in operands), transcendentals=0),
        name=name,
    )(meta, *operands, *after)


def chosen(meta, own_ref, got_ref):
    return jnp.where(pl.program_id(0) // 2 == meta[0], own_ref[0], got_ref[0])


def finish_pair_kernel(meta, own_ref, got_ref, *refs):
    up_ref, down_ref = refs[-2:]
    source = chosen(meta, own_ref, got_ref)
    width = up_ref.shape[1]
    up_ref[...] = source[:, :width].astype(jnp.float32)
    unit = source.shape[0]
    columns = down_ref.shape[1]
    for k in range(down_ref.shape[0] // unit):
        piece = source[:, width + k * columns : width + (k + 1) * columns]
        down_ref[k * unit : (k + 1) * unit, :] = piece.astype(jnp.float32)


def finish_pair(meta, own, got, rows, after):
    unit, total = own.shape[1:]
    width = total // 2
    columns = width * unit // rows
    place = lambda i, m: (0, 2 * (i // 2) + i % 2)
    return pl.pallas_call(
        finish_pair_kernel,
        grid_spec=pltpu.PrefetchScalarGridSpec(
            num_scalar_prefetch=1,
            grid=(4,),
            in_specs=[pl.BlockSpec((1, unit, total), lambda i, m: ((i % 2) ^ m[1], 0, 0))] * 2
            + [pl.BlockSpec(memory_space=pl.ANY)] * len(after),
            out_specs=[pl.BlockSpec((unit, width), place), pl.BlockSpec((rows, columns), place)],
        ),
        out_shape=[
            jax.ShapeDtypeStruct((unit, 4 * width), jnp.float32),
            jax.ShapeDtypeStruct((rows, 4 * columns), jnp.float32),
        ],
        compiler_params=pltpu.CompilerParams(vmem_limit_bytes=VMEM_LIMIT, dimension_semantics=IN_ORDER),
        cost_estimate=cost(flops=0, bytes_accessed=12 * own.size, transcendentals=0),
        name="finish_up_down",
    )(meta, own, got, *after)


def finish_qkv_kernel(eighth, half, meta, own_ref, got_ref, *refs):
    qkv_ref, out_ref = refs[-2:]
    step = pl.program_id(0)
    source = chosen(meta, own_ref, got_ref)
    core, y = step // 2, step % 2
    units = eighth // 128
    per_part = half // 128
    for begin, base in ((0, 0), (eighth, 2 * units)):
        for u in range(units):
            at = base + y * units + u
            at = (at // per_part) * 2 * per_part + core * per_part + at % per_part
            piece = source[:, begin + u * 128 : begin + (u + 1) * 128]
            qkv_ref[:, pl.ds(pl.multiple_of(at * 128, 128), 128)] = piece.astype(jnp.float32)
    quarter = half // 2
    first = pl.multiple_of(step * quarter, quarter)
    out_ref[:, pl.ds(first, quarter)] = source[:, 2 * eighth : 2 * eighth + quarter].astype(jnp.float32)


def finish_qkv(meta, own, got, half, after):
    unit, total = own.shape[1:]
    eighth = 3 * half // 4
    return pl.pallas_call(
        partial(finish_qkv_kernel, eighth, half),
        grid_spec=pltpu.PrefetchScalarGridSpec(
            num_scalar_prefetch=1,
            grid=(4,),
            in_specs=[pl.BlockSpec((1, unit, total), lambda i, m: ((i % 2) ^ m[1], 0, 0))] * 2
            + [pl.BlockSpec(memory_space=pl.ANY)] * len(after),
            out_specs=[
                pl.BlockSpec((unit, 6 * half), lambda i, m: (0, 0)),
                pl.BlockSpec((unit, 2 * half), lambda i, m: (0, 0)),
            ],
        ),
        out_shape=[
            jax.ShapeDtypeStruct((unit, 6 * half), jnp.float32),
            jax.ShapeDtypeStruct((unit, 2 * half), jnp.float32),
        ],
        compiler_params=pltpu.CompilerParams(vmem_limit_bytes=VMEM_LIMIT, dimension_semantics=IN_ORDER),
        cost_estimate=cost(flops=0, bytes_accessed=12 * own.size, transcendentals=0),
        name="finish_qkv_out",
    )(meta, own, got, *after)


AXES = ("y", "c", "z", "x")
LOSS_POWERS = (8, 7, 6, 5, 4, 3, 2, 1)


def device_pairs(place):
    pairs = []
    for y in range(2):
        for c in range(2):
            for z in range(4):
                for x in range(2):
                    ty, tc, tz, tx = place(y, c, z, x)
                    pairs.append((((y * 2 + c) * 4 + z) * 2 + x, ((ty * 2 + tc) * 4 + tz) * 2 + tx))
    return pairs


def move(values, place):
    return lax.ppermute(values, AXES, device_pairs(place))


def swap_core(values):
    return lax.ppermute(values, "c", [(0, 1), (1, 0)])


def swap_x(values):
    return lax.ppermute(values, "x", [(0, 1), (1, 0)])


def swap_y(values):
    return lax.ppermute(values, "y", [(0, 1), (1, 0)])


def swap_xy(values):
    return lax.ppermute(values, ("y", "x"), [(0, 3), (3, 0), (1, 2), (2, 1)])


def swap_z1(values):
    return lax.ppermute(values, "z", [(0, 1), (1, 0), (2, 3), (3, 2)])


def swap_z2(values):
    return lax.ppermute(values, "z", [(0, 2), (2, 0), (1, 3), (3, 1)])


def take(values, index, size, axis):
    return lax.dynamic_slice_in_dim(values, index * size, size, axis)


def once(values, *earlier):
    return lax.optimization_barrier((values,) + earlier)[0]


def ordered(index, mine, other, axis):
    first = jnp.where(index == 0, mine, other)
    second = jnp.where(index == 0, other, mine)
    return jnp.concatenate([first, second], axis=axis)


def to_rows(blocks, x, z):
    got = []
    for turn in range(2):
        mine = lax.dynamic_index_in_dim(blocks, x ^ turn, 0, keepdims=False)
        got.append(move(mine, lambda y, c, z, x: (y, z & 1, 2 * c + (x ^ turn), (z >> 1) ^ x ^ turn)))
    flip = (z & 1) == 0
    return jnp.where(flip, got[0], got[1]), jnp.where(flip, got[1], got[0])


def from_rows(frames, z):
    half = frames.shape[0] // 2
    got = []
    for turn in range(2):
        mine = take(frames, (z & 1) ^ turn, half, 0)
        got.append(move(mine, lambda y, c, z, x: (y, z >> 1, 2 * (x ^ (z & 1)) + c, (z & 1) ^ turn)))
    return got


def split_body(
    feats, segments, labels, conv_weight, w_qkv, w_out, w_up, w_down, head_w, head_b, gains, biases, up_bias
):
    y, c, z, x = (lax.axis_index(name) for name in AXES)
    block, features = feats.shape[1:]
    half = features // 2
    frames = 2 * block
    chip_frames = 2 * frames
    tokens = frames
    rim = KERNEL // 2
    rise = lax.axis_size("z") * lax.axis_size("x") // 2
    meta = jnp.stack([c, y, x, z]).astype(jnp.int32)
    side = x ^ (z & 1)

    label_rows = jnp.pad(labels.astype(jnp.bfloat16)[:, None, :], ((0, 0), (0, 15), (0, features - block)))
    first_block, second_block = to_rows(jnp.concatenate([feats, label_rows], axis=1), x, z)
    feats_own = jnp.concatenate([first_block[:block], second_block[:block]], axis=0)
    labels_own = jnp.concatenate([first_block[block, :block], second_block[block, :block]]).astype(jnp.int32)
    seg_rows = ordered(c, segments, swap_core(segments), 0)
    seg_row = lax.dynamic_index_in_dim(seg_rows, z, 0, keepdims=False)
    seg_halves = seg_row.reshape(2, 2, frames)
    seg_near = lax.dynamic_index_in_dim(seg_halves, side, 0, keepdims=False)
    seg_far = lax.dynamic_index_in_dim(seg_halves, 1 - side, 0, keepdims=False)
    seg_near, seg_far = (jnp.where(c == 0, item, item[::-1]).reshape(-1) for item in (seg_near, seg_far))
    seg_wide = jnp.pad(seg_row, (rim, rim), constant_values=-1)
    seg_ext = lax.dynamic_slice_in_dim(seg_wide, side * chip_frames, chip_frames + 2 * rim, 0)[None]

    def to_chip(values):
        return ordered(c, take(values, c, half, 1), swap_core(take(values, 1 - c, half, 1)), 0)

    def rimmed(values, edge):
        empty = jnp.zeros_like(edge)
        before = jnp.where(side == 0, empty, edge)
        after = jnp.where(side == 0, edge, empty)
        return jnp.concatenate([before, values, after], axis=0)[None]

    def with_rim(values):
        return rimmed(values, swap_x(jnp.where(side == 0, values[chip_frames - rim :], values[:rim])))

    def grouped(own, got_x, got_y, got_xy):
        return ordered(y, ordered(side, own, got_x, 0)[None], ordered(side, got_y, got_xy, 0)[None], 0)

    def to_groups(values):
        def part(yy, xx):
            return lax.dynamic_slice_in_dim(values, 256 * xx + 128 * yy, 128, 1)

        return grouped(
            part(y, x), swap_x(part(y, 1 - x)), swap_y(part(1 - y, x)), swap_xy(part(1 - y, 1 - x))
        )

    shift_bias = biases.T
    qkv_bias = jnp.concatenate([shift_bias[2], jnp.zeros((features,), jnp.float32), shift_bias[3]])[None]
    gain_rows = gains.T
    feats_chip = to_chip(feats_own)
    feats_group = jnp.pad(to_groups(feats_chip), ((0, 0), (rim, rim), (0, 0)))
    seg_pair = ordered(y, seg_row[None], swap_y(seg_row)[None], 0)
    seg_pair = jnp.pad(seg_pair, ((0, 0), (rim, rim)), constant_values=-1)
    position_chip, slope = grouped_conv(
        with_rim(feats_chip), seg_ext, conv_weight, take(shift_bias[0:1], c, half, 1), 4 * c, rise, False
    )
    theirs, ours, normed, position = mix_rows(
        meta,
        (
            take(position_chip, c, frames, 0),
            swap_core(take(position_chip, 1 - c, frames, 0)),
            gain_rows[0:1],
            shift_bias[1:2],
        ),
        w_qkv,
        qkv_bias,
        1,
        2,
        (seg_pair,),
    )
    near = jnp.concatenate([ours, swap_core(theirs)], axis=0)
    got_normed = swap_core(normed)
    far = swap_x(near)
    theirs, ours = mix_rows(meta, (normed,), w_qkv, qkv_bias, 0, 1, (feats_group,))
    queries = jnp.concatenate([ours, swap_core(theirs)], axis=0)
    mixed, state = attend_near(queries, near, seg_near, seg_near)
    attended, attended_ours, attended_away, lse = attend_far(queries, far, seg_near, seg_far, mixed, state)
    zero_row = jnp.zeros((features,), jnp.float32)
    rows = jnp.stack([gain_rows[1], shift_bias[5], shift_bias[4], shift_bias[6]] + [zero_row] * 4)
    (
        pack, output_low, out_ours, up_ours, branch_ours, att_ours, att_theirs, grad_resid, mid_sums, up_sums,
        grad_head_w, last,
    ) = middle(
        meta,
        attended_ours,
        swap_core(attended_away),
        position,
        w_out,
        w_up,
        w_down,
        up_bias[None],
        head_w,
        head_b[None],
        labels_own[:, None],
        rows,
    )

    grad_heads = jnp.concatenate([att_ours, swap_core(att_theirs)], axis=0)
    dq_far, dkv_far = attend_back(queries, far, grad_heads, attended, lse, seg_near, seg_far, jnp.bfloat16, att_ours)
    got_kv = swap_x(dkv_far)

    C, Y, X, Z = 0, 1, 2, 3
    places = pack_places(features, w_up.shape[1])
    got_pack = swap_core(once(pack, grad_heads))
    up_pair = ((up_ours, 0), (got_pack, places["up"]))
    down_pair = ((out_ours, 0), (got_pack, places["out"]))
    branch_pair = ((branch_ours, 0), (got_pack, places["branch"]))
    second_pair, active_pair, attended_pair = (
        ((pack, places[name]), (got_pack, places[name])) for name in ("second", "active", "attended")
    )
    unit = features // 8
    down_rows = w_down.shape[0] // 4
    up_wide = w_up.shape[1] // 4
    quarter = half // 2
    eighth = 3 * half // 4
    first_pieces, before = [], dkv_far
    for piece in range(2):
        up_piece, down_piece = weight_parts(
            meta,
            [
                weight_task(
                    [(0, 0)], second_pair, up_pair, half, 1, lambda i, m, k=piece: k, up_wide, lambda m: 1 - m[Y]
                ),
                weight_task(
                    [(1, 0)], active_pair, down_pair, down_rows, 1,
                    lambda i, m, k=piece: 2 * ((m[Z] >> 1) ^ (1 - k)) + 1 - (m[Z] & 1), half, lambda m: 0,
                ),
            ],
            [(half, up_wide), (down_rows, half)],
            "weight_first",
            (before,),
        )
        first_pieces.append((up_piece, down_piece))
        before = down_piece
    (up_low, down_away), (up_high, down_home) = first_pieces
    got_up_low, got_down_away = swap_y(up_low), swap_z1(down_away)
    got_up_high, got_down_home = swap_y(up_high), swap_z1(down_home)
    dq, dkv = attend_back(queries, near, grad_heads, attended, lse, seg_near, seg_near, jnp.float32, down_home)

    def mixed_grad(part):
        piece = slice(part * frames, (part + 1) * frames)
        return jnp.concatenate(
            [
                dq[piece] + dq_far[piece],
                dkv[0, piece] + got_kv[0, piece].astype(jnp.float32),
                dkv[1, piece] + got_kv[1, piece].astype(jnp.float32),
            ],
            axis=1,
        ).astype(jnp.bfloat16)

    grad_theirs = mixed_grad(1)
    grad_got = swap_core(grad_theirs)
    grad_ours = mixed_grad(0)
    position_ours, position_theirs, first_sums = unmix_rows(
        meta, grad_ours, grad_got, w_qkv, position, grad_resid, gain_rows[0:1], (got_up_low, got_down_away)
    )
    grad_position, grad_conv, edge, own_part, to_x, to_y, to_xy, conv_bias = conv_grad_rows(
        meta, position_ours, swap_core(position_theirs), slope, (got_up_high, got_down_home)
    )
    grad_rim = rimmed(grad_conv, swap_x(edge))
    grad_group = grouped(own_part, swap_x(to_x), swap_y(to_y), swap_xy(to_xy))

    x_bit, y_bit = (lambda m: m[X]), (lambda m: m[Y])
    own_sums, got_sums = (jnp.sum(item.astype(jnp.float32), axis=0, keepdims=True) for item in (grad_ours, grad_got))
    rest_loss, digits = last[1, 0], []
    for power in LOSS_POWERS:
        digit = jnp.floor(rest_loss / 8.0**power)
        digits.append(digit)
        rest_loss = rest_loss - digit * 8.0**power
    digits.append(rest_loss)
    final = jnp.concatenate(
        [last[0, :VOCAB], jnp.stack(digits), jnp.zeros((unit - VOCAB - len(digits),), jnp.float32)]
    )
    small = small_sums(
        meta, grad_head_w, mid_sums, first_sums, conv_bias, own_sums, got_sums, up_sums[:, 0].reshape(8, 1, -1), final[None]
    )

    normed_pair = ((normed, 0), (got_normed, 0))
    qkv_pair = ((grad_ours, 0), (grad_theirs, 0))
    a_first, b_first = weight_parts(
        meta,
        [
            weight_task([(0, 0)], normed_pair, qkv_pair, features, 1, lambda i, m: 0, eighth, lambda m: 1 - m[Y]),
            weight_task(
                [(1, 2 * eighth)], normed_pair, qkv_pair, unit, 4, lambda i, m: 2 * i + 1 - m[X], 2 * eighth, lambda m: 1
            ),
            weight_task(
                [(1, 0)], attended_pair, branch_pair, unit, 4, lambda i, m: 2 * i + 1 - m[X], half, lambda m: 0, joint=True
            ),
            weight_task([(1, half)], ((small, 0),), None, unit, 4, lambda i, m: 2 * i + 1 - m[X], 128, None, joint=True),
        ],
        [(features, eighth), (half, 4 * eighth)],
        "weight_qkv_first",
        (grad_conv,),
    )
    got_a, got_b = swap_y(a_first), swap_x(b_first)
    conv_send, conv_kept = grouped_conv_weight(
        feats_group, seg_pair, grad_group.reshape(-1, 128), rise, z, (a_first, grad_rim)
    )
    conv_got = swap_z1(conv_send)
    up_send, up_kept, down_send, down_kept = weight_parts(
        meta,
        [
            weight_task(
                [(0, 0), (1, 0)], second_pair, up_pair, half, 1, lambda i, m: 0, up_wide, lambda m: m[Y],
                got_up_low, lambda i, m: (0, 0), "rows", lambda m: m[Z] & 1, 2 * unit,
            ),
            weight_task(
                [(0, 0), (1, 0)], second_pair, up_pair, half, 1, lambda i, m: 1, up_wide, lambda m: m[Y],
                got_up_high, lambda i, m: (0, 0), "rows", lambda m: m[Z] & 1, 2 * unit, 1,
            ),
            weight_task(
                [(2, 0), (3, 0)], active_pair, down_pair, down_rows, 1,
                lambda i, m: 2 * (1 - (m[Z] >> 1)) + (m[Z] & 1), half, lambda m: 0, got_down_away, lambda i, m: (0, 0),
                "rows", x_bit, down_rows // 2,
            ),
            weight_task(
                [(2, 0), (3, 0)], active_pair, down_pair, down_rows, 1,
                lambda i, m: 2 * (m[Z] >> 1) + (m[Z] & 1), half, lambda m: 0, got_down_home, lambda i, m: (0, 0),
                "rows", x_bit, down_rows // 2, 1,
            ),
        ],
        [(half, up_wide), (half, up_wide), (down_rows, half), (down_rows, half)],
        "weight_second",
        (conv_send,),
    )
    up_got, down_got = swap_z1(up_send), swap_x(down_send)
    low_z, high_z = (lambda m: m[Z] & 1), (lambda m: m[Z] >> 1)

    def view(values, *lead):
        return values.reshape(lead + (-1, values.shape[-1]))

    conv_left = grouped_conv(grad_rim, seg_ext, conv_weight, grad_position, 4 * c, rise, True, 0, 2, (up_kept,))[0]

    conv_send, conv_kept = folds(
        meta,
        [fold_item(conv_kept[:, None], [conv_got[:, None]], 0, high_z, (0, 0, 1), (1, 0, 1))],
        [(1, 256, KERNEL * 8)] * 2,
        "fold_taps",
        (conv_left,),
    )
    conv_got = swap_z2(conv_send)
    a_send, b_send, qkv_kept = weight_parts(
        meta,
        [
            weight_task(
                [(0, 0), (2, 0)], normed_pair, qkv_pair, features, 1, lambda i, m: 0, eighth, lambda m: m[Y],
                got_a, lambda i, m: (0, 0), "rows", x_bit, unit,
            ),
            weight_task(
                [(1, 0), (2, eighth)], normed_pair, qkv_pair, unit, 4, lambda i, m: 2 * i + m[X], 2 * eighth, lambda m: 1,
                got_b, lambda i, m: (i, 1), "columns", y_bit,
            ),
            weight_task(
                [(1, eighth), (2, 2 * eighth)], attended_pair, branch_pair, unit, 4, lambda i, m: 2 * i + m[X], half,
                lambda m: 0, got_b, lambda i, m: (i, 0), "columns", y_bit, joint=True,
            ),
            weight_task(
                [(1, eighth + quarter), (2, 2 * eighth + quarter)], ((small, 0),), None, unit, 4,
                lambda i, m: 2 * i + m[X], 128, None, got_b, lambda i, m: (i, half // 128), joint=True,
            ),
        ],
        [(half, eighth), (half, eighth + quarter + 128), (half, 2 * eighth + quarter + 128)],
        "weight_qkv_second",
        (conv_kept,),
    )
    a_got, b_got = swap_x(a_send), swap_y(b_send)
    conv_right = grouped_conv(
        grad_rim, seg_ext, conv_weight, grad_position, 4 * c, rise, True, 2, 2, (qkv_kept,)
    )[0]
    wide = 2 * eighth + quarter + 128
    x_send, up_kept, qkv_kept, down_send, down_kept, conv_send, conv_kept, qkv_send = folds(
        meta,
        [
            fold_item(view(up_kept, 2, 2), [view(up_got, 2, 2)], 1, x_bit, (0, 0, 1), (1, 0, 1)),
            fold_item(view(qkv_kept, 2, 2), [view(a_got, 2, 2), view(b_got, 2, 2)], 1, low_z, (7, 0, 1), (2, 0, 1)),
            fold_item(view(down_kept, 2, 1), [view(down_got, 2, 1)], None, y_bit, (3, 0, 1), (4, 0, 1)),
            fold_item(view(conv_kept, 2, 1), [view(conv_got, 2, 1)], 0, x_bit, (5, 0, 1), (6, 0, 1)),
        ],
        [(2, unit, up_wide)] * 2 + [(2, unit, wide)] + [(2, down_rows // 2, quarter)] * 2
        + [(1, 128, KERNEL * 8)] * 2 + [(2, unit, wide)],
        "fold_first",
        (conv_right,),
    )
    qkv_got, up_got, down_got, conv_got = swap_z1(qkv_send), swap_x(x_send), swap_y(down_send), swap_x(conv_send)
    shard = ordered(x, conv_kept, conv_got, 0)
    shard = jnp.concatenate([shard, swap_y(shard)], axis=0)
    conv_input = jnp.concatenate([once(conv_left, x_send), conv_right], axis=1)
    away = swap_core(take(conv_input, 1 - c, frames, 0))
    back = jnp.concatenate([ordered(c, take(conv_input, c, frames, 0), away, 1), output_low], axis=1)
    qkv_send, qkv_kept, pair_send, pair_kept = folds(
        meta,
        [
            fold_item(qkv_kept[:, None], [qkv_got[:, None]], 0, high_z, (0, 0, 1), (1, 0, 1)),
            fold_item(up_kept[:, None], [up_got[:, None]], 0, high_z, (2, 0, 1), (3, 0, 1)),
            fold_item(down_kept[:, None], [down_got[:, None]], 0, lambda m: 1, (2, up_wide, 4), (3, up_wide, 4)),
        ],
        [(1, unit, wide)] * 2 + [(1, unit, 2 * up_wide)] * 2,
        "fold_second",
        (),
    )
    qkv_got, pair_got = swap_z2(qkv_send), swap_z2(pair_send)
    grad_conv_weight = flip_columns(meta, shard, swap_core(shard))

    def add(kept, got):
        return (kept.astype(jnp.float32) + got.astype(jnp.float32)).astype(jnp.bfloat16)

    def spread(shard, *earlier):
        shard = jnp.concatenate([shard, once(swap_y(shard), *earlier)], axis=0)
        return shard, swap_core(shard)

    pair_sum, qkv_sum = add(pair_kept, pair_got), add(qkv_kept, qkv_got)
    back = from_rows(once(back, pair_sum, qkv_sum), z)
    grad_w_up, grad_w_down = finish_pair(meta, *spread(pair_sum, grad_conv_weight), w_down.shape[0] // 8, ())
    qkv_own, qkv_other = spread(qkv_sum)
    grad_w_qkv, grad_w_out = finish_qkv(meta, qkv_own, qkv_other, half, (grad_w_up,))
    total = qkv_own[0, :, wide - 128 :].astype(jnp.float32) + qkv_other[0, :, wide - 128 :].astype(jnp.float32)
    back = [once(item, grad_w_up, grad_w_qkv)[None] for item in back]
    back = ordered(x, back[0], back[1], 0)
    grad_feats, layer_out = back[:, :, :features], back[:, :, features:]
    v = VOCAB
    powers = jnp.array([8.0**power for power in LOSS_POWERS] + [1.0], jnp.float32)
    loss = jnp.sum(total[v : v + len(LOSS_POWERS) + 1, v + 13] * powers) / (tokens * 32)
    gain_part = jnp.stack([total[:, v + 4], total[:, v]], axis=1)
    bias_part = jnp.stack([total[:, v + k] for k in (6, 5, 7, 8, 1, 2, 3)], axis=1)
    return (
        layer_out,
        loss,
        grad_feats.astype(jnp.float32),
        grad_conv_weight,
        grad_w_qkv,
        grad_w_out,
        grad_w_up,
        grad_w_down,
        total[:, :v],
        total[:v, v + 13],
        gain_part,
        bias_part,
        total[:, v + 9 : v + 13].T.reshape(-1),
    )


def split_solution(mesh):
    fine = Mesh(mesh.devices.reshape(2, 2, 4, 2), AXES)
    rows, parts = ("y", "c"), ("z", "x")
    return jax.shard_map(
        split_body,
        mesh=fine,
        in_specs=(P(rows, parts, None), P(rows, None), P(rows, parts)) + (P(),) * 10,
        out_specs=(
            P(rows, parts, None),
            P(),
            P(rows, parts, None),
            P(parts, None),
            P(parts, None),
            P(parts, None),
            P(parts, None),
            P(parts, None),
            P(parts, None),
            P(),
            P(parts, None),
            P(parts, None),
            P(parts),
        ),
        check_vma=False,
    )


def solution(mesh):
    if mesh.shape["dp"] == 4 and mesh.shape["seq"] == 8:
        return split_solution(mesh)
    return whole_solution(mesh)
```
